32 devices in a mesh: dp: 8 (over z, x), pix: 4 (over y, core).
Axes of the slice: x: 2, y: 2, z: 4, core: 2. Of those that a mesh axis runs over, the one named last changes fastest.
Arguments:
- images: bfloat16 [8, 32, 32, 1024], P('dp', 'pix'), may hold values from -6 to 6
- style_codes: bfloat16 [8, 512], P('dp'), may hold values from -6 to 6
- labels: int32 [8], P('dp'), may hold values from 0 to 999
- token_ids: int32 [8, 77], P('dp'), may hold values from 0 to 24703
- penalty_mask: int32 [8], P('dp'), may hold values 0 or 1
- class_table: bfloat16 [1000, 512], replicated, may hold values from -6 to 6
- text_table: bfloat16 [24704, 768], replicated, may hold values from -6 to 6
- conv_bank: bfloat16 [2, 3, 3, 1024, 1024], P(None, None, None, 'dp', 'pix'), may hold values from -0.0625 to 0.0625
- select_weight: bfloat16 [512, 2], replicated, may hold values from -0.25 to 0.25
- modulation: bfloat16 [512, 1024], replicated, may hold values from -0.125 to 0.125
- rgb_modulation: bfloat16 [512, 1024], replicated, may hold values from -0.125 to 0.125
- w_query: bfloat16 [1024, 1024], P('dp'), may hold values from -0.1875 to 0.1875
- w_key: bfloat16 [1024, 1024], P('dp'), may hold values from -0.1875 to 0.1875
- w_value: bfloat16 [1024, 1024], P('dp'), may hold values from -0.1875 to 0.1875
- w_out: bfloat16 [1024, 1024], P('dp'), may hold values from -0.375 to 0.375
- c_query: bfloat16 [1024, 1024], P('dp'), may hold values from -0.1875 to 0.1875
- c_key: bfloat16 [768, 1024], P('dp'), may hold values from -0.21875 to 0.21875
- c_value: bfloat16 [768, 1024], P('dp'), may hold values from -0.21875 to 0.21875
- c_out: bfloat16 [1024, 1024], P('dp'), may hold values from -0.75 to 0.75
- gain_self: float32 [1024], replicated, may hold values from 0.5 to 1.5
- gain_cross: float32 [1024], replicated, may hold values from 0.5 to 1.5
- rgb_weight: bfloat16 [1024, 3], replicated, may hold values from -0.1875 to 0.1875
- out_cotangent: bfloat16 [8, 32, 32, 1024], P('dp', 'pix'), may hold values from -6 to 6
- rgb_cotangent: float32 [8, 3, 32, 32], P('dp', None, 'pix'), may hold values from -6 to 6
Outputs:
- output: float32 [8, 32, 32, 1024], P('dp', 'pix')
- rgb_image: float32 [8, 3, 32, 32], P('dp', None, 'pix')
- grad_image: float32 [8, 32, 32, 1024], P('dp', 'pix')
- grad_style: float32 [8, 512], P('dp')
- grad_class_table: float32 [1000, 512], replicated
- grad_conv_bank: float32 [2, 3, 3, 1024, 1024], P(None, None, None, 'dp', 'pix')
- grad_select_weight: float32 [512, 2], replicated
- grad_modulation: float32 [512, 1024], replicated
- grad_rgb_modulation: float32 [512, 1024], replicated
- grad_w_query: float32 [1024, 1024], P('dp')
- grad_w_key: float32 [1024, 1024], P('dp')
- grad_w_value: float32 [1024, 1024], P('dp')
- grad_w_out: float32 [1024, 1024], P('dp')
- grad_c_query: float32 [1024, 1024], P('dp')
- grad_c_key: float32 [768, 1024], P('dp')
- grad_c_value: float32 [768, 1024], P('dp')
- grad_c_out: float32 [1024, 1024], P('dp')
- grad_gain_self: float32 [1024], replicated
- grad_gain_cross: float32 [1024], replicated
- grad_rgb_weight: float32 [1024, 3], replicated
The draws below stay inside these ranges and needn't reach their ends.
All inputs are finite; a program needn't handle non-finite values. No bound on the sum of `penalty_mask` on one device may be relied on, other than what follows from the above.
Results may differ from the reference program's by a relative error of at most 0.025.
The reference program's roundings to bfloat16 on the way count: a program that leaves them out, or rounds other values in their place, can miss the bound.
Values may be sent and summed in bfloat16 or wider, within the bound.
A program may use at most 320 MiB of HBM per device.

```python
import math
from functools import partial
import jax
import jax.numpy as jnp
import numpy as np
from jax import lax

D = 1024
STYLE = 512
HEADS = 16
CTEXT = 768
TEXT = 77
VOCAB = 24704
CLASSES = 1000
KERN = 2
IMG = 32
SAMPLES = 8


def with_ends(result, rng, smallest, largest):
    longest = result.shape.index(max(result.shape))
    spots = []
    for shift in (0, 1):
        where = [jax.random.randint(jax.random.fold_in(rng, axis), (), 0, length) for axis, length in enumerate(result.shape)]
        where[longest] = (where[longest] + shift) % result.shape[longest]
        spots.append(tuple(where))
    return result.at[spots[0]].set(smallest).at[spots[1]].set(largest)


def levels(rng, dims, cuts, least, high):
    def one(dim, shards_of):
        steps = jax.random.uniform(jax.random.fold_in(jax.random.fold_in(rng, 6), dim), (shards_of,), jnp.float32, least / len(cuts), high / len(cuts))
        return jnp.repeat(jnp.exp(steps), dims[dim] // shards_of).reshape((-1,) + (1,) * (len(dims) - dim - 1))

    level = one(*cuts[0])
    for cut in cuts[1:]:
        level = level * one(*cut)
    return level


def rank_table(count, lean):
    weights = [(1 << 20) // math.isqrt(standing ** lean) + 1 for standing in range(1, count + 1)]
    deviation = 1 + sum(weights) // (1 << 30)
    return np.cumsum(np.array([max(1, weight // deviation) for weight in weights]))


def ranked_ids(key, dims, number_of, slope):
    grid = rank_table(number_of, slope)
    lot = jax.random.randint(jax.random.fold_in(key, 1), dims, 0, int(grid[number_of - 1]))
    grade = jnp.searchsorted(jnp.asarray(grid, jnp.int32), lot, side="right")
    return jax.random.permutation(jax.random.fold_in(key, 2), number_of)[grade].astype(jnp.int32)


def gaussian(rng, shape, scale, most, shards=(), held_as=jnp.bfloat16):
    drawn = jax.random.normal(rng, shape, jnp.float32) * scale
    if len(shards) > 0:
        drawn = levels(rng, shape, shards, -0.22, 0.18) * drawn
    return jnp.clip(drawn, min=-most, max=most).astype(held_as)


def setup_inputs(seed: int = 0) -> dict:
    streams_of = jax.random.split(jax.random.key(seed), 25)
    images = gaussian(streams_of[0], (SAMPLES, IMG, IMG, D), 1.0, 6.0, ((0, 8), (1, 4)))
    style_codes = gaussian(streams_of[1], (SAMPLES, STYLE), 1.0, 6.0, ((0, 8),))
    labels = with_ends(jax.random.randint(streams_of[2], (SAMPLES,), 0, CLASSES), jax.random.fold_in(streams_of[2], 1), 0, CLASSES - 1).astype(jnp.int32)
    token_ids = with_ends(ranked_ids(streams_of[3], (SAMPLES, TEXT), VOCAB, 2), jax.random.fold_in(streams_of[3], 3), 0, VOCAB - 1).astype(jnp.int32)
    penalty_mask = with_ends((jax.random.randint(streams_of[4], (SAMPLES,), 0, 2) < 1).astype(jnp.int32), jax.random.fold_in(streams_of[4], 1), 0, 1)
    class_table = gaussian(streams_of[5], (CLASSES, STYLE), 1.0, 6.0)
    text_table = gaussian(streams_of[6], (VOCAB, CTEXT), 1.0, 6.0)
    conv_bank = gaussian(streams_of[7], (KERN, 3, 3, D, D), (9 * D) ** -0.5, 0.0625, ((3, 8), (4, 4)))
    select_weight = gaussian(streams_of[8], (STYLE, KERN), STYLE ** -0.5, 0.25)
    modulation = gaussian(streams_of[9], (STYLE, D), (4 * STYLE) ** -0.5, 0.125)
    rgb_modulation = gaussian(streams_of[10], (STYLE, D), (4 * STYLE) ** -0.5, 0.125)
    w_query = gaussian(streams_of[11], (D, D), D ** -0.5, 0.1875, ((0, 8),))
    w_key = gaussian(streams_of[12], (D, D), D ** -0.5, 0.1875, ((0, 8),))
    w_value = gaussian(streams_of[13], (D, D), D ** -0.5, 0.1875, ((0, 8),))
    w_out = gaussian(streams_of[14], (D, D), (D // 4) ** -0.5, 0.375, ((0, 8),))
    c_query = gaussian(streams_of[15], (D, D), D ** -0.5, 0.1875, ((0, 8),))
    c_key = gaussian(streams_of[16], (CTEXT, D), CTEXT ** -0.5, 0.21875, ((0, 8),))
    c_value = gaussian(streams_of[17], (CTEXT, D), CTEXT ** -0.5, 0.21875, ((0, 8),))
    c_out = gaussian(streams_of[18], (D, D), (D // 16) ** -0.5, 0.75, ((0, 8),))
    gain_self = jnp.clip(1.0 + 0.1 * jax.random.normal(streams_of[19], (D,), jnp.float32), 0.5, 1.5)
    gain_cross = jnp.clip(1.0 + 0.1 * jax.random.normal(streams_of[20], (D,), jnp.float32), 0.5, 1.5)
    rgb_weight = gaussian(streams_of[21], (D, 3), D ** -0.5, 0.1875)
    out_cotangent = gaussian(streams_of[22], (SAMPLES, IMG, IMG, D), 1.0, 6.0, ((0, 8), (1, 4)))
    rgb_cotangent = gaussian(streams_of[23], (SAMPLES, 3, IMG, IMG), 1.0, 6.0, ((0, 8), (2, 4)), jnp.float32)
    return dict(images=images, style_codes=style_codes, labels=labels, token_ids=token_ids, penalty_mask=penalty_mask, class_table=class_table, text_table=text_table, conv_bank=conv_bank, select_weight=select_weight, modulation=modulation, rgb_modulation=rgb_modulation, w_query=w_query, w_key=w_key, w_value=w_value, w_out=w_out, c_query=c_query, c_key=c_key, c_value=c_value, c_out=c_out, gain_self=gain_self, gain_cross=gain_cross, rgb_weight=rgb_weight, out_cotangent=out_cotangent, rgb_cotangent=rgb_cotangent)


penalty_weight = 1.0
highest = lax.Precision.HIGHEST

@jax.custom_vjp
def low(v):
    return lax.optimization_barrier(v.astype(jnp.bfloat16)).astype(jnp.float32)

@jax.custom_vjp
def low_back(v):
    return v

def low_keep(v):
    return (low(v), None)

def low_pass(kept, grad):
    return (grad,)

def back_keep(v):
    return (v, None)

def back_low(kept, grad):
    return (low(grad),)
low.defvjp(low_keep, low_pass)
low_back.defvjp(back_keep, back_low)

def rms_norm(hidden, gain):
    return hidden * lax.rsqrt(lax.optimization_barrier(jnp.mean(hidden * hidden, -1, keepdims=True)) + 1e-06) * gain

def style_path(onehot, style_in, class_rows, select_mat, modul_mat, rgb_mod_mat):
    styled = style_in + jnp.dot(onehot, class_rows, precision=highest)
    mixing = jax.nn.softmax(jnp.dot(styled, select_mat, precision=highest), -1)
    scaling = jnp.dot(styled, modul_mat, precision=highest) + 1.0
    rgb_scale = jnp.dot(styled, rgb_mod_mat, precision=highest) + 1.0
    return (mixing, scaling, rgb_scale)

def sample_block(block_mats, item):
    bank, query_mat, key_mat, value_mat, out_mat, cquery_mat, ckey_mat, cvalue_mat, cout_mat, gain_one, gain_two, rgb_mat = block_mats
    image, mixing, scaling, rgb_scale, text_rows = item
    height, width, channels = image.shape
    length = height * width
    head_dim = channels // HEADS
    score_scale = head_dim ** (-0.5)
    selected = jnp.tensordot(mixing, bank, axes=1)
    modded = selected * scaling[None, None, :, None]
    kernel = low(modded * lax.rsqrt(lax.optimization_barrier(jnp.sum(modded * modded, axis=(0, 1, 2))) + 1e-08))
    conv = lax.conv_general_dilated(image[None], kernel, (1, 1), 'SAME', dimension_numbers=('NHWC', 'HWIO', 'NHWC'), precision=highest)[0]
    conv = low_back(conv)
    hidden_one = (image + jax.nn.silu(conv)).reshape(length, channels)
    normed_one = low(rms_norm(hidden_one, gain_one))

    def project(source, matrix):
        return low(low_back(jnp.dot(source, matrix, precision=highest))).reshape(-1, HEADS, head_dim)
    query = project(normed_one, query_mat)
    key = project(normed_one, key_mat)
    value = project(normed_one, value_mat)
    key_norm = lax.optimization_barrier(jnp.sum(key * key, -1))
    scores = score_scale * (2.0 * jnp.einsum('qhd,khd->hqk', query, key, precision=highest) - key_norm.T[:, None, :])
    scores = low_back(scores)
    weights = low(jax.nn.softmax(scores, -1))
    attended = jnp.einsum('hqk,khd->qhd', weights, value, precision=highest).reshape(length, channels)
    attended = low(low_back(attended))
    hidden_two = hidden_one + low_back(jnp.dot(attended, out_mat, precision=highest))
    normed_two = low(rms_norm(hidden_two, gain_two))
    cross_query = project(normed_two, cquery_mat)
    cross_key = low(jnp.dot(text_rows, ckey_mat, precision=highest)).reshape(-1, HEADS, head_dim)
    cross_value = low(jnp.dot(text_rows, cvalue_mat, precision=highest)).reshape(-1, HEADS, head_dim)
    cross_scores = low_back(score_scale * jnp.einsum('qhd,khd->hqk', cross_query, cross_key, precision=highest))
    cross_weights = low(jax.nn.softmax(cross_scores, -1))
    cross_out = jnp.einsum('hqk,khd->qhd', cross_weights, cross_value, precision=highest).reshape(length, channels)
    cross_out = low(low_back(cross_out))
    hidden_three = hidden_two + low_back(jnp.dot(cross_out, cout_mat, precision=highest))
    mixed = low(hidden_three * rgb_scale)
    rgb_flat = jnp.dot(mixed, rgb_mat, precision=highest)
    return (hidden_three.reshape(height, width, channels), rgb_flat.T.reshape(3, height, width))

def reference(images, style_codes, labels, token_ids, penalty_mask, class_table, text_table, conv_bank, select_weight, modulation, rgb_modulation, w_query, w_key, w_value, w_out, c_query, c_key, c_value, c_out, gain_self, gain_cross, rgb_weight, out_cotangent, rgb_cotangent):
    floats = jnp.float32
    onehot = (labels[:, None] == jnp.arange(CLASSES, dtype=jnp.int32)[None, :]).astype(floats)
    text_rows = jnp.take(text_table, token_ids, axis=0).astype(floats)
    style_mats = (select_weight.astype(floats), modulation.astype(floats), rgb_modulation.astype(floats))
    block_mats = (conv_bank.astype(floats), w_query.astype(floats), w_key.astype(floats), w_value.astype(floats), w_out.astype(floats), c_query.astype(floats), c_key.astype(floats), c_value.astype(floats), c_out.astype(floats), gain_self.astype(floats), gain_cross.astype(floats), rgb_weight.astype(floats))

    def forward(image_in, style_in, table_in, style_params, block_params):
        mixing, scaling, rgb_scale = style_path(onehot, style_in, table_in, style_params[0], style_params[1], style_params[2])
        stepper = jax.checkpoint(partial(sample_block, block_params))
        return lax.map(stepper, (image_in, mixing, scaling, rgb_scale, text_rows))
    (hidden, rgb_image), backward = jax.vjp(forward, images.astype(floats), style_codes.astype(floats), class_table.astype(floats), style_mats, block_mats)
    rgb_grad = rgb_cotangent + penalty_weight * penalty_mask.astype(floats)[:, None, None, None] * rgb_image
    grad_image, grad_style, grad_table, grad_style_mats, grad_block = backward((out_cotangent.astype(floats), rgb_grad))
    return (hidden, rgb_image, grad_image, grad_style, grad_table, grad_block[0], grad_style_mats[0], grad_style_mats[1], grad_style_mats[2], grad_block[1], grad_block[2], grad_block[3], grad_block[4], grad_block[5], grad_block[6], grad_block[7], grad_block[8], grad_block[9], grad_block[10], grad_block[11])
```

```python
from functools import partial

import jax
import jax.numpy as jnp
from jax import lax
from jax.experimental import pallas as pl
from jax.experimental.pallas import tpu as pltpu
from jax.sharding import PartitionSpec as P

HEAD_DIM = 64
PIX = 4
MESH = pl.DeviceIdType.MESH
VMEM_LIMIT = 60 * 1024 * 1024

penalty_weight = 1.0
highest = lax.Precision.HIGHEST
floats = jnp.float32
halves = jnp.bfloat16

ANY = pl.BlockSpec(memory_space=pl.ANY)
VMEM = pl.BlockSpec(memory_space=pltpu.VMEM)
DMA = pltpu.SemaphoreType.DMA


def params(collective_id):
    return pltpu.CompilerParams(
        collective_id=collective_id, has_side_effects=True, vmem_limit_bytes=VMEM_LIMIT
    )


def remote(src, dst, send_sem, recv_sem, where):
    return pltpu.make_async_remote_copy(
        src_ref=src,
        dst_ref=dst,
        send_sem=send_sem,
        recv_sem=recv_sem,
        device_id=where,
        device_id_type=MESH,
    )


def greet(count, others):
    row, col = lax.axis_index("dp"), lax.axis_index("pix")
    barrier = pltpu.get_barrier_semaphore()

    def one(step, carry):
        pl.semaphore_signal(
            barrier, inc=1, device_id=(lax.rem(row + step, count), col), device_id_type=MESH
        )
        return carry

    if count > 1:
        lax.fori_loop(1, count, one, 0)
    for other in others:
        pl.semaphore_signal(barrier, inc=1, device_id=other, device_id_type=MESH)
    pl.semaphore_wait(barrier, count - 1 + len(others))


def loop(count, body):
    def step(i, carry):
        body(i)
        return carry

    lax.fori_loop(0, count, step, 0)


def flip(index, bit):
    part = lax.rem(lax.div(index, bit), 2)
    return index + bit - 2 * bit * part


def gather_kernel(
    count,
    style_ref,
    bank_ref,
    parts_ref,
    images_ref,
    kernel_ref,
    styles_ref,
    inverse_ref,
    squares,
    squares_in,
    local_sem,
    style_send,
    style_recv,
    square_send,
    square_recv,
    part_send,
    part_recv,
    core_send,
    core_recv,
    line_send,
    line_recv,
    pass_send,
    pass_recv,
):
    row, col = lax.axis_index("dp"), lax.axis_index("pix")
    near, far = flip(col, 1), flip(col, 2)
    depth = bank_ref.shape[2]
    greet(count, [(row, near), (row, far)])

    def style_copy(step):
        other = lax.rem(row + step, count)
        return remote(
            style_ref.at[other], styles_ref.at[row], style_send.at[step], style_recv.at[step], (other, col)
        )

    def square_copy(step):
        other = lax.rem(row + step, count)
        return remote(
            squares, squares_in.at[row], square_send.at[step], square_recv.at[step], (other, col)
        )

    def part_copy(step):
        other = lax.rem(row + step, count)
        return remote(
            parts_ref.at[other], images_ref.at[row, col], part_send.at[step], part_recv.at[step], (other, col)
        )

    def part_arrives(step):
        origin = lax.rem(row - step + count, count)
        remote(
            parts_ref.at[0], images_ref.at[origin, col], part_send.at[step], part_recv.at[step], (row, near)
        ).wait_recv()

    def core_copy(step):
        origin = lax.rem(row - step + count, count)
        block = images_ref.at[origin, col]
        return remote(block, block, core_send.at[step], core_recv.at[step], (row, near))

    def line_copy(step):
        origin = lax.rem(row - step + count, count)
        block = images_ref.at[origin, col]
        return remote(block, block, line_send.at[step], line_recv.at[step], (row, far))

    def pass_copy(step):
        origin = lax.rem(row - step + count, count)
        block = images_ref.at[origin, far]
        return remote(block, block, pass_send.at[step], pass_recv.at[step], (row, near))

    def core_arrives(step):
        origin = lax.rem(row - step + count, count)
        block = images_ref.at[origin, near]
        remote(block, block, core_send.at[step], core_recv.at[step], (row, near)).wait_recv()

    def line_arrives(step):
        origin = lax.rem(row - step + count, count)
        block = images_ref.at[origin, far]
        remote(block, block, line_send.at[step], line_recv.at[step], (row, far)).wait_recv()

    def pass_arrives(step):
        origin = lax.rem(row - step + count, count)
        block = images_ref.at[origin, flip(near, 2)]
        remote(block, block, pass_send.at[step], pass_recv.at[step], (row, near)).wait_recv()

    own = pltpu.make_async_copy(parts_ref.at[row], images_ref.at[row, col], local_sem)
    own.start()

    def send_all(step):
        style_copy(step).start()

    lax.fori_loop(1, count, lambda i, c: (send_all(i), c)[1], 0)
    lax.fori_loop(1, count, lambda i, c: (part_copy(i).start(), c)[1], 0)
    styles_ref[row] = style_ref[row]
    own.wait()
    line_copy(0).start()
    core_copy(0).start()

    def style_wait(step):
        origin = lax.rem(row - step + count, count)
        remote(
            style_ref.at[0], styles_ref.at[origin], style_send.at[step], style_recv.at[step], (row, near)
        ).wait_recv()

    lax.fori_loop(1, count, lambda i, c: (style_wait(i), c)[1], 0)

    def mixed_tap(sample, tap, column, first, second):
        total = first * bank_ref[0, tap].astype(floats) + second * bank_ref[1, tap].astype(floats)
        return total * column

    def factors(sample):
        block = styles_ref[sample]
        column = jnp.transpose(block)[:depth, 0:1]
        return column, block[1:2, 0:1], block[2:3, 0:1]

    def square_sum(sample):
        column, first, second = factors(sample)
        total = jnp.zeros((depth, bank_ref.shape[3]), floats)
        for tap in range(9):
            modded = mixed_tap(sample, tap, column, first, second)
            total = total + modded * modded
        squares[pl.ds(sample, 1), :] = jnp.sum(total, axis=0, keepdims=True)

    loop(count, square_sum)
    lax.fori_loop(1, count, lambda i, c: (square_copy(i).start(), c)[1], 0)
    squares_in[row] = squares[...]

    def relay(step):
        part_arrives(step)
        line_copy(step).start()
        core_copy(step).start()

    lax.fori_loop(1, count, lambda i, c: (relay(i), c)[1], 0)

    def square_wait(step):
        origin = lax.rem(row - step + count, count)
        remote(
            squares, squares_in.at[origin], square_send.at[step], square_recv.at[step], (row, near)
        ).wait_recv()

    lax.fori_loop(1, count, lambda i, c: (square_wait(i), c)[1], 0)
    inverse_ref[...] = lax.rsqrt(jnp.sum(squares_in[...], axis=0) + 1e-08)

    def forward(step):
        line_arrives(step)
        pass_copy(step).start()

    def make_kernel(sample):
        column, first, second = factors(sample)
        scale = inverse_ref[pl.ds(sample, 1), :]
        for tap in range(9):
            modded = mixed_tap(sample, tap, column, first, second)
            kernel_ref[sample, tap] = (modded * scale).astype(halves)
        forward(sample)

    loop(count, make_kernel)
    loop(count, core_arrives)
    loop(count, pass_arrives)
    lax.fori_loop(
        1,
        count,
        lambda i, c: (
            style_copy(i).wait_send(),
            square_copy(i).wait_send(),
            part_copy(i).wait_send(),
            c,
        )[3],
        0,
    )
    loop(count, lambda i: core_copy(i).wait_send())
    loop(count, lambda i: line_copy(i).wait_send())
    loop(count, lambda i: pass_copy(i).wait_send())


def gather_inputs(style_rows, bank, parts):
    count, rows, depth = parts.shape
    width = bank.shape[-1]
    sems = [DMA((count,)) for _ in range(12)]
    return pl.pallas_call(
        partial(gather_kernel, count),
        out_shape=(
            jax.ShapeDtypeStruct((count, PIX, rows, depth), halves),
            jax.ShapeDtypeStruct((count, 9, depth, width), halves),
            jax.ShapeDtypeStruct((count, 8, 128), floats),
            jax.ShapeDtypeStruct((count, width), floats),
        ),
        in_specs=[VMEM, VMEM, ANY],
        out_specs=(ANY, VMEM, VMEM, VMEM),
        scratch_shapes=[
            pltpu.VMEM((count, width), floats),
            pltpu.VMEM((count, count, width), floats),
            DMA,
        ]
        + sems,
        compiler_params=params(0),
        name="gather_inputs",
    )(style_rows, bank, parts)


def conv_kernel(
    count,
    width,
    images_ref,
    kernel_ref,
    own_ref,
    gain_ref,
    conv_ref,
    conv_own_ref,
    hidden_ref,
    normed_ref,
    image_buf,
    padded,
    total,
    pair_out,
    pair_in,
    line_out,
    line_in,
    block_out,
    block_in,
    image_sem,
    pair_send,
    pair_recv,
    line_send,
    line_recv,
    block_send,
    block_recv,
    norm_send,
    norm_recv,
):
    row, col = lax.axis_index("dp"), lax.axis_index("pix")
    groups = count // 2
    slots = pair_out.shape[0]
    side = lax.rem(row, 2)
    level = lax.div(row, 2)
    partner = flip(row, 1)
    near, far = flip(col, 1), flip(col, 2)
    cross = flip(near, 2)
    tokens, depth = image_buf.shape[1], image_buf.shape[2]
    channels = total.shape[1]
    rows = tokens // PIX
    halo = width

    barrier = pltpu.get_barrier_semaphore()

    def hello(step, carry):
        other = 2 * lax.rem(level + step, groups) + side
        pl.semaphore_signal(barrier, inc=1, device_id=(other, col), device_id_type=MESH)
        return carry

    lax.fori_loop(1, groups, hello, 0)
    for other in ((partner, col), (row, near), (row, far), (row, cross)):
        pl.semaphore_signal(barrier, inc=1, device_id=other, device_id_type=MESH)
    pl.semaphore_wait(barrier, groups - 1 + 4)

    def group_of(step):
        return lax.rem(level + 1 + step, groups)

    def sample_of(index):
        mine = lax.div(index, groups)
        group = group_of(lax.rem(index, groups))
        return 2 * group + jnp.where(mine == 1, side, 1 - side)

    def fetch(index):
        slot = lax.rem(index, 2)
        return pltpu.make_async_copy(
            images_ref.at[sample_of(index)], image_buf.at[slot], image_sem.at[slot]
        )

    zeros = jnp.zeros((3, halo, depth), halves)
    padded[:, 0:halo, :] = zeros
    padded[:, halo + tokens : halo + tokens + halo, :] = zeros
    fetch(0).start()
    place = lax.rem(lax.broadcasted_iota(jnp.int32, (tokens, depth), 0), width)

    def stage(index):
        fetch(index).wait()

        @pl.when(index + 1 < count)
        def _():
            fetch(index + 1).start()

        source = image_buf[lax.rem(index, 2)]
        wide = source.astype(floats)
        padded[1, halo : halo + tokens, :] = source
        before = jnp.where(place == 0, 0.0, pltpu.roll(wide, 1, 0))
        padded[0, halo : halo + tokens, :] = before.astype(halves)
        after = jnp.where(place == width - 1, 0.0, pltpu.roll(wide, tokens - 1, 0))
        padded[2, halo : halo + tokens, :] = after.astype(halves)

    def rows_of(sample, start):
        acc = jnp.zeros((rows, channels), floats)
        for a in range(3):
            for b in range(3):
                window = padded[b, pl.ds(pl.multiple_of(start + a * width, 16), rows), :]
                acc = acc + jnp.dot(
                    window, kernel_ref[sample, 3 * a + b], preferred_element_type=floats
                )
        return acc

    def pair_copy(step):
        return remote(
            pair_out.at[lax.rem(step, slots)],
            pair_in.at[step],
            pair_send.at[step],
            pair_recv.at[step],
            (partner, col),
        )

    def line_copy(step):
        group = group_of(step)
        return remote(
            line_out.at[lax.rem(step, slots)],
            line_in.at[step],
            line_send.at[step],
            line_recv.at[step],
            (2 * group + side, col),
        )

    def give(step):
        @pl.when(step >= slots)
        def _():
            pair_copy(step - slots).wait_send()

        stage(step)
        sample = sample_of(step)

        def chunk(i):
            start = pl.multiple_of(i * rows, rows)
            pair_out[lax.rem(step, slots), pl.ds(start, rows), :] = rows_of(sample, start).astype(
                halves
            )

        loop(PIX, chunk)
        pair_copy(step).start()

    loop(groups, give)

    def keep(step):
        @pl.when(step >= slots)
        def _():
            line_copy(step - slots).wait_send()

        stage(groups + step)
        sample = sample_of(groups + step)
        pair_copy(step).wait_recv()

        def chunk(i):
            start = pl.multiple_of(i * rows, rows)
            here = pl.ds(start, rows)
            line_out[lax.rem(step, slots), here, :] = (
                rows_of(sample, start) + pair_in[step, here, :].astype(floats)
            ).astype(halves)

        loop(PIX, chunk)
        line_copy(step).start()

    loop(groups - 1, keep)
    last = groups - 1
    stage(count - 1)

    def own_chunk(i):
        start = pl.multiple_of(i * rows, rows)
        total[pl.ds(start, rows), :] = rows_of(row, start)

    loop(PIX, own_chunk)
    pair_copy(last).wait_recv()
    loop(groups - 1, lambda i: line_copy(i).wait_recv())

    def block_copy(turn):
        target = (far, cross, near)[turn]
        return remote(
            block_out.at[turn], block_in.at[col], block_send.at[turn], block_recv.at[turn], (row, target)
        )

    def block_arrives(turn):
        origin = (far, cross, near)[turn]
        remote(
            block_out.at[turn], block_in.at[origin], block_send.at[turn], block_recv.at[turn], (row, near)
        ).wait_recv()

    for turn, target in enumerate((far, cross, near, col)):
        here = pl.ds(pl.multiple_of(target * rows, rows), rows)
        value = total[here, :] + pair_in[last, here, :].astype(floats)
        for i in range(groups - 1):
            value = value + line_in[i, here, :].astype(floats)
        rounded = value.astype(halves)
        conv_own_ref[here, :] = rounded
        if turn < 3:
            block_out[turn] = rounded
            block_copy(turn).start()
        else:
            block_in[col] = rounded
    for turn in range(3):
        block_arrives(turn)

    part = rows // 4

    def norm_rows(i):
        here = pl.ds(pl.multiple_of(i * part, part), part)
        for j in range(PIX):
            conv_ref[here, j * channels : (j + 1) * channels] = block_in[j, here, :]
        conv = conv_ref[here, :].astype(floats)
        hidden = own_ref[here, :].astype(floats) + conv * jax.nn.sigmoid(conv)
        hidden_ref[here, :] = hidden
        mean = jnp.mean(hidden * hidden, -1, keepdims=True)
        normed_ref[col, here, :] = (hidden * lax.rsqrt(mean + 1e-06) * gain_ref[...]).astype(halves)

    loop(4, norm_rows)
    mine, theirs = normed_ref.at[col], normed_ref.at[far]
    to_far = remote(mine, mine, norm_send.at[0], norm_recv.at[0], (row, far))
    to_near = remote(mine, mine, norm_send.at[1], norm_recv.at[1], (row, near))
    to_far.start()
    to_near.start()
    remote(mine, theirs, norm_send.at[0], norm_recv.at[0], (row, far)).wait_recv()
    onward = remote(theirs, theirs, norm_send.at[2], norm_recv.at[2], (row, near))
    onward.start()
    remote(mine, normed_ref.at[near], norm_send.at[1], norm_recv.at[1], (row, near)).wait_recv()
    remote(mine, normed_ref.at[cross], norm_send.at[2], norm_recv.at[2], (row, near)).wait_recv()
    to_far.wait_send()
    to_near.wait_send()
    onward.wait_send()
    for turn in range(3):
        block_copy(turn).wait_send()
    for step in range(max(0, groups - slots), groups):
        pair_copy(step).wait_send()
    for step in range(max(0, groups - 1 - slots), groups - 1):
        line_copy(step).wait_send()


def conv_forward(images_all, kernels, own, gain, width):
    count, tokens, depth = images_all.shape
    channels = kernels.shape[-1]
    rows, full = own.shape
    groups = count // 2
    slots = min(groups, 4)
    block = (tokens, channels)
    return pl.pallas_call(
        partial(conv_kernel, count, width),
        out_shape=(
            jax.ShapeDtypeStruct((rows, full), halves),
            jax.ShapeDtypeStruct((tokens, channels), halves),
            jax.ShapeDtypeStruct((rows, full), floats),
            jax.ShapeDtypeStruct((PIX, rows, full), halves),
        ),
        in_specs=[ANY, VMEM, VMEM, VMEM],
        out_specs=(VMEM, VMEM, VMEM, VMEM),
        scratch_shapes=[
            pltpu.VMEM((2, tokens, depth), halves),
            pltpu.VMEM((3, tokens + 2 * width, depth), halves),
            pltpu.VMEM(block, floats),
            pltpu.VMEM((slots,) + block, halves),
            pltpu.VMEM((groups,) + block, halves),
            pltpu.VMEM((slots,) + block, halves),
            pltpu.VMEM((max(groups - 1, 1),) + block, halves),
            pltpu.VMEM((3, rows, channels), halves),
            pltpu.VMEM((PIX, rows, channels), halves),
            DMA((2,)),
            DMA((groups,)),
            DMA((groups,)),
            DMA((groups,)),
            DMA((groups,)),
            DMA((3,)),
            DMA((3,)),
            DMA((3,)),
            DMA((3,)),
        ],
        compiler_params=params(1),
        name="conv_forward",
    )(images_all, kernels, own, gain.reshape(1, -1))


def peers(col):
    near, far = flip(col, 1), flip(col, 2)
    return near, far, flip(near, 2)


def greet_pixels(row, others):
    barrier = pltpu.get_barrier_semaphore()
    for other in others:
        pl.semaphore_signal(barrier, inc=1, device_id=(row, other), device_id_type=MESH)
    pl.semaphore_wait(barrier, len(others))


NT = (((1,), (1,)), ((), ()))
TN = (((0,), (0,)), ((), ()))


def mul_nt(a, b, precision=None):
    return lax.dot_general(a, b, NT, preferred_element_type=floats, precision=precision)


def mul_tn(a, b, precision=None):
    return lax.dot_general(a, b, TN, preferred_element_type=floats, precision=precision)


def mul(a, b):
    return jnp.dot(a, b, preferred_element_type=floats)


def attend_kernel(
    normed_ref,
    weight_ref,
    text_ref,
    text_weight_ref,
    query_ref,
    key_ref,
    value_ref,
    total_ref,
    attended_ref,
    text_out_ref,
    block_out,
    key_norm,
    block_send,
    block_recv,
    text_send,
    text_recv,
):
    row, col = lax.axis_index("dp"), lax.axis_index("pix")
    near, far, cross = peers(col)
    targets = (far, cross, near)
    greet_pixels(row, targets)
    rows = normed_ref.shape[1]
    width = query_ref.shape[1]
    heads = width // HEAD_DIM
    score_scale = HEAD_DIM ** (-0.5)

    for j in range(2):
        here = slice(j * width, (j + 1) * width)
        text_out_ref[col, :, here] = mul(text_ref[...], text_weight_ref[:, here]).astype(halves)

    def text_copy(turn):
        block = text_out_ref.at[col]
        return remote(block, block, text_send.at[turn], text_recv.at[turn], (row, targets[turn]))

    for turn in range(3):
        text_copy(turn).start()

    def project(i):
        source = normed_ref[i]
        here = pl.ds(pl.multiple_of(i * rows, rows), rows)
        for j, out in enumerate((query_ref, key_ref, value_ref)):
            out[here, :] = mul(source, weight_ref[:, j * width : (j + 1) * width]).astype(halves)

    loop(PIX, project)
    ones = jnp.ones((8, HEAD_DIM), floats)
    for h in range(heads):
        key = key_ref[:, h * HEAD_DIM : (h + 1) * HEAD_DIM].astype(floats)
        key_norm[h] = mul_nt(ones, key * key, highest)

    def attend(target, store):
        here = pl.ds(pl.multiple_of(target * rows, rows), rows)
        for h in range(heads):
            lanes = slice(h * HEAD_DIM, (h + 1) * HEAD_DIM)
            inner = mul_nt(query_ref[here, lanes], key_ref[:, lanes])
            scores = score_scale * (2.0 * inner - key_norm[h, 0:1, :])
            largest = jnp.max(scores, -1, keepdims=True)
            expanded = jnp.exp(scores - largest)
            summed = jnp.sum(expanded, -1, keepdims=True)
            weights = (expanded * (1.0 / summed)).astype(halves)
            store(lanes, mul(weights, value_ref[:, lanes]).astype(halves))
            total_ref[here, h : h + 1] = largest + jnp.log(summed)

    def block_copy(turn):
        return remote(
            block_out.at[turn],
            attended_ref.at[col],
            block_send.at[turn],
            block_recv.at[turn],
            (row, targets[turn]),
        )

    def turn_body(turn):
        target = jnp.where(turn == 0, far, jnp.where(turn == 1, cross, jnp.where(turn == 2, near, col)))

        def store(lanes, result):
            block_out[turn, :, lanes] = result

        attend(target, store)
        for k in range(3):

            @pl.when(turn == k)
            def _(k=k):
                block_copy(k).start()

    loop(4, turn_body)
    attended_ref[col] = block_out[3]
    for turn in range(3):
        remote(
            block_out.at[turn],
            attended_ref.at[targets[turn]],
            block_send.at[turn],
            block_recv.at[turn],
            (row, near),
        ).wait_recv()
        block = text_out_ref.at[targets[turn]]
        remote(block, block, text_send.at[turn], text_recv.at[turn], (row, near)).wait_recv()
    for turn in range(3):
        block_copy(turn).wait_send()
        text_copy(turn).wait_send()


def attend_forward(normed, weights, text, text_weights):
    count, rows, full = normed.shape
    tokens, width = count * rows, weights.shape[1] // 3
    heads = width // HEAD_DIM
    flat = jax.ShapeDtypeStruct((tokens, width), halves)
    return pl.pallas_call(
        attend_kernel,
        out_shape=(
            flat,
            flat,
            flat,
            jax.ShapeDtypeStruct((tokens, 128), floats),
            jax.ShapeDtypeStruct((PIX, rows, width), halves),
            jax.ShapeDtypeStruct((PIX, text.shape[0], 2 * width), halves),
        ),
        in_specs=[VMEM] * 4,
        out_specs=(VMEM,) * 6,
        scratch_shapes=[
            pltpu.VMEM((4, rows, width), halves),
            pltpu.VMEM((heads, 8, tokens), floats),
            DMA((3,)),
            DMA((3,)),
            DMA((3,)),
            DMA((3,)),
        ],
        compiler_params=params(2),
        name="attend_forward",
    )(normed, weights, text, text_weights)


def cross_kernel(
    words,
    attended_ref,
    hidden_ref,
    weight_ref,
    text_ref,
    gain_ref,
    rgb_scale_ref,
    rgb_weight_ref,
    cotangent_ref,
    rgb_cotangent_ref,
    penalty_ref,
    output_ref,
    rgb_ref,
    weight_grad_ref,
    text_grad_ref,
    grad_two_ref,
    grad_attended_ref,
    small_ref,
    attended,
    two,
    normed,
    query,
    probs,
    crossed,
    mixed,
    grad_three,
    grad_proj,
    grad_crossed,
    grad_query,
    grad_norm,
    grad_attn,
):
    rows, full = hidden_ref.shape
    tile = full // PIX
    score_scale = HEAD_DIM ** (-0.5)
    W_OUT, C_QUERY, C_OUT = (slice(i * tile, (i + 1) * tile) for i in range(3))
    part = 64

    def cols(j):
        return pl.ds(pl.multiple_of(j * tile, tile), tile)

    for j in range(PIX):
        attended[:, j * tile : (j + 1) * tile] = attended_ref[j]

    def out_two(j):
        two[:, cols(j)] = hidden_ref[:, cols(j)] + mul(attended[...], weight_ref[j, :, W_OUT])

    loop(PIX, out_two)

    def norm_two(i):
        here = pl.ds(pl.multiple_of(i * part, part), part)
        hidden = two[here, :]
        mean = jnp.mean(hidden * hidden, -1, keepdims=True)
        normed[here, :] = (hidden * lax.rsqrt(mean + 1e-06) * gain_ref[...]).astype(halves)

    loop(rows // part, norm_two)

    def out_query(j):
        query[:, cols(j)] = mul(normed[...], weight_ref[j, :, C_QUERY]).astype(halves)

    loop(PIX, out_query)
    slots = text_ref.shape[1]
    known = lax.broadcasted_iota(jnp.int32, (rows, slots), 1) < words
    pairs = tile // 128

    def text_lanes(pair, side):
        return pl.ds(pl.multiple_of(side * tile + lax.rem(pair, pairs) * 128, 128), 128)

    def cross_pair(pair):
        here = pl.ds(pl.multiple_of(pair * 128, 128), 128)
        group = lax.div(pair, pairs)
        queries = query[:, here]
        keys = text_ref[group, :, text_lanes(pair, 0)]
        values = text_ref[group, :, text_lanes(pair, 1)]
        outs = []
        for h in range(2):
            lanes = slice(h * HEAD_DIM, (h + 1) * HEAD_DIM)
            scores = score_scale * mul_nt(queries[:, lanes], keys[:, lanes])
            scores = jnp.where(known, scores, -1e30)
            expanded = jnp.exp(scores - jnp.max(scores, -1, keepdims=True))
            prob = expanded / jnp.sum(expanded, -1, keepdims=True)
            probs[2 * pair + h] = prob
            outs.append(mul(prob.astype(halves), values[:, lanes]))
        crossed[:, here] = jnp.concatenate(outs, axis=1).astype(halves)

    loop(full // 128, cross_pair)
    rgb_ref[...] = jnp.zeros_like(rgb_ref)

    def out_three(j):
        three = two[:, cols(j)] + mul(crossed[...], weight_ref[j, :, C_OUT])
        output_ref[:, cols(j)] = three
        blend = (three * rgb_scale_ref[:, cols(j)]).astype(halves)
        mixed[:, cols(j)] = blend
        rgb_ref[...] += mul(blend, rgb_weight_ref[cols(j), :])

    loop(PIX, out_three)
    rgb_grad = rgb_cotangent_ref[...] + penalty_weight * penalty_ref[...] * rgb_ref[...]

    def back_three(j):
        color = mul_tn(rgb_grad, mixed[:, cols(j)].astype(floats), highest)
        small_ref[2:5, cols(j)] = color[0:3]
        grad_mixed = mul_nt(rgb_grad, rgb_weight_ref[cols(j), :].astype(floats), highest)
        small_ref[1:2, cols(j)] = jnp.sum(grad_mixed * output_ref[:, cols(j)], 0, keepdims=True)
        grad = cotangent_ref[:, cols(j)].astype(floats) + grad_mixed * rgb_scale_ref[:, cols(j)]
        grad_three[:, cols(j)] = grad
        grad_proj[:, cols(j)] = grad.astype(halves)

    loop(PIX, back_three)

    def times_transposed(source, j, which):
        acc = jnp.zeros((rows, tile), floats)
        for i in range(PIX):
            acc = acc + mul_nt(source[:, i * tile : (i + 1) * tile], weight_ref[i, cols(j), which])
        return acc

    def back_crossed(j):
        grad_crossed[:, cols(j)] = times_transposed(grad_proj, j, C_OUT).astype(halves)

    loop(PIX, back_crossed)

    def back_pair(pair):
        here = pl.ds(pl.multiple_of(pair * 128, 128), 128)
        group = lax.div(pair, pairs)
        queries, grads = query[:, here], grad_crossed[:, here]
        keys = text_ref[group, :, text_lanes(pair, 0)]
        values = text_ref[group, :, text_lanes(pair, 1)]
        grad_q, grad_k, grad_v = [], [], []
        for h in range(2):
            lanes = slice(h * HEAD_DIM, (h + 1) * HEAD_DIM)
            prob = probs[2 * pair + h]
            grad = grads[:, lanes]
            grad_prob = mul_nt(grad, values[:, lanes])
            grad_v.append(mul_tn(prob.astype(halves), grad))
            inner = jnp.sum(grad_prob * prob, -1, keepdims=True)
            score = (prob * (grad_prob - inner)).astype(halves)
            grad_q.append(score_scale * mul(score, keys[:, lanes]))
            grad_k.append(score_scale * mul_tn(score, queries[:, lanes]))
        grad_query[:, here] = jnp.concatenate(grad_q, axis=1).astype(halves)
        text_grad_ref[group, :, text_lanes(pair, 0)] = jnp.concatenate(grad_k, axis=1)
        text_grad_ref[group, :, text_lanes(pair, 1)] = jnp.concatenate(grad_v, axis=1)

    loop(full // 128, back_pair)

    def back_query(j):
        grad_norm[:, cols(j)] = times_transposed(grad_query, j, C_QUERY)

    loop(PIX, back_query)
    small_ref[0:1, :] = jnp.zeros((1, full), floats)

    def back_norm(i):
        here = pl.ds(pl.multiple_of(i * part, part), part)
        hidden, grad = two[here, :], grad_norm[here, :]
        inverse = lax.rsqrt(jnp.mean(hidden * hidden, -1, keepdims=True) + 1e-06)
        small_ref[0:1, :] += jnp.sum(grad * hidden * inverse, 0, keepdims=True)
        scaled = grad * gain_ref[...]
        mean = jnp.mean(scaled * hidden, -1, keepdims=True)
        total = grad_three[here, :] + inverse * scaled - hidden * (inverse * inverse * inverse * mean)
        grad_two_ref[here, :] = total
        grad_attn[here, :] = total.astype(halves)

    loop(rows // part, back_norm)

    def back_attended(j):
        grad_attended_ref[j] = times_transposed(grad_attn, j, W_OUT).astype(halves)

    loop(PIX, back_attended)

    def weight_grads(index):
        i, j = lax.div(index, PIX), lax.rem(index, PIX)
        for which, left, right in (
            (W_OUT, attended, grad_attn),
            (C_QUERY, normed, grad_query),
            (C_OUT, crossed, grad_proj),
        ):
            weight_grad_ref[j, cols(i), which] = mul_tn(left[:, cols(i)], right[:, cols(j)]).astype(
                halves
            )

    loop(PIX * PIX, weight_grads)
    small_ref[5:8, :] = jnp.zeros((3, full), floats)


def cross_part(
    words, attended, hidden, weights, text, gain, rgb_scale, rgb_weight, cotangent, rgb_cotangent, penalty
):
    rows, full = hidden.shape
    tile = full // PIX
    heads = full // HEAD_DIM
    wide = pltpu.VMEM((rows, full), floats)
    slim = pltpu.VMEM((rows, full), halves)
    return pl.pallas_call(
        partial(cross_kernel, words),
        out_shape=(
            jax.ShapeDtypeStruct((rows, full), floats),
            jax.ShapeDtypeStruct((rows, 128), floats),
            jax.ShapeDtypeStruct(weights.shape, halves),
            jax.ShapeDtypeStruct(text.shape, floats),
            jax.ShapeDtypeStruct((rows, full), floats),
            jax.ShapeDtypeStruct((PIX, rows, tile), halves),
            jax.ShapeDtypeStruct((8, full), floats),
        ),
        in_specs=[VMEM] * 10,
        out_specs=(VMEM,) * 7,
        scratch_shapes=[
            slim,
            wide,
            slim,
            slim,
            pltpu.VMEM((heads, rows, text.shape[1]), floats),
            slim,
            slim,
            wide,
            slim,
            slim,
            slim,
            wide,
            slim,
        ],
        compiler_params=pltpu.CompilerParams(vmem_limit_bytes=VMEM_LIMIT),
        name="cross_part",
    )(
        attended,
        hidden,
        weights,
        text,
        gain.reshape(1, -1),
        rgb_scale,
        rgb_weight,
        cotangent,
        rgb_cotangent,
        penalty,
    )


def attend_back_kernel(
    grad_ref,
    query_ref,
    key_ref,
    value_ref,
    total_ref,
    normed_ref,
    weight_ref,
    hidden_ref,
    conv_ref,
    grad_two_ref,
    gain_ref,
    weight_grad_ref,
    grad_one_ref,
    grad_conv_ref,
    small_ref,
    grads,
    grad_query,
    grad_key,
    grad_value,
    key_acc,
    value_acc,
    totals,
    pair_out,
    pair_in,
    line_out,
    line_in,
    own,
    conv_out,
    grad_send,
    grad_recv,
    pair_send,
    pair_recv,
    line_send,
    line_recv,
    conv_send,
    conv_recv,
):
    row, col = lax.axis_index("dp"), lax.axis_index("pix")
    near, far, cross = peers(col)
    targets = (far, cross, near)
    greet_pixels(row, targets)
    rows, full = hidden_ref.shape
    tokens, width = query_ref.shape
    heads = width // HEAD_DIM
    score_scale = HEAD_DIM ** (-0.5)

    def grad_copy(turn):
        return remote(
            grad_ref.at[targets[turn]],
            grads.at[col],
            grad_send.at[turn],
            grad_recv.at[turn],
            (row, targets[turn]),
        )

    for turn in range(3):
        grad_copy(turn).start()
    grads[col] = grad_ref[col]
    totals[...] = jnp.transpose(total_ref[...])
    for turn in range(3):
        remote(
            grad_ref.at[0],
            grads.at[targets[turn]],
            grad_send.at[turn],
            grad_recv.at[turn],
            (row, near),
        ).wait_recv()
    ones = jnp.ones((rows, HEAD_DIM), halves)
    for h in range(heads):
        lanes = slice(h * HEAD_DIM, (h + 1) * HEAD_DIM)
        keys, values = key_ref[:, lanes], value_ref[:, lanes]
        wide = keys.astype(floats)
        norm = score_scale * jnp.sum(wide * wide, -1, keepdims=True)
        key_acc[...] = jnp.zeros_like(key_acc)
        value_acc[...] = jnp.zeros_like(value_acc)

        def block(i, lanes=lanes, keys=keys, values=values, norm=norm, h=h):
            here = pl.ds(pl.multiple_of(i * rows, rows), rows)
            queries, grad = query_ref[here, lanes], grads[i, :, lanes]
            inner = mul_nt(keys, queries)
            prob = jnp.exp((2.0 * score_scale) * inner - norm - totals[h : h + 1, here])
            grad_prob = mul_nt(values, grad)
            value_acc[...] += mul(prob.astype(halves), grad)
            mean = jnp.sum(grad_prob * prob, 0, keepdims=True)
            score = (prob * (grad_prob - mean)).astype(halves)
            key_acc[...] += mul(score, jnp.concatenate([queries, ones], axis=1))
            grad_query[here, lanes] = (2.0 * score_scale * mul_tn(score, keys)).astype(halves)

        loop(PIX, block)
        acc = key_acc[...]
        grad_key[:, lanes] = (
            2.0 * score_scale * (acc[:, :HEAD_DIM] - wide * acc[:, HEAD_DIM : HEAD_DIM + 1])
        ).astype(halves)
        grad_value[:, lanes] = value_acc[...].astype(halves)

    def norm_grad(block, store):
        here = pl.ds(pl.multiple_of(block * rows, rows), rows)

        def tile(j):
            cols = pl.ds(pl.multiple_of(j * width, width), width)
            acc = jnp.zeros((rows, width), floats)
            for k, source in enumerate((grad_query, grad_key, grad_value)):
                acc = acc + mul_nt(source[here, :], weight_ref[cols, k * width : (k + 1) * width])
            store(cols, acc)

        loop(full // width, tile)

    def pair_copy(turn):
        return remote(
            pair_out.at[turn], pair_in.at[turn], pair_send.at[turn], pair_recv.at[turn], (row, near)
        )

    for turn, target in enumerate((cross, near)):

        def store(cols, value, turn=turn):
            pair_out[turn, :, cols] = value.astype(halves)

        norm_grad(target, store)
        pair_copy(turn).start()
    line = remote(line_out, line_in, line_send, line_recv, (row, far))

    def store_far(cols, value):
        line_out[:, cols] = (value + pair_in[0, :, cols].astype(floats)).astype(halves)

    pair_copy(0).wait_recv()
    norm_grad(far, store_far)
    line.start()

    def store_own(cols, value):
        own[:, cols] = value + pair_in[1, :, cols].astype(floats)

    pair_copy(1).wait_recv()
    norm_grad(col, store_own)

    def weight_grads(j):
        cols = pl.ds(pl.multiple_of(j * width, width), width)
        for k, right in enumerate((grad_query, grad_key, grad_value)):
            acc = jnp.zeros((width, width), floats)
            for i in range(PIX):
                acc = acc + mul_tn(normed_ref[i, :, cols], right[i * rows : (i + 1) * rows, :])
            weight_grad_ref[cols, k * width : (k + 1) * width] = acc.astype(halves)

    loop(full // width, weight_grads)
    line.wait_recv()
    small_ref[...] = jnp.zeros_like(small_ref)
    part = 64

    def back_norm(i):
        here = pl.ds(pl.multiple_of(i * part, part), part)
        hidden = hidden_ref[here, :]
        grad = own[here, :] + line_in[here, :].astype(floats)
        inverse = lax.rsqrt(jnp.mean(hidden * hidden, -1, keepdims=True) + 1e-06)
        small_ref[0:1, :] += jnp.sum(grad * hidden * inverse, 0, keepdims=True)
        scaled = grad * gain_ref[...]
        mean = jnp.mean(scaled * hidden, -1, keepdims=True)
        total = (
            grad_two_ref[here, :] + inverse * scaled - hidden * (inverse * inverse * inverse * mean)
        )
        grad_one_ref[here, :] = total
        conv = conv_ref[here, :].astype(floats)
        gate = jax.nn.sigmoid(conv)
        result = (total * gate * (1.0 + conv * (1.0 - gate))).astype(halves)
        for j in range(PIX):
            conv_out[j, here, :] = result[:, j * width : (j + 1) * width]

    loop(rows // part, back_norm)

    def conv_copy(turn):
        return remote(
            conv_out.at[targets[turn]],
            grad_conv_ref.at[col],
            conv_send.at[turn],
            conv_recv.at[turn],
            (row, targets[turn]),
        )

    for turn in range(3):
        conv_copy(turn).start()
    grad_conv_ref[col] = conv_out[col]
    for turn in range(3):
        remote(
            conv_out.at[0],
            grad_conv_ref.at[targets[turn]],
            conv_send.at[turn],
            conv_recv.at[turn],
            (row, near),
        ).wait_recv()
    for turn in range(3):
        conv_copy(turn).wait_send()
        grad_copy(turn).wait_send()
    pair_copy(0).wait_send()
    pair_copy(1).wait_send()
    line.wait_send()


def attend_backward(grad, query, key, value, totals, normed, weights, hidden, conv, grad_two, gain):
    rows, full = hidden.shape
    tokens, width = query.shape
    flat = pltpu.VMEM((tokens, width), halves)
    return pl.pallas_call(
        attend_back_kernel,
        out_shape=(
            jax.ShapeDtypeStruct(weights.shape, halves),
            jax.ShapeDtypeStruct((rows, full), floats),
            jax.ShapeDtypeStruct((PIX, rows, width), halves),
            jax.ShapeDtypeStruct((8, full), floats),
        ),
        in_specs=[VMEM] * 11,
        out_specs=(VMEM,) * 4,
        scratch_shapes=[
            pltpu.VMEM((PIX, rows, width), halves),
            flat,
            flat,
            flat,
            pltpu.VMEM((tokens, 2 * HEAD_DIM), floats),
            pltpu.VMEM((tokens, HEAD_DIM), floats),
            pltpu.VMEM((128, tokens), floats),
            pltpu.VMEM((2, rows, full), halves),
            pltpu.VMEM((2, rows, full), halves),
            pltpu.VMEM((rows, full), halves),
            pltpu.VMEM((rows, full), halves),
            pltpu.VMEM((rows, full), floats),
            pltpu.VMEM((PIX, rows, width), halves),
            DMA((3,)),
            DMA((3,)),
            DMA((2,)),
            DMA((2,)),
            DMA,
            DMA,
            DMA((3,)),
            DMA((3,)),
        ],
        compiler_params=params(3),
        name="attend_backward",
    )(
        grad,
        query,
        key,
        value,
        totals,
        normed,
        weights,
        hidden,
        conv,
        grad_two,
        gain.reshape(1, -1),
    )


def conv_back_kernel(
    count,
    width,
    images_ref,
    kernel_ref,
    bank_ref,
    styles_ref,
    inverse_ref,
    grad_ref,
    conv_ref,
    bank_grad_ref,
    stats_ref,
    image_grad_ref,
    grads_ref,
    image_buf,
    padded_image,
    padded_grad,
    turned,
    acc,
    sums_out,
    sums_in,
    kept,
    kept_own,
    pixel_out,
    pixel_in,
    line_out,
    line_in,
    owner_out,
    local_sem,
    image_sem,
    load_sem,
    sums_send,
    sums_recv,
    level_send,
    level_recv,
    pair_send,
    pair_recv,
    pixel_send,
    pixel_recv,
    line_send,
    line_recv,
    owner_send,
    owner_recv,
):
    row, col = lax.axis_index("dp"), lax.axis_index("pix")
    groups = count // 2
    side, level = lax.rem(row, 2), lax.div(row, 2)
    partner = flip(row, 1)
    near, far, cross = peers(col)
    tokens, channels = grad_ref.shape
    depth = image_buf.shape[2]
    rows = tokens // PIX
    halo = width
    greet(count, [(row, near), (row, far)])

    def sample_of(step):
        group = lax.rem(level - lax.div(step, 2) + groups, groups)
        return 2 * group + jnp.where(lax.rem(step, 2) == 0, side, 1 - side)

    def level_copy(k):
        target = 2 * lax.rem(level + k, groups) + side
        return remote(
            grad_ref, grads_ref.at[row], level_send.at[k], level_recv.at[k], (target, col)
        )

    def pair_copy(k):
        block = grads_ref.at[sample_of(2 * k)]
        return remote(block, block, pair_send.at[k], pair_recv.at[k], (partner, col))

    def sums_copy(k):
        return remote(
            sums_out,
            sums_in.at[row],
            sums_send.at[k],
            sums_recv.at[k],
            (lax.rem(row + k, count), col),
        )

    own = pltpu.make_async_copy(grad_ref, grads_ref.at[row], local_sem)
    own.start()
    lax.fori_loop(1, groups, lambda k, c: (level_copy(k).start(), c)[1], 0)
    own.wait()
    pair_copy(0).start()

    def fetch(step):
        slot = lax.rem(step, 2)
        return pltpu.make_async_copy(
            images_ref.at[sample_of(step)], image_buf.at[slot], image_sem.at[slot]
        )

    fetch(0).start()
    products = jnp.zeros((8, channels), floats)

    def add_product(i, total):
        here = pl.ds(pl.multiple_of(i * 64, 64), 64)
        product = grad_ref[here, :].astype(floats) * conv_ref[here, :].astype(floats)
        return total + jnp.sum(product.reshape(8, 8, channels), axis=0)

    products = lax.fori_loop(0, tokens // 64, add_product, products)
    sums_out[...] = jnp.broadcast_to(jnp.sum(products, 0, keepdims=True), (8, channels))
    lax.fori_loop(1, count, lambda k, c: (sums_copy(k).start(), c)[1], 0)
    sums_in[row] = sums_out[...]
    acc[...] = jnp.zeros_like(acc)
    stats_ref[...] = jnp.zeros_like(stats_ref)
    for buffer, lanes in ((padded_image, depth), (padded_grad, channels)):
        zeros = jnp.zeros((3, halo, lanes), halves)
        buffer[:, 0:halo, :] = zeros
        buffer[:, halo + tokens : halo + tokens + halo, :] = zeros

    def sums_arrive(k, carry):
        origin = lax.rem(row - k + count, count)
        remote(
            sums_out, sums_in.at[origin], sums_send.at[k], sums_recv.at[k], (partner, col)
        ).wait_recv()
        return carry

    def fill(buffer, source):
        wide = source.astype(floats)
        place = lax.rem(lax.broadcasted_iota(jnp.int32, wide.shape, 0), width)
        here = slice(halo, halo + tokens)
        buffer[0, here, :] = jnp.where(place == 0, 0.0, pltpu.roll(wide, 1, 0)).astype(halves)
        buffer[2, here, :] = jnp.where(
            place == width - 1, 0.0, pltpu.roll(wide, tokens - 1, 0)
        ).astype(halves)

    centre = pl.ds(halo, tokens)

    def pixel_copy(step):
        return remote(
            pixel_out.at[lax.rem(step, 2)],
            pixel_in.at[step],
            pixel_send.at[step],
            pixel_recv.at[step],
            (row, near),
        )

    def line_copy(step):
        return remote(
            line_out.at[lax.rem(step, 2)],
            line_in.at[step],
            line_send.at[step],
            line_recv.at[step],
            (row, far),
        )

    def owner_copy(step):
        return remote(
            owner_out.at[lax.rem(step, 2)],
            image_grad_ref.at[row],
            owner_send.at[step],
            owner_recv.at[row],
            (sample_of(step), col),
        )

    def work(step):
        k, odd = lax.div(step, 2), lax.rem(step, 2)
        sample = sample_of(step)

        @pl.when(odd == 1)
        def _():
            block = grads_ref.at[sample]
            remote(block, block, pair_send.at[k], pair_recv.at[k], (partner, col)).wait_recv()

        @pl.when((odd == 0) & (k > 0))
        def _():
            block = grads_ref.at[sample]
            remote(block, block, level_send.at[k], level_recv.at[k], (partner, col)).wait_recv()
            pair_copy(k).start()

        load = pltpu.make_async_copy(
            grads_ref.at[sample], padded_grad.at[1, centre, :], load_sem
        )
        load.start()
        fetch(step).wait()

        @pl.when(step + 1 < count)
        def _():
            fetch(step + 1).start()

        image = image_buf[lax.rem(step, 2)]
        padded_image[1, centre, :] = image
        fill(padded_image, image)
        load.wait()
        grad = padded_grad[1, centre, :]
        fill(padded_grad, grad)
        turned[...] = jnp.transpose(grad)
        slot = lax.rem(step, 2)

        @pl.when(step >= 2)
        def _():
            pixel_copy(step - 2).wait_send()

        def through(target):
            start = pl.multiple_of(target * rows, rows)
            total = jnp.zeros((rows, depth), floats)
            for a in range(3):
                for b in range(3):
                    window = padded_grad[
                        2 - b, pl.ds(pl.multiple_of(start + (2 - a) * width, 16), rows), :
                    ]
                    total = total + mul_nt(window, kernel_ref[sample, 3 * a + b])
            return total

        def give(i):
            pixel_out[slot, i] = through(jnp.where(i == 0, near, cross)).astype(halves)

        def keep(i):
            kept[slot, i] = through(jnp.where(i == 0, col, far))

        loop(2, give)
        pixel_copy(step).start()
        loop(2, keep)
        style = styles_ref[sample]
        scale = style[0:1, :depth]
        first, second = style[1:2, 0:1], style[2:3, 0:1]
        both = jnp.concatenate(
            [
                jnp.broadcast_to(inverse_ref[pl.ds(sample, 1), :], (8, channels)),
                sums_in[sample],
            ],
            axis=0,
        )
        columns = jnp.transpose(both)
        inverse, total = columns[:, 0:1], columns[:, 8:9]
        factor = inverse * inverse * total
        by_scale = jnp.zeros((1, depth), floats)
        by_first = jnp.zeros((1, depth), floats)
        by_second = jnp.zeros((1, depth), floats)
        for a in range(3):
            for b in range(3):
                tap = 3 * a + b
                found = mul(turned[...], padded_image[b, pl.ds(a * width, tokens), :])
                one, two = bank_ref[0, tap].astype(floats), bank_ref[1, tap].astype(floats)
                selected = first * one + second * two
                modded = inverse * found - factor * (selected * scale)
                by_scale = by_scale + jnp.sum(modded * selected, 0, keepdims=True)
                grad_selected = modded * scale
                acc[0, tap] += first * grad_selected
                acc[1, tap] += second * grad_selected
                by_first = by_first + jnp.sum(grad_selected * one, 0, keepdims=True)
                by_second = by_second + jnp.sum(grad_selected * two, 0, keepdims=True)
        stats_ref[sample, 0:1, :depth] = by_scale
        stats_ref[sample, 1:2, :depth] = by_first
        stats_ref[sample, 2:3, :depth] = by_second

    def across(step):
        slot = lax.rem(step, 2)
        pixel_copy(step).wait_recv()

        @pl.when(step >= 2)
        def _():
            line_copy(step - 2).wait_send()

        line_out[slot] = (kept[slot, 1] + pixel_in[step, 1].astype(floats)).astype(halves)
        line_copy(step).start()
        kept_own[slot] = kept[slot, 0] + pixel_in[step, 0].astype(floats)

    def home(step):
        slot = lax.rem(step, 2)
        line_copy(step).wait_recv()

        @pl.when(step >= 3)
        def _():
            owner_copy(step - 2).wait_send()

        owner_out[slot] = (kept_own[slot] + line_in[step].astype(floats)).astype(halves)

        @pl.when(step > 0)
        def _():
            owner_copy(step).start()

        @pl.when(step == 0)
        def _():
            mine = pltpu.make_async_copy(owner_out.at[slot], image_grad_ref.at[row], local_sem)
            mine.start()
            mine.wait()

    lax.fori_loop(1, count, sums_arrive, 0)

    def step_body(step):
        @pl.when(step < count)
        def _():
            work(step)

        @pl.when((step >= 1) & (step <= count))
        def _():
            across(step - 1)

        @pl.when(step >= 2)
        def _():
            home(step - 2)

    loop(count + 2, step_body)

    def write(index):
        bank_grad_ref[lax.div(index, 9), lax.rem(index, 9)] = jnp.transpose(
            acc[lax.div(index, 9), lax.rem(index, 9)]
        )

    loop(18, write)

    def owner_arrives(k, carry):
        origin = lax.rem(row - k + count, count)
        remote(
            owner_out.at[0],
            image_grad_ref.at[origin],
            owner_send.at[k],
            owner_recv.at[origin],
            (partner, col),
        ).wait_recv()
        return carry

    lax.fori_loop(1, count, owner_arrives, 0)
    for step in (count - 2, count - 1):
        pixel_copy(step).wait_send()
        line_copy(step).wait_send()
        owner_copy(step).wait_send()
    lax.fori_loop(1, groups, lambda k, c: (level_copy(k).wait_send(), c)[1], 0)
    loop(groups, lambda k: pair_copy(k).wait_send())
    lax.fori_loop(1, count, lambda k, c: (sums_copy(k).wait_send(), c)[1], 0)


def conv_backward(images_all, kernels, bank, styles, inverse, grad, conv, width):
    count, tokens, depth = images_all.shape
    channels = grad.shape[1]
    rows = tokens // PIX
    groups = count // 2
    piece = (rows, depth)
    return pl.pallas_call(
        partial(conv_back_kernel, count, width),
        out_shape=(
            jax.ShapeDtypeStruct((2, 9, depth, channels), floats),
            jax.ShapeDtypeStruct((count, 8, 128), floats),
            jax.ShapeDtypeStruct((count,) + piece, halves),
            jax.ShapeDtypeStruct((count, tokens, channels), halves),
        ),
        in_specs=[ANY] + [VMEM] * 6,
        out_specs=(VMEM, VMEM, ANY, ANY),
        scratch_shapes=[
            pltpu.VMEM((2, tokens, depth), halves),
            pltpu.VMEM((3, tokens + 2 * width, depth), halves),
            pltpu.VMEM((3, tokens + 2 * width, channels), halves),
            pltpu.VMEM((channels, tokens), halves),
            pltpu.VMEM((2, 9, channels, depth), floats),
            pltpu.VMEM((8, channels), floats),
            pltpu.VMEM((count, 8, channels), floats),
            pltpu.VMEM((2, 2) + piece, floats),
            pltpu.VMEM((2,) + piece, floats),
            pltpu.VMEM((2, 2) + piece, halves),
            pltpu.VMEM((count, 2) + piece, halves),
            pltpu.VMEM((2,) + piece, halves),
            pltpu.VMEM((count,) + piece, halves),
            pltpu.VMEM((2,) + piece, halves),
            DMA,
            DMA((2,)),
            DMA,
            DMA((count,)),
            DMA((count,)),
            DMA((groups,)),
            DMA((groups,)),
            DMA((groups,)),
            DMA((groups,)),
            DMA((count,)),
            DMA((count,)),
            DMA((count,)),
            DMA((count,)),
            DMA((count,)),
            DMA((count,)),
        ],
        compiler_params=params(4),
        name="conv_backward",
    )(images_all, kernels, bank, styles, inverse, grad, conv)


def small_kernel(
    count,
    small_ref,
    last_ref,
    stats_ref,
    rows_ref,
    stats_all_ref,
    rows_out,
    rows_in,
    stats_in,
    rows_send,
    rows_recv,
    stats_send,
    stats_recv,
    far_rows_send,
    far_rows_recv,
    far_stats_send,
    far_stats_recv,
):
    row, col = lax.axis_index("dp"), lax.axis_index("pix")
    near, far, cross = peers(col)
    targets = (far, cross, near)
    greet(count, [(row, near), (row, far), (row, cross)])
    rows_out[...] = small_ref[...]
    rows_out[5:6, :] = last_ref[0:1, :]

    def rows_copy(turn):
        return remote(
            rows_out, rows_in.at[turn], rows_send.at[turn], rows_recv.at[turn], (row, targets[turn])
        )

    def stats_copy(turn):
        return remote(
            stats_ref, stats_in.at[turn], stats_send.at[turn], stats_recv.at[turn], (row, targets[turn])
        )

    for turn in range(3):
        rows_copy(turn).start()
        stats_copy(turn).start()
    for turn in range(3):
        rows_copy(turn).wait()
        stats_copy(turn).wait()
    rows_in[3] = rows_out[...]
    stats_in[3] = stats_ref[...]

    def in_order(buffer):
        total = None
        for which in range(PIX):
            turn = jnp.where(
                which == col, 3, jnp.where(which == far, 0, jnp.where(which == cross, 1, 2))
            )
            total = buffer[turn] if total is None else total + buffer[turn]
        return total

    rows_ref[row] = in_order(rows_in)
    stats_all_ref[row] = in_order(stats_in)

    def far_rows(k):
        block = rows_ref.at[row]
        return remote(
            block, block, far_rows_send.at[k], far_rows_recv.at[k], (lax.rem(row + k, count), col)
        )

    def far_stats(k):
        block = stats_all_ref.at[row]
        return remote(
            block, block, far_stats_send.at[k], far_stats_recv.at[k], (lax.rem(row + k, count), col)
        )

    lax.fori_loop(1, count, lambda k, c: (far_rows(k).start(), far_stats(k).start(), c)[2], 0)

    def arrive(k, carry):
        origin = lax.rem(row - k + count, count)
        block = rows_ref.at[origin]
        remote(block, block, far_rows_send.at[k], far_rows_recv.at[k], (row, near)).wait_recv()
        block = stats_all_ref.at[origin]
        remote(block, block, far_stats_send.at[k], far_stats_recv.at[k], (row, near)).wait_recv()
        return carry

    lax.fori_loop(1, count, arrive, 0)
    lax.fori_loop(
        1, count, lambda k, c: (far_rows(k).wait_send(), far_stats(k).wait_send(), c)[2], 0
    )


def small_sums(small, last, stats):
    count = stats.shape[0]
    block = small.shape
    return pl.pallas_call(
        partial(small_kernel, count),
        out_shape=(
            jax.ShapeDtypeStruct((count,) + block, floats),
            jax.ShapeDtypeStruct((count,) + stats.shape, floats),
        ),
        in_specs=[VMEM] * 3,
        out_specs=(VMEM,) * 2,
        scratch_shapes=[
            pltpu.VMEM(block, floats),
            pltpu.VMEM((4,) + block, floats),
            pltpu.VMEM((4,) + stats.shape, floats),
            DMA((3,)),
            DMA((3,)),
            DMA((3,)),
            DMA((3,)),
            DMA((count,)),
            DMA((count,)),
            DMA((count,)),
            DMA((count,)),
        ],
        compiler_params=params(5),
        name="small_sums",
    )(small, last, stats)


def style_rows(style_codes, labels, class_table, select_weight, modulation, rgb_modulation):
    class_row = jnp.take(class_table, labels, axis=0).astype(floats)
    styled = style_codes.astype(floats) + class_row
    mixing = jax.nn.softmax(jnp.dot(styled, select_weight.astype(floats), precision=highest), -1)
    scaling = jnp.dot(styled, modulation.astype(floats), precision=highest) + 1.0
    rgb_scale = jnp.dot(styled, rgb_modulation.astype(floats), precision=highest) + 1.0
    return styled, mixing, scaling, rgb_scale


def pack_style(styled, labels, mixing, scaling, count):
    depth = scaling.shape[-1] // count
    pieces = jnp.pad(scaling.reshape(count, 1, depth), ((0, 0), (0, 0), (0, 128 - depth)))
    same = jnp.concatenate(
        [
            jnp.broadcast_to(mixing.reshape(2, 1), (2, 128)),
            styled.reshape(4, 128),
            jnp.broadcast_to(labels.astype(floats).reshape(1, 1), (1, 128)),
        ]
    )
    return jnp.concatenate([pieces, jnp.broadcast_to(same, (count, 7, 128))], axis=1)


def on_device(
    images,
    style_codes,
    labels,
    token_ids,
    penalty_mask,
    class_table,
    text_table,
    conv_bank,
    select_weight,
    modulation,
    rgb_modulation,
    w_query,
    w_key,
    w_value,
    w_out,
    c_query,
    c_key,
    c_value,
    c_out,
    gain_self,
    gain_cross,
    rgb_weight,
    out_cotangent,
    rgb_cotangent,
):
    count = lax.axis_size("dp")
    row, col = lax.axis_index("dp"), lax.axis_index("pix")
    _, height, width, channels = images.shape
    rows = height * width
    quarter = channels // PIX
    depth = channels // count

    def my_columns(*weights):
        return jnp.concatenate(
            [lax.dynamic_slice_in_dim(w, col * quarter, quarter, axis=1) for w in weights], axis=1
        )

    attention = lax.all_gather(my_columns(w_query, w_key, w_value), "dp", axis=0, tiled=True)
    text_weights = lax.all_gather(my_columns(c_key, c_value), "dp", axis=0, tiled=True)
    others = lax.all_gather(my_columns(w_out, c_query, c_out), "dp", axis=0, tiled=True)
    others = lax.all_gather(others, "pix", axis=0)

    styled, mixing, scaling, rgb_scale = style_rows(
        style_codes, labels, class_table, select_weight, modulation, rgb_modulation
    )
    own = images.reshape(rows, channels)
    parts = own.reshape(rows, count, depth).transpose(1, 0, 2)
    bank = conv_bank.reshape(2, 9, depth, quarter)
    bank_turned = bank.transpose(0, 1, 3, 2)
    words = token_ids.shape[1]
    text = jnp.take(text_table, token_ids[0], axis=0)
    text_padded = jnp.pad(text, ((0, 128 - words), (0, 0)))

    images_all, kernels, styles, inverse = gather_inputs(
        pack_style(styled, labels, mixing, scaling, count), bank, parts
    )
    images_all = images_all.reshape(count, PIX * rows, depth)
    conv, conv_own, hidden_one, normed_one = conv_forward(images_all, kernels, own, gain_self, width)
    query, key, value, totals, attended, text_all = attend_forward(
        normed_one, attention, text_padded, text_weights
    )
    rgb_rows = jnp.pad(rgb_cotangent.reshape(3, rows).T, ((0, 0), (0, 125)))
    penalty = jnp.broadcast_to(penalty_mask.astype(floats).reshape(1, 1), (1, 128))
    output, rgb, other_grads, text_grads, grad_two, grad_attended, small = cross_part(
        words,
        attended,
        hidden_one,
        others,
        text_all,
        gain_cross,
        rgb_scale,
        jnp.pad(rgb_weight, ((0, 0), (0, 125))),
        out_cotangent.reshape(rows, channels),
        rgb_rows,
        penalty,
    )
    other_owned = lax.psum_scatter(
        lax.psum_scatter(other_grads, "pix", scatter_dimension=0, tiled=False),
        "dp",
        scatter_dimension=0,
        tiled=True,
    )
    text_cols = lax.psum_scatter(text_grads, "pix", scatter_dimension=0, tiled=False)
    text_grad = lax.dot_general(
        text.astype(floats), text_cols[:words], TN, precision=highest, preferred_element_type=floats
    ).astype(halves)
    text_owned = lax.psum_scatter(text_grad, "dp", scatter_dimension=0, tiled=True)

    attention_grads, grad_one, grad_conv, last = attend_backward(
        grad_attended,
        query,
        key,
        value,
        totals,
        normed_one,
        attention,
        hidden_one,
        conv,
        grad_two,
        gain_self,
    )
    attention_owned = lax.psum_scatter(attention_grads, "dp", scatter_dimension=0, tiled=True)

    def whole(owned):
        full = lax.all_gather(owned, "pix", axis=0).astype(floats)
        pieces = owned.shape[1] // quarter
        full = full.reshape(PIX, owned.shape[0], pieces, quarter).transpose(2, 1, 0, 3)
        return full.reshape(pieces, owned.shape[0], channels)

    grad_w_query, grad_w_key, grad_w_value = whole(attention_owned)
    grad_w_out, grad_c_query, grad_c_out = whole(other_owned)
    grad_c_key, grad_c_value = whole(text_owned)

    bank_grad, stats, image_parts, _ = conv_backward(
        images_all,
        kernels,
        bank_turned,
        styles,
        inverse,
        grad_conv.reshape(PIX * rows, quarter),
        conv_own,
        width,
    )
    grad_image = grad_one + image_parts.transpose(1, 0, 2).reshape(rows, channels).astype(floats)
    all_rows, all_stats = small_sums(small, last, stats)

    styled_all = styles[:, 3:7, :].reshape(count, -1)
    mixing_all = styles[:, 1:3, 0]
    labels_all = styles[:, 7, 0].astype(jnp.int32)
    grad_scaling = all_stats[:, :, 0, :depth].transpose(1, 0, 2).reshape(count, channels)
    grad_mixing = jnp.sum(all_stats[:, :, 1:3, :], axis=(0, 3))
    grad_rgb_scale = all_rows[:, 1, :]
    inner = jnp.sum(grad_mixing * mixing_all, -1, keepdims=True)
    grad_logits = mixing_all * (grad_mixing - inner)

    def outer(right):
        return lax.dot_general(
            styled_all, right, TN, precision=highest, preferred_element_type=floats
        )

    def back(left, right):
        return lax.dot_general(
            left, right.astype(floats), NT, precision=highest, preferred_element_type=floats
        )

    grad_styles = (
        back(grad_logits, select_weight)
        + back(grad_scaling, modulation)
        + back(grad_rgb_scale, rgb_modulation)
    )
    classes = class_table.shape[0]
    chosen = (labels_all[:, None] == jnp.arange(classes, dtype=jnp.int32)[None, :]).astype(floats)
    grad_table = lax.dot_general(
        chosen, grad_styles, TN, precision=highest, preferred_element_type=floats
    )
    sums = jnp.sum(all_rows, axis=0)
    shape = images.shape
    return (
        output.reshape(shape),
        rgb[:, :3].T.reshape(1, 3, height, width),
        grad_image.reshape(shape),
        lax.dynamic_slice_in_dim(grad_styles, row, 1, axis=0),
        grad_table,
        bank_grad.reshape(conv_bank.shape),
        outer(grad_logits),
        outer(grad_scaling),
        outer(grad_rgb_scale),
        grad_w_query,
        grad_w_key,
        grad_w_value,
        grad_w_out,
        grad_c_query,
        grad_c_key,
        grad_c_value,
        grad_c_out,
        sums[5],
        sums[0],
        sums[2:5].T,
    )


def solution(mesh):
    return jax.shard_map(
        on_device,
        mesh=mesh,
        in_specs=(
            P("dp", "pix", None, None),
            P("dp", None),
            P("dp"),
            P("dp", None),
            P("dp"),
            P(),
            P(),
            P(None, None, None, "dp", "pix"),
            P(),
            P(),
            P(),
            P("dp", None),
            P("dp", None),
            P("dp", None),
            P("dp", None),
            P("dp", None),
            P("dp", None),
            P("dp", None),
            P("dp", None),
            P(),
            P(),
            P(),
            P("dp", "pix", None, None),
            P("dp", None, "pix", None),
        ),
        out_specs=(
            P("dp", "pix", None, None),
            P("dp", None, "pix", None),
            P("dp", "pix", None, None),
            P("dp", None),
            P(),
            P(None, None, None, "dp", "pix"),
            P(),
            P(),
            P(),
            P("dp", None),
            P("dp", None),
            P("dp", None),
            P("dp", None),
            P("dp", None),
            P("dp", None),
            P("dp", None),
            P("dp", None),
            P(),
            P(),
            P(),
        ),
        check_vma=False,
    )
```

```python
from functools import partial

import jax
import jax.numpy as jnp
from jax import lax
from jax.experimental import pallas as pl
from jax.experimental.pallas import tpu as pltpu
from jax.sharding import PartitionSpec as P

HEAD_DIM = 64
PIX = 4
MESH = pl.DeviceIdType.MESH
VMEM_LIMIT = 60 * 1024 * 1024

penalty_weight = 1.0
highest = lax.Precision.HIGHEST
floats = jnp.float32
halves = jnp.bfloat16

ANY = pl.BlockSpec(memory_space=pl.ANY)
VMEM = pl.BlockSpec(memory_space=pltpu.VMEM)
DMA = pltpu.SemaphoreType.DMA


def params(collective_id):
    return pltpu.CompilerParams(
        collective_id=collective_id, has_side_effects=True, vmem_limit_bytes=VMEM_LIMIT
    )


def remote(src, dst, send_sem, recv_sem, where):
    return pltpu.make_async_remote_copy(
        src_ref=src,
        dst_ref=dst,
        send_sem=send_sem,
        recv_sem=recv_sem,
        device_id=where,
        device_id_type=MESH,
    )


def greet(count, others):
    row, col = lax.axis_index("dp"), lax.axis_index("pix")
    barrier = pltpu.get_barrier_semaphore()

    def one(step, carry):
        pl.semaphore_signal(
            barrier, inc=1, device_id=(lax.rem(row + step, count), col), device_id_type=MESH
        )
        return carry

    if count > 1:
        lax.fori_loop(1, count, one, 0)
    for other in others:
        pl.semaphore_signal(barrier, inc=1, device_id=other, device_id_type=MESH)
    pl.semaphore_wait(barrier, count - 1 + len(others))


def loop(count, body):
    def step(i, carry):
        body(i)
        return carry

    lax.fori_loop(0, count, step, 0)


def flip(index, bit):
    part = lax.rem(lax.div(index, bit), 2)
    return index + bit - 2 * bit * part


def level_at(level, groups, index):
    both = jnp.minimum(level, groups - 1 - level)
    step = lax.div(index + 1, 2)
    near = jnp.where(lax.rem(index, 2) == 1, level - step, level + step)
    rest = index - both
    far = jnp.where(level > groups - 1 - level, level - rest, level + rest)
    return jnp.where(index == 0, level, jnp.where(index <= 2 * both, near, far))


def gather_kernel(
    count,
    style_ref,
    bank_ref,
    parts_ref,
    images_ref,
    kernel_ref,
    styles_ref,
    inverse_ref,
    squares,
    squares_in,
    local_sem,
    style_send,
    style_recv,
    square_send,
    square_recv,
    part_send,
    part_recv,
    core_send,
    core_recv,
    line_send,
    line_recv,
    pass_send,
    pass_recv,
):
    row, col = lax.axis_index("dp"), lax.axis_index("pix")
    near, far = flip(col, 1), flip(col, 2)
    depth = bank_ref.shape[2]
    greet(count, [(row, near), (row, far)])

    def style_copy(step):
        other = lax.rem(row + step, count)
        return remote(
            style_ref.at[other], styles_ref.at[row], style_send.at[step], style_recv.at[step], (other, col)
        )

    def square_copy(step):
        other = lax.rem(row + step, count)
        return remote(
            squares, squares_in.at[row], square_send.at[step], square_recv.at[step], (other, col)
        )

    def part_copy(step):
        other = lax.rem(row + step, count)
        return remote(
            parts_ref.at[other], images_ref.at[row, col], part_send.at[step], part_recv.at[step], (other, col)
        )

    def part_arrives(step):
        origin = lax.rem(row - step + count, count)
        remote(
            parts_ref.at[0], images_ref.at[origin, col], part_send.at[step], part_recv.at[step], (row, near)
        ).wait_recv()

    def core_copy(step):
        origin = lax.rem(row - step + count, count)
        block = images_ref.at[origin, col]
        return remote(block, block, core_send.at[step], core_recv.at[step], (row, near))

    def line_copy(step):
        origin = lax.rem(row - step + count, count)
        block = images_ref.at[origin, col]
        return remote(block, block, line_send.at[step], line_recv.at[step], (row, far))

    def pass_copy(step):
        origin = lax.rem(row - step + count, count)
        block = images_ref.at[origin, far]
        return remote(block, block, pass_send.at[step], pass_recv.at[step], (row, near))

    def core_arrives(step):
        origin = lax.rem(row - step + count, count)
        block = images_ref.at[origin, near]
        remote(block, block, core_send.at[step], core_recv.at[step], (row, near)).wait_recv()

    def line_arrives(step):
        origin = lax.rem(row - step + count, count)
        block = images_ref.at[origin, far]
        remote(block, block, line_send.at[step], line_recv.at[step], (row, far)).wait_recv()

    def pass_arrives(step):
        origin = lax.rem(row - step + count, count)
        block = images_ref.at[origin, flip(near, 2)]
        remote(block, block, pass_send.at[step], pass_recv.at[step], (row, near)).wait_recv()

    own = pltpu.make_async_copy(parts_ref.at[row], images_ref.at[row, col], local_sem)
    own.start()

    def send_all(step):
        style_copy(step).start()

    lax.fori_loop(1, count, lambda i, c: (send_all(i), c)[1], 0)
    lax.fori_loop(1, count, lambda i, c: (part_copy(i).start(), c)[1], 0)
    styles_ref[row] = style_ref[row]
    own.wait()
    line_copy(0).start()
    core_copy(0).start()

    def style_wait(step):
        origin = lax.rem(row - step + count, count)
        remote(
            style_ref.at[0], styles_ref.at[origin], style_send.at[step], style_recv.at[step], (row, near)
        ).wait_recv()

    lax.fori_loop(1, count, lambda i, c: (style_wait(i), c)[1], 0)

    def mixed_tap(sample, tap, column, first, second):
        total = first * bank_ref[0, tap].astype(floats) + second * bank_ref[1, tap].astype(floats)
        return total * column

    def factors(sample):
        block = styles_ref[sample]
        column = jnp.transpose(block)[:depth, 0:1]
        return column, block[1:2, 0:1], block[2:3, 0:1]

    def square_sum(sample):
        column, first, second = factors(sample)
        total = jnp.zeros((depth, bank_ref.shape[3]), floats)
        for tap in range(9):
            modded = mixed_tap(sample, tap, column, first, second)
            total = total + modded * modded
        squares[pl.ds(sample, 1), :] = jnp.sum(total, axis=0, keepdims=True)

    loop(count, square_sum)
    lax.fori_loop(1, count, lambda i, c: (square_copy(i).start(), c)[1], 0)
    squares_in[row] = squares[...]

    def relay(step):
        part_arrives(step)
        line_copy(step).start()
        core_copy(step).start()

    lax.fori_loop(1, count, lambda i, c: (relay(i), c)[1], 0)

    def square_wait(step):
        origin = lax.rem(row - step + count, count)
        remote(
            squares, squares_in.at[origin], square_send.at[step], square_recv.at[step], (row, near)
        ).wait_recv()

    lax.fori_loop(1, count, lambda i, c: (square_wait(i), c)[1], 0)
    inverse_ref[...] = lax.rsqrt(jnp.sum(squares_in[...], axis=0) + 1e-08)

    def forward(step):
        line_arrives(step)
        pass_copy(step).start()

    def make_kernel(sample):
        column, first, second = factors(sample)
        scale = inverse_ref[pl.ds(sample, 1), :]
        for tap in range(9):
            modded = mixed_tap(sample, tap, column, first, second)
            kernel_ref[sample, tap] = (modded * scale).astype(halves)
        forward(sample)

    loop(count, make_kernel)
    loop(count, core_arrives)
    loop(count, pass_arrives)
    lax.fori_loop(
        1,
        count,
        lambda i, c: (
            style_copy(i).wait_send(),
            square_copy(i).wait_send(),
            part_copy(i).wait_send(),
            c,
        )[3],
        0,
    )
    loop(count, lambda i: core_copy(i).wait_send())
    loop(count, lambda i: line_copy(i).wait_send())
    loop(count, lambda i: pass_copy(i).wait_send())


def gather_inputs(style_rows, bank, parts):
    count, rows, depth = parts.shape
    width = bank.shape[-1]
    sems = [DMA((count,)) for _ in range(12)]
    return pl.pallas_call(
        partial(gather_kernel, count),
        out_shape=(
            jax.ShapeDtypeStruct((count, PIX, rows, depth), halves),
            jax.ShapeDtypeStruct((count, 9, depth, width), halves),
            jax.ShapeDtypeStruct((count, 8, 128), floats),
            jax.ShapeDtypeStruct((count, width), floats),
        ),
        in_specs=[VMEM, VMEM, ANY],
        out_specs=(ANY, VMEM, VMEM, VMEM),
        scratch_shapes=[
            pltpu.VMEM((count, width), floats),
            pltpu.VMEM((count, count, width), floats),
            DMA,
        ]
        + sems,
        compiler_params=params(0),
        name="gather_inputs",
    )(style_rows, bank, parts)


def conv_kernel(
    count,
    width,
    images_ref,
    kernel_ref,
    own_ref,
    gain_ref,
    conv_ref,
    conv_own_ref,
    hidden_ref,
    normed_ref,
    image_buf,
    padded,
    total,
    pair_out,
    pair_in,
    line_out,
    line_in,
    block_out,
    block_in,
    image_sem,
    pair_send,
    pair_recv,
    line_send,
    line_recv,
    block_send,
    block_recv,
    norm_send,
    norm_recv,
):
    row, col = lax.axis_index("dp"), lax.axis_index("pix")
    groups = count // 2
    slots = pair_out.shape[0]
    side = lax.rem(row, 2)
    level = lax.div(row, 2)
    partner = flip(row, 1)
    near, far = flip(col, 1), flip(col, 2)
    cross = flip(near, 2)
    tokens, depth = image_buf.shape[1], image_buf.shape[2]
    channels = total.shape[1]
    rows = tokens // PIX
    halo = width

    has_below, has_above = level > 0, level < groups - 1
    below, above = jnp.maximum(row - 2, 0), jnp.minimum(row + 2, count - 1)

    barrier = pltpu.get_barrier_semaphore()
    for known, other in ((has_below, below), (has_above, above)):

        @pl.when(known)
        def _(other=other):
            pl.semaphore_signal(barrier, inc=1, device_id=(other, col), device_id_type=MESH)

    for other in ((partner, col), (row, near), (row, far), (row, cross)):
        pl.semaphore_signal(barrier, inc=1, device_id=other, device_id_type=MESH)
    pl.semaphore_wait(barrier, 4 + has_below.astype(jnp.int32) + has_above.astype(jnp.int32))

    def group_of(step):
        return level_at(level, groups, groups - 1 - step)

    def sample_of(index):
        mine = lax.div(index, groups)
        group = group_of(lax.rem(index, groups))
        return 2 * group + jnp.where(mine == 1, side, 1 - side)

    def fetch(index):
        slot = lax.rem(index, 2)
        return pltpu.make_async_copy(
            images_ref.at[sample_of(index)], image_buf.at[slot], image_sem.at[slot]
        )

    zeros = jnp.zeros((3, halo, depth), halves)
    padded[:, 0:halo, :] = zeros
    padded[:, halo + tokens : halo + tokens + halo, :] = zeros
    fetch(0).start()
    place = lax.rem(lax.broadcasted_iota(jnp.int32, (tokens, depth), 0), width)

    def stage(index):
        fetch(index).wait()

        @pl.when(index + 1 < count)
        def _():
            fetch(index + 1).start()

        source = image_buf[lax.rem(index, 2)]
        wide = source.astype(floats)
        padded[1, halo : halo + tokens, :] = source
        before = jnp.where(place == 0, 0.0, pltpu.roll(wide, 1, 0))
        padded[0, halo : halo + tokens, :] = before.astype(halves)
        after = jnp.where(place == width - 1, 0.0, pltpu.roll(wide, tokens - 1, 0))
        padded[2, halo : halo + tokens, :] = after.astype(halves)

    def rows_of(sample, start):
        acc = jnp.zeros((rows, channels), floats)
        for a in range(3):
            for b in range(3):
                window = padded[b, pl.ds(pl.multiple_of(start + a * width, 16), rows), :]
                acc = acc + jnp.dot(
                    window, kernel_ref[sample, 3 * a + b], preferred_element_type=floats
                )
        return acc

    def pair_copy(step):
        return remote(
            pair_out.at[lax.rem(step, slots)],
            pair_in.at[step],
            pair_send.at[step],
            pair_recv.at[step],
            (partner, col),
        )

    def line_copy(step, upward):
        group = group_of(step)
        if upward:
            slot, target = group, above
        else:
            slot, target = jnp.where(group == level - 1, groups, group), below
        return remote(
            line_out.at[lax.rem(step, slots)],
            line_in.at[slot],
            line_send.at[step],
            line_recv.at[slot],
            (target, col),
        )

    def line_arrives(slot):
        remote(
            line_out.at[0], line_in.at[slot], line_send.at[0], line_recv.at[slot], (partner, col)
        ).wait_recv()

    def give(step):
        @pl.when(step >= slots)
        def _():
            pair_copy(step - slots).wait_send()

        stage(step)
        sample = sample_of(step)

        def chunk(i):
            start = pl.multiple_of(i * rows, rows)
            pair_out[lax.rem(step, slots), pl.ds(start, rows), :] = rows_of(sample, start).astype(
                halves
            )

        loop(PIX, chunk)
        pair_copy(step).start()

    loop(groups, give)

    def keep(step):
        @pl.when(step >= slots)
        def _():
            line_copy(step - slots, True).wait_send()

        stage(groups + step)
        group = group_of(step)
        sample = 2 * group + side
        out = lax.rem(step, slots)

        def chunk(i):
            start = pl.multiple_of(i * rows, rows)
            total[pl.ds(start, rows), :] = rows_of(sample, start)

        loop(PIX, chunk)
        pair_copy(step).wait_recv()
        passing = jnp.where(group > level, has_below, has_above)

        @pl.when(passing)
        def _():
            line_arrives(group)

            def add(i):
                here = pl.ds(pl.multiple_of(i * rows, rows), rows)
                line_out[out, here, :] = (
                    total[here, :]
                    + pair_in[step, here, :].astype(floats)
                    + line_in[group, here, :].astype(floats)
                ).astype(halves)

            loop(PIX, add)

        @pl.when(jnp.logical_not(passing))
        def _():
            def add(i):
                here = pl.ds(pl.multiple_of(i * rows, rows), rows)
                line_out[out, here, :] = (
                    total[here, :] + pair_in[step, here, :].astype(floats)
                ).astype(halves)

            loop(PIX, add)

        @pl.when(group > level)
        def _():
            line_copy(step, True).start()

        @pl.when(group < level)
        def _():
            line_copy(step, False).start()

    loop(groups - 1, keep)
    last = groups - 1
    stage(count - 1)

    def own_chunk(i):
        start = pl.multiple_of(i * rows, rows)
        total[pl.ds(start, rows), :] = rows_of(row, start)

    loop(PIX, own_chunk)
    pair_copy(last).wait_recv()
    for known, slot in ((has_below, level), (has_above, groups)):

        @pl.when(known)
        def _(slot=slot):
            line_arrives(slot)

            def add(i):
                here = pl.ds(pl.multiple_of(i * rows, rows), rows)
                total[here, :] += line_in[slot, here, :].astype(floats)

            loop(PIX, add)

    def block_copy(turn):
        target = (far, cross, near)[turn]
        return remote(
            block_out.at[turn], block_in.at[col], block_send.at[turn], block_recv.at[turn], (row, target)
        )

    def block_arrives(turn):
        origin = (far, cross, near)[turn]
        remote(
            block_out.at[turn], block_in.at[origin], block_send.at[turn], block_recv.at[turn], (row, near)
        ).wait_recv()

    for turn, target in enumerate((far, cross, near, col)):
        here = pl.ds(pl.multiple_of(target * rows, rows), rows)
        value = total[here, :] + pair_in[last, here, :].astype(floats)
        rounded = value.astype(halves)
        conv_own_ref[here, :] = rounded
        if turn < 3:
            block_out[turn] = rounded
            block_copy(turn).start()
        else:
            block_in[col] = rounded
    for turn in range(3):
        block_arrives(turn)

    part = rows // 4

    def norm_rows(i):
        here = pl.ds(pl.multiple_of(i * part, part), part)
        for j in range(PIX):
            conv_ref[here, j * channels : (j + 1) * channels] = block_in[j, here, :]
        conv = conv_ref[here, :].astype(floats)
        hidden = own_ref[here, :].astype(floats) + conv * jax.nn.sigmoid(conv)
        hidden_ref[here, :] = hidden
        mean = jnp.mean(hidden * hidden, -1, keepdims=True)
        normed_ref[col, here, :] = (hidden * lax.rsqrt(mean + 1e-06) * gain_ref[...]).astype(halves)

    loop(4, norm_rows)
    mine, theirs = normed_ref.at[col], normed_ref.at[far]
    to_far = remote(mine, mine, norm_send.at[0], norm_recv.at[0], (row, far))
    to_near = remote(mine, mine, norm_send.at[1], norm_recv.at[1], (row, near))
    to_far.start()
    to_near.start()
    remote(mine, theirs, norm_send.at[0], norm_recv.at[0], (row, far)).wait_recv()
    onward = remote(theirs, theirs, norm_send.at[2], norm_recv.at[2], (row, near))
    onward.start()
    remote(mine, normed_ref.at[near], norm_send.at[1], norm_recv.at[1], (row, near)).wait_recv()
    remote(mine, normed_ref.at[cross], norm_send.at[2], norm_recv.at[2], (row, near)).wait_recv()
    to_far.wait_send()
    to_near.wait_send()
    onward.wait_send()
    for turn in range(3):
        block_copy(turn).wait_send()
    for step in range(max(0, groups - slots), groups):
        pair_copy(step).wait_send()
    for step in range(max(0, groups - 1 - slots), groups - 1):
        line_copy(step, True).wait_send()


def conv_forward(images_all, kernels, own, gain, width):
    count, tokens, depth = images_all.shape
    channels = kernels.shape[-1]
    rows, full = own.shape
    groups = count // 2
    slots = min(groups, 4)
    block = (tokens, channels)
    return pl.pallas_call(
        partial(conv_kernel, count, width),
        out_shape=(
            jax.ShapeDtypeStruct((rows, full), halves),
            jax.ShapeDtypeStruct((tokens, channels), halves),
            jax.ShapeDtypeStruct((rows, full), floats),
            jax.ShapeDtypeStruct((PIX, rows, full), halves),
        ),
        in_specs=[ANY, VMEM, VMEM, VMEM],
        out_specs=(VMEM, VMEM, VMEM, VMEM),
        scratch_shapes=[
            pltpu.VMEM((2, tokens, depth), halves),
            pltpu.VMEM((3, tokens + 2 * width, depth), halves),
            pltpu.VMEM(block, floats),
            pltpu.VMEM((slots,) + block, halves),
            pltpu.VMEM((groups,) + block, halves),
            pltpu.VMEM((slots,) + block, halves),
            pltpu.VMEM((groups + 1,) + block, halves),
            pltpu.VMEM((3, rows, channels), halves),
            pltpu.VMEM((PIX, rows, channels), halves),
            DMA((2,)),
            DMA((groups,)),
            DMA((groups,)),
            DMA((groups,)),
            DMA((groups + 1,)),
            DMA((3,)),
            DMA((3,)),
            DMA((3,)),
            DMA((3,)),
        ],
        compiler_params=params(1),
        name="conv_forward",
    )(images_all, kernels, own, gain.reshape(1, -1))


def peers(col):
    near, far = flip(col, 1), flip(col, 2)
    return near, far, flip(near, 2)


def greet_pixels(row, others):
    barrier = pltpu.get_barrier_semaphore()
    for other in others:
        pl.semaphore_signal(barrier, inc=1, device_id=(row, other), device_id_type=MESH)
    pl.semaphore_wait(barrier, len(others))


NT = (((1,), (1,)), ((), ()))
TN = (((0,), (0,)), ((), ()))


def mul_nt(a, b, precision=None):
    return lax.dot_general(a, b, NT, preferred_element_type=floats, precision=precision)


def mul_tn(a, b, precision=None):
    return lax.dot_general(a, b, TN, preferred_element_type=floats, precision=precision)


def mul(a, b):
    return jnp.dot(a, b, preferred_element_type=floats)


def attend_kernel(
    normed_ref,
    weight_ref,
    text_ref,
    query_ref,
    key_ref,
    value_ref,
    total_ref,
    attended_ref,
    text_out_ref,
    block_out,
    key_norm,
    block_send,
    block_recv,
    text_send,
    text_recv,
):
    row, col = lax.axis_index("dp"), lax.axis_index("pix")
    near, far, cross = peers(col)
    targets = (far, cross, near)
    greet_pixels(row, targets)
    rows = normed_ref.shape[1]
    width = query_ref.shape[1]
    heads = width // HEAD_DIM
    score_scale = HEAD_DIM ** (-0.5)

    for j in range(2):
        here = slice(j * width, (j + 1) * width)
        weight = weight_ref[:, (3 + j) * width : (4 + j) * width]
        text_out_ref[col, :, here] = mul(text_ref[...], weight).astype(halves)

    def text_copy(turn):
        block = text_out_ref.at[col]
        return remote(block, block, text_send.at[turn], text_recv.at[turn], (row, targets[turn]))

    for turn in range(3):
        text_copy(turn).start()

    def project(i):
        source = normed_ref[i]
        here = pl.ds(pl.multiple_of(i * rows, rows), rows)
        for j, out in enumerate((query_ref, key_ref, value_ref)):
            out[here, :] = mul(source, weight_ref[:, j * width : (j + 1) * width]).astype(halves)

    loop(PIX, project)
    ones = jnp.ones((8, HEAD_DIM), floats)
    for h in range(heads):
        key = key_ref[:, h * HEAD_DIM : (h + 1) * HEAD_DIM].astype(floats)
        key_norm[h] = mul_nt(ones, key * key, highest)

    def attend(target, store):
        here = pl.ds(pl.multiple_of(target * rows, rows), rows)
        for h in range(heads):
            lanes = slice(h * HEAD_DIM, (h + 1) * HEAD_DIM)
            inner = mul_nt(query_ref[here, lanes], key_ref[:, lanes])
            scores = score_scale * (2.0 * inner - key_norm[h, 0:1, :])
            largest = jnp.max(scores, -1, keepdims=True)
            expanded = jnp.exp(scores - largest)
            summed = jnp.sum(expanded, -1, keepdims=True)
            weights = (expanded * (1.0 / summed)).astype(halves)
            store(lanes, mul(weights, value_ref[:, lanes]).astype(halves))
            total_ref[here, h : h + 1] = largest + jnp.log(summed)

    def block_copy(turn):
        return remote(
            block_out.at[turn],
            attended_ref.at[col],
            block_send.at[turn],
            block_recv.at[turn],
            (row, targets[turn]),
        )

    def turn_body(turn):
        target = jnp.where(turn == 0, far, jnp.where(turn == 1, cross, jnp.where(turn == 2, near, col)))

        def store(lanes, result):
            block_out[turn, :, lanes] = result

        attend(target, store)
        for k in range(3):

            @pl.when(turn == k)
            def _(k=k):
                block_copy(k).start()

    loop(4, turn_body)
    attended_ref[col] = block_out[3]
    for turn in range(3):
        remote(
            block_out.at[turn],
            attended_ref.at[targets[turn]],
            block_send.at[turn],
            block_recv.at[turn],
            (row, near),
        ).wait_recv()
        block = text_out_ref.at[targets[turn]]
        remote(block, block, text_send.at[turn], text_recv.at[turn], (row, near)).wait_recv()
    for turn in range(3):
        block_copy(turn).wait_send()
        text_copy(turn).wait_send()


def attend_forward(normed, weights, text):
    count, rows, full = normed.shape
    tokens, width = count * rows, weights.shape[1] // 5
    heads = width // HEAD_DIM
    flat = jax.ShapeDtypeStruct((tokens, width), halves)
    return pl.pallas_call(
        attend_kernel,
        out_shape=(
            flat,
            flat,
            flat,
            jax.ShapeDtypeStruct((tokens, 128), floats),
            jax.ShapeDtypeStruct((PIX, rows, width), halves),
            jax.ShapeDtypeStruct((PIX, text.shape[0], 2 * width), halves),
        ),
        in_specs=[VMEM] * 3,
        out_specs=(VMEM,) * 6,
        scratch_shapes=[
            pltpu.VMEM((4, rows, width), halves),
            pltpu.VMEM((heads, 8, tokens), floats),
            DMA((3,)),
            DMA((3,)),
            DMA((3,)),
            DMA((3,)),
        ],
        compiler_params=params(2),
        name="attend_forward",
    )(normed, weights, text)


def cross_kernel(
    words,
    attended_ref,
    hidden_ref,
    weight_ref,
    text_ref,
    gain_ref,
    rgb_scale_ref,
    rgb_weight_ref,
    cotangent_ref,
    rgb_cotangent_ref,
    penalty_ref,
    output_ref,
    rgb_ref,
    reduced_ref,
    text_grad_ref,
    grad_two_ref,
    grad_attended_ref,
    small_ref,
    attended,
    grad_attn,
    two,
    normed,
    query,
    probs,
    crossed,
    mixed,
    grad_three,
    grad_proj,
    grad_crossed,
    grad_query,
    grad_norm,
    near_out,
    near_in,
    kept,
    line_out,
    line_in,
    near_send,
    near_recv,
    line_send,
    line_recv,
):
    row, col = lax.axis_index("dp"), lax.axis_index("pix")
    near, far, cross = peers(col)
    greet_pixels(row, (near, far))
    rows, full = hidden_ref.shape
    tile = full // PIX
    score_scale = HEAD_DIM ** (-0.5)
    W_OUT, C_QUERY, C_OUT = (slice(i * tile, (i + 1) * tile) for i in range(3))
    part = 64

    def cols(j):
        return pl.ds(pl.multiple_of(j * tile, tile), tile)

    def near_copy(which):
        return remote(
            near_out.at[which], near_in.at[which], near_send.at[which], near_recv.at[which], (row, near)
        )

    def line_copy(which):
        return remote(
            line_out.at[which], line_in.at[which], line_send.at[which], line_recv.at[which], (row, far)
        )

    def start_grad(which, left, right):
        def tile_of(index, targets):
            i, b = lax.div(index, 2), lax.rem(index, 2)
            return i, b, mul_tn(left[:, cols(i)], right[:, cols(jnp.where(b == 0, *targets))])

        def give(index):
            i, b, value = tile_of(index, (near, cross))
            near_out[which, b, cols(i), :] = value.astype(halves)

        def keep(index):
            i, b, value = tile_of(index, (col, far))
            kept[which, b, cols(i), :] = value

        loop(2 * PIX, give)
        near_copy(which).start()
        loop(2 * PIX, keep)

    def pass_grad(which):
        near_copy(which).wait_recv()

        def add(i):
            here = cols(i)
            line_out[which, here, :] = (
                kept[which, 1, here, :] + near_in[which, 1, here, :].astype(floats)
            ).astype(halves)

        loop(PIX, add)
        line_copy(which).start()

    def end_grad(which):
        line_copy(which).wait_recv()

        def add(i):
            here = cols(i)
            reduced_ref[here, which * tile : (which + 1) * tile] = (
                kept[which, 0, here, :]
                + near_in[which, 0, here, :].astype(floats)
                + line_in[which, here, :].astype(floats)
            ).astype(halves)

        loop(PIX, add)
        near_copy(which).wait_send()
        line_copy(which).wait_send()

    for j in range(PIX):
        attended[:, j * tile : (j + 1) * tile] = attended_ref[j]

    def out_two(j):
        two[:, cols(j)] = hidden_ref[:, cols(j)] + mul(attended[...], weight_ref[j, :, W_OUT])

    loop(PIX, out_two)

    def norm_two(i):
        here = pl.ds(pl.multiple_of(i * part, part), part)
        hidden = two[here, :]
        mean = jnp.mean(hidden * hidden, -1, keepdims=True)
        normed[here, :] = (hidden * lax.rsqrt(mean + 1e-06) * gain_ref[...]).astype(halves)

    loop(rows // part, norm_two)

    def out_query(j):
        query[:, cols(j)] = mul(normed[...], weight_ref[j, :, C_QUERY]).astype(halves)

    loop(PIX, out_query)
    slots = text_ref.shape[1]
    known = lax.broadcasted_iota(jnp.int32, (rows, slots), 1) < words
    pairs = tile // 128

    def text_lanes(pair, side):
        return pl.ds(pl.multiple_of(side * tile + lax.rem(pair, pairs) * 128, 128), 128)

    def cross_pair(pair):
        here = pl.ds(pl.multiple_of(pair * 128, 128), 128)
        group = lax.div(pair, pairs)
        queries = query[:, here]
        keys = text_ref[group, :, text_lanes(pair, 0)]
        values = text_ref[group, :, text_lanes(pair, 1)]
        outs = []
        for h in range(2):
            lanes = slice(h * HEAD_DIM, (h + 1) * HEAD_DIM)
            scores = score_scale * mul_nt(queries[:, lanes], keys[:, lanes])
            scores = jnp.where(known, scores, -1e30)
            expanded = jnp.exp(scores - jnp.max(scores, -1, keepdims=True))
            prob = expanded / jnp.sum(expanded, -1, keepdims=True)
            probs[2 * pair + h] = prob
            outs.append(mul(prob.astype(halves), values[:, lanes]))
        crossed[:, here] = jnp.concatenate(outs, axis=1).astype(halves)

    loop(full // 128, cross_pair)
    rgb_ref[...] = jnp.zeros_like(rgb_ref)

    def out_three(j):
        three = two[:, cols(j)] + mul(crossed[...], weight_ref[j, :, C_OUT])
        output_ref[:, cols(j)] = three
        blend = (three * rgb_scale_ref[:, cols(j)]).astype(halves)
        mixed[:, cols(j)] = blend
        rgb_ref[...] += mul(blend, rgb_weight_ref[cols(j), :])

    loop(PIX, out_three)
    rgb_grad = rgb_cotangent_ref[...] + penalty_weight * penalty_ref[...] * rgb_ref[...]

    def back_three(j):
        color = mul_tn(rgb_grad, mixed[:, cols(j)].astype(floats), highest)
        small_ref[2:5, cols(j)] = color[0:3]
        grad_mixed = mul_nt(rgb_grad, rgb_weight_ref[cols(j), :].astype(floats), highest)
        small_ref[1:2, cols(j)] = jnp.sum(grad_mixed * output_ref[:, cols(j)], 0, keepdims=True)
        grad = cotangent_ref[:, cols(j)].astype(floats) + grad_mixed * rgb_scale_ref[:, cols(j)]
        grad_three[:, cols(j)] = grad
        grad_proj[:, cols(j)] = grad.astype(halves)

    loop(PIX, back_three)
    start_grad(1, crossed, grad_proj)

    def times_transposed(source, j, which):
        acc = jnp.zeros((rows, tile), floats)
        for i in range(PIX):
            acc = acc + mul_nt(source[:, i * tile : (i + 1) * tile], weight_ref[i, cols(j), which])
        return acc

    def back_crossed(j):
        grad_crossed[:, cols(j)] = times_transposed(grad_proj, j, C_OUT).astype(halves)

    loop(PIX, back_crossed)

    def back_pair(pair):
        here = pl.ds(pl.multiple_of(pair * 128, 128), 128)
        group = lax.div(pair, pairs)
        queries, grads = query[:, here], grad_crossed[:, here]
        keys = text_ref[group, :, text_lanes(pair, 0)]
        values = text_ref[group, :, text_lanes(pair, 1)]
        grad_q, grad_k, grad_v = [], [], []
        for h in range(2):
            lanes = slice(h * HEAD_DIM, (h + 1) * HEAD_DIM)
            prob = probs[2 * pair + h]
            grad = grads[:, lanes]
            grad_prob = mul_nt(grad, values[:, lanes])
            grad_v.append(mul_tn(prob.astype(halves), grad))
            inner = jnp.sum(grad_prob * prob, -1, keepdims=True)
            score = (prob * (grad_prob - inner)).astype(halves)
            grad_q.append(score_scale * mul(score, keys[:, lanes]))
            grad_k.append(score_scale * mul_tn(score, queries[:, lanes]))
        grad_query[:, here] = jnp.concatenate(grad_q, axis=1).astype(halves)
        text_grad_ref[group, :, text_lanes(pair, 0)] = jnp.concatenate(grad_k, axis=1).astype(halves)
        text_grad_ref[group, :, text_lanes(pair, 1)] = jnp.concatenate(grad_v, axis=1).astype(halves)

    loop(full // 128, back_pair)
    pass_grad(1)
    start_grad(0, normed, grad_query)

    def back_query(j):
        grad_norm[:, cols(j)] = times_transposed(grad_query, j, C_QUERY)

    loop(PIX, back_query)
    pass_grad(0)
    small_ref[0:1, :] = jnp.zeros((1, full), floats)

    def back_norm(i):
        here = pl.ds(pl.multiple_of(i * part, part), part)
        hidden, grad = two[here, :], grad_norm[here, :]
        inverse = lax.rsqrt(jnp.mean(hidden * hidden, -1, keepdims=True) + 1e-06)
        small_ref[0:1, :] += jnp.sum(grad * hidden * inverse, 0, keepdims=True)
        scaled = grad * gain_ref[...]
        mean = jnp.mean(scaled * hidden, -1, keepdims=True)
        total = grad_three[here, :] + inverse * scaled - hidden * (inverse * inverse * inverse * mean)
        grad_two_ref[here, :] = total
        grad_attn[here, :] = total.astype(halves)

    loop(rows // part, back_norm)

    def back_attended(j):
        grad_attended_ref[j] = times_transposed(grad_attn, j, W_OUT).astype(halves)

    loop(PIX, back_attended)

    small_ref[5:8, :] = jnp.zeros((3, full), floats)
    end_grad(1)
    end_grad(0)


def cross_part(
    words, attended, hidden, weights, text, gain, rgb_scale, rgb_weight, cotangent, rgb_cotangent, penalty
):
    rows, full = hidden.shape
    tile = full // PIX
    heads = full // HEAD_DIM
    wide = pltpu.VMEM((rows, full), floats)
    slim = pltpu.VMEM((rows, full), halves)
    return pl.pallas_call(
        partial(cross_kernel, words),
        out_shape=(
            jax.ShapeDtypeStruct((rows, full), floats),
            jax.ShapeDtypeStruct((rows, 128), floats),
            jax.ShapeDtypeStruct((full, 2 * tile), halves),
            jax.ShapeDtypeStruct(text.shape, halves),
            jax.ShapeDtypeStruct((rows, full), floats),
            jax.ShapeDtypeStruct((PIX, rows, tile), halves),
            jax.ShapeDtypeStruct((8, full), floats),
            jax.ShapeDtypeStruct((rows, full), halves),
            jax.ShapeDtypeStruct((rows, full), halves),
        ),
        in_specs=[VMEM] * 10,
        out_specs=(VMEM,) * 9,
        scratch_shapes=[
            wide,
            slim,
            slim,
            pltpu.VMEM((heads, rows, text.shape[1]), floats),
            slim,
            slim,
            wide,
            slim,
            slim,
            slim,
            wide,
            pltpu.VMEM((2, 2, full, tile), halves),
            pltpu.VMEM((2, 2, full, tile), halves),
            pltpu.VMEM((2, 2, full, tile), floats),
            pltpu.VMEM((2, full, tile), halves),
            pltpu.VMEM((2, full, tile), halves),
            DMA((2,)),
            DMA((2,)),
            DMA((2,)),
            DMA((2,)),
        ],
        compiler_params=params(6),
        name="cross_part",
    )(
        attended,
        hidden,
        weights,
        text,
        gain.reshape(1, -1),
        rgb_scale,
        rgb_weight,
        cotangent,
        rgb_cotangent,
        penalty,
    )


def attend_back_kernel(
    grad_ref,
    query_ref,
    key_ref,
    value_ref,
    total_ref,
    normed_ref,
    weight_ref,
    hidden_ref,
    conv_ref,
    grad_two_ref,
    gain_ref,
    text_ref,
    text_grad_ref,
    reduced_ref,
    attended_ref,
    grad_attn_ref,
    attention_ref,
    others_ref,
    grad_one_ref,
    grad_conv_ref,
    small_ref,
    grads,
    grad_query,
    grad_key,
    grad_value,
    key_acc,
    value_acc,
    totals,
    pair_out,
    pair_in,
    line_out,
    line_in,
    own,
    conv_out,
    text_in,
    near_out,
    near_in,
    near_kept,
    far_out,
    far_in,
    side_in,
    level_out,
    level_in,
    out_grad,
    out_side_in,
    out_level_out,
    out_level_in,
    attention_grad,
    attention_in,
    grad_send,
    grad_recv,
    text_send,
    text_recv,
    pair_send,
    pair_recv,
    line_send,
    line_recv,
    conv_send,
    conv_recv,
    near_send,
    near_recv,
    far_send,
    far_recv,
    side_send,
    side_recv,
    level_send,
    level_recv,
    out_side_send,
    out_side_recv,
    out_level_send,
    out_level_recv,
    attention_send,
    attention_recv,
):
    row, col = lax.axis_index("dp"), lax.axis_index("pix")
    near, far, cross = peers(col)
    targets = (far, cross, near)
    groups, _, owned, _ = attention_grad.shape
    side, level = lax.rem(row, 2), lax.div(row, 2)
    partner = flip(row, 1)
    barrier = pltpu.get_barrier_semaphore()

    def hello(step, carry):
        other = 2 * lax.rem(level + step, groups) + side
        pl.semaphore_signal(barrier, inc=1, device_id=(other, col), device_id_type=MESH)
        return carry

    lax.fori_loop(1, groups, hello, 0)
    for other in ((partner, col), (row, near), (row, far), (row, cross)):
        pl.semaphore_signal(barrier, inc=1, device_id=other, device_id_type=MESH)
    pl.semaphore_wait(barrier, groups - 1 + 4)
    rows, full = hidden_ref.shape
    tokens, width = query_ref.shape
    heads = width // HEAD_DIM
    score_scale = HEAD_DIM ** (-0.5)

    def grad_copy(turn):
        return remote(
            grad_ref.at[targets[turn]],
            grads.at[col],
            grad_send.at[turn],
            grad_recv.at[turn],
            (row, targets[turn]),
        )

    used = text_in.shape[1]

    def text_copy(turn):
        return remote(
            text_grad_ref.at[targets[turn], pl.ds(0, used), :],
            text_in.at[turn],
            text_send.at[turn],
            text_recv.at[turn],
            (row, targets[turn]),
        )

    for turn in range(3):
        grad_copy(turn).start()
    for turn in range(3):
        text_copy(turn).start()

    def side_copy():
        return remote(
            reduced_ref.at[:, 1 - side], side_in, side_send, side_recv, (partner, col)
        )

    def out_side_copy():
        return remote(
            out_grad.at[:, 1 - side], out_side_in, out_side_send, out_side_recv, (partner, col)
        )

    def level_copy(k):
        group = lax.rem(level + k, groups)
        return remote(
            level_out.at[group], level_in.at[k], level_send.at[k], level_recv.at[k], (2 * group + side, col)
        )

    def out_level_copy(k):
        group = lax.rem(level + k, groups)
        return remote(
            out_level_out.at[group],
            out_level_in.at[k],
            out_level_send.at[k],
            out_level_recv.at[k],
            (2 * group + side, col),
        )

    def level_sum(copy, source, arrived, out):
        copy().wait_recv()

        def add(group):
            out[group] = (source[group, side].astype(floats) + arrived[group].astype(floats)).astype(
                halves
            )

        loop(groups, add)

    side_copy().start()

    def near_copy():
        return remote(near_out, near_in, near_send, near_recv, (row, near))

    def far_copy():
        return remote(far_out, far_in, far_send, far_recv, (row, far))

    def row_tile(i):
        return pl.ds(pl.multiple_of(i * width, width), width)

    def out_tile(index, first, second):
        i, b = lax.div(index, 2), lax.rem(index, 2)
        right = grad_attn_ref[:, row_tile(jnp.where(b == 0, first, second))]
        return i, b, mul_tn(attended_ref[:, row_tile(i)], right)

    def out_give(index):
        i, b, value = out_tile(index, near, cross)
        near_out[b, row_tile(i), :] = value.astype(halves)

    def out_keep(index):
        i, b, value = out_tile(index, col, far)
        near_kept[b, row_tile(i), :] = value

    loop(2 * PIX, out_give)
    near_copy().start()
    loop(2 * PIX, out_keep)
    per_tile = width // (2 * owned)

    def out_pass():
        near_copy().wait_recv()

        def add(i):
            here = row_tile(i)
            far_out[here, :] = (
                near_kept[1, here, :] + near_in[1, here, :].astype(floats)
            ).astype(halves)

        loop(PIX, add)
        far_copy().start()

    def out_end():
        far_copy().wait_recv()

        def add(i):
            here = row_tile(i)
            value = (
                near_kept[0, here, :]
                + near_in[0, here, :].astype(floats)
                + far_in[here, :].astype(floats)
            ).astype(halves)
            out_grad[pl.ds(i * per_tile, per_tile)] = value.reshape(per_tile, 2, owned, width)

        loop(PIX, add)
        out_side_copy().start()

    def between(h):
        if h == 0:
            out_pass()
            level_sum(side_copy, reduced_ref, side_in, level_out)
            lax.fori_loop(1, groups, lambda k, c: (level_copy(k).start(), c)[1], 0)
        if h == 1:
            out_end()
        if h == 2:
            level_sum(out_side_copy, out_grad, out_side_in, out_level_out)
            lax.fori_loop(1, groups, lambda k, c: (out_level_copy(k).start(), c)[1], 0)

    grads[col] = grad_ref[col]
    totals[...] = jnp.transpose(total_ref[...])
    for turn in range(3):
        remote(
            grad_ref.at[0],
            grads.at[targets[turn]],
            grad_send.at[turn],
            grad_recv.at[turn],
            (row, near),
        ).wait_recv()
    ones = jnp.ones((rows, HEAD_DIM), halves)
    for h in range(heads):
        lanes = slice(h * HEAD_DIM, (h + 1) * HEAD_DIM)
        keys, values = key_ref[:, lanes], value_ref[:, lanes]
        wide = keys.astype(floats)
        norm = score_scale * jnp.sum(wide * wide, -1, keepdims=True)
        key_acc[...] = jnp.zeros_like(key_acc)
        value_acc[...] = jnp.zeros_like(value_acc)

        def block(i, lanes=lanes, keys=keys, values=values, norm=norm, h=h):
            here = pl.ds(pl.multiple_of(i * rows, rows), rows)
            queries, grad = query_ref[here, lanes], grads[i, :, lanes]
            inner = mul_nt(keys, queries)
            prob = jnp.exp((2.0 * score_scale) * inner - norm - totals[h : h + 1, here])
            grad_prob = mul_nt(values, grad)
            value_acc[...] += mul(prob.astype(halves), grad)
            mean = jnp.sum(grad_prob * prob, 0, keepdims=True)
            score = (prob * (grad_prob - mean)).astype(halves)
            key_acc[...] += mul(score, jnp.concatenate([queries, ones], axis=1))
            grad_query[here, lanes] = (2.0 * score_scale * mul_tn(score, keys)).astype(halves)

        loop(PIX, block)
        acc = key_acc[...]
        grad_key[:, lanes] = (
            2.0 * score_scale * (acc[:, :HEAD_DIM] - wide * acc[:, HEAD_DIM : HEAD_DIM + 1])
        ).astype(halves)
        grad_value[:, lanes] = value_acc[...].astype(halves)
        between(h)

    def norm_grad(block, store):
        here = pl.ds(pl.multiple_of(block * rows, rows), rows)

        def tile(j):
            cols = pl.ds(pl.multiple_of(j * width, width), width)
            acc = jnp.zeros((rows, width), floats)
            for k, source in enumerate((grad_query, grad_key, grad_value)):
                acc = acc + mul_nt(source[here, :], weight_ref[cols, k * width : (k + 1) * width])
            store(cols, acc)

        loop(full // width, tile)

    def pair_copy(turn):
        return remote(
            pair_out.at[turn], pair_in.at[turn], pair_send.at[turn], pair_recv.at[turn], (row, near)
        )

    for turn, target in enumerate((cross, near)):

        def store(cols, value, turn=turn):
            pair_out[turn, :, cols] = value.astype(halves)

        norm_grad(target, store)
        pair_copy(turn).start()
    line = remote(line_out, line_in, line_send, line_recv, (row, far))

    def store_far(cols, value):
        line_out[:, cols] = (value + pair_in[0, :, cols].astype(floats)).astype(halves)

    pair_copy(0).wait_recv()
    norm_grad(far, store_far)
    line.start()

    def store_own(cols, value):
        own[:, cols] = value + pair_in[1, :, cols].astype(floats)

    pair_copy(1).wait_recv()
    norm_grad(col, store_own)

    text_total = text_grad_ref[col, 0:used, :].astype(floats)
    for turn in range(3):
        text_copy(turn).wait_recv()
        text_total = text_total + text_in[turn].astype(floats)
    text_total = jnp.concatenate(
        [text_total, jnp.zeros((text_ref.shape[0] - used, 2 * width), floats)], axis=0
    )

    def attention_copy(j):
        here = pl.ds(j * per_tile, per_tile)
        return remote(
            attention_grad.at[here, 1 - side],
            attention_in.at[here],
            attention_send.at[j],
            attention_recv.at[j],
            (partner, col),
        )

    def weight_grads(j):
        cols = row_tile(j)
        here = pl.ds(j * per_tile, per_tile)

        def put(k, value):
            attention_grad[here, :, :, k * width : (k + 1) * width] = value.astype(halves).reshape(
                per_tile, 2, owned, width
            )

        for k, right in enumerate((grad_query, grad_key, grad_value)):
            acc = jnp.zeros((width, width), floats)
            for i in range(PIX):
                acc = acc + mul_tn(normed_ref[i, :, cols], right[i * rows : (i + 1) * rows, :])
            put(k, acc)
        for k in range(2):
            right = text_total[:, k * width : (k + 1) * width]
            put(3 + k, mul_tn(text_ref[:, cols].astype(floats), right, highest))
        attention_copy(j).start()

    loop(full // width, weight_grads)
    line.wait_recv()
    small_ref[...] = jnp.zeros_like(small_ref)
    part = 64

    def back_norm(i):
        here = pl.ds(pl.multiple_of(i * part, part), part)
        hidden = hidden_ref[here, :]
        grad = own[here, :] + line_in[here, :].astype(floats)
        inverse = lax.rsqrt(jnp.mean(hidden * hidden, -1, keepdims=True) + 1e-06)
        small_ref[0:1, :] += jnp.sum(grad * hidden * inverse, 0, keepdims=True)
        scaled = grad * gain_ref[...]
        mean = jnp.mean(scaled * hidden, -1, keepdims=True)
        total = (
            grad_two_ref[here, :] + inverse * scaled - hidden * (inverse * inverse * inverse * mean)
        )
        grad_one_ref[here, :] = total
        conv = conv_ref[here, :].astype(floats)
        gate = jax.nn.sigmoid(conv)
        result = (total * gate * (1.0 + conv * (1.0 - gate))).astype(halves)
        for j in range(PIX):
            conv_out[j, here, :] = result[:, j * width : (j + 1) * width]

    loop(rows // part, back_norm)

    def conv_copy(turn):
        return remote(
            conv_out.at[targets[turn]],
            grad_conv_ref.at[col],
            conv_send.at[turn],
            conv_recv.at[turn],
            (row, targets[turn]),
        )

    for turn in range(3):
        conv_copy(turn).start()
    grad_conv_ref[col] = conv_out[col]
    for turn in range(3):
        remote(
            conv_out.at[0],
            grad_conv_ref.at[targets[turn]],
            conv_send.at[turn],
            conv_recv.at[turn],
            (row, near),
        ).wait_recv()
    for turn in range(3):
        conv_copy(turn).wait_send()
        grad_copy(turn).wait_send()
        text_copy(turn).wait_send()
    total = level_out[level].astype(floats)
    out_total = out_level_out[level].astype(floats)
    for k in range(1, groups):
        level_copy(k).wait()
        out_level_copy(k).wait()
        total = total + level_in[k].astype(floats)
        out_total = out_total + out_level_in[k].astype(floats)
    others_ref[:, 0:width] = out_total.astype(halves)
    others_ref[:, width : 3 * width] = total.astype(halves)

    def attention_sum(j):
        attention_copy(j).wait_recv()
        here = pl.ds(j * per_tile, per_tile)
        attention_ref[here] = (
            attention_grad[here, side].astype(floats) + attention_in[here].astype(floats)
        ).astype(halves)

    loop(full // width, attention_sum)
    loop(full // width, lambda j: attention_copy(j).wait_send())
    side_copy().wait_send()
    out_side_copy().wait_send()
    near_copy().wait_send()
    far_copy().wait_send()
    pair_copy(0).wait_send()
    pair_copy(1).wait_send()
    line.wait_send()


def attend_backward(
    words,
    grad,
    query,
    key,
    value,
    totals,
    normed,
    weights,
    hidden,
    conv,
    grad_two,
    gain,
    text,
    text_grads,
    reduced,
    attended,
    grad_attn,
):
    rows, full = hidden.shape
    groups, _, owned, _ = reduced.shape
    used = -(-words // 16) * 16
    tokens, width = query.shape
    flat = pltpu.VMEM((tokens, width), halves)
    return pl.pallas_call(
        attend_back_kernel,
        out_shape=(
            jax.ShapeDtypeStruct((groups, owned, 5 * width), halves),
            jax.ShapeDtypeStruct((owned, 3 * width), halves),
            jax.ShapeDtypeStruct((rows, full), floats),
            jax.ShapeDtypeStruct((PIX, rows, width), halves),
            jax.ShapeDtypeStruct((8, full), floats),
        ),
        in_specs=[VMEM] * 16,
        out_specs=(VMEM,) * 5,
        scratch_shapes=[
            pltpu.VMEM((PIX, rows, width), halves),
            flat,
            flat,
            flat,
            pltpu.VMEM((tokens, 2 * HEAD_DIM), floats),
            pltpu.VMEM((tokens, HEAD_DIM), floats),
            pltpu.VMEM((128, tokens), floats),
            pltpu.VMEM((2, rows, full), halves),
            pltpu.VMEM((2, rows, full), halves),
            pltpu.VMEM((rows, full), halves),
            pltpu.VMEM((rows, full), halves),
            pltpu.VMEM((rows, full), floats),
            pltpu.VMEM((PIX, rows, width), halves),
            pltpu.VMEM((3, used, 2 * width), halves),
            pltpu.VMEM((2, full, width), halves),
            pltpu.VMEM((2, full, width), halves),
            pltpu.VMEM((2, full, width), floats),
            pltpu.VMEM((full, width), halves),
            pltpu.VMEM((full, width), halves),
            pltpu.VMEM((groups, owned, 2 * width), halves),
            pltpu.VMEM((groups, owned, 2 * width), halves),
            pltpu.VMEM((groups, owned, 2 * width), halves),
            pltpu.VMEM((groups, 2, owned, width), halves),
            pltpu.VMEM((groups, owned, width), halves),
            pltpu.VMEM((groups, owned, width), halves),
            pltpu.VMEM((groups, owned, width), halves),
            pltpu.VMEM((groups, 2, owned, 5 * width), halves),
            pltpu.VMEM((groups, owned, 5 * width), halves),
            DMA((3,)),
            DMA((3,)),
            DMA((3,)),
            DMA((3,)),
            DMA((2,)),
            DMA((2,)),
            DMA,
            DMA,
            DMA((3,)),
            DMA((3,)),
            DMA,
            DMA,
            DMA,
            DMA,
            DMA,
            DMA,
            DMA((groups,)),
            DMA((groups,)),
            DMA,
            DMA,
            DMA((groups,)),
            DMA((groups,)),
            DMA((PIX,)),
            DMA((PIX,)),
        ],
        compiler_params=params(3),
        name="attend_backward",
    )(
        grad,
        query,
        key,
        value,
        totals,
        normed,
        weights,
        hidden,
        conv,
        grad_two,
        gain.reshape(1, -1),
        text,
        text_grads,
        reduced,
        attended,
        grad_attn,
    )


def conv_back_kernel(
    count,
    width,
    images_ref,
    kernel_ref,
    bank_ref,
    styles_ref,
    inverse_ref,
    grad_ref,
    conv_ref,
    attention_ref,
    bank_grad_ref,
    stats_ref,
    attention_sum_ref,
    image_grad_ref,
    grads_ref,
    image_buf,
    padded_image,
    padded_grad,
    turned,
    acc,
    sums_out,
    sums_in,
    kept,
    kept_own,
    pixel_out,
    pixel_in,
    line_out,
    line_in,
    owner_out,
    attention_in,
    local_sem,
    image_sem,
    load_sem,
    sums_send,
    sums_recv,
    up_send,
    down_send,
    level_recv,
    pair_send,
    pair_recv,
    pixel_send,
    pixel_recv,
    line_send,
    line_recv,
    owner_send,
    owner_recv,
    attention_send,
    attention_recv,
):
    row, col = lax.axis_index("dp"), lax.axis_index("pix")
    groups = count // 2
    side, level = lax.rem(row, 2), lax.div(row, 2)
    partner = flip(row, 1)
    near, far, cross = peers(col)
    tokens, channels = grad_ref.shape

    def attention_copy(k):
        group = lax.rem(level + k, groups)
        return remote(
            attention_ref.at[group],
            attention_in.at[k],
            attention_send.at[k],
            attention_recv.at[k],
            (2 * group + side, col),
        )

    depth = image_buf.shape[2]
    rows = tokens // PIX
    halo = width
    greet(count, [(row, near), (row, far)])

    def sample_of(step):
        paired, k = turn_of(step)
        return 2 * level_at(level, groups, k) + jnp.where(paired, 1 - side, side)

    def turn_of(step):
        final = step == count - 1
        even = lax.rem(step, 2) == 0
        paired = final | (even & (step > 0))
        k = jnp.where(even, jnp.maximum(lax.div(step, 2) - 1, 0), lax.div(step + 1, 2))
        return paired, jnp.where(final, groups - 1, k)

    has_below, has_above = level > 0, level < groups - 1
    reach = jnp.minimum(level, groups - 1 - level)

    def line_block(origin, upward):
        block = grads_ref.at[2 * origin + side]
        sem = (up_send if upward else down_send).at[origin]
        target = jnp.minimum(row + 2, count - 1) if upward else jnp.maximum(row - 2, 0)
        return remote(block, block, sem, level_recv.at[origin], (target, col))

    def relay(k):
        origin = level_at(level, groups, k)
        block = grads_ref.at[2 * origin + side]
        remote(
            block, block, up_send.at[origin], level_recv.at[origin], (partner, col)
        ).wait_recv()

        @pl.when((origin < level) & has_above)
        def _():
            line_block(origin, True).start()

        @pl.when((origin > level) & has_below)
        def _():
            line_block(origin, False).start()

        pair_copy(k).start()

    def pair_copy(k):
        block = grads_ref.at[2 * level_at(level, groups, k) + side]
        return remote(block, block, pair_send.at[k], pair_recv.at[k], (partner, col))

    def sums_copy(k):
        return remote(
            sums_out,
            sums_in.at[row],
            sums_send.at[k],
            sums_recv.at[k],
            (lax.rem(row + k, count), col),
        )

    own = pltpu.make_async_copy(grad_ref, grads_ref.at[row], local_sem)
    own.start()
    own.wait()

    @pl.when(has_above)
    def _():
        line_block(level, True).start()

    @pl.when(has_below)
    def _():
        line_block(level, False).start()

    pair_copy(0).start()

    def fetch(step):
        slot = lax.rem(step, 2)
        return pltpu.make_async_copy(
            images_ref.at[sample_of(step)], image_buf.at[slot], image_sem.at[slot]
        )

    fetch(0).start()
    products = jnp.zeros((8, channels), floats)

    def add_product(i, total):
        here = pl.ds(pl.multiple_of(i * 64, 64), 64)
        product = grad_ref[here, :].astype(floats) * conv_ref[here, :].astype(floats)
        return total + jnp.sum(product.reshape(8, 8, channels), axis=0)

    products = lax.fori_loop(0, tokens // 64, add_product, products)
    sums_out[...] = jnp.broadcast_to(jnp.sum(products, 0, keepdims=True), (8, channels))
    lax.fori_loop(1, count, lambda k, c: (sums_copy(k).start(), c)[1], 0)
    sums_in[row] = sums_out[...]
    acc[...] = jnp.zeros_like(acc)
    stats_ref[...] = jnp.zeros_like(stats_ref)
    for buffer, lanes in ((padded_image, depth), (padded_grad, channels)):
        zeros = jnp.zeros((3, halo, lanes), halves)
        buffer[:, 0:halo, :] = zeros
        buffer[:, halo + tokens : halo + tokens + halo, :] = zeros

    def sums_arrive(k, carry):
        origin = lax.rem(row - k + count, count)
        remote(
            sums_out, sums_in.at[origin], sums_send.at[k], sums_recv.at[k], (partner, col)
        ).wait_recv()
        return carry

    def fill(buffer, source):
        wide = source.astype(floats)
        place = lax.rem(lax.broadcasted_iota(jnp.int32, wide.shape, 0), width)
        here = slice(halo, halo + tokens)
        buffer[0, here, :] = jnp.where(place == 0, 0.0, pltpu.roll(wide, 1, 0)).astype(halves)
        buffer[2, here, :] = jnp.where(
            place == width - 1, 0.0, pltpu.roll(wide, tokens - 1, 0)
        ).astype(halves)

    centre = pl.ds(halo, tokens)

    def pixel_copy(step):
        return remote(
            pixel_out.at[lax.rem(step, 2)],
            pixel_in.at[step],
            pixel_send.at[step],
            pixel_recv.at[step],
            (row, near),
        )

    def line_copy(step):
        return remote(
            line_out.at[lax.rem(step, 2)],
            line_in.at[step],
            line_send.at[step],
            line_recv.at[step],
            (row, far),
        )

    def owner_copy(step):
        return remote(
            owner_out.at[lax.rem(step, 2)],
            image_grad_ref.at[row],
            owner_send.at[step],
            owner_recv.at[row],
            (sample_of(step), col),
        )

    def work(step):
        paired, k = turn_of(step)
        sample = sample_of(step)

        @pl.when(paired)
        def _():
            block = grads_ref.at[sample]
            remote(block, block, pair_send.at[k], pair_recv.at[k], (partner, col)).wait_recv()

        direct = jnp.logical_not(paired) & (step > 0)

        @pl.when(direct & (k <= 2 * reach) & (lax.rem(k, 2) == 1))
        def _():
            relay(k)
            relay(k + 1)

        @pl.when(direct & (k > 2 * reach))
        def _():
            relay(k)

        load = pltpu.make_async_copy(
            grads_ref.at[sample], padded_grad.at[1, centre, :], load_sem
        )
        load.start()
        fetch(step).wait()

        @pl.when(step + 1 < count)
        def _():
            fetch(step + 1).start()

        image = image_buf[lax.rem(step, 2)]
        padded_image[1, centre, :] = image
        fill(padded_image, image)
        load.wait()
        grad = padded_grad[1, centre, :]
        fill(padded_grad, grad)
        turned[...] = jnp.transpose(grad)
        slot = lax.rem(step, 2)

        @pl.when(step >= 2)
        def _():
            pixel_copy(step - 2).wait_send()

        def through(target):
            start = pl.multiple_of(target * rows, rows)
            total = jnp.zeros((rows, depth), floats)
            for a in range(3):
                for b in range(3):
                    window = padded_grad[
                        2 - b, pl.ds(pl.multiple_of(start + (2 - a) * width, 16), rows), :
                    ]
                    total = total + mul_nt(window, kernel_ref[sample, 3 * a + b])
            return total

        def give(i):
            pixel_out[slot, i] = through(jnp.where(i == 0, near, cross)).astype(halves)

        def keep(i):
            kept[slot, i] = through(jnp.where(i == 0, col, far))

        loop(2, give)
        pixel_copy(step).start()
        loop(2, keep)
        style = styles_ref[sample]
        scale = style[0:1, :depth]
        first, second = style[1:2, 0:1], style[2:3, 0:1]
        both = jnp.concatenate(
            [
                jnp.broadcast_to(inverse_ref[pl.ds(sample, 1), :], (8, channels)),
                sums_in[sample],
            ],
            axis=0,
        )
        columns = jnp.transpose(both)
        inverse, total = columns[:, 0:1], columns[:, 8:9]
        factor = inverse * inverse * total
        by_scale = jnp.zeros((1, depth), floats)
        by_first = jnp.zeros((1, depth), floats)
        by_second = jnp.zeros((1, depth), floats)
        for a in range(3):
            for b in range(3):
                tap = 3 * a + b
                found = mul(turned[...], padded_image[b, pl.ds(a * width, tokens), :])
                one, two = bank_ref[0, tap].astype(floats), bank_ref[1, tap].astype(floats)
                selected = first * one + second * two
                modded = inverse * found - factor * (selected * scale)
                by_scale = by_scale + jnp.sum(modded * selected, 0, keepdims=True)
                grad_selected = modded * scale
                acc[0, tap] += first * grad_selected
                acc[1, tap] += second * grad_selected
                by_first = by_first + jnp.sum(grad_selected * one, 0, keepdims=True)
                by_second = by_second + jnp.sum(grad_selected * two, 0, keepdims=True)
        stats_ref[sample, 0:1, :depth] = by_scale
        stats_ref[sample, 1:2, :depth] = by_first
        stats_ref[sample, 2:3, :depth] = by_second

    def across(step):
        slot = lax.rem(step, 2)
        pixel_copy(step).wait_recv()

        @pl.when(step >= 2)
        def _():
            line_copy(step - 2).wait_send()

        line_out[slot] = (kept[slot, 1] + pixel_in[step, 1].astype(floats)).astype(halves)
        line_copy(step).start()
        kept_own[slot] = kept[slot, 0] + pixel_in[step, 0].astype(floats)

    def home(step):
        slot = lax.rem(step, 2)
        line_copy(step).wait_recv()

        @pl.when(step >= 3)
        def _():
            owner_copy(step - 2).wait_send()

        owner_out[slot] = (kept_own[slot] + line_in[step].astype(floats)).astype(halves)

        @pl.when(step > 0)
        def _():
            owner_copy(step).start()

        @pl.when(step == 0)
        def _():
            mine = pltpu.make_async_copy(owner_out.at[slot], image_grad_ref.at[row], local_sem)
            mine.start()
            mine.wait()

    lax.fori_loop(1, count, sums_arrive, 0)

    def step_body(step):
        @pl.when(step == count - 2)
        def _():
            lax.fori_loop(1, groups, lambda k, c: (attention_copy(k).start(), c)[1], 0)

        @pl.when(step < count)
        def _():
            work(step)

        @pl.when((step >= 1) & (step <= count))
        def _():
            across(step - 1)

        @pl.when(step >= 2)
        def _():
            home(step - 2)

    loop(count + 2, step_body)

    def write(index):
        bank_grad_ref[lax.div(index, 9), lax.rem(index, 9)] = jnp.transpose(
            acc[lax.div(index, 9), lax.rem(index, 9)]
        )

    loop(18, write)

    def owner_arrives(k, carry):
        origin = lax.rem(row - k + count, count)
        remote(
            owner_out.at[0],
            image_grad_ref.at[origin],
            owner_send.at[k],
            owner_recv.at[origin],
            (partner, col),
        ).wait_recv()
        return carry

    lax.fori_loop(1, count, owner_arrives, 0)
    lax.fori_loop(1, groups, lambda k, c: (attention_copy(k).wait(), c)[1], 0)
    attention_total = attention_ref[level].astype(floats)
    for k in range(1, groups):
        attention_total = attention_total + attention_in[k].astype(floats)
    attention_sum_ref[...] = attention_total.astype(halves)
    for step in (count - 2, count - 1):
        pixel_copy(step).wait_send()
        line_copy(step).wait_send()
        owner_copy(step).wait_send()

    def sent(origin):
        @pl.when((origin <= level) & has_above)
        def _():
            line_block(origin, True).wait_send()

        @pl.when((origin >= level) & has_below)
        def _():
            line_block(origin, False).wait_send()

    loop(groups, sent)
    loop(groups, lambda k: pair_copy(k).wait_send())
    lax.fori_loop(1, count, lambda k, c: (sums_copy(k).wait_send(), c)[1], 0)


def conv_backward(images_all, kernels, bank, styles, inverse, grad, conv, attention, width):
    count, tokens, depth = images_all.shape
    channels = grad.shape[1]
    rows = tokens // PIX
    groups = count // 2
    piece = (rows, depth)
    return pl.pallas_call(
        partial(conv_back_kernel, count, width),
        out_shape=(
            jax.ShapeDtypeStruct((2, 9, depth, channels), floats),
            jax.ShapeDtypeStruct((count, 8, 128), floats),
            jax.ShapeDtypeStruct(attention.shape[1:], halves),
            jax.ShapeDtypeStruct((count,) + piece, halves),
            jax.ShapeDtypeStruct((count, tokens, channels), halves),
        ),
        in_specs=[ANY] + [VMEM] * 7,
        out_specs=(VMEM, VMEM, VMEM, ANY, ANY),
        scratch_shapes=[
            pltpu.VMEM((2, tokens, depth), halves),
            pltpu.VMEM((3, tokens + 2 * width, depth), halves),
            pltpu.VMEM((3, tokens + 2 * width, channels), halves),
            pltpu.VMEM((channels, tokens), halves),
            pltpu.VMEM((2, 9, channels, depth), floats),
            pltpu.VMEM((8, channels), floats),
            pltpu.VMEM((count, 8, channels), floats),
            pltpu.VMEM((2, 2) + piece, floats),
            pltpu.VMEM((2,) + piece, floats),
            pltpu.VMEM((2, 2) + piece, halves),
            pltpu.VMEM((count, 2) + piece, halves),
            pltpu.VMEM((2,) + piece, halves),
            pltpu.VMEM((count,) + piece, halves),
            pltpu.VMEM((2,) + piece, halves),
            pltpu.VMEM(attention.shape, halves),
            DMA,
            DMA((2,)),
            DMA,
            DMA((count,)),
            DMA((count,)),
            DMA((groups,)),
            DMA((groups,)),
            DMA((groups,)),
            DMA((groups,)),
            DMA((groups,)),
            DMA((count,)),
            DMA((count,)),
            DMA((count,)),
            DMA((count,)),
            DMA((count,)),
            DMA((count,)),
            DMA((groups,)),
            DMA((groups,)),
        ],
        compiler_params=params(4),
        name="conv_backward",
    )(images_all, kernels, bank, styles, inverse, grad, conv, attention)


def close_kernel(
    count,
    small_ref,
    last_ref,
    stats_ref,
    attention_ref,
    others_ref,
    rows_ref,
    stats_all_ref,
    grad_query_ref,
    grad_key_ref,
    grad_value_ref,
    grad_out_ref,
    grad_cross_query_ref,
    grad_cross_out_ref,
    grad_text_key_ref,
    grad_text_value_ref,
    rows_out,
    rows_in,
    stats_in,
    attention_in,
    others_in,
    rows_send,
    rows_recv,
    stats_send,
    stats_recv,
    far_rows_send,
    far_rows_recv,
    far_stats_send,
    far_stats_recv,
    weight_send,
    weight_recv,
):
    row, col = lax.axis_index("dp"), lax.axis_index("pix")
    near, far, cross = peers(col)
    targets = (far, cross, near)
    greet(count, [(row, near), (row, far), (row, cross)])
    rows_out[...] = small_ref[...]
    rows_out[5:6, :] = last_ref[0:1, :]

    def rows_copy(turn):
        return remote(
            rows_out, rows_in.at[turn], rows_send.at[turn], rows_recv.at[turn], (row, targets[turn])
        )

    def stats_copy(turn):
        return remote(
            stats_ref, stats_in.at[turn], stats_send.at[turn], stats_recv.at[turn], (row, targets[turn])
        )

    for turn in range(3):
        rows_copy(turn).start()
        stats_copy(turn).start()
    attention_in[col] = attention_ref[...]
    others_in[col] = others_ref[...]
    buffers = (attention_in, others_in)

    def weight_copy(which, hop):
        block = buffers[which].at[far if hop == 2 else col]
        index = 3 * which + hop
        return remote(
            block, block, weight_send.at[index], weight_recv.at[index], (row, far if hop == 0 else near)
        )

    def weight_arrives(which, hop):
        block = buffers[which].at[(far, near, cross)[hop]]
        index = 3 * which + hop
        remote(
            block, block, weight_send.at[index], weight_recv.at[index], (row, near)
        ).wait_recv()

    for which in range(2):
        weight_copy(which, 0).start()
        weight_copy(which, 1).start()
    for turn in range(3):
        rows_copy(turn).wait()
        stats_copy(turn).wait()
    rows_in[3] = rows_out[...]
    stats_in[3] = stats_ref[...]

    def in_order(buffer):
        total = None
        for which in range(PIX):
            turn = jnp.where(
                which == col, 3, jnp.where(which == far, 0, jnp.where(which == cross, 1, 2))
            )
            total = buffer[turn] if total is None else total + buffer[turn]
        return total

    rows_ref[row] = in_order(rows_in)
    stats_all_ref[row] = in_order(stats_in)

    def far_rows(k):
        block = rows_ref.at[row]
        return remote(
            block, block, far_rows_send.at[k], far_rows_recv.at[k], (lax.rem(row + k, count), col)
        )

    def far_stats(k):
        block = stats_all_ref.at[row]
        return remote(
            block, block, far_stats_send.at[k], far_stats_recv.at[k], (lax.rem(row + k, count), col)
        )

    lax.fori_loop(1, count, lambda k, c: (far_rows(k).start(), far_stats(k).start(), c)[2], 0)
    for which in range(2):
        weight_arrives(which, 0)
        weight_copy(which, 2).start()
    width = attention_ref.shape[1] // 5
    short = grad_text_key_ref.shape[0]
    for which in range(2):
        weight_arrives(which, 1)
        weight_arrives(which, 2)
    attention_outs = (
        grad_query_ref,
        grad_key_ref,
        grad_value_ref,
        grad_text_key_ref,
        grad_text_value_ref,
    )
    other_outs = (grad_out_ref, grad_cross_query_ref, grad_cross_out_ref)
    for buffer, outs in ((attention_in, attention_outs), (others_in, other_outs)):
        for k, out in enumerate(outs):
            for p in range(PIX):
                block = buffer[p, :, k * width : (k + 1) * width].astype(floats)
                out[:, p * width : (p + 1) * width] = block[: out.shape[0]]

    def arrive(k, carry):
        origin = lax.rem(row - k + count, count)
        block = rows_ref.at[origin]
        remote(block, block, far_rows_send.at[k], far_rows_recv.at[k], (row, near)).wait_recv()
        block = stats_all_ref.at[origin]
        remote(block, block, far_stats_send.at[k], far_stats_recv.at[k], (row, near)).wait_recv()
        return carry

    lax.fori_loop(1, count, arrive, 0)
    lax.fori_loop(
        1, count, lambda k, c: (far_rows(k).wait_send(), far_stats(k).wait_send(), c)[2], 0
    )
    for which in range(2):
        for hop in range(3):
            weight_copy(which, hop).wait_send()


def close(small, last, stats, attention, others, text_rows):
    count = stats.shape[0]
    block = small.shape
    owned, full = attention.shape[0], small.shape[1]
    weight = jax.ShapeDtypeStruct((owned, full), floats)
    text = jax.ShapeDtypeStruct((text_rows, full), floats)
    return pl.pallas_call(
        partial(close_kernel, count),
        out_shape=(
            jax.ShapeDtypeStruct((count,) + block, floats),
            jax.ShapeDtypeStruct((count,) + stats.shape, floats),
        )
        + (weight,) * 6
        + (text,) * 2,
        in_specs=[VMEM] * 5,
        out_specs=(VMEM,) * 10,
        scratch_shapes=[
            pltpu.VMEM(block, floats),
            pltpu.VMEM((4,) + block, floats),
            pltpu.VMEM((4,) + stats.shape, floats),
            pltpu.VMEM((PIX,) + attention.shape, halves),
            pltpu.VMEM((PIX,) + others.shape, halves),
            DMA((3,)),
            DMA((3,)),
            DMA((3,)),
            DMA((3,)),
            DMA((count,)),
            DMA((count,)),
            DMA((count,)),
            DMA((count,)),
            DMA((6,)),
            DMA((6,)),
        ],
        compiler_params=params(5),
        name="close",
    )(small, last, stats, attention, others)


def style_rows(style_codes, labels, class_table, select_weight, modulation, rgb_modulation):
    class_row = jnp.take(class_table, labels, axis=0).astype(floats)
    styled = style_codes.astype(floats) + class_row
    mixing = jax.nn.softmax(jnp.dot(styled, select_weight.astype(floats), precision=highest), -1)
    scaling = jnp.dot(styled, modulation.astype(floats), precision=highest) + 1.0
    rgb_scale = jnp.dot(styled, rgb_modulation.astype(floats), precision=highest) + 1.0
    return styled, mixing, scaling, rgb_scale


def pack_style(styled, labels, mixing, scaling, count):
    depth = scaling.shape[-1] // count
    pieces = jnp.pad(scaling.reshape(count, 1, depth), ((0, 0), (0, 0), (0, 128 - depth)))
    same = jnp.concatenate(
        [
            jnp.broadcast_to(mixing.reshape(2, 1), (2, 128)),
            styled.reshape(4, 128),
            jnp.broadcast_to(labels.astype(floats).reshape(1, 1), (1, 128)),
        ]
    )
    return jnp.concatenate([pieces, jnp.broadcast_to(same, (count, 7, 128))], axis=1)


def on_device(
    images,
    style_codes,
    labels,
    token_ids,
    penalty_mask,
    class_table,
    text_table,
    conv_bank,
    select_weight,
    modulation,
    rgb_modulation,
    w_query,
    w_key,
    w_value,
    w_out,
    c_query,
    c_key,
    c_value,
    c_out,
    gain_self,
    gain_cross,
    rgb_weight,
    out_cotangent,
    rgb_cotangent,
):
    count = lax.axis_size("dp")
    row, col = lax.axis_index("dp"), lax.axis_index("pix")
    _, height, width, channels = images.shape
    rows = height * width
    quarter = channels // PIX
    depth = channels // count

    def my_columns(*weights):
        return jnp.concatenate(
            [lax.dynamic_slice_in_dim(w, col * quarter, quarter, axis=1) for w in weights], axis=1
        )

    owned, text_owned = w_query.shape[0], c_key.shape[0]
    text_columns = jnp.pad(my_columns(c_key, c_value), ((0, owned - text_owned), (0, 0)))
    attention = jnp.concatenate([my_columns(w_query, w_key, w_value), text_columns], axis=1)
    attention = lax.all_gather(attention, "dp", axis=0, tiled=True)
    others = lax.all_gather(my_columns(w_out, c_query, c_out), ("pix", "dp"), axis=0, tiled=True)
    others = others.reshape(PIX, channels, 3 * quarter)

    styled, mixing, scaling, rgb_scale = style_rows(
        style_codes, labels, class_table, select_weight, modulation, rgb_modulation
    )
    own = images.reshape(rows, channels)
    parts = own.reshape(rows, count, depth).transpose(1, 0, 2)
    bank = conv_bank.reshape(2, 9, depth, quarter)
    bank_turned = bank.transpose(0, 1, 3, 2)
    words = token_ids.shape[1]
    text = jnp.take(text_table, token_ids[0], axis=0)
    text = text.reshape(words, count, text_owned)
    text = jnp.pad(text, ((0, 128 - words), (0, 0), (0, owned - text_owned)))
    text = text.reshape(128, channels)

    images_all, kernels, styles, inverse = gather_inputs(
        pack_style(styled, labels, mixing, scaling, count), bank, parts
    )
    images_all = images_all.reshape(count, PIX * rows, depth)
    conv, conv_own, hidden_one, normed_one = conv_forward(images_all, kernels, own, gain_self, width)
    query, key, value, totals, attended, text_all = attend_forward(
        normed_one, attention, text
    )
    rgb_rows = jnp.pad(rgb_cotangent.reshape(3, rows).T, ((0, 0), (0, 125)))
    penalty = jnp.broadcast_to(penalty_mask.astype(floats).reshape(1, 1), (1, 128))
    (
        output,
        rgb,
        reduced,
        text_grads,
        grad_two,
        grad_attended,
        small,
        attended_rows,
        grad_attn,
    ) = cross_part(
        words,
        attended,
        hidden_one,
        others,
        text_all,
        gain_cross,
        rgb_scale,
        jnp.pad(rgb_weight, ((0, 0), (0, 125))),
        out_cotangent.reshape(rows, channels),
        rgb_rows,
        penalty,
    )
    attention_grads, others_owned, grad_one, grad_conv, last = attend_backward(
        words,
        grad_attended,
        query,
        key,
        value,
        totals,
        normed_one,
        attention,
        hidden_one,
        conv,
        grad_two,
        gain_self,
        text,
        text_grads,
        reduced.reshape(count // 2, 2, owned, 2 * quarter),
        attended_rows,
        grad_attn,
    )

    bank_grad, stats, attention_owned, image_parts, _ = conv_backward(
        images_all,
        kernels,
        bank_turned,
        styles,
        inverse,
        grad_conv.reshape(PIX * rows, quarter),
        conv_own,
        attention_grads,
        width,
    )
    grad_image = grad_one + image_parts.transpose(1, 0, 2).reshape(rows, channels).astype(floats)
    (
        all_rows,
        all_stats,
        grad_w_query,
        grad_w_key,
        grad_w_value,
        grad_w_out,
        grad_c_query,
        grad_c_out,
        grad_c_key,
        grad_c_value,
    ) = close(small, last, stats, attention_owned, others_owned, text_owned)

    styled_all = styles[:, 3:7, :].reshape(count, -1)
    mixing_all = styles[:, 1:3, 0]
    labels_all = styles[:, 7, 0].astype(jnp.int32)
    grad_scaling = all_stats[:, :, 0, :depth].transpose(1, 0, 2).reshape(count, channels)
    grad_mixing = jnp.sum(all_stats[:, :, 1:3, :], axis=(0, 3))
    grad_rgb_scale = all_rows[:, 1, :]
    inner = jnp.sum(grad_mixing * mixing_all, -1, keepdims=True)
    grad_logits = mixing_all * (grad_mixing - inner)

    def outer(right):
        return lax.dot_general(
            styled_all, right, TN, precision=highest, preferred_element_type=floats
        )

    def back(left, right):
        return lax.dot_general(
            left, right.astype(floats), NT, precision=highest, preferred_element_type=floats
        )

    grad_styles = (
        back(grad_logits, select_weight)
        + back(grad_scaling, modulation)
        + back(grad_rgb_scale, rgb_modulation)
    )
    classes = class_table.shape[0]
    chosen = (labels_all[:, None] == jnp.arange(classes, dtype=jnp.int32)[None, :]).astype(floats)
    grad_table = lax.dot_general(
        chosen, grad_styles, TN, precision=highest, preferred_element_type=floats
    )
    sums = jnp.sum(all_rows, axis=0)
    shape = images.shape
    return (
        output.reshape(shape),
        rgb[:, :3].T.reshape(1, 3, height, width),
        grad_image.reshape(shape),
        lax.dynamic_slice_in_dim(grad_styles, row, 1, axis=0),
        grad_table,
        bank_grad.reshape(conv_bank.shape),
        outer(grad_logits),
        outer(grad_scaling),
        outer(grad_rgb_scale),
        grad_w_query,
        grad_w_key,
        grad_w_value,
        grad_w_out,
        grad_c_query,
        grad_c_key,
        grad_c_value,
        grad_c_out,
        sums[5],
        sums[0],
        sums[2:5].T,
    )


def solution(mesh):
    return jax.shard_map(
        on_device,
        mesh=mesh,
        in_specs=(
            P("dp", "pix", None, None),
            P("dp", None),
            P("dp"),
            P("dp", None),
            P("dp"),
            P(),
            P(),
            P(None, None, None, "dp", "pix"),
            P(),
            P(),
            P(),
            P("dp", None),
            P("dp", None),
            P("dp", None),
            P("dp", None),
            P("dp", None),
            P("dp", None),
            P("dp", None),
            P("dp", None),
            P(),
            P(),
            P(),
            P("dp", "pix", None, None),
            P("dp", None, "pix", None),
        ),
        out_specs=(
            P("dp", "pix", None, None),
            P("dp", None, "pix", None),
            P("dp", "pix", None, None),
            P("dp", None),
            P(),
            P(None, None, None, "dp", "pix"),
            P(),
            P(),
            P(),
            P("dp", None),
            P("dp", None),
            P("dp", None),
            P("dp", None),
            P("dp", None),
            P("dp", None),
            P("dp", None),
            P("dp", None),
            P(),
            P(),
            P(),
        ),
        check_vma=False,
    )
```

```python
from functools import partial

import jax
import jax.numpy as jnp
from jax import lax
from jax.experimental import pallas as pl
from jax.experimental.pallas import tpu as pltpu
from jax.sharding import PartitionSpec as P

HEAD_DIM = 64
PIX = 4
MESH = pl.DeviceIdType.MESH
VMEM_LIMIT = 60 * 1024 * 1024

penalty_weight = 1.0
highest = lax.Precision.HIGHEST
floats = jnp.float32
halves = jnp.bfloat16

ANY = pl.BlockSpec(memory_space=pl.ANY)
VMEM = pl.BlockSpec(memory_space=pltpu.VMEM)
DMA = pltpu.SemaphoreType.DMA


def params(collective_id):
    return pltpu.CompilerParams(
        collective_id=collective_id, has_side_effects=True, vmem_limit_bytes=VMEM_LIMIT
    )


def remote(src, dst, send_sem, recv_sem, where):
    return pltpu.make_async_remote_copy(
        src_ref=src,
        dst_ref=dst,
        send_sem=send_sem,
        recv_sem=recv_sem,
        device_id=where,
        device_id_type=MESH,
    )


def greet(count, others):
    row, col = lax.axis_index("dp"), lax.axis_index("pix")
    barrier = pltpu.get_barrier_semaphore()

    def one(step, carry):
        pl.semaphore_signal(
            barrier, inc=1, device_id=(lax.rem(row + step, count), col), device_id_type=MESH
        )
        return carry

    if count > 1:
        lax.fori_loop(1, count, one, 0)
    for other in others:
        pl.semaphore_signal(barrier, inc=1, device_id=other, device_id_type=MESH)
    pl.semaphore_wait(barrier, count - 1 + len(others))


def loop(count, body):
    def step(i, carry):
        body(i)
        return carry

    lax.fori_loop(0, count, step, 0)


def flip(index, bit):
    part = lax.rem(lax.div(index, bit), 2)
    return index + bit - 2 * bit * part


def level_at(level, groups, index):
    both = jnp.minimum(level, groups - 1 - level)
    step = lax.div(index + 1, 2)
    near = jnp.where(lax.rem(index, 2) == 1, level - step, level + step)
    rest = index - both
    far = jnp.where(level > groups - 1 - level, level - rest, level + rest)
    return jnp.where(index == 0, level, jnp.where(index <= 2 * both, near, far))


def gather_kernel(
    count,
    style_ref,
    bank_ref,
    parts_ref,
    images_ref,
    kernel_ref,
    styles_ref,
    inverse_ref,
    squares,
    squares_in,
    local_sem,
    style_send,
    style_recv,
    square_send,
    square_recv,
    part_send,
    part_recv,
    core_send,
    core_recv,
    line_send,
    line_recv,
    pass_send,
    pass_recv,
):
    row, col = lax.axis_index("dp"), lax.axis_index("pix")
    near, far = flip(col, 1), flip(col, 2)
    depth = bank_ref.shape[2]
    greet(count, [(row, near), (row, far)])

    def style_copy(step):
        other = lax.rem(row + step, count)
        return remote(
            style_ref.at[other], styles_ref.at[row], style_send.at[step], style_recv.at[step], (other, col)
        )

    def square_copy(step):
        other = lax.rem(row + step, count)
        return remote(
            squares, squares_in.at[row], square_send.at[step], square_recv.at[step], (other, col)
        )

    def part_copy(step):
        other = lax.rem(row + step, count)
        return remote(
            parts_ref.at[other], images_ref.at[row, col], part_send.at[step], part_recv.at[step], (other, col)
        )

    def part_arrives(step):
        origin = lax.rem(row - step + count, count)
        remote(
            parts_ref.at[0], images_ref.at[origin, col], part_send.at[step], part_recv.at[step], (row, near)
        ).wait_recv()

    def core_copy(step):
        origin = lax.rem(row - step + count, count)
        block = images_ref.at[origin, col]
        return remote(block, block, core_send.at[step], core_recv.at[step], (row, near))

    def line_copy(step):
        origin = lax.rem(row - step + count, count)
        block = images_ref.at[origin, col]
        return remote(block, block, line_send.at[step], line_recv.at[step], (row, far))

    def pass_copy(step):
        origin = lax.rem(row - step + count, count)
        block = images_ref.at[origin, far]
        return remote(block, block, pass_send.at[step], pass_recv.at[step], (row, near))

    def core_arrives(step):
        origin = lax.rem(row - step + count, count)
        block = images_ref.at[origin, near]
        remote(block, block, core_send.at[step], core_recv.at[step], (row, near)).wait_recv()

    def line_arrives(step):
        origin = lax.rem(row - step + count, count)
        block = images_ref.at[origin, far]
        remote(block, block, line_send.at[step], line_recv.at[step], (row, far)).wait_recv()

    def pass_arrives(step):
        origin = lax.rem(row - step + count, count)
        block = images_ref.at[origin, flip(near, 2)]
        remote(block, block, pass_send.at[step], pass_recv.at[step], (row, near)).wait_recv()

    own = pltpu.make_async_copy(parts_ref.at[row], images_ref.at[row, col], local_sem)
    own.start()

    def send_all(step):
        style_copy(step).start()

    lax.fori_loop(1, count, lambda i, c: (send_all(i), c)[1], 0)
    lax.fori_loop(1, count, lambda i, c: (part_copy(i).start(), c)[1], 0)
    styles_ref[row] = style_ref[row]
    own.wait()
    line_copy(0).start()
    core_copy(0).start()

    def style_wait(step):
        origin = lax.rem(row - step + count, count)
        remote(
            style_ref.at[0], styles_ref.at[origin], style_send.at[step], style_recv.at[step], (row, near)
        ).wait_recv()

    lax.fori_loop(1, count, lambda i, c: (style_wait(i), c)[1], 0)

    def mixed_tap(sample, tap, column, first, second):
        total = first * bank_ref[0, tap].astype(floats) + second * bank_ref[1, tap].astype(floats)
        return total * column

    def factors(sample):
        block = styles_ref[sample]
        column = jnp.transpose(block)[:depth, 0:1]
        return column, block[1:2, 0:1], block[2:3, 0:1]

    def square_sum(sample):
        column, first, second = factors(sample)
        total = jnp.zeros((depth, bank_ref.shape[3]), floats)
        for tap in range(9):
            modded = mixed_tap(sample, tap, column, first, second)
            total = total + modded * modded
        squares[pl.ds(sample, 1), :] = jnp.sum(total, axis=0, keepdims=True)

    loop(count, square_sum)
    lax.fori_loop(1, count, lambda i, c: (square_copy(i).start(), c)[1], 0)
    squares_in[row] = squares[...]

    def relay(step):
        part_arrives(step)
        line_copy(step).start()
        core_copy(step).start()

    lax.fori_loop(1, count, lambda i, c: (relay(i), c)[1], 0)

    def square_wait(step):
        origin = lax.rem(row - step + count, count)
        remote(
            squares, squares_in.at[origin], square_send.at[step], square_recv.at[step], (row, near)
        ).wait_recv()

    lax.fori_loop(1, count, lambda i, c: (square_wait(i), c)[1], 0)
    inverse_ref[...] = lax.rsqrt(jnp.sum(squares_in[...], axis=0) + 1e-08)

    def forward(step):
        line_arrives(step)
        pass_copy(step).start()

    def make_kernel(sample):
        column, first, second = factors(sample)
        scale = inverse_ref[pl.ds(sample, 1), :]
        for tap in range(9):
            modded = mixed_tap(sample, tap, column, first, second)
            kernel_ref[sample, tap] = (modded * scale).astype(halves)
        forward(sample)

    loop(count, make_kernel)
    loop(count, core_arrives)
    loop(count, pass_arrives)
    lax.fori_loop(
        1,
        count,
        lambda i, c: (
            style_copy(i).wait_send(),
            square_copy(i).wait_send(),
            part_copy(i).wait_send(),
            c,
        )[3],
        0,
    )
    loop(count, lambda i: core_copy(i).wait_send())
    loop(count, lambda i: line_copy(i).wait_send())
    loop(count, lambda i: pass_copy(i).wait_send())


def gather_inputs(style_rows, bank, parts):
    count, rows, depth = parts.shape
    width = bank.shape[-1]
    sems = [DMA((count,)) for _ in range(12)]
    return pl.pallas_call(
        partial(gather_kernel, count),
        out_shape=(
            jax.ShapeDtypeStruct((count, PIX, rows, depth), halves),
            jax.ShapeDtypeStruct((count, 9, depth, width), halves),
            jax.ShapeDtypeStruct((count, 8, 128), floats),
            jax.ShapeDtypeStruct((count, width), floats),
        ),
        in_specs=[VMEM, VMEM, ANY],
        out_specs=(ANY, VMEM, VMEM, VMEM),
        scratch_shapes=[
            pltpu.VMEM((count, width), floats),
            pltpu.VMEM((count, count, width), floats),
            DMA,
        ]
        + sems,
        compiler_params=params(0),
        name="gather_inputs",
    )(style_rows, bank, parts)


def conv_kernel(
    count,
    width,
    images_ref,
    kernel_ref,
    own_ref,
    gain_ref,
    conv_ref,
    conv_own_ref,
    hidden_ref,
    normed_ref,
    image_buf,
    padded,
    total,
    pair_out,
    pair_in,
    line_out,
    line_in,
    block_out,
    block_in,
    image_sem,
    pair_send,
    pair_recv,
    line_send,
    line_recv,
    block_send,
    block_recv,
    norm_send,
    norm_recv,
):
    row, col = lax.axis_index("dp"), lax.axis_index("pix")
    groups = count // 2
    slots = pair_out.shape[0]
    side = lax.rem(row, 2)
    level = lax.div(row, 2)
    partner = flip(row, 1)
    near, far = flip(col, 1), flip(col, 2)
    cross = flip(near, 2)
    tokens, depth = image_buf.shape[1], image_buf.shape[2]
    channels = total.shape[1]
    rows = tokens // PIX
    halo = width

    has_below, has_above = level > 0, level < groups - 1
    below, above = jnp.maximum(row - 2, 0), jnp.minimum(row + 2, count - 1)

    barrier = pltpu.get_barrier_semaphore()
    for known, other in ((has_below, below), (has_above, above)):

        @pl.when(known)
        def _(other=other):
            pl.semaphore_signal(barrier, inc=1, device_id=(other, col), device_id_type=MESH)

    for other in ((partner, col), (row, near), (row, far), (row, cross)):
        pl.semaphore_signal(barrier, inc=1, device_id=other, device_id_type=MESH)
    pl.semaphore_wait(barrier, 4 + has_below.astype(jnp.int32) + has_above.astype(jnp.int32))

    def group_of(step):
        return level_at(level, groups, groups - 1 - step)

    def sample_of(index):
        mine = lax.div(index, groups)
        group = group_of(lax.rem(index, groups))
        return 2 * group + jnp.where(mine == 1, side, 1 - side)

    def fetch(index):
        slot = lax.rem(index, 2)
        return pltpu.make_async_copy(
            images_ref.at[sample_of(index)], image_buf.at[slot], image_sem.at[slot]
        )

    zeros = jnp.zeros((3, halo, depth), halves)
    padded[:, 0:halo, :] = zeros
    padded[:, halo + tokens : halo + tokens + halo, :] = zeros
    fetch(0).start()
    place = lax.rem(lax.broadcasted_iota(jnp.int32, (tokens, depth), 0), width)

    def stage(index):
        fetch(index).wait()

        @pl.when(index + 1 < count)
        def _():
            fetch(index + 1).start()

        source = image_buf[lax.rem(index, 2)]
        wide = source.astype(floats)
        padded[1, halo : halo + tokens, :] = source
        before = jnp.where(place == 0, 0.0, pltpu.roll(wide, 1, 0))
        padded[0, halo : halo + tokens, :] = before.astype(halves)
        after = jnp.where(place == width - 1, 0.0, pltpu.roll(wide, tokens - 1, 0))
        padded[2, halo : halo + tokens, :] = after.astype(halves)

    def rows_of(sample, start):
        acc = jnp.zeros((rows, channels), floats)
        for a in range(3):
            for b in range(3):
                window = padded[b, pl.ds(pl.multiple_of(start + a * width, 16), rows), :]
                acc = acc + jnp.dot(
                    window, kernel_ref[sample, 3 * a + b], preferred_element_type=floats
                )
        return acc

    def pair_copy(step):
        return remote(
            pair_out.at[lax.rem(step, slots)],
            pair_in.at[step],
            pair_send.at[step],
            pair_recv.at[step],
            (partner, col),
        )

    def line_copy(step, upward):
        group = group_of(step)
        if upward:
            slot, target = group, above
        else:
            slot, target = jnp.where(group == level - 1, groups, group), below
        return remote(
            line_out.at[lax.rem(step, slots)],
            line_in.at[slot],
            line_send.at[step],
            line_recv.at[slot],
            (target, col),
        )

    def line_arrives(slot):
        remote(
            line_out.at[0], line_in.at[slot], line_send.at[0], line_recv.at[slot], (partner, col)
        ).wait_recv()

    def give(step):
        @pl.when(step >= slots)
        def _():
            pair_copy(step - slots).wait_send()

        stage(step)
        sample = sample_of(step)

        def chunk(i):
            start = pl.multiple_of(i * rows, rows)
            pair_out[lax.rem(step, slots), pl.ds(start, rows), :] = rows_of(sample, start).astype(
                halves
            )

        loop(PIX, chunk)
        pair_copy(step).start()

    loop(groups, give)

    def keep(step):
        @pl.when(step >= slots)
        def _():
            line_copy(step - slots, True).wait_send()

        stage(groups + step)
        group = group_of(step)
        sample = 2 * group + side
        out = lax.rem(step, slots)

        def chunk(i):
            start = pl.multiple_of(i * rows, rows)
            total[pl.ds(start, rows), :] = rows_of(sample, start)

        loop(PIX, chunk)
        pair_copy(step).wait_recv()
        passing = jnp.where(group > level, has_below, has_above)

        @pl.when(passing)
        def _():
            line_arrives(group)

            def add(i):
                here = pl.ds(pl.multiple_of(i * rows, rows), rows)
                line_out[out, here, :] = (
                    total[here, :]
                    + pair_in[step, here, :].astype(floats)
                    + line_in[group, here, :].astype(floats)
                ).astype(halves)

            loop(PIX, add)

        @pl.when(jnp.logical_not(passing))
        def _():
            def add(i):
                here = pl.ds(pl.multiple_of(i * rows, rows), rows)
                line_out[out, here, :] = (
                    total[here, :] + pair_in[step, here, :].astype(floats)
                ).astype(halves)

            loop(PIX, add)

        @pl.when(group > level)
        def _():
            line_copy(step, True).start()

        @pl.when(group < level)
        def _():
            line_copy(step, False).start()

    loop(groups - 1, keep)
    last = groups - 1
    stage(count - 1)

    def own_chunk(i):
        start = pl.multiple_of(i * rows, rows)
        total[pl.ds(start, rows), :] = rows_of(row, start)

    loop(PIX, own_chunk)
    pair_copy(last).wait_recv()
    for known, slot in ((has_below, level), (has_above, groups)):

        @pl.when(known)
        def _(slot=slot):
            line_arrives(slot)

            def add(i):
                here = pl.ds(pl.multiple_of(i * rows, rows), rows)
                total[here, :] += line_in[slot, here, :].astype(floats)

            loop(PIX, add)

    def block_copy(turn):
        target = (far, cross, near)[turn]
        return remote(
            block_out.at[turn], block_in.at[col], block_send.at[turn], block_recv.at[turn], (row, target)
        )

    def block_arrives(turn):
        origin = (far, cross, near)[turn]
        remote(
            block_out.at[turn], block_in.at[origin], block_send.at[turn], block_recv.at[turn], (row, near)
        ).wait_recv()

    for turn, target in enumerate((far, cross, near, col)):
        here = pl.ds(pl.multiple_of(target * rows, rows), rows)
        value = total[here, :] + pair_in[last, here, :].astype(floats)
        rounded = value.astype(halves)
        conv_own_ref[here, :] = rounded
        if turn < 3:
            block_out[turn] = rounded
            block_copy(turn).start()
        else:
            block_in[col] = rounded
    for turn in range(3):
        block_arrives(turn)

    part = rows // 4

    def norm_rows(i):
        here = pl.ds(pl.multiple_of(i * part, part), part)
        for j in range(PIX):
            conv_ref[here, j * channels : (j + 1) * channels] = block_in[j, here, :]
        conv = conv_ref[here, :].astype(floats)
        hidden = own_ref[here, :].astype(floats) + conv * jax.nn.sigmoid(conv)
        hidden_ref[here, :] = hidden
        mean = jnp.mean(hidden * hidden, -1, keepdims=True)
        normed_ref[col, here, :] = (hidden * lax.rsqrt(mean + 1e-06) * gain_ref[...]).astype(halves)

    loop(4, norm_rows)
    mine, theirs = normed_ref.at[col], normed_ref.at[far]
    to_far = remote(mine, mine, norm_send.at[0], norm_recv.at[0], (row, far))
    to_near = remote(mine, mine, norm_send.at[1], norm_recv.at[1], (row, near))
    to_far.start()
    to_near.start()
    remote(mine, theirs, norm_send.at[0], norm_recv.at[0], (row, far)).wait_recv()
    onward = remote(theirs, theirs, norm_send.at[2], norm_recv.at[2], (row, near))
    onward.start()
    remote(mine, normed_ref.at[near], norm_send.at[1], norm_recv.at[1], (row, near)).wait_recv()
    remote(mine, normed_ref.at[cross], norm_send.at[2], norm_recv.at[2], (row, near)).wait_recv()
    to_far.wait_send()
    to_near.wait_send()
    onward.wait_send()
    for turn in range(3):
        block_copy(turn).wait_send()
    for step in range(max(0, groups - slots), groups):
        pair_copy(step).wait_send()
    for step in range(max(0, groups - 1 - slots), groups - 1):
        line_copy(step, True).wait_send()


def conv_forward(images_all, kernels, own, gain, width):
    count, tokens, depth = images_all.shape
    channels = kernels.shape[-1]
    rows, full = own.shape
    groups = count // 2
    slots = min(groups, 4)
    block = (tokens, channels)
    return pl.pallas_call(
        partial(conv_kernel, count, width),
        out_shape=(
            jax.ShapeDtypeStruct((rows, full), halves),
            jax.ShapeDtypeStruct((tokens, channels), halves),
            jax.ShapeDtypeStruct((rows, full), floats),
            jax.ShapeDtypeStruct((PIX, rows, full), halves),
        ),
        in_specs=[ANY, VMEM, VMEM, VMEM],
        out_specs=(VMEM, VMEM, VMEM, VMEM),
        scratch_shapes=[
            pltpu.VMEM((2, tokens, depth), halves),
            pltpu.VMEM((3, tokens + 2 * width, depth), halves),
            pltpu.VMEM(block, floats),
            pltpu.VMEM((slots,) + block, halves),
            pltpu.VMEM((groups,) + block, halves),
            pltpu.VMEM((slots,) + block, halves),
            pltpu.VMEM((groups + 1,) + block, halves),
            pltpu.VMEM((3, rows, channels), halves),
            pltpu.VMEM((PIX, rows, channels), halves),
            DMA((2,)),
            DMA((groups,)),
            DMA((groups,)),
            DMA((groups,)),
            DMA((groups + 1,)),
            DMA((3,)),
            DMA((3,)),
            DMA((3,)),
            DMA((3,)),
        ],
        compiler_params=params(1),
        name="conv_forward",
    )(images_all, kernels, own, gain.reshape(1, -1))


def peers(col):
    near, far = flip(col, 1), flip(col, 2)
    return near, far, flip(near, 2)


def greet_pixels(row, others):
    barrier = pltpu.get_barrier_semaphore()
    for other in others:
        pl.semaphore_signal(barrier, inc=1, device_id=(row, other), device_id_type=MESH)
    pl.semaphore_wait(barrier, len(others))


NT = (((1,), (1,)), ((), ()))
TN = (((0,), (0,)), ((), ()))


def mul_nt(a, b, precision=None):
    return lax.dot_general(a, b, NT, preferred_element_type=floats, precision=precision)


def mul_tn(a, b, precision=None):
    return lax.dot_general(a, b, TN, preferred_element_type=floats, precision=precision)


def mul(a, b):
    return jnp.dot(a, b, preferred_element_type=floats)


def split(value):
    high = value.astype(halves)
    rest = value - high.astype(floats)
    middle = rest.astype(halves)
    return high, middle, (rest - middle.astype(floats)).astype(halves)


def exact(product, left, right):
    count = left.shape[0]
    found = product(jnp.concatenate(split(left), axis=0), right)
    return found[2 * count :] + found[count : 2 * count] + found[:count]


def outer_sum(left, right):
    lefts, rights = split(left), split(right)
    pairs = ((0, 2), (2, 0), (1, 1), (0, 1), (1, 0), (0, 0))
    return mul_tn(
        jnp.concatenate([lefts[i] for i, _ in pairs], axis=0),
        jnp.concatenate([rights[j] for _, j in pairs], axis=0),
    )


def attend_kernel(
    normed_ref,
    weight_ref,
    text_ref,
    query_ref,
    key_ref,
    value_ref,
    total_ref,
    attended_ref,
    text_out_ref,
    block_out,
    key_norm,
    block_send,
    block_recv,
    text_send,
    text_recv,
):
    row, col = lax.axis_index("dp"), lax.axis_index("pix")
    near, far, cross = peers(col)
    targets = (far, cross, near)
    greet_pixels(row, targets)
    rows = normed_ref.shape[1]
    width = query_ref.shape[1]
    heads = width // HEAD_DIM
    score_scale = HEAD_DIM ** (-0.5)

    for j in range(2):
        here = slice(j * width, (j + 1) * width)
        weight = weight_ref[:, (3 + j) * width : (4 + j) * width]
        text_out_ref[col, :, here] = mul(text_ref[...], weight).astype(halves)

    def text_copy(turn):
        block = text_out_ref.at[col]
        return remote(block, block, text_send.at[turn], text_recv.at[turn], (row, targets[turn]))

    for turn in range(3):
        text_copy(turn).start()

    def project(i):
        source = normed_ref[i]
        here = pl.ds(pl.multiple_of(i * rows, rows), rows)
        for j, out in enumerate((query_ref, key_ref, value_ref)):
            out[here, :] = mul(source, weight_ref[:, j * width : (j + 1) * width]).astype(halves)

    loop(PIX, project)
    ones = jnp.ones((8, HEAD_DIM), floats)
    for h in range(heads):
        key = key_ref[:, h * HEAD_DIM : (h + 1) * HEAD_DIM].astype(floats)
        key_norm[h] = mul_nt(ones, key * key, highest)

    def attend(target, store):
        here = pl.ds(pl.multiple_of(target * rows, rows), rows)
        for h in range(heads):
            lanes = slice(h * HEAD_DIM, (h + 1) * HEAD_DIM)
            inner = mul_nt(query_ref[here, lanes], key_ref[:, lanes])
            scores = score_scale * (2.0 * inner - key_norm[h, 0:1, :])
            largest = jnp.max(scores, -1, keepdims=True)
            expanded = jnp.exp(scores - largest)
            summed = jnp.sum(expanded, -1, keepdims=True)
            weights = (expanded * (1.0 / summed)).astype(halves)
            store(lanes, mul(weights, value_ref[:, lanes]).astype(halves))
            total_ref[here, h : h + 1] = largest + jnp.log(summed)

    def block_copy(turn):
        return remote(
            block_out.at[turn],
            attended_ref.at[col],
            block_send.at[turn],
            block_recv.at[turn],
            (row, targets[turn]),
        )

    def turn_body(turn):
        target = jnp.where(turn == 0, far, jnp.where(turn == 1, cross, jnp.where(turn == 2, near, col)))

        def store(lanes, result):
            block_out[turn, :, lanes] = result

        attend(target, store)
        for k in range(3):

            @pl.when(turn == k)
            def _(k=k):
                block_copy(k).start()

    loop(4, turn_body)
    attended_ref[col] = block_out[3]
    for turn in range(3):
        remote(
            block_out.at[turn],
            attended_ref.at[targets[turn]],
            block_send.at[turn],
            block_recv.at[turn],
            (row, near),
        ).wait_recv()
        block = text_out_ref.at[targets[turn]]
        remote(block, block, text_send.at[turn], text_recv.at[turn], (row, near)).wait_recv()
    for turn in range(3):
        block_copy(turn).wait_send()
        text_copy(turn).wait_send()


def attend_forward(normed, weights, text):
    count, rows, full = normed.shape
    tokens, width = count * rows, weights.shape[1] // 5
    heads = width // HEAD_DIM
    flat = jax.ShapeDtypeStruct((tokens, width), halves)
    return pl.pallas_call(
        attend_kernel,
        out_shape=(
            flat,
            flat,
            flat,
            jax.ShapeDtypeStruct((tokens, 128), floats),
            jax.ShapeDtypeStruct((PIX, rows, width), halves),
            jax.ShapeDtypeStruct((PIX, text.shape[0], 2 * width), halves),
        ),
        in_specs=[VMEM] * 3,
        out_specs=(VMEM,) * 6,
        scratch_shapes=[
            pltpu.VMEM((4, rows, width), halves),
            pltpu.VMEM((heads, 8, tokens), floats),
            DMA((3,)),
            DMA((3,)),
            DMA((3,)),
            DMA((3,)),
        ],
        compiler_params=params(2),
        name="attend_forward",
    )(normed, weights, text)


def cross_kernel(
    words,
    attended_ref,
    hidden_ref,
    weight_ref,
    text_ref,
    gain_ref,
    rgb_scale_ref,
    rgb_weight_ref,
    cotangent_ref,
    rgb_cotangent_ref,
    penalty_ref,
    output_ref,
    rgb_ref,
    reduced_ref,
    text_grad_ref,
    grad_two_ref,
    grad_attended_ref,
    small_ref,
    attended,
    grad_attn,
    normed,
    grad_query,
    two,
    query,
    probs,
    crossed,
    mixed,
    grad_three,
    grad_proj,
    grad_crossed,
    grad_norm,
    near_out,
    near_in,
    kept,
    line_out,
    line_in,
    near_send,
    near_recv,
    line_send,
    line_recv,
):
    row, col = lax.axis_index("dp"), lax.axis_index("pix")
    near, far, cross = peers(col)
    greet_pixels(row, (near, far))
    rows, full = hidden_ref.shape
    tile = full // PIX
    score_scale = HEAD_DIM ** (-0.5)
    W_OUT, C_QUERY, C_OUT = (slice(i * tile, (i + 1) * tile) for i in range(3))
    part = 64

    def cols(j):
        return pl.ds(pl.multiple_of(j * tile, tile), tile)

    def near_copy(which):
        return remote(
            near_out.at[which], near_in.at[which], near_send.at[which], near_recv.at[which], (row, near)
        )

    def line_copy(which):
        return remote(
            line_out.at[which], line_in.at[which], line_send.at[which], line_recv.at[which], (row, far)
        )

    def start_grad(which, left, right):
        def tile_of(index, targets):
            i, b = lax.div(index, 2), lax.rem(index, 2)
            return i, b, mul_tn(left[:, cols(i)], right[:, cols(jnp.where(b == 0, *targets))])

        def give(index):
            i, b, value = tile_of(index, (near, cross))
            near_out[which, b, cols(i), :] = value.astype(halves)

        def keep(index):
            i, b, value = tile_of(index, (col, far))
            kept[which, b, cols(i), :] = value

        loop(2 * PIX, give)
        near_copy(which).start()
        loop(2 * PIX, keep)

    def pass_grad(which):
        near_copy(which).wait_recv()

        def add(i):
            here = cols(i)
            line_out[which, here, :] = (
                kept[which, 1, here, :] + near_in[which, 1, here, :].astype(floats)
            ).astype(halves)

        loop(PIX, add)
        line_copy(which).start()

    def end_grad(which):
        line_copy(which).wait_recv()

        def add(i):
            here = cols(i)
            reduced_ref[here, which * tile : (which + 1) * tile] = (
                kept[which, 0, here, :]
                + near_in[which, 0, here, :].astype(floats)
                + line_in[which, here, :].astype(floats)
            ).astype(halves)

        loop(PIX, add)
        near_copy(which).wait_send()
        line_copy(which).wait_send()

    for j in range(PIX):
        attended[:, j * tile : (j + 1) * tile] = attended_ref[j]

    def out_two(j):
        two[:, cols(j)] = hidden_ref[:, cols(j)] + mul(attended[...], weight_ref[j, :, W_OUT])

    loop(PIX, out_two)

    def norm_two(i):
        here = pl.ds(pl.multiple_of(i * part, part), part)
        hidden = two[here, :]
        mean = jnp.mean(hidden * hidden, -1, keepdims=True)
        normed[here, :] = (hidden * lax.rsqrt(mean + 1e-06) * gain_ref[...]).astype(halves)

    loop(rows // part, norm_two)

    def out_query(j):
        query[:, cols(j)] = mul(normed[...], weight_ref[j, :, C_QUERY]).astype(halves)

    loop(PIX, out_query)
    slots = text_ref.shape[1]
    known = lax.broadcasted_iota(jnp.int32, (rows, slots), 1) < words
    pairs = tile // 128

    def text_lanes(pair, side):
        return pl.ds(pl.multiple_of(side * tile + lax.rem(pair, pairs) * 128, 128), 128)

    def cross_pair(pair):
        here = pl.ds(pl.multiple_of(pair * 128, 128), 128)
        group = lax.div(pair, pairs)
        queries = query[:, here]
        keys = text_ref[group, :, text_lanes(pair, 0)]
        values = text_ref[group, :, text_lanes(pair, 1)]
        outs = []
        for h in range(2):
            lanes = slice(h * HEAD_DIM, (h + 1) * HEAD_DIM)
            scores = score_scale * mul_nt(queries[:, lanes], keys[:, lanes])
            scores = jnp.where(known, scores, -1e30)
            expanded = jnp.exp(scores - jnp.max(scores, -1, keepdims=True))
            prob = expanded / jnp.sum(expanded, -1, keepdims=True)
            probs[2 * pair + h] = prob
            outs.append(mul(prob.astype(halves), values[:, lanes]))
        crossed[:, here] = jnp.concatenate(outs, axis=1).astype(halves)

    def cross_four(i):
        cross_pair(2 * i)
        cross_pair(2 * i + 1)

    loop(full // 256, cross_four)
    rgb_ref[...] = jnp.zeros_like(rgb_ref)

    def out_three(j):
        three = two[:, cols(j)] + mul(crossed[...], weight_ref[j, :, C_OUT])
        output_ref[:, cols(j)] = three
        blend = (three * rgb_scale_ref[:, cols(j)]).astype(halves)
        mixed[:, cols(j)] = blend
        rgb_ref[...] += mul(blend, rgb_weight_ref[cols(j), :])

    loop(PIX, out_three)
    rgb_grad = rgb_cotangent_ref[...] + penalty_weight * penalty_ref[...] * rgb_ref[...]

    def back_three(j):
        color = mul_tn(rgb_grad, mixed[:, cols(j)].astype(floats), highest)
        small_ref[2:5, cols(j)] = color[0:3]
        grad_mixed = mul_nt(rgb_grad, rgb_weight_ref[cols(j), :].astype(floats), highest)
        small_ref[1:2, cols(j)] = jnp.sum(grad_mixed * output_ref[:, cols(j)], 0, keepdims=True)
        grad = cotangent_ref[:, cols(j)].astype(floats) + grad_mixed * rgb_scale_ref[:, cols(j)]
        grad_three[:, cols(j)] = grad
        grad_proj[:, cols(j)] = grad.astype(halves)

    loop(PIX, back_three)
    start_grad(0, crossed, grad_proj)

    def times_transposed(source, j, which):
        acc = jnp.zeros((rows, tile), floats)
        for i in range(PIX):
            acc = acc + mul_nt(source[:, i * tile : (i + 1) * tile], weight_ref[i, cols(j), which])
        return acc

    def back_crossed(j):
        grad_crossed[:, cols(j)] = times_transposed(grad_proj, j, C_OUT).astype(halves)

    loop(PIX, back_crossed)

    def back_pair(pair):
        here = pl.ds(pl.multiple_of(pair * 128, 128), 128)
        group = lax.div(pair, pairs)
        queries, grads = query[:, here], grad_crossed[:, here]
        keys = text_ref[group, :, text_lanes(pair, 0)]
        values = text_ref[group, :, text_lanes(pair, 1)]
        grad_q, grad_k, grad_v = [], [], []
        for h in range(2):
            lanes = slice(h * HEAD_DIM, (h + 1) * HEAD_DIM)
            prob = probs[2 * pair + h]
            grad = grads[:, lanes]
            grad_prob = mul_nt(grad, values[:, lanes])
            grad_v.append(mul_tn(prob.astype(halves), grad))
            inner = jnp.sum(grad_prob * prob, -1, keepdims=True)
            score = (prob * (grad_prob - inner)).astype(halves)
            grad_q.append(score_scale * mul(score, keys[:, lanes]))
            grad_k.append(score_scale * mul_tn(score, queries[:, lanes]))
        grad_query[:, here] = jnp.concatenate(grad_q, axis=1).astype(halves)
        text_grad_ref[group, :, text_lanes(pair, 0)] = jnp.concatenate(grad_k, axis=1).astype(halves)
        text_grad_ref[group, :, text_lanes(pair, 1)] = jnp.concatenate(grad_v, axis=1).astype(halves)

    def back_four(i):
        back_pair(2 * i)
        back_pair(2 * i + 1)

    loop(full // 256, back_four)
    pass_grad(0)

    def back_query(j):
        grad_norm[:, cols(j)] = times_transposed(grad_query, j, C_QUERY)

    loop(PIX, back_query)
    small_ref[0:1, :] = jnp.zeros((1, full), floats)

    def back_norm(i):
        here = pl.ds(pl.multiple_of(i * part, part), part)
        hidden, grad = two[here, :], grad_norm[here, :]
        inverse = lax.rsqrt(jnp.mean(hidden * hidden, -1, keepdims=True) + 1e-06)
        small_ref[0:1, :] += jnp.sum(grad * hidden * inverse, 0, keepdims=True)
        scaled = grad * gain_ref[...]
        mean = jnp.mean(scaled * hidden, -1, keepdims=True)
        total = grad_three[here, :] + inverse * scaled - hidden * (inverse * inverse * inverse * mean)
        grad_two_ref[here, :] = total
        grad_attn[here, :] = total.astype(halves)

    loop(rows // part, back_norm)

    def back_attended(j):
        grad_attended_ref[j] = times_transposed(grad_attn, j, W_OUT).astype(halves)

    loop(PIX, back_attended)

    small_ref[5:8, :] = jnp.zeros((3, full), floats)
    end_grad(0)


def cross_part(
    words, attended, hidden, weights, text, gain, rgb_scale, rgb_weight, cotangent, rgb_cotangent, penalty
):
    rows, full = hidden.shape
    tile = full // PIX
    heads = full // HEAD_DIM
    wide = pltpu.VMEM((rows, full), floats)
    slim = pltpu.VMEM((rows, full), halves)
    return pl.pallas_call(
        partial(cross_kernel, words),
        out_shape=(
            jax.ShapeDtypeStruct((rows, full), floats),
            jax.ShapeDtypeStruct((rows, 128), floats),
            jax.ShapeDtypeStruct((full, tile), halves),
            jax.ShapeDtypeStruct(text.shape, halves),
            jax.ShapeDtypeStruct((rows, full), floats),
            jax.ShapeDtypeStruct((PIX, rows, tile), halves),
            jax.ShapeDtypeStruct((8, full), floats),
        )
        + (jax.ShapeDtypeStruct((rows, full), halves),) * 4,
        in_specs=[VMEM] * 10,
        out_specs=(VMEM,) * 11,
        scratch_shapes=[
            wide,
            slim,
            pltpu.VMEM((heads, rows, text.shape[1]), floats),
            slim,
            slim,
            wide,
            slim,
            slim,
            wide,
            pltpu.VMEM((1, 2, full, tile), halves),
            pltpu.VMEM((1, 2, full, tile), halves),
            pltpu.VMEM((1, 2, full, tile), floats),
            pltpu.VMEM((1, full, tile), halves),
            pltpu.VMEM((1, full, tile), halves),
            DMA((1,)),
            DMA((1,)),
            DMA((1,)),
            DMA((1,)),
        ],
        compiler_params=params(6),
        name="cross_part",
    )(
        attended,
        hidden,
        weights,
        text,
        gain.reshape(1, -1),
        rgb_scale,
        rgb_weight,
        cotangent,
        rgb_cotangent,
        penalty,
    )


def attend_back_kernel(
    grad_ref,
    query_ref,
    key_ref,
    value_ref,
    total_ref,
    normed_from,
    weight_from,
    hidden_from,
    conv_from,
    grad_two_from,
    gain_ref,
    text_ref,
    text_grad_ref,
    reduced_ref,
    attended_ref,
    grad_attn_ref,
    normed_two_ref,
    grad_cross_ref,
    attention_ref,
    others_ref,
    text_owned_ref,
    grad_one_ref,
    grad_conv_ref,
    small_ref,
    normed_ref,
    weight_ref,
    hidden_ref,
    conv_ref,
    grad_two_ref,
    load_sem,
    grads,
    grad_query,
    grad_key,
    grad_value,
    key_acc,
    value_acc,
    totals,
    pair_out,
    pair_in,
    line_out,
    line_in,
    own,
    conv_out,
    text_in,
    near_out,
    near_in,
    near_kept,
    far_out,
    far_in,
    side_in,
    level_out,
    level_in,
    out_grad,
    out_side_in,
    out_level_out,
    out_level_in,
    words_grad,
    words_side_in,
    words_level_out,
    words_level_in,
    attention_grad,
    attention_in,
    attention_out,
    attention_landed,
    grad_send,
    grad_recv,
    text_send,
    text_recv,
    pair_send,
    pair_recv,
    line_send,
    line_recv,
    conv_send,
    conv_recv,
    near_send,
    near_recv,
    far_send,
    far_recv,
    attention_send,
    attention_recv,
    landed_send,
    landed_recv,
    *reduce_sems,
):
    row, col = lax.axis_index("dp"), lax.axis_index("pix")
    near, far, cross = peers(col)
    targets = (far, cross, near)
    _, groups, _, owned, _ = attention_grad.shape
    side, level = lax.rem(row, 2), lax.div(row, 2)
    partner = flip(row, 1)
    loads = [
        pltpu.make_async_copy(source, buffer, load_sem.at[i])
        for i, (source, buffer) in enumerate(
            (
                (normed_from, normed_ref),
                (weight_from.at[:, pl.ds(0, weight_ref.shape[1])], weight_ref),
                (hidden_from, hidden_ref),
                (conv_from, conv_ref),
                (grad_two_from, grad_two_ref),
            )
        )
    ]
    for load in loads:
        load.start()
    barrier = pltpu.get_barrier_semaphore()

    def hello(step, carry):
        other = 2 * lax.rem(level + step, groups) + side
        pl.semaphore_signal(barrier, inc=1, device_id=(other, col), device_id_type=MESH)
        return carry

    lax.fori_loop(1, groups, hello, 0)
    for other in ((partner, col), (row, near), (row, far), (row, cross)):
        pl.semaphore_signal(barrier, inc=1, device_id=other, device_id_type=MESH)
    pl.semaphore_wait(barrier, groups - 1 + 4)
    rows, full = hidden_ref.shape
    tokens, width = query_ref.shape
    heads = width // HEAD_DIM
    score_scale = HEAD_DIM ** (-0.5)

    def grad_copy(turn):
        return remote(
            grad_ref.at[targets[turn]],
            grads.at[col],
            grad_send.at[turn],
            grad_recv.at[turn],
            (row, targets[turn]),
        )

    used = text_in.shape[1]

    def text_copy(turn):
        return remote(
            text_grad_ref.at[targets[turn], pl.ds(0, used), :],
            text_in.at[turn],
            text_send.at[turn],
            text_recv.at[turn],
            (row, targets[turn]),
        )

    for turn in range(3):
        grad_copy(turn).start()
    for turn in range(3):
        text_copy(turn).start()

    def reduction(which, source, arrived, out, landed):
        side_send, side_recv, level_send, level_recv = reduce_sems[4 * which : 4 * which + 4]

        def to_side():
            return remote(source.at[:, 1 - side], arrived, side_send, side_recv, (partner, col))

        def to_level(k):
            group = lax.rem(level + k, groups)
            return remote(
                out.at[group], landed.at[k], level_send.at[k], level_recv.at[k], (2 * group + side, col)
            )

        def middle():
            to_side().wait_recv()

            def add(group):
                out[group] = (
                    source[group, side].astype(floats) + arrived[group].astype(floats)
                ).astype(halves)

            loop(groups, add)
            lax.fori_loop(1, groups, lambda k, c: (to_level(k).start(), c)[1], 0)

        def finish():
            total = out[level].astype(floats)
            for k in range(1, groups):
                to_level(k).wait()
                total = total + landed[k].astype(floats)
            to_side().wait_send()
            return total.astype(halves)

        return to_side, middle, finish

    sides = reduction(0, reduced_ref, side_in, level_out, level_in)
    outs = reduction(1, out_grad, out_side_in, out_level_out, out_level_in)
    word = reduction(2, words_grad, words_side_in, words_level_out, words_level_in)
    sides[0]().start()

    def near_copy(which):
        return remote(
            near_out.at[which], near_in.at[which], near_send.at[which], near_recv.at[which], (row, near)
        )

    def far_copy(which):
        return remote(
            far_out.at[which], far_in.at[which], far_send.at[which], far_recv.at[which], (row, far)
        )

    def row_tile(i):
        return pl.ds(pl.multiple_of(i * width, width), width)

    lefts, rights = (attended_ref, normed_two_ref), (grad_attn_ref, grad_cross_ref)
    per_tile = width // (2 * owned)
    for which in range(2):

        def out_tile(index, first, second, which=which):
            i, b = lax.div(index, 2), lax.rem(index, 2)
            right = rights[which][:, row_tile(jnp.where(b == 0, first, second))]
            return i, b, mul_tn(lefts[which][:, row_tile(i)], right)

        def out_give(index, which=which, out_tile=out_tile):
            i, b, value = out_tile(index, near, cross)
            near_out[which, b, row_tile(i), :] = value.astype(halves)

        def out_keep(index, which=which, out_tile=out_tile):
            i, b, value = out_tile(index, col, far)
            near_kept[which, b, row_tile(i), :] = value

        loop(2 * PIX, out_give)
        near_copy(which).start()
        loop(2 * PIX, out_keep)

    def out_pass():
        for which in range(2):
            near_copy(which).wait_recv()

            def add(i, which=which):
                here = row_tile(i)
                far_out[which, here, :] = (
                    near_kept[which, 1, here, :] + near_in[which, 1, here, :].astype(floats)
                ).astype(halves)

            loop(PIX, add)
            far_copy(which).start()

    def out_end():
        for which in range(2):
            far_copy(which).wait_recv()

            def add(i, which=which):
                here = row_tile(i)
                value = (
                    near_kept[which, 0, here, :]
                    + near_in[which, 0, here, :].astype(floats)
                    + far_in[which, here, :].astype(floats)
                ).astype(halves)
                out_grad[pl.ds(i * per_tile, per_tile), :, :, which * width : (which + 1) * width] = (
                    value.reshape(per_tile, 2, owned, width)
                )

            loop(PIX, add)
        outs[0]().start()

    def words_grads():
        text_total = text_grad_ref[col, 0:used, :].astype(floats)
        for turn in range(3):
            text_copy(turn).wait_recv()
            text_total = text_total + text_in[turn].astype(floats)
        text_total = jnp.concatenate(
            [text_total, jnp.zeros((text_ref.shape[0] - used, 2 * width), floats)], axis=0
        )

        def put(j):
            for k in range(2):
                right = text_total[:, k * width : (k + 1) * width]
                value = mul_tn(text_ref[:, row_tile(j)].astype(floats), right, highest)
                words_grad[pl.ds(j * per_tile, per_tile), :, :, k * width : (k + 1) * width] = (
                    value.astype(halves).reshape(per_tile, 2, owned, width)
                )

        loop(full // width, put)
        word[0]().start()

    def attention_copy(part, j):
        here = pl.ds(j * per_tile, per_tile)
        return remote(
            attention_grad.at[part, here, 1 - side],
            attention_in.at[part, here],
            attention_send.at[part, j],
            attention_recv.at[part, j],
            (partner, col),
        )

    def weight_grads(part):
        lanes = slice(part * 128, (part + 1) * 128)

        def tile(j):
            here = pl.ds(j * per_tile, per_tile)
            for k, right in enumerate((grad_query, grad_key, grad_value)):
                acc = jnp.zeros((width, 128), floats)
                for i in range(PIX):
                    acc = acc + mul_tn(
                        normed_ref[i, :, row_tile(j)], right[i * rows : (i + 1) * rows, lanes]
                    )
                attention_grad[part, here, :, :, k * 128 : (k + 1) * 128] = acc.astype(
                    halves
                ).reshape(per_tile, 2, owned, 128)
            attention_copy(part, j).start()

        loop(full // width, tile)

    def landed_copy(k):
        group = lax.rem(level + k, groups)
        return remote(
            attention_out.at[group],
            attention_landed.at[k],
            landed_send.at[k],
            landed_recv.at[k],
            (2 * group + side, col),
        )

    def attention_sum(part, out):
        def add(j):
            attention_copy(part, j).wait_recv()
            here = pl.ds(j * per_tile, per_tile)
            out[here] = (
                attention_grad[part, here, side].astype(floats)
                + attention_in[part, here].astype(floats)
            ).astype(halves)

        loop(full // width, add)

    def attention_level():
        attention_sum(0, attention_out)
        lax.fori_loop(1, groups, lambda k, c: (landed_copy(k).start(), c)[1], 0)

    def between(h):
        if h == 0:
            words_grads()
            sides[1]()
        if h == 1:
            for load in loads:
                load.wait()
            weight_grads(0)
        if h == 2:
            word[1]()

    grads[col] = grad_ref[col]
    totals[...] = jnp.transpose(total_ref[...])
    for turn in range(3):
        remote(
            grad_ref.at[0],
            grads.at[targets[turn]],
            grad_send.at[turn],
            grad_recv.at[turn],
            (row, near),
        ).wait_recv()
    out_pass()
    ones = jnp.ones((rows, HEAD_DIM), halves)
    for h in range(heads):
        lanes = slice(h * HEAD_DIM, (h + 1) * HEAD_DIM)
        keys, values = key_ref[:, lanes], value_ref[:, lanes]
        wide = keys.astype(floats)
        norm = score_scale * jnp.sum(wide * wide, -1, keepdims=True)
        key_acc[...] = jnp.zeros_like(key_acc)
        value_acc[...] = jnp.zeros_like(value_acc)

        def block(i, lanes=lanes, keys=keys, values=values, norm=norm, h=h):
            here = pl.ds(pl.multiple_of(i * rows, rows), rows)
            queries, grad = query_ref[here, lanes], grads[i, :, lanes]
            inner = mul_nt(keys, queries)
            prob = jnp.exp((2.0 * score_scale) * inner - norm - totals[h : h + 1, here])
            grad_prob = mul_nt(values, grad)
            value_acc[...] += mul(prob.astype(halves), grad)
            mean = jnp.sum(grad_prob * prob, 0, keepdims=True)
            score = (prob * (grad_prob - mean)).astype(halves)
            key_acc[...] += mul(score, jnp.concatenate([queries, ones], axis=1))
            grad_query[here, lanes] = (2.0 * score_scale * mul_tn(score, keys)).astype(halves)

        loop(PIX, block)
        acc = key_acc[...]
        grad_key[:, lanes] = (
            2.0 * score_scale * (acc[:, :HEAD_DIM] - wide * acc[:, HEAD_DIM : HEAD_DIM + 1])
        ).astype(halves)
        grad_value[:, lanes] = value_acc[...].astype(halves)
        between(h)

    def norm_grad(block, store):
        here = pl.ds(pl.multiple_of(block * rows, rows), rows)

        def tile(j):
            cols = pl.ds(pl.multiple_of(j * width, width), width)
            acc = jnp.zeros((rows, width), floats)
            for k, source in enumerate((grad_query, grad_key, grad_value)):
                acc = acc + mul_nt(source[here, :], weight_ref[cols, k * width : (k + 1) * width])
            store(cols, acc)

        loop(full // width, tile)

    def pair_copy(turn):
        return remote(
            pair_out.at[turn], pair_in.at[turn], pair_send.at[turn], pair_recv.at[turn], (row, near)
        )

    for turn, target in enumerate((cross, near)):

        def store(cols, value, turn=turn):
            pair_out[turn, :, cols] = value.astype(halves)

        norm_grad(target, store)
        pair_copy(turn).start()
    half = rows // 2

    def line_copy(i):
        here = pl.ds(i * half, half)
        return remote(
            line_out.at[here], line_in.at[here], line_send.at[i], line_recv.at[i], (row, far)
        )

    def store_far(cols, value):
        line_out[:, cols] = (value + pair_in[0, :, cols].astype(floats)).astype(halves)

    pair_copy(0).wait_recv()
    norm_grad(far, store_far)
    line_copy(0).start()
    line_copy(1).start()

    def store_own(cols, value):
        own[:, cols] = value + pair_in[1, :, cols].astype(floats)

    pair_copy(1).wait_recv()
    norm_grad(col, store_own)

    out_end()
    weight_grads(1)
    attention_level()
    outs[1]()
    small_ref[...] = jnp.zeros_like(small_ref)
    part = 64

    def back_norm(i):
        here = pl.ds(pl.multiple_of(i * part, part), part)
        hidden = hidden_ref[here, :]
        grad = own[here, :] + line_in[here, :].astype(floats)
        inverse = lax.rsqrt(jnp.mean(hidden * hidden, -1, keepdims=True) + 1e-06)
        small_ref[0:1, :] += jnp.sum(grad * hidden * inverse, 0, keepdims=True)
        scaled = grad * gain_ref[...]
        mean = jnp.mean(scaled * hidden, -1, keepdims=True)
        total = (
            grad_two_ref[here, :] + inverse * scaled - hidden * (inverse * inverse * inverse * mean)
        )
        grad_one_ref[here, :] = total
        conv = conv_ref[here, :].astype(floats)
        gate = jax.nn.sigmoid(conv)
        result = (total * gate * (1.0 + conv * (1.0 - gate))).astype(halves)
        for j in range(PIX):
            conv_out[j, here, :] = result[:, j * width : (j + 1) * width]

    def conv_copy(turn, i, block=None):
        here = pl.ds(i * half, half)
        return remote(
            conv_out.at[targets[turn], here],
            grad_conv_ref.at[col if block is None else block, here],
            conv_send.at[2 * turn + i],
            conv_recv.at[2 * turn + i],
            (row, targets[turn]),
        )

    per_half = half // part
    for i in range(2):
        line_copy(i).wait_recv()
        lax.fori_loop(i * per_half, (i + 1) * per_half, lambda j, c: (back_norm(j), c)[1], 0)
        for turn in range(3):
            conv_copy(turn, i).start()
    grad_conv_ref[col] = conv_out[col]
    for i in range(2):
        for turn in range(3):
            conv_copy(turn, i, targets[turn]).wait_recv()
    for turn in range(3):
        conv_copy(turn, 0).wait_send()
        conv_copy(turn, 1).wait_send()
        grad_copy(turn).wait_send()
        text_copy(turn).wait_send()
    others_ref[:, 0 : 2 * width] = outs[2]()
    others_ref[:, 2 * width : 3 * width] = sides[2]()
    total = attention_out[level].astype(floats)
    for k in range(1, groups):
        landed_copy(k).wait()
        total = total + attention_landed[k].astype(floats)
    others_ref[:, 3 * width :] = total.astype(halves)
    text_owned_ref[...] = word[2]()

    attention_sum(1, attention_ref)
    for p in range(2):
        loop(full // width, lambda j, p=p: attention_copy(p, j).wait_send())
    for which in range(2):
        near_copy(which).wait_send()
        far_copy(which).wait_send()
    pair_copy(0).wait_send()
    pair_copy(1).wait_send()
    line_copy(0).wait_send()
    line_copy(1).wait_send()


def attend_backward(
    words,
    grad,
    query,
    key,
    value,
    totals,
    normed,
    weights,
    hidden,
    conv,
    grad_two,
    gain,
    text,
    text_grads,
    reduced,
    *factors,
):
    rows, full = hidden.shape
    groups, _, owned, _ = reduced.shape
    used = -(-words // 16) * 16
    tokens, width = query.shape
    flat = pltpu.VMEM((tokens, width), halves)
    return pl.pallas_call(
        attend_back_kernel,
        out_shape=(
            jax.ShapeDtypeStruct((groups, owned, 384), halves),
            jax.ShapeDtypeStruct((owned, 3 * width + 384), halves),
            jax.ShapeDtypeStruct((owned, 2 * width), halves),
            jax.ShapeDtypeStruct((rows, full), floats),
            jax.ShapeDtypeStruct((PIX, rows, width), halves),
            jax.ShapeDtypeStruct((8, full), floats),
        ),
        in_specs=[VMEM] * 5 + [ANY] * 5 + [VMEM] * 8,
        out_specs=(VMEM,) * 6,
        scratch_shapes=[
            pltpu.VMEM(normed.shape, halves),
            pltpu.VMEM((full, 3 * width), halves),
            pltpu.VMEM((rows, full), floats),
            pltpu.VMEM((rows, full), halves),
            pltpu.VMEM((rows, full), floats),
            DMA((5,)),
            pltpu.VMEM((PIX, rows, width), halves),
            flat,
            flat,
            flat,
            pltpu.VMEM((tokens, 2 * HEAD_DIM), floats),
            pltpu.VMEM((tokens, HEAD_DIM), floats),
            pltpu.VMEM((128, tokens), floats),
            pltpu.VMEM((2, rows, full), halves),
            pltpu.VMEM((2, rows, full), halves),
            pltpu.VMEM((rows, full), halves),
            pltpu.VMEM((rows, full), halves),
            pltpu.VMEM((rows, full), floats),
            pltpu.VMEM((PIX, rows, width), halves),
            pltpu.VMEM((3, used, 2 * width), halves),
            pltpu.VMEM((2, 2, full, width), halves),
            pltpu.VMEM((2, 2, full, width), halves),
            pltpu.VMEM((2, 2, full, width), floats),
            pltpu.VMEM((2, full, width), halves),
            pltpu.VMEM((2, full, width), halves),
            pltpu.VMEM((groups, owned, width), halves),
            pltpu.VMEM((groups, owned, width), halves),
            pltpu.VMEM((groups, owned, width), halves),
            pltpu.VMEM((groups, 2, owned, 2 * width), halves),
            pltpu.VMEM((groups, owned, 2 * width), halves),
            pltpu.VMEM((groups, owned, 2 * width), halves),
            pltpu.VMEM((groups, owned, 2 * width), halves),
            pltpu.VMEM((groups, 2, owned, 2 * width), halves),
            pltpu.VMEM((groups, owned, 2 * width), halves),
            pltpu.VMEM((groups, owned, 2 * width), halves),
            pltpu.VMEM((groups, owned, 2 * width), halves),
            pltpu.VMEM((2, groups, 2, owned, 384), halves),
            pltpu.VMEM((2, groups, owned, 384), halves),
            pltpu.VMEM((groups, owned, 384), halves),
            pltpu.VMEM((groups, owned, 384), halves),
            DMA((3,)),
            DMA((3,)),
            DMA((3,)),
            DMA((3,)),
            DMA((2,)),
            DMA((2,)),
            DMA((2,)),
            DMA((2,)),
            DMA((6,)),
            DMA((6,)),
            DMA((2,)),
            DMA((2,)),
            DMA((2,)),
            DMA((2,)),
            DMA((2, PIX)),
            DMA((2, PIX)),
            DMA((groups,)),
            DMA((groups,)),
        ]
        + [DMA, DMA, DMA((groups,)), DMA((groups,))] * 3,
        compiler_params=params(3),
        name="attend_backward",
    )(
        grad,
        query,
        key,
        value,
        totals,
        normed,
        weights,
        hidden,
        conv,
        grad_two,
        gain.reshape(1, -1),
        text,
        text_grads,
        reduced,
        *factors,
    )


def conv_back_kernel(
    count,
    width,
    images_ref,
    kernel_from,
    bank_from,
    styles_ref,
    inverse_ref,
    grad_ref,
    conv_ref,
    attention_ref,
    others_ref,
    words_ref,
    small_ref,
    last_ref,
    bank_grad_ref,
    attention_all,
    others_all,
    words_all,
    rows_all_ref,
    stats_all_ref,
    image_grad_ref,
    grads_ref,
    kernel_ref,
    bank_ref,
    table_sem,
    stats_ref,
    rows_out,
    rows_in,
    stats_in,
    rows_sum,
    stats_sum,
    image_buf,
    padded_image,
    padded_grad,
    turned,
    acc,
    sums_out,
    sums_in,
    kept,
    kept_own,
    pixel_out,
    pixel_in,
    line_out,
    line_in,
    owner_out,
    attention_in,
    local_sem,
    image_sem,
    load_sem,
    sums_send,
    sums_recv,
    up_send,
    down_send,
    level_recv,
    pair_send,
    pair_recv,
    pixel_send,
    pixel_recv,
    line_send,
    line_recv,
    owner_send,
    owner_recv,
    attention_send,
    attention_recv,
    weight_send,
    weight_recv,
    rows_send,
    rows_recv,
    stats_send,
    stats_recv,
    far_rows_send,
    far_rows_recv,
    far_stats_send,
    far_stats_recv,
    rows_sem,
    stats_sem,
):
    row, col = lax.axis_index("dp"), lax.axis_index("pix")
    groups = count // 2
    side, level = lax.rem(row, 2), lax.div(row, 2)
    partner = flip(row, 1)
    near, far, cross = peers(col)
    targets = (far, cross, near)
    tokens, channels = grad_ref.shape

    buffers = (attention_all, others_all, words_all)

    def weight_copy(which, hop):
        block = buffers[which].at[far if hop == 2 else col]
        index = 3 * which + hop
        return remote(
            block, block, weight_send.at[index], weight_recv.at[index], (row, far if hop == 0 else near)
        )

    def weight_arrives(which, hop):
        block = buffers[which].at[(far, near, cross)[hop]]
        index = 3 * which + hop
        remote(block, block, weight_send.at[index], weight_recv.at[index], (row, near)).wait_recv()

    def weight_start(which):
        weight_copy(which, 0).start()
        weight_copy(which, 1).start()

    def weight_pass(which):
        weight_arrives(which, 0)
        weight_copy(which, 2).start()

    def weight_end(which):
        weight_arrives(which, 1)
        weight_arrives(which, 2)
        for hop in range(3):
            weight_copy(which, hop).wait_send()

    def group_copy(turn, source, landed, send, recv):
        return remote(source, landed.at[turn], send.at[turn], recv.at[turn], (row, targets[turn]))

    def group_sum(source, landed, send, recv):
        for turn in range(3):
            group_copy(turn, source, landed, send, recv).wait()
        landed[3] = source[...]
        total = None
        for which in range(PIX):
            turn = jnp.where(
                which == col, 3, jnp.where(which == far, 0, jnp.where(which == cross, 1, 2))
            )
            total = landed[turn] if total is None else total + landed[turn]
        return total

    def far_copy(k, total, everyone, send, recv):
        return remote(
            total, everyone.at[row], send.at[k], recv.at[k], (lax.rem(row + k, count), col)
        )

    def far_start(total, everyone, send, recv, sem):
        pltpu.make_async_copy(total, everyone.at[row], sem).start()
        lax.fori_loop(
            1, count, lambda k, c: (far_copy(k, total, everyone, send, recv).start(), c)[1], 0
        )

    def far_end(total, everyone, send, recv, sem):
        pltpu.make_async_copy(total, everyone.at[row], sem).wait()

        def arrive(k, carry):
            origin = lax.rem(row - k + count, count)
            remote(total, everyone.at[origin], send.at[k], recv.at[k], (row, near)).wait_recv()
            return carry

        lax.fori_loop(1, count, arrive, 0)
        lax.fori_loop(
            1, count, lambda k, c: (far_copy(k, total, everyone, send, recv).wait_send(), c)[1], 0
        )

    rows_group = (rows_out, rows_in, rows_send, rows_recv)
    stats_group = (stats_ref, stats_in, stats_send, stats_recv)
    rows_far = (rows_sum, rows_all_ref, far_rows_send, far_rows_recv, rows_sem)
    stats_far = (stats_sum, stats_all_ref, far_stats_send, far_stats_recv, stats_sem)

    def attention_copy(k):
        group = lax.rem(level + k, groups)
        return remote(
            attention_ref.at[group],
            attention_in.at[k],
            attention_send.at[k],
            attention_recv.at[k],
            (2 * group + side, col),
        )

    depth = image_buf.shape[2]
    rows = tokens // PIX
    halo = width
    greet(count, [(row, near), (row, far), (row, cross)])

    def sample_of(step):
        paired, k = turn_of(step)
        return 2 * level_at(level, groups, k) + jnp.where(paired, 1 - side, side)

    def turn_of(step):
        final = step == count - 1
        even = lax.rem(step, 2) == 0
        paired = final | (even & (step > 0))
        k = jnp.where(even, jnp.maximum(lax.div(step, 2) - 1, 0), lax.div(step + 1, 2))
        return paired, jnp.where(final, groups - 1, k)

    has_below, has_above = level > 0, level < groups - 1
    reach = jnp.minimum(level, groups - 1 - level)

    def line_block(origin, upward):
        block = grads_ref.at[2 * origin + side]
        sem = (up_send if upward else down_send).at[origin]
        target = jnp.minimum(row + 2, count - 1) if upward else jnp.maximum(row - 2, 0)
        return remote(block, block, sem, level_recv.at[origin], (target, col))

    def relay(k):
        origin = level_at(level, groups, k)
        block = grads_ref.at[2 * origin + side]
        remote(
            block, block, up_send.at[origin], level_recv.at[origin], (partner, col)
        ).wait_recv()

        @pl.when((origin < level) & has_above)
        def _():
            line_block(origin, True).start()

        @pl.when((origin > level) & has_below)
        def _():
            line_block(origin, False).start()

        pair_copy(k).start()

    def pair_copy(k):
        block = grads_ref.at[2 * level_at(level, groups, k) + side]
        return remote(block, block, pair_send.at[k], pair_recv.at[k], (partner, col))

    def sums_copy(k):
        return remote(
            sums_out,
            sums_in.at[row],
            sums_send.at[k],
            sums_recv.at[k],
            (lax.rem(row + k, count), col),
        )

    loads = [
        pltpu.make_async_copy(kernel_from, kernel_ref, table_sem.at[0]),
        pltpu.make_async_copy(bank_from, bank_ref, table_sem.at[1]),
    ]
    own = pltpu.make_async_copy(grad_ref, grads_ref.at[row], local_sem)
    own.start()
    for load in loads:
        load.start()
    own.wait()

    @pl.when(has_above)
    def _():
        line_block(level, True).start()

    @pl.when(has_below)
    def _():
        line_block(level, False).start()

    pair_copy(0).start()

    def fetch(step):
        slot = lax.rem(step, 2)
        return pltpu.make_async_copy(
            images_ref.at[sample_of(step)], image_buf.at[slot], image_sem.at[slot]
        )

    fetch(0).start()
    others_all[col] = others_ref[...]
    words_all[col] = words_ref[...]
    rows_out[...] = small_ref[...]
    rows_out[5:6, :] = last_ref[0:1, :]
    for which in (1, 2):
        weight_start(which)
    for turn in range(3):
        group_copy(turn, *rows_group).start()
    products = jnp.zeros((8, channels), floats)

    def add_product(i, total):
        here = pl.ds(pl.multiple_of(i * 64, 64), 64)
        product = grad_ref[here, :].astype(floats) * conv_ref[here, :].astype(floats)
        return total + jnp.sum(product.reshape(8, 8, channels), axis=0)

    products = lax.fori_loop(0, tokens // 64, add_product, products)
    sums_out[...] = jnp.broadcast_to(jnp.sum(products, 0, keepdims=True), (8, channels))
    lax.fori_loop(1, count, lambda k, c: (sums_copy(k).start(), c)[1], 0)
    sums_in[row] = sums_out[...]
    acc[...] = jnp.zeros_like(acc)
    stats_ref[...] = jnp.zeros_like(stats_ref)
    for buffer, lanes in ((padded_image, depth), (padded_grad, channels)):
        zeros = jnp.zeros((3, halo, lanes), halves)
        buffer[:, 0:halo, :] = zeros
        buffer[:, halo + tokens : halo + tokens + halo, :] = zeros

    def sums_arrive(k, carry):
        origin = lax.rem(row - k + count, count)
        remote(
            sums_out, sums_in.at[origin], sums_send.at[k], sums_recv.at[k], (partner, col)
        ).wait_recv()
        return carry

    def fill(buffer, source):
        wide = source.astype(floats)
        place = lax.rem(lax.broadcasted_iota(jnp.int32, wide.shape, 0), width)
        here = slice(halo, halo + tokens)
        buffer[0, here, :] = jnp.where(place == 0, 0.0, pltpu.roll(wide, 1, 0)).astype(halves)
        buffer[2, here, :] = jnp.where(
            place == width - 1, 0.0, pltpu.roll(wide, tokens - 1, 0)
        ).astype(halves)

    centre = pl.ds(halo, tokens)

    def pixel_copy(step):
        return remote(
            pixel_out.at[lax.rem(step, 2)],
            pixel_in.at[step],
            pixel_send.at[step],
            pixel_recv.at[step],
            (row, near),
        )

    def line_copy(step):
        return remote(
            line_out.at[lax.rem(step, 2)],
            line_in.at[step],
            line_send.at[step],
            line_recv.at[step],
            (row, far),
        )

    def owner_copy(step):
        return remote(
            owner_out.at[lax.rem(step, 2)],
            image_grad_ref.at[row],
            owner_send.at[step],
            owner_recv.at[row],
            (sample_of(step), col),
        )

    def work(step):
        paired, k = turn_of(step)
        sample = sample_of(step)

        @pl.when(paired)
        def _():
            block = grads_ref.at[sample]
            remote(block, block, pair_send.at[k], pair_recv.at[k], (partner, col)).wait_recv()

        distance = lax.div(step + 1, 2)
        odd = lax.rem(step, 2) == 1

        @pl.when(odd & (distance <= reach))
        def _():
            relay(2 * distance - 1)
            relay(2 * distance)

        @pl.when(odd & (distance > reach) & (distance <= groups - 1 - reach))
        def _():
            relay(distance + reach)

        load = pltpu.make_async_copy(
            grads_ref.at[sample], padded_grad.at[1, centre, :], load_sem
        )
        load.start()
        fetch(step).wait()

        @pl.when(step + 1 < count)
        def _():
            fetch(step + 1).start()

        image = image_buf[lax.rem(step, 2)]
        padded_image[1, centre, :] = image
        fill(padded_image, image)
        load.wait()
        grad = padded_grad[1, centre, :]
        fill(padded_grad, grad)
        turned[...] = jnp.transpose(grad)
        slot = lax.rem(step, 2)

        @pl.when(step >= 2)
        def _():
            pixel_copy(step - 2).wait_send()

        def through(target):
            start = pl.multiple_of(target * rows, rows)
            total = jnp.zeros((rows, depth), floats)
            for a in range(3):
                for b in range(3):
                    window = padded_grad[
                        2 - b, pl.ds(pl.multiple_of(start + (2 - a) * width, 16), rows), :
                    ]
                    total = total + mul_nt(window, kernel_ref[sample, 3 * a + b])
            return total

        def give(i):
            pixel_out[slot, i] = through(jnp.where(i == 0, near, cross)).astype(halves)

        def keep(i):
            kept[slot, i] = through(jnp.where(i == 0, col, far))

        loop(2, give)
        pixel_copy(step).start()
        loop(2, keep)
        style = styles_ref[sample]
        scale = style[0:1, :depth]
        first, second = style[1:2, 0:1], style[2:3, 0:1]
        both = jnp.concatenate(
            [
                jnp.broadcast_to(inverse_ref[pl.ds(sample, 1), :], (8, channels)),
                sums_in[sample],
            ],
            axis=0,
        )
        columns = jnp.transpose(both)
        inverse, total = columns[:, 0:1], columns[:, 8:9]
        factor = inverse * inverse * total
        by_scale = jnp.zeros((1, depth), floats)
        by_first = jnp.zeros((1, depth), floats)
        by_second = jnp.zeros((1, depth), floats)
        for a in range(3):
            for b in range(3):
                tap = 3 * a + b
                found = mul(turned[...], padded_image[b, pl.ds(a * width, tokens), :])
                one, two = bank_ref[0, tap].astype(floats), bank_ref[1, tap].astype(floats)
                selected = first * one + second * two
                modded = inverse * found - factor * (selected * scale)
                by_scale = by_scale + jnp.sum(modded * selected, 0, keepdims=True)
                grad_selected = modded * scale
                acc[0, tap] += first * grad_selected
                acc[1, tap] += second * grad_selected
                by_first = by_first + jnp.sum(grad_selected * one, 0, keepdims=True)
                by_second = by_second + jnp.sum(grad_selected * two, 0, keepdims=True)
        stats_ref[sample, 0:1, :depth] = by_scale
        stats_ref[sample, 1:2, :depth] = by_first
        stats_ref[sample, 2:3, :depth] = by_second

    def across(step):
        slot = lax.rem(step, 2)
        pixel_copy(step).wait_recv()

        @pl.when(step >= 2)
        def _():
            line_copy(step - 2).wait_send()

        line_out[slot] = (kept[slot, 1] + pixel_in[step, 1].astype(floats)).astype(halves)
        line_copy(step).start()
        kept_own[slot] = kept[slot, 0] + pixel_in[step, 0].astype(floats)

    def home(step):
        slot = lax.rem(step, 2)
        line_copy(step).wait_recv()

        @pl.when(step >= 3)
        def _():
            owner_copy(step - 2).wait_send()

        owner_out[slot] = (kept_own[slot] + line_in[step].astype(floats)).astype(halves)

        @pl.when(step > 0)
        def _():
            owner_copy(step).start()

        @pl.when(step == 0)
        def _():
            mine = pltpu.make_async_copy(owner_out.at[slot], image_grad_ref.at[row], local_sem)
            mine.start()
            mine.wait()

    lax.fori_loop(1, count, sums_arrive, 0)

    for load in loads:
        load.wait()

    def step_body(step):
        @pl.when(step == 2)
        def _():
            for which in (1, 2):
                weight_pass(which)
            rows_sum[...] = group_sum(*rows_group)
            far_start(*rows_far)

        @pl.when(step == count - 2)
        def _():
            lax.fori_loop(1, groups, lambda k, c: (attention_copy(k).start(), c)[1], 0)

        @pl.when(step < count)
        def _():
            work(step)

        @pl.when(step == count)
        def _():
            for turn in range(3):
                group_copy(turn, *stats_group).start()

        @pl.when((step >= 1) & (step <= count))
        def _():
            across(step - 1)

        @pl.when(step >= 2)
        def _():
            home(step - 2)

    loop(count + 2, step_body)
    lax.fori_loop(1, groups, lambda k, c: (attention_copy(k).wait(), c)[1], 0)
    attention_total = attention_ref[level].astype(floats)
    for k in range(1, groups):
        attention_total = attention_total + attention_in[k].astype(floats)
    attention_all[col] = attention_total.astype(halves)
    weight_start(0)
    stats_sum[...] = group_sum(*stats_group)
    far_start(*stats_far)

    def write(index):
        bank_grad_ref[lax.div(index, 9), lax.rem(index, 9)] = jnp.transpose(
            acc[lax.div(index, 9), lax.rem(index, 9)]
        )

    loop(18, write)

    def owner_arrives(k, carry):
        origin = lax.rem(row - k + count, count)
        remote(
            owner_out.at[0],
            image_grad_ref.at[origin],
            owner_send.at[k],
            owner_recv.at[origin],
            (partner, col),
        ).wait_recv()
        return carry

    lax.fori_loop(1, count, owner_arrives, 0)
    weight_pass(0)
    far_end(*rows_far)
    far_end(*stats_far)
    for which in (1, 2, 0):
        weight_end(which)
    for step in (count - 2, count - 1):
        pixel_copy(step).wait_send()
        line_copy(step).wait_send()
        owner_copy(step).wait_send()

    def sent(origin):
        @pl.when((origin <= level) & has_above)
        def _():
            line_block(origin, True).wait_send()

        @pl.when((origin >= level) & has_below)
        def _():
            line_block(origin, False).wait_send()

    loop(groups, sent)
    loop(groups, lambda k: pair_copy(k).wait_send())
    lax.fori_loop(1, count, lambda k, c: (sums_copy(k).wait_send(), c)[1], 0)


def conv_backward(images_all, kernels, bank, styles, inverse, grad, conv, owned, rows_here, width):
    attention, others, words = owned
    small, last = rows_here
    count, tokens, depth = images_all.shape
    channels = grad.shape[1]
    rows = tokens // PIX
    groups = count // 2
    piece = (rows, depth)
    return pl.pallas_call(
        partial(conv_back_kernel, count, width),
        out_shape=(
            jax.ShapeDtypeStruct((2, 9, depth, channels), floats),
            jax.ShapeDtypeStruct((PIX,) + attention.shape[1:], halves),
            jax.ShapeDtypeStruct((PIX,) + others.shape, halves),
            jax.ShapeDtypeStruct((PIX,) + words.shape, halves),
            jax.ShapeDtypeStruct((count,) + small.shape, floats),
            jax.ShapeDtypeStruct((count, count, 8, 128), floats),
            jax.ShapeDtypeStruct((count,) + piece, halves),
            jax.ShapeDtypeStruct((count, tokens, channels), halves),
        ),
        in_specs=[ANY] * 3 + [VMEM] * 9,
        out_specs=(VMEM,) * 4 + (ANY,) * 4,
        scratch_shapes=[
            pltpu.VMEM(kernels.shape, halves),
            pltpu.VMEM(bank.shape, halves),
            DMA((2,)),
            pltpu.VMEM((count, 8, 128), floats),
            pltpu.VMEM(small.shape, floats),
            pltpu.VMEM((4,) + small.shape, floats),
            pltpu.VMEM((4, count, 8, 128), floats),
            pltpu.VMEM(small.shape, floats),
            pltpu.VMEM((count, 8, 128), floats),
            pltpu.VMEM((2, tokens, depth), halves),
            pltpu.VMEM((3, tokens + 2 * width, depth), halves),
            pltpu.VMEM((3, tokens + 2 * width, channels), halves),
            pltpu.VMEM((channels, tokens), halves),
            pltpu.VMEM((2, 9, channels, depth), floats),
            pltpu.VMEM((8, channels), floats),
            pltpu.VMEM((count, 8, channels), floats),
            pltpu.VMEM((2, 2) + piece, floats),
            pltpu.VMEM((2,) + piece, floats),
            pltpu.VMEM((2, 2) + piece, halves),
            pltpu.VMEM((count, 2) + piece, halves),
            pltpu.VMEM((2,) + piece, halves),
            pltpu.VMEM((count,) + piece, halves),
            pltpu.VMEM((2,) + piece, halves),
            pltpu.VMEM(attention.shape, halves),
            DMA,
            DMA((2,)),
            DMA,
            DMA((count,)),
            DMA((count,)),
            DMA((groups,)),
            DMA((groups,)),
            DMA((groups,)),
            DMA((groups,)),
            DMA((groups,)),
            DMA((count,)),
            DMA((count,)),
            DMA((count,)),
            DMA((count,)),
            DMA((count,)),
            DMA((count,)),
            DMA((groups,)),
            DMA((groups,)),
            DMA((9,)),
            DMA((9,)),
            DMA((3,)),
            DMA((3,)),
            DMA((3,)),
            DMA((3,)),
            DMA((count,)),
            DMA((count,)),
            DMA((count,)),
            DMA((count,)),
            DMA,
            DMA,
        ],
        compiler_params=params(4),
        name="conv_backward",
    )(
        images_all,
        kernels,
        bank,
        styles,
        inverse,
        grad,
        conv,
        attention,
        others,
        words,
        small,
        last,
    )


def prepare_kernel(
    styled_ref,
    label_ref,
    select_ref,
    modulation_ref,
    rgb_modulation_ref,
    images_ref,
    query_ref,
    key_ref,
    value_ref,
    out_ref,
    cross_query_ref,
    cross_out_ref,
    text_key_ref,
    text_value_ref,
    attention_ref,
    others_ref,
    style_ref,
    rgb_scale_ref,
    parts_ref,
):
    col = lax.axis_index("pix")
    count, rows, depth = parts_ref.shape
    width = attention_ref.shape[1] // 5
    short = text_key_ref.shape[0]
    mine = pl.ds(pl.multiple_of(col * width, width), width)
    for k, source in enumerate((query_ref, key_ref, value_ref)):
        attention_ref[:, k * width : (k + 1) * width] = source[:, mine]
    attention_ref[:, 3 * width :] = jnp.zeros((attention_ref.shape[0], 2 * width), halves)
    for k, source in enumerate((text_key_ref, text_value_ref)):
        attention_ref[0:short, (3 + k) * width : (4 + k) * width] = source[:, mine]
    for k, source in enumerate((out_ref, cross_query_ref, cross_out_ref)):
        others_ref[:, k * width : (k + 1) * width] = source[:, mine]
    styled = styled_ref[...]
    logits = jnp.sum(styled * select_ref[...], -1, keepdims=True)
    first, second = logits[0:1], logits[1:2]
    largest = jnp.maximum(first, second)
    first, second = jnp.exp(first - largest), jnp.exp(second - largest)
    total = first + second
    eight = jnp.broadcast_to(styled, (8, styled.shape[1]))

    def through(matrix):
        return exact(mul, eight, matrix[...]) + 1.0

    scaling = through(modulation_ref)
    rgb_scale_ref[...] = through(rgb_modulation_ref)[0:1]
    same = jnp.concatenate(
        [jnp.broadcast_to(first / total, (1, 128)), jnp.broadcast_to(second / total, (1, 128))]
        + [styled[:, k * 128 : (k + 1) * 128] for k in range(4)]
        + [label_ref[...]],
        axis=0,
    )
    for d in range(count):
        lanes = slice(d * depth, (d + 1) * depth)
        style_ref[d, 0:1, :] = jnp.zeros((1, 128), floats)
        style_ref[d, 0:1, 0:depth] = scaling[0:1, lanes]
        style_ref[d, 1:8, :] = same
        parts_ref[d] = images_ref[:, lanes]


def prepare(styled, label, select_rows, modulation, rgb_modulation, images, weights, count):
    rows, channels = images.shape
    owned, quarter = weights[0].shape[0], channels // PIX
    return pl.pallas_call(
        prepare_kernel,
        out_shape=(
            jax.ShapeDtypeStruct((owned, 5 * quarter), halves),
            jax.ShapeDtypeStruct((owned, 3 * quarter), halves),
            jax.ShapeDtypeStruct((count, 8, 128), floats),
            jax.ShapeDtypeStruct((1, channels), floats),
            jax.ShapeDtypeStruct((count, rows, channels // count), halves),
        ),
        in_specs=[VMEM] * 14,
        out_specs=(VMEM,) * 5,
        compiler_params=pltpu.CompilerParams(vmem_limit_bytes=VMEM_LIMIT),
        name="prepare",
    )(styled, label, select_rows, modulation, rgb_modulation, images, *weights)


def finish_kernel(
    rows_ref,
    stats_ref,
    styles_ref,
    select_ref,
    modulation_ref,
    rgb_modulation_ref,
    attention_ref,
    others_ref,
    words_ref,
    grad_one_ref,
    image_parts_ref,
    grad_query_ref,
    grad_key_ref,
    grad_value_ref,
    grad_out_ref,
    grad_cross_query_ref,
    grad_cross_out_ref,
    grad_text_key_ref,
    grad_text_value_ref,
    grad_image_ref,
    grad_style_ref,
    grad_table_ref,
    grad_select_ref,
    grad_modulation_ref,
    grad_rgb_ref,
    gain_self_ref,
    gain_cross_ref,
    rgb_weight_ref,
    scaling,
    styles_grad,
):
    row = lax.axis_index("dp")
    count, rows, depth = image_parts_ref.shape
    width = words_ref.shape[2] // 2
    for d in range(count):
        lanes = slice(d * depth, (d + 1) * depth)
        grad_image_ref[:, lanes] = grad_one_ref[:, lanes] + image_parts_ref[d].astype(floats)
        scaling[:, lanes] = stats_ref[d, :, 0, :][:, :depth]
    for k, out in enumerate((grad_query_ref, grad_key_ref, grad_value_ref)):
        for p in range(2 * PIX):
            first = 3 * width + k * 128 if p % 2 == 0 else k * 128
            source = others_ref if p % 2 == 0 else attention_ref
            out[:, p * 128 : (p + 1) * 128] = source[p // 2, :, first : first + 128].astype(floats)
    for buffer, outs in (
        (others_ref, (grad_out_ref, grad_cross_query_ref, grad_cross_out_ref)),
        (words_ref, (grad_text_key_ref, grad_text_value_ref)),
    ):
        for k, out in enumerate(outs):
            for p in range(PIX):
                block = buffer[p, :, k * width : (k + 1) * width].astype(floats)
                out[:, p * width : (p + 1) * width] = block[: out.shape[0]]
    sums = rows_ref[0]
    for d in range(1, count):
        sums = sums + rows_ref[d]
    gain_self_ref[...] = sums[5:6]
    gain_cross_ref[...] = sums[0:1]
    rgb_weight_ref[...] = sums[2:5]
    mixing, grads = [], []
    for k in (1, 2):
        total = stats_ref[0, :, k, :]
        for d in range(1, count):
            total = total + stats_ref[d, :, k, :]
        grads.append(jnp.sum(total, -1, keepdims=True))
        mixing.append(styles_ref[:, k, :][:, 0:1])
    inner = grads[0] * mixing[0] + grads[1] * mixing[1]
    logits = [m * (g - inner) for m, g in zip(mixing, grads)]
    styled = jnp.concatenate([styles_ref[:, 3 + k, :] for k in range(4)], axis=1)
    rgb = rows_ref[:, 1, :]
    grad_modulation_ref[...] = outer_sum(styled, scaling[...])
    grad_rgb_ref[...] = outer_sum(styled, rgb)
    place = lax.broadcasted_iota(jnp.int32, (count, 128), 1)
    both = jnp.where(place == 0, logits[0], jnp.where(place == 1, logits[1], 0.0))
    grad_select_ref[...] = outer_sum(both, styled)[0:2]
    grad_styles = (
        exact(mul_nt, scaling[...], modulation_ref[...])
        + exact(mul_nt, rgb, rgb_modulation_ref[...])
        + logits[0] * select_ref[0:1, :]
        + logits[1] * select_ref[1:2, :]
    )
    styles_grad[...] = grad_styles
    grad_style_ref[...] = styles_grad[pl.ds(row, 1), :]
    label = styles_ref[:, 7, :][:, 0:1].astype(jnp.int32)
    classes = grad_table_ref.shape[0]
    chosen = lax.broadcasted_iota(jnp.int32, (count, classes), 1) == label
    chosen = chosen.astype(floats).astype(halves)
    grad_table_ref[...] = mul_tn(
        jnp.concatenate([chosen] * 3, axis=0),
        jnp.concatenate(split(grad_styles)[::-1], axis=0),
    )


def finish(
    all_rows,
    all_stats,
    styles,
    select_rows,
    modulation,
    rgb_modulation,
    gathered,
    grad_one,
    image_parts,
    classes,
    text_rows,
):
    count = styles.shape[0]
    rows, channels = grad_one.shape
    owned = gathered[0].shape[1]
    wide = modulation.shape[0]

    def out(*shape):
        return jax.ShapeDtypeStruct(shape, floats)

    return pl.pallas_call(
        finish_kernel,
        out_shape=(out(owned, channels),) * 6
        + (out(text_rows, channels),) * 2
        + (
            out(rows, channels),
            out(1, wide),
            out(classes, wide),
            out(2, wide),
            out(wide, channels),
            out(wide, channels),
            out(1, channels),
            out(1, channels),
            out(3, channels),
        ),
        in_specs=[VMEM] * 11,
        out_specs=(VMEM,) * 17,
        scratch_shapes=[pltpu.VMEM((count, channels), floats), pltpu.VMEM((count, wide), floats)],
        compiler_params=pltpu.CompilerParams(vmem_limit_bytes=VMEM_LIMIT),
        name="finish",
    )(
        all_rows,
        all_stats,
        styles,
        select_rows,
        modulation,
        rgb_modulation,
        *gathered,
        grad_one,
        image_parts,
    )


def on_device(
    images,
    style_codes,
    labels,
    token_ids,
    penalty_mask,
    class_table,
    text_table,
    conv_bank,
    select_weight,
    modulation,
    rgb_modulation,
    w_query,
    w_key,
    w_value,
    w_out,
    c_query,
    c_key,
    c_value,
    c_out,
    gain_self,
    gain_cross,
    rgb_weight,
    out_cotangent,
    rgb_cotangent,
):
    count = lax.axis_size("dp")
    _, height, width, channels = images.shape
    rows = height * width
    quarter = channels // PIX
    depth = channels // count

    owned, text_owned = w_query.shape[0], c_key.shape[0]
    class_row = jnp.take(class_table, labels, axis=0).astype(floats)
    styled = style_codes.astype(floats) + class_row
    label = jnp.broadcast_to(labels.astype(floats).reshape(1, 1), (1, 128))
    select_rows = jnp.pad(select_weight.T, ((0, 6), (0, 0))).astype(floats)
    own = images.reshape(rows, channels)
    attention, others, style, rgb_scale, parts = prepare(
        styled,
        label,
        select_rows,
        modulation,
        rgb_modulation,
        own,
        (w_query, w_key, w_value, w_out, c_query, c_out, c_key, c_value),
        count,
    )
    attention = lax.all_gather(attention, "dp", axis=0, tiled=True)
    others = lax.all_gather(others, ("pix", "dp"), axis=0, tiled=True)
    others = others.reshape(PIX, channels, 3 * quarter)
    bank = conv_bank.reshape(2, 9, depth, quarter)
    bank_turned = bank.transpose(0, 1, 3, 2)
    words = token_ids.shape[1]
    text = jnp.take(text_table, token_ids[0], axis=0)
    text = text.reshape(words, count, text_owned)
    text = jnp.pad(text, ((0, 128 - words), (0, 0), (0, owned - text_owned)))
    text = text.reshape(128, channels)

    images_all, kernels, styles, inverse = gather_inputs(style, bank, parts)
    images_all = images_all.reshape(count, PIX * rows, depth)
    conv, conv_own, hidden_one, normed_one = conv_forward(images_all, kernels, own, gain_self, width)
    query, key, value, totals, attended, text_all = attend_forward(
        normed_one, attention, text
    )
    rgb_rows = jnp.pad(rgb_cotangent.reshape(3, rows).T, ((0, 0), (0, 125)))
    penalty = jnp.broadcast_to(penalty_mask.astype(floats).reshape(1, 1), (1, 128))
    (
        output,
        rgb,
        reduced,
        text_grads,
        grad_two,
        grad_attended,
        small,
        *factors,
    ) = cross_part(
        words,
        attended,
        hidden_one,
        others,
        text_all,
        gain_cross,
        rgb_scale,
        jnp.pad(rgb_weight, ((0, 0), (0, 125))),
        out_cotangent.reshape(rows, channels),
        rgb_rows,
        penalty,
    )
    attention_grads, others_owned, words_owned, grad_one, grad_conv, last = attend_backward(
        words,
        grad_attended,
        query,
        key,
        value,
        totals,
        normed_one,
        attention,
        hidden_one,
        conv,
        grad_two,
        gain_self,
        text,
        text_grads,
        reduced.reshape(count // 2, 2, owned, quarter),
        *factors,
    )

    bank_grad, *gathered, all_rows, all_stats, image_parts, _ = conv_backward(
        images_all,
        kernels,
        bank_turned,
        styles,
        inverse,
        grad_conv.reshape(PIX * rows, quarter),
        conv_own,
        (attention_grads, others_owned, words_owned),
        (small, last),
        width,
    )
    (
        grad_w_query,
        grad_w_key,
        grad_w_value,
        grad_w_out,
        grad_c_query,
        grad_c_out,
        grad_c_key,
        grad_c_value,
        grad_image,
        grad_style,
        grad_table,
        grad_select,
        grad_modulation,
        grad_rgb_modulation,
        grad_gain_self,
        grad_gain_cross,
        grad_rgb_weight,
    ) = finish(
        all_rows,
        all_stats,
        styles,
        select_rows,
        modulation,
        rgb_modulation,
        gathered,
        grad_one,
        image_parts,
        class_table.shape[0],
        text_owned,
    )
    shape = images.shape
    return (
        output.reshape(shape),
        rgb[:, :3].T.reshape(1, 3, height, width),
        grad_image.reshape(shape),
        grad_style,
        grad_table,
        bank_grad.reshape(conv_bank.shape),
        grad_select.T,
        grad_modulation,
        grad_rgb_modulation,
        grad_w_query,
        grad_w_key,
        grad_w_value,
        grad_w_out,
        grad_c_query,
        grad_c_key,
        grad_c_value,
        grad_c_out,
        grad_gain_self.reshape(-1),
        grad_gain_cross.reshape(-1),
        grad_rgb_weight.T,
    )


def solution(mesh):
    return jax.shard_map(
        on_device,
        mesh=mesh,
        in_specs=(
            P("dp", "pix", None, None),
            P("dp", None),
            P("dp"),
            P("dp", None),
            P("dp"),
            P(),
            P(),
            P(None, None, None, "dp", "pix"),
            P(),
            P(),
            P(),
            P("dp", None),
            P("dp", None),
            P("dp", None),
            P("dp", None),
            P("dp", None),
            P("dp", None),
            P("dp", None),
            P("dp", None),
            P(),
            P(),
            P(),
            P("dp", "pix", None, None),
            P("dp", None, "pix", None),
        ),
        out_specs=(
            P("dp", "pix", None, None),
            P("dp", None, "pix", None),
            P("dp", "pix", None, None),
            P("dp", None),
            P(),
            P(None, None, None, "dp", "pix"),
            P(),
            P(),
            P(),
            P("dp", None),
            P("dp", None),
            P("dp", None),
            P("dp", None),
            P("dp", None),
            P("dp", None),
            P("dp", None),
            P("dp", None),
            P(),
            P(),
            P(),
        ),
        check_vma=False,
    )
```

```python
from functools import partial

import jax
import jax.numpy as jnp
from jax import lax
from jax.experimental import pallas as pl
from jax.experimental.pallas import tpu as pltpu
from jax.sharding import PartitionSpec as P

HEAD_DIM = 64
PIX = 4
MESH = pl.DeviceIdType.MESH
VMEM_LIMIT = 60 * 1024 * 1024

penalty_weight = 1.0
highest = lax.Precision.HIGHEST
floats = jnp.float32
halves = jnp.bfloat16

ANY = pl.BlockSpec(memory_space=pl.ANY)
VMEM = pl.BlockSpec(memory_space=pltpu.VMEM)
DMA = pltpu.SemaphoreType.DMA


def params(collective_id):
    return pltpu.CompilerParams(
        collective_id=collective_id, has_side_effects=True, vmem_limit_bytes=VMEM_LIMIT
    )


def remote(src, dst, send_sem, recv_sem, where):
    return pltpu.make_async_remote_copy(
        src_ref=src,
        dst_ref=dst,
        send_sem=send_sem,
        recv_sem=recv_sem,
        device_id=where,
        device_id_type=MESH,
    )


def greet(count, others):
    row, col = lax.axis_index("dp"), lax.axis_index("pix")
    barrier = pltpu.get_barrier_semaphore()

    def one(step, carry):
        pl.semaphore_signal(
            barrier, inc=1, device_id=(lax.rem(row + step, count), col), device_id_type=MESH
        )
        return carry

    if count > 1:
        lax.fori_loop(1, count, one, 0)
    for other in others:
        pl.semaphore_signal(barrier, inc=1, device_id=other, device_id_type=MESH)
    pl.semaphore_wait(barrier, count - 1 + len(others))


def loop(count, body):
    def step(i, carry):
        body(i)
        return carry

    lax.fori_loop(0, count, step, 0)


def flip(index, bit):
    part = lax.rem(lax.div(index, bit), 2)
    return index + bit - 2 * bit * part


def level_at(level, groups, index):
    both = jnp.minimum(level, groups - 1 - level)
    step = lax.div(index + 1, 2)
    near = jnp.where(lax.rem(index, 2) == 1, level - step, level + step)
    rest = index - both
    far = jnp.where(level > groups - 1 - level, level - rest, level + rest)
    return jnp.where(index == 0, level, jnp.where(index <= 2 * both, near, far))


def gather_kernel(
    count,
    style_ref,
    bank_ref,
    parts_ref,
    images_ref,
    kernel_ref,
    styles_ref,
    inverse_ref,
    squares,
    squares_in,
    local_sem,
    style_send,
    style_recv,
    square_send,
    square_recv,
    part_send,
    part_recv,
    core_send,
    core_recv,
    line_send,
    line_recv,
    pass_send,
    pass_recv,
):
    row, col = lax.axis_index("dp"), lax.axis_index("pix")
    near, far = flip(col, 1), flip(col, 2)
    depth = bank_ref.shape[2]
    greet(count, [(row, near), (row, far)])

    def style_copy(step):
        other = lax.rem(row + step, count)
        return remote(
            style_ref.at[other], styles_ref.at[row], style_send.at[step], style_recv.at[step], (other, col)
        )

    def square_copy(step):
        other = lax.rem(row + step, count)
        return remote(
            squares, squares_in.at[row], square_send.at[step], square_recv.at[step], (other, col)
        )

    def part_copy(step):
        other = lax.rem(row + step, count)
        return remote(
            parts_ref.at[other], images_ref.at[row, col], part_send.at[step], part_recv.at[step], (other, col)
        )

    def part_arrives(step):
        origin = lax.rem(row - step + count, count)
        remote(
            parts_ref.at[0], images_ref.at[origin, col], part_send.at[step], part_recv.at[step], (row, near)
        ).wait_recv()

    def core_copy(step):
        origin = lax.rem(row - step + count, count)
        block = images_ref.at[origin, col]
        return remote(block, block, core_send.at[step], core_recv.at[step], (row, near))

    def line_copy(step):
        origin = lax.rem(row - step + count, count)
        block = images_ref.at[origin, col]
        return remote(block, block, line_send.at[step], line_recv.at[step], (row, far))

    def pass_copy(step):
        origin = lax.rem(row - step + count, count)
        block = images_ref.at[origin, far]
        return remote(block, block, pass_send.at[step], pass_recv.at[step], (row, near))

    def core_arrives(step):
        origin = lax.rem(row - step + count, count)
        block = images_ref.at[origin, near]
        remote(block, block, core_send.at[step], core_recv.at[step], (row, near)).wait_recv()

    def line_arrives(step):
        origin = lax.rem(row - step + count, count)
        block = images_ref.at[origin, far]
        remote(block, block, line_send.at[step], line_recv.at[step], (row, far)).wait_recv()

    def pass_arrives(step):
        origin = lax.rem(row - step + count, count)
        block = images_ref.at[origin, flip(near, 2)]
        remote(block, block, pass_send.at[step], pass_recv.at[step], (row, near)).wait_recv()

    own = pltpu.make_async_copy(parts_ref.at[row], images_ref.at[row, col], local_sem)
    own.start()

    def send_all(step):
        style_copy(step).start()

    lax.fori_loop(1, count, lambda i, c: (send_all(i), c)[1], 0)
    lax.fori_loop(1, count, lambda i, c: (part_copy(i).start(), c)[1], 0)
    styles_ref[row] = style_ref[row]
    own.wait()
    line_copy(0).start()
    core_copy(0).start()

    def style_wait(step):
        origin = lax.rem(row - step + count, count)
        remote(
            style_ref.at[0], styles_ref.at[origin], style_send.at[step], style_recv.at[step], (row, near)
        ).wait_recv()

    lax.fori_loop(1, count, lambda i, c: (style_wait(i), c)[1], 0)

    def mixed_tap(sample, tap, column, first, second):
        total = first * bank_ref[0, tap].astype(floats) + second * bank_ref[1, tap].astype(floats)
        return total * column

    def factors(sample):
        block = styles_ref[sample]
        column = jnp.transpose(block)[:depth, 0:1]
        return column, block[1:2, 0:1], block[2:3, 0:1]

    def square_sum(sample):
        column, first, second = factors(sample)
        total = jnp.zeros((depth, bank_ref.shape[3]), floats)
        for tap in range(9):
            modded = mixed_tap(sample, tap, column, first, second)
            total = total + modded * modded
        squares[pl.ds(sample, 1), :] = jnp.sum(total, axis=0, keepdims=True)

    loop(count, square_sum)
    lax.fori_loop(1, count, lambda i, c: (square_copy(i).start(), c)[1], 0)
    squares_in[row] = squares[...]

    def relay(step):
        part_arrives(step)
        line_copy(step).start()
        core_copy(step).start()

    lax.fori_loop(1, count, lambda i, c: (relay(i), c)[1], 0)

    def square_wait(step):
        origin = lax.rem(row - step + count, count)
        remote(
            squares, squares_in.at[origin], square_send.at[step], square_recv.at[step], (row, near)
        ).wait_recv()

    lax.fori_loop(1, count, lambda i, c: (square_wait(i), c)[1], 0)
    inverse_ref[...] = lax.rsqrt(jnp.sum(squares_in[...], axis=0) + 1e-08)

    def forward(step):
        line_arrives(step)
        pass_copy(step).start()

    def make_kernel(sample):
        column, first, second = factors(sample)
        scale = inverse_ref[pl.ds(sample, 1), :]
        for tap in range(9):
            modded = mixed_tap(sample, tap, column, first, second)
            kernel_ref[sample, tap] = (modded * scale).astype(halves)
        forward(sample)

    loop(count, make_kernel)
    loop(count, core_arrives)
    loop(count, pass_arrives)
    lax.fori_loop(
        1,
        count,
        lambda i, c: (
            style_copy(i).wait_send(),
            square_copy(i).wait_send(),
            part_copy(i).wait_send(),
            c,
        )[3],
        0,
    )
    loop(count, lambda i: core_copy(i).wait_send())
    loop(count, lambda i: line_copy(i).wait_send())
    loop(count, lambda i: pass_copy(i).wait_send())


def gather_inputs(style_rows, bank, parts):
    count, rows, depth = parts.shape
    width = bank.shape[-1]
    sems = [DMA((count,)) for _ in range(12)]
    return pl.pallas_call(
        partial(gather_kernel, count),
        out_shape=(
            jax.ShapeDtypeStruct((count, PIX, rows, depth), halves),
            jax.ShapeDtypeStruct((count, 9, depth, width), halves),
            jax.ShapeDtypeStruct((count, 8, 128), floats),
            jax.ShapeDtypeStruct((count, width), floats),
        ),
        in_specs=[VMEM, VMEM, ANY],
        out_specs=(ANY, VMEM, VMEM, VMEM),
        scratch_shapes=[
            pltpu.VMEM((count, width), floats),
            pltpu.VMEM((count, count, width), floats),
            DMA,
        ]
        + sems,
        compiler_params=params(0),
        name="gather_inputs",
    )(style_rows, bank, parts)


def conv_kernel(
    count,
    width,
    images_ref,
    kernel_ref,
    own_ref,
    gain_ref,
    conv_ref,
    conv_own_ref,
    hidden_ref,
    normed_ref,
    image_buf,
    padded,
    total,
    pair_out,
    pair_in,
    line_out,
    line_in,
    block_out,
    block_in,
    image_sem,
    pair_send,
    pair_recv,
    line_send,
    line_recv,
    block_send,
    block_recv,
    norm_send,
    norm_recv,
):
    row, col = lax.axis_index("dp"), lax.axis_index("pix")
    groups = count // 2
    slots = pair_out.shape[0]
    side = lax.rem(row, 2)
    level = lax.div(row, 2)
    partner = flip(row, 1)
    near, far = flip(col, 1), flip(col, 2)
    cross = flip(near, 2)
    tokens, depth = image_buf.shape[1], image_buf.shape[2]
    channels = total.shape[1]
    rows = tokens // PIX
    halo = width

    has_below, has_above = level > 0, level < groups - 1
    below, above = jnp.maximum(row - 2, 0), jnp.minimum(row + 2, count - 1)

    barrier = pltpu.get_barrier_semaphore()
    for known, other in ((has_below, below), (has_above, above)):

        @pl.when(known)
        def _(other=other):
            pl.semaphore_signal(barrier, inc=1, device_id=(other, col), device_id_type=MESH)

    for other in ((partner, col), (row, near), (row, far), (row, cross)):
        pl.semaphore_signal(barrier, inc=1, device_id=other, device_id_type=MESH)
    pl.semaphore_wait(barrier, 4 + has_below.astype(jnp.int32) + has_above.astype(jnp.int32))

    def group_of(step):
        return level_at(level, groups, groups - 1 - step)

    def sample_of(index):
        mine = lax.div(index, groups)
        group = group_of(lax.rem(index, groups))
        return 2 * group + jnp.where(mine == 1, side, 1 - side)

    def fetch(index):
        slot = lax.rem(index, 2)
        return pltpu.make_async_copy(
            images_ref.at[sample_of(index)], image_buf.at[slot], image_sem.at[slot]
        )

    zeros = jnp.zeros((3, halo, depth), halves)
    padded[:, 0:halo, :] = zeros
    padded[:, halo + tokens : halo + tokens + halo, :] = zeros
    fetch(0).start()
    place = lax.rem(lax.broadcasted_iota(jnp.int32, (tokens, depth), 0), width)

    def stage(index):
        fetch(index).wait()

        @pl.when(index + 1 < count)
        def _():
            fetch(index + 1).start()

        source = image_buf[lax.rem(index, 2)]
        wide = source.astype(floats)
        padded[1, halo : halo + tokens, :] = source
        before = jnp.where(place == 0, 0.0, pltpu.roll(wide, 1, 0))
        padded[0, halo : halo + tokens, :] = before.astype(halves)
        after = jnp.where(place == width - 1, 0.0, pltpu.roll(wide, tokens - 1, 0))
        padded[2, halo : halo + tokens, :] = after.astype(halves)

    def rows_of(sample, start):
        acc = jnp.zeros((rows, channels), floats)
        for a in range(3):
            for b in range(3):
                window = padded[b, pl.ds(pl.multiple_of(start + a * width, 16), rows), :]
                acc = acc + jnp.dot(
                    window, kernel_ref[sample, 3 * a + b], preferred_element_type=floats
                )
        return acc

    half = tokens // 2
    per_half = PIX // 2

    def half_of(h):
        return pl.ds(h * half, half)

    def pair_copy(step, h):
        return remote(
            pair_out.at[lax.rem(step, slots), half_of(h)],
            pair_in.at[step, half_of(h)],
            pair_send.at[step, h],
            pair_recv.at[step, h],
            (partner, col),
        )

    def line_copy(step, upward, h):
        group = group_of(step)
        if upward:
            slot, target = group, above
        else:
            slot, target = jnp.where(group == level - 1, groups, group), below
        return remote(
            line_out.at[lax.rem(step, slots), half_of(h)],
            line_in.at[slot, half_of(h)],
            line_send.at[step, h],
            line_recv.at[slot, h],
            (target, col),
        )

    def line_arrives(slot, h):
        remote(
            line_out.at[0, half_of(h)],
            line_in.at[slot, half_of(h)],
            line_send.at[0, h],
            line_recv.at[slot, h],
            (partner, col),
        ).wait_recv()

    def give(step):
        @pl.when(step >= slots)
        def _():
            for h in range(2):
                pair_copy(step - slots, h).wait_send()

        stage(step)
        sample = sample_of(step)
        for h in range(2):

            def chunk(i, h=h):
                start = pl.multiple_of(h * half + i * rows, rows)
                pair_out[lax.rem(step, slots), pl.ds(start, rows), :] = rows_of(
                    sample, start
                ).astype(halves)

            loop(per_half, chunk)
            pair_copy(step, h).start()

    loop(groups, give)

    def keep(step):
        @pl.when(step >= slots)
        def _():
            for h in range(2):
                line_copy(step - slots, True, h).wait_send()

        stage(groups + step)
        group = group_of(step)
        sample = 2 * group + side
        out = lax.rem(step, slots)

        def chunk(i):
            start = pl.multiple_of(i * rows, rows)
            total[pl.ds(start, rows), :] = rows_of(sample, start)

        loop(PIX, chunk)
        passing = jnp.where(group > level, has_below, has_above)
        for h in range(2):
            pair_copy(step, h).wait_recv()

            @pl.when(passing)
            def _(h=h):
                line_arrives(group, h)

                def add(i):
                    here = pl.ds(pl.multiple_of(h * half + i * rows, rows), rows)
                    line_out[out, here, :] = (
                        total[here, :]
                        + pair_in[step, here, :].astype(floats)
                        + line_in[group, here, :].astype(floats)
                    ).astype(halves)

                loop(per_half, add)

            @pl.when(jnp.logical_not(passing))
            def _(h=h):
                def add(i):
                    here = pl.ds(pl.multiple_of(h * half + i * rows, rows), rows)
                    line_out[out, here, :] = (
                        total[here, :] + pair_in[step, here, :].astype(floats)
                    ).astype(halves)

                loop(per_half, add)

            @pl.when(group > level)
            def _(h=h):
                line_copy(step, True, h).start()

            @pl.when(group < level)
            def _(h=h):
                line_copy(step, False, h).start()

    loop(groups - 1, keep)
    last = groups - 1
    stage(count - 1)

    def own_chunk(i):
        start = pl.multiple_of(i * rows, rows)
        total[pl.ds(start, rows), :] = rows_of(row, start)

    loop(PIX, own_chunk)
    for h in range(2):
        for known, slot in ((has_below, level), (has_above, groups)):

            @pl.when(known)
            def _(slot=slot, h=h):
                line_arrives(slot, h)

                def add(i):
                    here = pl.ds(pl.multiple_of(h * half + i * rows, rows), rows)
                    total[here, :] += line_in[slot, here, :].astype(floats)

                loop(per_half, add)

        pair_copy(last, h).wait_recv()

    short = rows // 2
    part = rows // 4

    def block_copy(turn, i, origin=None):
        here = pl.ds(i * short, short)
        return remote(
            block_out.at[turn, here],
            block_in.at[col if origin is None else origin, here],
            block_send.at[2 * turn + i],
            block_recv.at[2 * turn + i],
            (row, (far, cross, near)[turn]),
        )

    for i in range(2):
        for turn, target in enumerate((far, cross, near, col)):
            here = pl.ds(pl.multiple_of(target * rows + i * short, short), short)
            rounded = (total[here, :] + pair_in[last, here, :].astype(floats)).astype(halves)
            conv_own_ref[here, :] = rounded
            if turn < 3:
                block_out[turn, i * short : (i + 1) * short, :] = rounded
                block_copy(turn, i).start()
            else:
                block_in[col, i * short : (i + 1) * short, :] = rounded

    def norm_rows(i):
        here = pl.ds(pl.multiple_of(i * part, part), part)
        for j in range(PIX):
            conv_ref[here, j * channels : (j + 1) * channels] = block_in[j, here, :]
        conv = conv_ref[here, :].astype(floats)
        hidden = own_ref[here, :].astype(floats) + conv * jax.nn.sigmoid(conv)
        hidden_ref[here, :] = hidden
        mean = jnp.mean(hidden * hidden, -1, keepdims=True)
        normed_ref[col, here, :] = (hidden * lax.rsqrt(mean + 1e-06) * gain_ref[...]).astype(halves)

    def norm_copy(hop, i, block):
        source = normed_ref.at[block, pl.ds(i * short, short)]
        index = 2 * hop + i
        return remote(
            source, source, norm_send.at[index], norm_recv.at[index], (row, far if hop == 0 else near)
        )

    for i in range(2):
        for turn, origin in enumerate((far, cross, near)):
            block_copy(turn, i, origin).wait_recv()
        norm_rows(2 * i)
        norm_rows(2 * i + 1)
        norm_copy(0, i, col).start()
        norm_copy(1, i, col).start()
    for i in range(2):
        norm_copy(0, i, far).wait_recv()
        norm_copy(2, i, far).start()
    for i in range(2):
        norm_copy(1, i, near).wait_recv()
        norm_copy(2, i, cross).wait_recv()
        for hop, block in enumerate((col, col, far)):
            norm_copy(hop, i, block).wait_send()
        for turn in range(3):
            block_copy(turn, i).wait_send()
        for step in range(max(0, groups - slots), groups):
            pair_copy(step, i).wait_send()
        for step in range(max(0, groups - 1 - slots), groups - 1):
            line_copy(step, True, i).wait_send()


def conv_forward(images_all, kernels, own, gain, width):
    count, tokens, depth = images_all.shape
    channels = kernels.shape[-1]
    rows, full = own.shape
    groups = count // 2
    slots = min(groups, 4)
    block = (tokens, channels)
    return pl.pallas_call(
        partial(conv_kernel, count, width),
        out_shape=(
            jax.ShapeDtypeStruct((rows, full), halves),
            jax.ShapeDtypeStruct((tokens, channels), halves),
            jax.ShapeDtypeStruct((rows, full), floats),
            jax.ShapeDtypeStruct((PIX, rows, full), halves),
        ),
        in_specs=[ANY, VMEM, VMEM, VMEM],
        out_specs=(VMEM, VMEM, VMEM, VMEM),
        scratch_shapes=[
            pltpu.VMEM((2, tokens, depth), halves),
            pltpu.VMEM((3, tokens + 2 * width, depth), halves),
            pltpu.VMEM(block, floats),
            pltpu.VMEM((slots,) + block, halves),
            pltpu.VMEM((groups,) + block, halves),
            pltpu.VMEM((slots,) + block, halves),
            pltpu.VMEM((groups + 1,) + block, halves),
            pltpu.VMEM((3, rows, channels), halves),
            pltpu.VMEM((PIX, rows, channels), halves),
            DMA((2,)),
            DMA((groups, 2)),
            DMA((groups, 2)),
            DMA((groups, 2)),
            DMA((groups + 1, 2)),
            DMA((6,)),
            DMA((6,)),
            DMA((6,)),
            DMA((6,)),
        ],
        compiler_params=params(1),
        name="conv_forward",
    )(images_all, kernels, own, gain.reshape(1, -1))


def peers(col):
    near, far = flip(col, 1), flip(col, 2)
    return near, far, flip(near, 2)


def greet_pixels(row, others):
    barrier = pltpu.get_barrier_semaphore()
    for other in others:
        pl.semaphore_signal(barrier, inc=1, device_id=(row, other), device_id_type=MESH)
    pl.semaphore_wait(barrier, len(others))


NT = (((1,), (1,)), ((), ()))
TN = (((0,), (0,)), ((), ()))


def mul_nt(a, b, precision=None):
    return lax.dot_general(a, b, NT, preferred_element_type=floats, precision=precision)


def mul_tn(a, b, precision=None):
    return lax.dot_general(a, b, TN, preferred_element_type=floats, precision=precision)


def mul(a, b):
    return jnp.dot(a, b, preferred_element_type=floats)


def split(value):
    high = value.astype(halves)
    rest = value - high.astype(floats)
    middle = rest.astype(halves)
    return high, middle, (rest - middle.astype(floats)).astype(halves)


def exact(product, left, right):
    count = left.shape[0]
    found = product(jnp.concatenate(split(left), axis=0), right)
    return found[2 * count :] + found[count : 2 * count] + found[:count]


def outer_sum(left, right):
    lefts, rights = split(left), split(right)
    pairs = ((0, 2), (2, 0), (1, 1), (0, 1), (1, 0), (0, 0))
    return mul_tn(
        jnp.concatenate([lefts[i] for i, _ in pairs], axis=0),
        jnp.concatenate([rights[j] for _, j in pairs], axis=0),
    )


def attend_kernel(
    normed_ref,
    weight_ref,
    text_ref,
    query_ref,
    key_ref,
    value_ref,
    total_ref,
    attended_ref,
    text_out_ref,
    block_out,
    key_norm,
    block_send,
    block_recv,
    text_send,
    text_recv,
):
    row, col = lax.axis_index("dp"), lax.axis_index("pix")
    near, far, cross = peers(col)
    targets = (far, cross, near)
    greet_pixels(row, targets)
    rows = normed_ref.shape[1]
    width = query_ref.shape[1]
    heads = width // HEAD_DIM
    score_scale = HEAD_DIM ** (-0.5)

    for j in range(2):
        here = slice(j * width, (j + 1) * width)
        weight = weight_ref[:, (3 + j) * width : (4 + j) * width]
        text_out_ref[col, :, here] = mul(text_ref[...], weight).astype(halves)

    def text_copy(turn):
        block = text_out_ref.at[col]
        return remote(block, block, text_send.at[turn], text_recv.at[turn], (row, targets[turn]))

    for turn in range(3):
        text_copy(turn).start()

    def project(i):
        source = normed_ref[i]
        here = pl.ds(pl.multiple_of(i * rows, rows), rows)
        for j, out in enumerate((query_ref, key_ref, value_ref)):
            out[here, :] = mul(source, weight_ref[:, j * width : (j + 1) * width]).astype(halves)

    loop(PIX, project)
    ones = jnp.ones((8, HEAD_DIM), floats)
    for h in range(heads):
        key = key_ref[:, h * HEAD_DIM : (h + 1) * HEAD_DIM].astype(floats)
        key_norm[h] = mul_nt(ones, key * key, highest)

    def attend(target, store):
        here = pl.ds(pl.multiple_of(target * rows, rows), rows)
        for h in range(heads):
            lanes = slice(h * HEAD_DIM, (h + 1) * HEAD_DIM)
            inner = mul_nt(query_ref[here, lanes], key_ref[:, lanes])
            scores = score_scale * (2.0 * inner - key_norm[h, 0:1, :])
            largest = jnp.max(scores, -1, keepdims=True)
            expanded = jnp.exp(scores - largest)
            summed = jnp.sum(expanded, -1, keepdims=True)
            weights = (expanded * (1.0 / summed)).astype(halves)
            store(lanes, mul(weights, value_ref[:, lanes]).astype(halves))
            total_ref[here, h : h + 1] = largest + jnp.log(summed)

    def block_copy(turn):
        return remote(
            block_out.at[turn],
            attended_ref.at[col],
            block_send.at[turn],
            block_recv.at[turn],
            (row, targets[turn]),
        )

    def turn_body(turn):
        target = jnp.where(turn == 0, far, jnp.where(turn == 1, cross, jnp.where(turn == 2, near, col)))

        def store(lanes, result):
            block_out[turn, :, lanes] = result

        attend(target, store)
        for k in range(3):

            @pl.when(turn == k)
            def _(k=k):
                block_copy(k).start()

    loop(4, turn_body)
    attended_ref[col] = block_out[3]
    for turn in range(3):
        remote(
            block_out.at[turn],
            attended_ref.at[targets[turn]],
            block_send.at[turn],
            block_recv.at[turn],
            (row, near),
        ).wait_recv()
        block = text_out_ref.at[targets[turn]]
        remote(block, block, text_send.at[turn], text_recv.at[turn], (row, near)).wait_recv()
    for turn in range(3):
        block_copy(turn).wait_send()
        text_copy(turn).wait_send()


def attend_forward(normed, weights, text):
    count, rows, full = normed.shape
    tokens, width = count * rows, weights.shape[1] // 5
    heads = width // HEAD_DIM
    flat = jax.ShapeDtypeStruct((tokens, width), halves)
    return pl.pallas_call(
        attend_kernel,
        out_shape=(
            flat,
            flat,
            flat,
            jax.ShapeDtypeStruct((tokens, 128), floats),
            jax.ShapeDtypeStruct((PIX, rows, width), halves),
            jax.ShapeDtypeStruct((PIX, text.shape[0], 2 * width), halves),
        ),
        in_specs=[VMEM] * 3,
        out_specs=(VMEM,) * 6,
        scratch_shapes=[
            pltpu.VMEM((4, rows, width), halves),
            pltpu.VMEM((heads, 8, tokens), floats),
            DMA((3,)),
            DMA((3,)),
            DMA((3,)),
            DMA((3,)),
        ],
        compiler_params=params(2),
        name="attend_forward",
    )(normed, weights, text)


def cross_kernel(
    words,
    attended_ref,
    hidden_ref,
    weight_ref,
    text_ref,
    gain_ref,
    rgb_scale_ref,
    rgb_weight_ref,
    cotangent_ref,
    rgb_cotangent_ref,
    penalty_ref,
    output_ref,
    rgb_ref,
    reduced_ref,
    text_grad_ref,
    grad_two_ref,
    grad_attended_ref,
    small_ref,
    attended,
    grad_attn,
    normed,
    grad_query,
    two,
    query,
    probs,
    crossed,
    mixed,
    grad_three,
    grad_proj,
    grad_crossed,
    grad_norm,
    near_out,
    near_in,
    kept,
    line_out,
    line_in,
    near_send,
    near_recv,
    line_send,
    line_recv,
):
    row, col = lax.axis_index("dp"), lax.axis_index("pix")
    near, far, cross = peers(col)
    greet_pixels(row, (near, far))
    rows, full = hidden_ref.shape
    tile = full // PIX
    score_scale = HEAD_DIM ** (-0.5)
    W_OUT, C_QUERY, C_OUT = (slice(i * tile, (i + 1) * tile) for i in range(3))
    part = 64

    def cols(j):
        return pl.ds(pl.multiple_of(j * tile, tile), tile)

    def near_copy(which):
        return remote(
            near_out.at[which], near_in.at[which], near_send.at[which], near_recv.at[which], (row, near)
        )

    def line_copy(which):
        return remote(
            line_out.at[which], line_in.at[which], line_send.at[which], line_recv.at[which], (row, far)
        )

    def start_grad(which, left, right):
        def tile_of(index, targets):
            i, b = lax.div(index, 2), lax.rem(index, 2)
            return i, b, mul_tn(left[:, cols(i)], right[:, cols(jnp.where(b == 0, *targets))])

        def give(index):
            i, b, value = tile_of(index, (near, cross))
            near_out[which, b, cols(i), :] = value.astype(halves)

        def keep(index):
            i, b, value = tile_of(index, (col, far))
            kept[which, b, cols(i), :] = value

        loop(2 * PIX, give)
        near_copy(which).start()
        loop(2 * PIX, keep)

    def pass_grad(which):
        near_copy(which).wait_recv()

        def add(i):
            here = cols(i)
            line_out[which, here, :] = (
                kept[which, 1, here, :] + near_in[which, 1, here, :].astype(floats)
            ).astype(halves)

        loop(PIX, add)
        line_copy(which).start()

    def end_grad(which):
        line_copy(which).wait_recv()

        def add(i):
            here = cols(i)
            reduced_ref[here, which * tile : (which + 1) * tile] = (
                kept[which, 0, here, :]
                + near_in[which, 0, here, :].astype(floats)
                + line_in[which, here, :].astype(floats)
            ).astype(halves)

        loop(PIX, add)
        near_copy(which).wait_send()
        line_copy(which).wait_send()

    for j in range(PIX):
        attended[:, j * tile : (j + 1) * tile] = attended_ref[j]

    def out_two(j):
        two[:, cols(j)] = hidden_ref[:, cols(j)] + mul(attended[...], weight_ref[j, :, W_OUT])

    loop(PIX, out_two)

    def norm_two(i):
        here = pl.ds(pl.multiple_of(i * part, part), part)
        hidden = two[here, :]
        mean = jnp.mean(hidden * hidden, -1, keepdims=True)
        normed[here, :] = (hidden * lax.rsqrt(mean + 1e-06) * gain_ref[...]).astype(halves)

    loop(rows // part, norm_two)

    def out_query(j):
        query[:, cols(j)] = mul(normed[...], weight_ref[j, :, C_QUERY]).astype(halves)

    loop(PIX, out_query)
    slots = text_ref.shape[1]
    known = lax.broadcasted_iota(jnp.int32, (rows, slots), 1) < words
    pairs = tile // 128

    def text_lanes(pair, side):
        return pl.ds(pl.multiple_of(side * tile + lax.rem(pair, pairs) * 128, 128), 128)

    def cross_pair(pair):
        here = pl.ds(pl.multiple_of(pair * 128, 128), 128)
        group = lax.div(pair, pairs)
        queries = query[:, here]
        keys = text_ref[group, :, text_lanes(pair, 0)]
        values = text_ref[group, :, text_lanes(pair, 1)]
        outs = []
        for h in range(2):
            lanes = slice(h * HEAD_DIM, (h + 1) * HEAD_DIM)
            scores = score_scale * mul_nt(queries[:, lanes], keys[:, lanes])
            scores = jnp.where(known, scores, -1e30)
            expanded = jnp.exp(scores - jnp.max(scores, -1, keepdims=True))
            prob = expanded / jnp.sum(expanded, -1, keepdims=True)
            probs[2 * pair + h] = prob
            outs.append(mul(prob.astype(halves), values[:, lanes]))
        crossed[:, here] = jnp.concatenate(outs, axis=1).astype(halves)

    def cross_four(i):
        cross_pair(2 * i)
        cross_pair(2 * i + 1)

    loop(full // 256, cross_four)
    rgb_ref[...] = jnp.zeros_like(rgb_ref)

    def out_three(j):
        three = two[:, cols(j)] + mul(crossed[...], weight_ref[j, :, C_OUT])
        output_ref[:, cols(j)] = three
        blend = (three * rgb_scale_ref[:, cols(j)]).astype(halves)
        mixed[:, cols(j)] = blend
        rgb_ref[...] += mul(blend, rgb_weight_ref[cols(j), :])

    loop(PIX, out_three)
    rgb_grad = rgb_cotangent_ref[...] + penalty_weight * penalty_ref[...] * rgb_ref[...]

    def back_three(j):
        color = mul_tn(rgb_grad, mixed[:, cols(j)].astype(floats), highest)
        small_ref[2:5, cols(j)] = color[0:3]
        grad_mixed = mul_nt(rgb_grad, rgb_weight_ref[cols(j), :].astype(floats), highest)
        small_ref[1:2, cols(j)] = jnp.sum(grad_mixed * output_ref[:, cols(j)], 0, keepdims=True)
        grad = cotangent_ref[:, cols(j)].astype(floats) + grad_mixed * rgb_scale_ref[:, cols(j)]
        grad_three[:, cols(j)] = grad
        grad_proj[:, cols(j)] = grad.astype(halves)

    loop(PIX, back_three)
    start_grad(0, crossed, grad_proj)

    def times_transposed(source, j, which):
        acc = jnp.zeros((rows, tile), floats)
        for i in range(PIX):
            acc = acc + mul_nt(source[:, i * tile : (i + 1) * tile], weight_ref[i, cols(j), which])
        return acc

    def back_crossed(j):
        grad_crossed[:, cols(j)] = times_transposed(grad_proj, j, C_OUT).astype(halves)

    loop(PIX, back_crossed)

    def back_pair(pair):
        here = pl.ds(pl.multiple_of(pair * 128, 128), 128)
        group = lax.div(pair, pairs)
        queries, grads = query[:, here], grad_crossed[:, here]
        keys = text_ref[group, :, text_lanes(pair, 0)]
        values = text_ref[group, :, text_lanes(pair, 1)]
        grad_q, grad_k, grad_v = [], [], []
        for h in range(2):
            lanes = slice(h * HEAD_DIM, (h + 1) * HEAD_DIM)
            prob = probs[2 * pair + h]
            grad = grads[:, lanes]
            grad_prob = mul_nt(grad, values[:, lanes])
            grad_v.append(mul_tn(prob.astype(halves), grad))
            inner = jnp.sum(grad_prob * prob, -1, keepdims=True)
            score = (prob * (grad_prob - inner)).astype(halves)
            grad_q.append(score_scale * mul(score, keys[:, lanes]))
            grad_k.append(score_scale * mul_tn(score, queries[:, lanes]))
        grad_query[:, here] = jnp.concatenate(grad_q, axis=1).astype(halves)
        text_grad_ref[group, :, text_lanes(pair, 0)] = jnp.concatenate(grad_k, axis=1).astype(halves)
        text_grad_ref[group, :, text_lanes(pair, 1)] = jnp.concatenate(grad_v, axis=1).astype(halves)

    def back_four(i):
        back_pair(2 * i)
        back_pair(2 * i + 1)

    loop(full // 256, back_four)
    pass_grad(0)

    def back_query(j):
        grad_norm[:, cols(j)] = times_transposed(grad_query, j, C_QUERY)

    loop(PIX, back_query)
    small_ref[0:1, :] = jnp.zeros((1, full), floats)

    def back_norm(i):
        here = pl.ds(pl.multiple_of(i * part, part), part)
        hidden, grad = two[here, :], grad_norm[here, :]
        inverse = lax.rsqrt(jnp.mean(hidden * hidden, -1, keepdims=True) + 1e-06)
        small_ref[0:1, :] += jnp.sum(grad * hidden * inverse, 0, keepdims=True)
        scaled = grad * gain_ref[...]
        mean = jnp.mean(scaled * hidden, -1, keepdims=True)
        total = grad_three[here, :] + inverse * scaled - hidden * (inverse * inverse * inverse * mean)
        grad_two_ref[here, :] = total
        grad_attn[here, :] = total.astype(halves)

    loop(rows // part, back_norm)

    def back_attended(j):
        grad_attended_ref[j] = times_transposed(grad_attn, j, W_OUT).astype(halves)

    loop(PIX, back_attended)

    small_ref[5:8, :] = jnp.zeros((3, full), floats)
    end_grad(0)


def cross_part(
    words, attended, hidden, weights, text, gain, rgb_scale, rgb_weight, cotangent, rgb_cotangent, penalty
):
    rows, full = hidden.shape
    tile = full // PIX
    heads = full // HEAD_DIM
    wide = pltpu.VMEM((rows, full), floats)
    slim = pltpu.VMEM((rows, full), halves)
    return pl.pallas_call(
        partial(cross_kernel, words),
        out_shape=(
            jax.ShapeDtypeStruct((rows, full), floats),
            jax.ShapeDtypeStruct((rows, 128), floats),
            jax.ShapeDtypeStruct((full, tile), halves),
            jax.ShapeDtypeStruct(text.shape, halves),
            jax.ShapeDtypeStruct((rows, full), floats),
            jax.ShapeDtypeStruct((PIX, rows, tile), halves),
            jax.ShapeDtypeStruct((8, full), floats),
        )
        + (jax.ShapeDtypeStruct((rows, full), halves),) * 4,
        in_specs=[VMEM] * 10,
        out_specs=(VMEM,) * 11,
        scratch_shapes=[
            wide,
            slim,
            pltpu.VMEM((heads, rows, text.shape[1]), floats),
            slim,
            slim,
            wide,
            slim,
            slim,
            wide,
            pltpu.VMEM((1, 2, full, tile), halves),
            pltpu.VMEM((1, 2, full, tile), halves),
            pltpu.VMEM((1, 2, full, tile), floats),
            pltpu.VMEM((1, full, tile), halves),
            pltpu.VMEM((1, full, tile), halves),
            DMA((1,)),
            DMA((1,)),
            DMA((1,)),
            DMA((1,)),
        ],
        compiler_params=params(6),
        name="cross_part",
    )(
        attended,
        hidden,
        weights,
        text,
        gain.reshape(1, -1),
        rgb_scale,
        rgb_weight,
        cotangent,
        rgb_cotangent,
        penalty,
    )


def group_copy(turn, source, landed, send, recv):
    row, col = lax.axis_index("dp"), lax.axis_index("pix")
    near, far, cross = peers(col)
    target = (far, cross, near)[turn]
    return remote(source, landed.at[turn], send.at[turn], recv.at[turn], (row, target))


def group_sum(source, landed, send, recv):
    col = lax.axis_index("pix")
    _, far, cross = peers(col)
    for turn in range(3):
        group_copy(turn, source, landed, send, recv).wait()
    landed[3] = source[...]
    total = None
    for which in range(PIX):
        turn = jnp.where(
            which == col, 3, jnp.where(which == far, 0, jnp.where(which == cross, 1, 2))
        )
        total = landed[turn] if total is None else total + landed[turn]
    return total


def far_copy_of(k, total, everyone, send, recv):
    row, col = lax.axis_index("dp"), lax.axis_index("pix")
    other = lax.rem(row + k, everyone.shape[0])
    return remote(total, everyone.at[row], send.at[k], recv.at[k], (other, col))


def far_start(total, everyone, send, recv, sem):
    row, count = lax.axis_index("dp"), everyone.shape[0]
    pltpu.make_async_copy(total, everyone.at[row], sem).start()
    lax.fori_loop(
        1, count, lambda k, c: (far_copy_of(k, total, everyone, send, recv).start(), c)[1], 0
    )


def far_end(total, everyone, send, recv, sem):
    row, col = lax.axis_index("dp"), lax.axis_index("pix")
    count = everyone.shape[0]
    pltpu.make_async_copy(total, everyone.at[row], sem).wait()

    def arrive(k, carry):
        origin = lax.rem(row - k + count, count)
        remote(
            total, everyone.at[origin], send.at[k], recv.at[k], (row, flip(col, 1))
        ).wait_recv()
        return carry

    lax.fori_loop(1, count, arrive, 0)
    lax.fori_loop(
        1, count, lambda k, c: (far_copy_of(k, total, everyone, send, recv).wait_send(), c)[1], 0
    )


def attend_back_kernel(
    grad_ref,
    query_ref,
    key_ref,
    value_ref,
    total_ref,
    normed_from,
    weight_from,
    hidden_from,
    conv_from,
    grad_two_from,
    gain_ref,
    text_ref,
    text_grad_ref,
    reduced_ref,
    attended_ref,
    grad_attn_ref,
    normed_two_ref,
    grad_cross_ref,
    rows_ref,
    attention_ref,
    others_ref,
    text_owned_ref,
    grad_one_ref,
    grad_conv_ref,
    last_ref,
    rows_all_ref,
    small_ref,
    rows_in,
    rows_sum,
    normed_ref,
    weight_ref,
    hidden_ref,
    conv_ref,
    grad_two_ref,
    load_sem,
    grads,
    grad_query,
    grad_key,
    grad_value,
    key_acc,
    value_acc,
    totals,
    pair_out,
    pair_in,
    line_out,
    line_in,
    own,
    conv_out,
    text_in,
    near_out,
    near_in,
    near_kept,
    far_out,
    far_in,
    side_in,
    level_out,
    level_in,
    out_grad,
    out_side_in,
    out_level_out,
    out_level_in,
    words_grad,
    words_side_in,
    words_level_out,
    words_level_in,
    attention_grad,
    attention_in,
    attention_out,
    attention_landed,
    grad_send,
    grad_recv,
    text_send,
    text_recv,
    pair_send,
    pair_recv,
    line_send,
    line_recv,
    conv_send,
    conv_recv,
    near_send,
    near_recv,
    far_send,
    far_recv,
    attention_send,
    attention_recv,
    landed_send,
    landed_recv,
    rows_send,
    rows_recv,
    far_rows_send,
    far_rows_recv,
    rows_sem,
    *reduce_sems,
):
    row, col = lax.axis_index("dp"), lax.axis_index("pix")
    near, far, cross = peers(col)
    targets = (far, cross, near)
    _, groups, _, owned, _ = attention_grad.shape
    side, level = lax.rem(row, 2), lax.div(row, 2)
    partner = flip(row, 1)
    loads = [
        pltpu.make_async_copy(source, buffer, load_sem.at[i])
        for i, (source, buffer) in enumerate(
            (
                (normed_from, normed_ref),
                (weight_from.at[:, pl.ds(0, weight_ref.shape[1])], weight_ref),
                (hidden_from, hidden_ref),
                (conv_from, conv_ref),
                (grad_two_from, grad_two_ref),
            )
        )
    ]
    for load in loads:
        load.start()
    greet(2 * groups, [(row, near), (row, far), (row, cross)])
    rows_group = (rows_ref, rows_in, rows_send, rows_recv)
    rows_far = (rows_sum, rows_all_ref, far_rows_send, far_rows_recv, rows_sem)
    rows, full = hidden_ref.shape
    tokens, width = query_ref.shape
    heads = width // HEAD_DIM
    score_scale = HEAD_DIM ** (-0.5)

    def grad_copy(turn):
        return remote(
            grad_ref.at[targets[turn]],
            grads.at[col],
            grad_send.at[turn],
            grad_recv.at[turn],
            (row, targets[turn]),
        )

    used = text_in.shape[1]

    def text_copy(turn):
        return remote(
            text_grad_ref.at[targets[turn], pl.ds(0, used), :],
            text_in.at[turn],
            text_send.at[turn],
            text_recv.at[turn],
            (row, targets[turn]),
        )

    for turn in range(3):
        grad_copy(turn).start()
    for turn in range(3):
        text_copy(turn).start()

    def reduction(which, source, arrived, out, landed):
        side_send, side_recv, level_send, level_recv = reduce_sems[4 * which : 4 * which + 4]

        def to_side():
            return remote(source.at[:, 1 - side], arrived, side_send, side_recv, (partner, col))

        def to_level(k):
            group = lax.rem(level + k, groups)
            return remote(
                out.at[group], landed.at[k], level_send.at[k], level_recv.at[k], (2 * group + side, col)
            )

        def middle():
            to_side().wait_recv()

            def add(group):
                out[group] = (
                    source[group, side].astype(floats) + arrived[group].astype(floats)
                ).astype(halves)

            loop(groups, add)
            lax.fori_loop(1, groups, lambda k, c: (to_level(k).start(), c)[1], 0)

        def finish():
            total = out[level].astype(floats)
            for k in range(1, groups):
                to_level(k).wait()
                total = total + landed[k].astype(floats)
            to_side().wait_send()
            return total.astype(halves)

        return to_side, middle, finish

    sides = reduction(0, reduced_ref, side_in, level_out, level_in)
    word = reduction(1, words_grad, words_side_in, words_level_out, words_level_in)
    outs = [
        reduction(
            2 + w, out_grad.at[w], out_side_in.at[w], out_level_out.at[w], out_level_in.at[w]
        )
        for w in range(2)
    ]
    sides[0]().start()
    for turn in range(3):
        group_copy(turn, *rows_group).start()

    def near_copy(which):
        return remote(
            near_out.at[which], near_in.at[which], near_send.at[which], near_recv.at[which], (row, near)
        )

    def far_copy(which):
        return remote(
            far_out.at[which], far_in.at[which], far_send.at[which], far_recv.at[which], (row, far)
        )

    def row_tile(i):
        return pl.ds(pl.multiple_of(i * width, width), width)

    lefts, rights = (attended_ref, normed_two_ref), (grad_attn_ref, grad_cross_ref)
    per_tile = width // (2 * owned)
    for which in range(2):

        def out_tile(index, first, second, which=which):
            i, b = lax.div(index, 2), lax.rem(index, 2)
            right = rights[which][:, row_tile(jnp.where(b == 0, first, second))]
            return i, b, mul_tn(lefts[which][:, row_tile(i)], right)

        def out_give(index, which=which, out_tile=out_tile):
            i, b, value = out_tile(index, near, cross)
            near_out[which, b, row_tile(i), :] = value.astype(halves)

        def out_keep(index, which=which, out_tile=out_tile):
            i, b, value = out_tile(index, col, far)
            near_kept[which, b, row_tile(i), :] = value

        loop(2 * PIX, out_give)
        near_copy(which).start()
        loop(2 * PIX, out_keep)

    def out_pass():
        for which in range(2):
            near_copy(which).wait_recv()

            def add(i, which=which):
                here = row_tile(i)
                far_out[which, here, :] = (
                    near_kept[which, 1, here, :] + near_in[which, 1, here, :].astype(floats)
                ).astype(halves)

            loop(PIX, add)
            far_copy(which).start()

    def out_end(which):
        far_copy(which).wait_recv()

        def add(i):
            here = row_tile(i)
            value = (
                near_kept[which, 0, here, :]
                + near_in[which, 0, here, :].astype(floats)
                + far_in[which, here, :].astype(floats)
            ).astype(halves)
            out_grad[which, pl.ds(i * per_tile, per_tile)] = value.reshape(
                per_tile, 2, owned, width
            )

        loop(PIX, add)
        outs[which][0]().start()

    def words_grads():
        text_total = text_grad_ref[col, 0:used, :].astype(floats)
        for turn in range(3):
            text_copy(turn).wait_recv()
            text_total = text_total + text_in[turn].astype(floats)
        text_total = jnp.concatenate(
            [text_total, jnp.zeros((text_ref.shape[0] - used, 2 * width), floats)], axis=0
        )

        def put(j):
            for k in range(2):
                right = text_total[:, k * width : (k + 1) * width]
                value = mul_tn(text_ref[:, row_tile(j)].astype(floats), right, highest)
                words_grad[pl.ds(j * per_tile, per_tile), :, :, k * width : (k + 1) * width] = (
                    value.astype(halves).reshape(per_tile, 2, owned, width)
                )

        loop(full // width, put)
        word[0]().start()

    def attention_copy(part, j):
        here = pl.ds(j * per_tile, per_tile)
        return remote(
            attention_grad.at[part, here, 1 - side],
            attention_in.at[part, here],
            attention_send.at[part, j],
            attention_recv.at[part, j],
            (partner, col),
        )

    def weight_grads(part):
        lanes = slice(part * 128, (part + 1) * 128)

        def tile(j):
            here = pl.ds(j * per_tile, per_tile)
            for k, right in enumerate((grad_query, grad_key, grad_value)):
                acc = jnp.zeros((width, 128), floats)
                for i in range(PIX):
                    acc = acc + mul_tn(
                        normed_ref[i, :, row_tile(j)], right[i * rows : (i + 1) * rows, lanes]
                    )
                attention_grad[part, here, :, :, k * 128 : (k + 1) * 128] = acc.astype(
                    halves
                ).reshape(per_tile, 2, owned, 128)
            attention_copy(part, j).start()

        loop(full // width, tile)

    def landed_copy(k):
        group = lax.rem(level + k, groups)
        return remote(
            attention_out.at[group],
            attention_landed.at[k],
            landed_send.at[k],
            landed_recv.at[k],
            (2 * group + side, col),
        )

    def attention_sum(part, out):
        def add(j):
            attention_copy(part, j).wait_recv()
            here = pl.ds(j * per_tile, per_tile)
            out[here] = (
                attention_grad[part, here, side].astype(floats)
                + attention_in[part, here].astype(floats)
            ).astype(halves)

        loop(full // width, add)

    def attention_level():
        attention_sum(0, attention_out)
        lax.fori_loop(1, groups, lambda k, c: (landed_copy(k).start(), c)[1], 0)

    def between(h):
        if h == 0:
            words_grads()
            sides[1]()
        if h == 1:
            for load in loads:
                load.wait()
            weight_grads(0)
            rows_sum[...] = group_sum(*rows_group)
            far_start(*rows_far)
        if h == 2:
            word[1]()
            out_end(0)
        if h == 3:
            out_end(1)

    grads[col] = grad_ref[col]
    totals[...] = jnp.transpose(total_ref[...])
    for turn in range(3):
        remote(
            grad_ref.at[0],
            grads.at[targets[turn]],
            grad_send.at[turn],
            grad_recv.at[turn],
            (row, near),
        ).wait_recv()
    out_pass()
    ones = jnp.ones((rows, HEAD_DIM), halves)
    for h in range(heads):
        lanes = slice(h * HEAD_DIM, (h + 1) * HEAD_DIM)
        keys, values = key_ref[:, lanes], value_ref[:, lanes]
        wide = keys.astype(floats)
        norm = score_scale * jnp.sum(wide * wide, -1, keepdims=True)
        key_acc[...] = jnp.zeros_like(key_acc)
        value_acc[...] = jnp.zeros_like(value_acc)

        def block(i, lanes=lanes, keys=keys, values=values, norm=norm, h=h):
            here = pl.ds(pl.multiple_of(i * rows, rows), rows)
            queries, grad = query_ref[here, lanes], grads[i, :, lanes]
            inner = mul_nt(keys, queries)
            prob = jnp.exp((2.0 * score_scale) * inner - norm - totals[h : h + 1, here])
            grad_prob = mul_nt(values, grad)
            value_acc[...] += mul(prob.astype(halves), grad)
            mean = jnp.sum(grad_prob * prob, 0, keepdims=True)
            score = (prob * (grad_prob - mean)).astype(halves)
            key_acc[...] += mul(score, jnp.concatenate([queries, ones], axis=1))
            grad_query[here, lanes] = (2.0 * score_scale * mul_tn(score, keys)).astype(halves)

        loop(PIX, block)
        acc = key_acc[...]
        grad_key[:, lanes] = (
            2.0 * score_scale * (acc[:, :HEAD_DIM] - wide * acc[:, HEAD_DIM : HEAD_DIM + 1])
        ).astype(halves)
        grad_value[:, lanes] = value_acc[...].astype(halves)
        between(h)

    def norm_grad(block, store):
        here = pl.ds(pl.multiple_of(block * rows, rows), rows)

        def tile(j):
            cols = pl.ds(pl.multiple_of(j * width, width), width)
            acc = jnp.zeros((rows, width), floats)
            for k, source in enumerate((grad_query, grad_key, grad_value)):
                acc = acc + mul_nt(source[here, :], weight_ref[cols, k * width : (k + 1) * width])
            store(cols, acc)

        loop(full // width, tile)

    def pair_copy(turn):
        return remote(
            pair_out.at[turn], pair_in.at[turn], pair_send.at[turn], pair_recv.at[turn], (row, near)
        )

    for turn, target in enumerate((cross, near)):

        def store(cols, value, turn=turn):
            pair_out[turn, :, cols] = value.astype(halves)

        norm_grad(target, store)
        pair_copy(turn).start()
    half = rows // 2

    def line_copy(i):
        here = pl.ds(i * half, half)
        return remote(
            line_out.at[here], line_in.at[here], line_send.at[i], line_recv.at[i], (row, far)
        )

    def store_far(cols, value):
        line_out[:, cols] = (value + pair_in[0, :, cols].astype(floats)).astype(halves)

    pair_copy(0).wait_recv()
    norm_grad(far, store_far)
    line_copy(0).start()
    line_copy(1).start()

    def store_own(cols, value):
        own[:, cols] = value + pair_in[1, :, cols].astype(floats)

    pair_copy(1).wait_recv()
    norm_grad(col, store_own)

    weight_grads(1)
    attention_level()
    outs[0][1]()
    outs[1][1]()
    small_ref[...] = jnp.zeros_like(small_ref)
    part = 64

    def back_norm(i):
        here = pl.ds(pl.multiple_of(i * part, part), part)
        hidden = hidden_ref[here, :]
        grad = own[here, :] + line_in[here, :].astype(floats)
        inverse = lax.rsqrt(jnp.mean(hidden * hidden, -1, keepdims=True) + 1e-06)
        small_ref[0:1, :] += jnp.sum(grad * hidden * inverse, 0, keepdims=True)
        scaled = grad * gain_ref[...]
        mean = jnp.mean(scaled * hidden, -1, keepdims=True)
        total = (
            grad_two_ref[here, :] + inverse * scaled - hidden * (inverse * inverse * inverse * mean)
        )
        grad_one_ref[here, :] = total
        conv = conv_ref[here, :].astype(floats)
        gate = jax.nn.sigmoid(conv)
        result = (total * gate * (1.0 + conv * (1.0 - gate))).astype(halves)
        for j in range(PIX):
            conv_out[j, here, :] = result[:, j * width : (j + 1) * width]

    def conv_copy(turn, i, block=None):
        here = pl.ds(i * half, half)
        return remote(
            conv_out.at[targets[turn], here],
            grad_conv_ref.at[col if block is None else block, here],
            conv_send.at[2 * turn + i],
            conv_recv.at[2 * turn + i],
            (row, targets[turn]),
        )

    per_half = half // part
    for i in range(2):
        line_copy(i).wait_recv()
        lax.fori_loop(i * per_half, (i + 1) * per_half, lambda j, c: (back_norm(j), c)[1], 0)
        for turn in range(3):
            conv_copy(turn, i).start()
    grad_conv_ref[col] = conv_out[col]
    for i in range(2):
        for turn in range(3):
            conv_copy(turn, i, targets[turn]).wait_recv()
    for turn in range(3):
        conv_copy(turn, 0).wait_send()
        conv_copy(turn, 1).wait_send()
        grad_copy(turn).wait_send()
        text_copy(turn).wait_send()
    for j in range(8):
        last_ref[j : j + 1, :] = small_ref[0:1, j * 128 : (j + 1) * 128]
    far_end(*rows_far)
    for w in range(2):
        others_ref[:, w * width : (w + 1) * width] = outs[w][2]()
    others_ref[:, 2 * width : 3 * width] = sides[2]()
    total = attention_out[level].astype(floats)
    for k in range(1, groups):
        landed_copy(k).wait()
        total = total + attention_landed[k].astype(floats)
    others_ref[:, 3 * width :] = total.astype(halves)
    text_owned_ref[...] = word[2]()

    attention_sum(1, attention_ref)
    for p in range(2):
        loop(full // width, lambda j, p=p: attention_copy(p, j).wait_send())
    for which in range(2):
        near_copy(which).wait_send()
        far_copy(which).wait_send()
    pair_copy(0).wait_send()
    pair_copy(1).wait_send()
    line_copy(0).wait_send()
    line_copy(1).wait_send()


def attend_backward(
    words,
    small,
    grad,
    query,
    key,
    value,
    totals,
    normed,
    weights,
    hidden,
    conv,
    grad_two,
    gain,
    text,
    text_grads,
    reduced,
    *factors,
):
    rows, full = hidden.shape
    groups, _, owned, _ = reduced.shape
    used = -(-words // 16) * 16
    tokens, width = query.shape
    flat = pltpu.VMEM((tokens, width), halves)
    return pl.pallas_call(
        attend_back_kernel,
        out_shape=(
            jax.ShapeDtypeStruct((groups, owned, 384), halves),
            jax.ShapeDtypeStruct((owned, 3 * width + 384), halves),
            jax.ShapeDtypeStruct((owned, 2 * width), halves),
            jax.ShapeDtypeStruct((rows, full), floats),
            jax.ShapeDtypeStruct((PIX, rows, width), halves),
            jax.ShapeDtypeStruct((8, 128), floats),
            jax.ShapeDtypeStruct((2 * groups,) + small.shape, floats),
        ),
        in_specs=[VMEM] * 5 + [ANY] * 5 + [VMEM] * 9,
        out_specs=(VMEM,) * 6 + (ANY,),
        scratch_shapes=[
            pltpu.VMEM((8, full), floats),
            pltpu.VMEM((4,) + small.shape, floats),
            pltpu.VMEM(small.shape, floats),
            pltpu.VMEM(normed.shape, halves),
            pltpu.VMEM((full, 3 * width), halves),
            pltpu.VMEM((rows, full), floats),
            pltpu.VMEM((rows, full), halves),
            pltpu.VMEM((rows, full), floats),
            DMA((5,)),
            pltpu.VMEM((PIX, rows, width), halves),
            flat,
            flat,
            flat,
            pltpu.VMEM((tokens, 2 * HEAD_DIM), floats),
            pltpu.VMEM((tokens, HEAD_DIM), floats),
            pltpu.VMEM((128, tokens), floats),
            pltpu.VMEM((2, rows, full), halves),
            pltpu.VMEM((2, rows, full), halves),
            pltpu.VMEM((rows, full), halves),
            pltpu.VMEM((rows, full), halves),
            pltpu.VMEM((rows, full), floats),
            pltpu.VMEM((PIX, rows, width), halves),
            pltpu.VMEM((3, used, 2 * width), halves),
            pltpu.VMEM((2, 2, full, width), halves),
            pltpu.VMEM((2, 2, full, width), halves),
            pltpu.VMEM((2, 2, full, width), floats),
            pltpu.VMEM((2, full, width), halves),
            pltpu.VMEM((2, full, width), halves),
            pltpu.VMEM((groups, owned, width), halves),
            pltpu.VMEM((groups, owned, width), halves),
            pltpu.VMEM((groups, owned, width), halves),
            pltpu.VMEM((2, groups, 2, owned, width), halves),
            pltpu.VMEM((2, groups, owned, width), halves),
            pltpu.VMEM((2, groups, owned, width), halves),
            pltpu.VMEM((2, groups, owned, width), halves),
            pltpu.VMEM((groups, 2, owned, 2 * width), halves),
            pltpu.VMEM((groups, owned, 2 * width), halves),
            pltpu.VMEM((groups, owned, 2 * width), halves),
            pltpu.VMEM((groups, owned, 2 * width), halves),
            pltpu.VMEM((2, groups, 2, owned, 384), halves),
            pltpu.VMEM((2, groups, owned, 384), halves),
            pltpu.VMEM((groups, owned, 384), halves),
            pltpu.VMEM((groups, owned, 384), halves),
            DMA((3,)),
            DMA((3,)),
            DMA((3,)),
            DMA((3,)),
            DMA((2,)),
            DMA((2,)),
            DMA((2,)),
            DMA((2,)),
            DMA((6,)),
            DMA((6,)),
            DMA((2,)),
            DMA((2,)),
            DMA((2,)),
            DMA((2,)),
            DMA((2, PIX)),
            DMA((2, PIX)),
            DMA((groups,)),
            DMA((groups,)),
            DMA((3,)),
            DMA((3,)),
            DMA((2 * groups,)),
            DMA((2 * groups,)),
            DMA,
        ]
        + [DMA, DMA, DMA((groups,)), DMA((groups,))] * 4,
        compiler_params=params(3),
        name="attend_backward",
    )(
        grad,
        query,
        key,
        value,
        totals,
        normed,
        weights,
        hidden,
        conv,
        grad_two,
        gain.reshape(1, -1),
        text,
        text_grads,
        reduced,
        *factors,
        small,
    )


def conv_back_kernel(
    count,
    width,
    images_ref,
    kernel_from,
    bank_from,
    styles_ref,
    inverse_ref,
    grad_ref,
    conv_ref,
    attention_ref,
    others_ref,
    words_ref,
    last_ref,
    bank_grad_ref,
    attention_all,
    others_all,
    words_all,
    stats_all_ref,
    image_grad_ref,
    grads_ref,
    kernel_ref,
    bank_ref,
    table_sem,
    stats_ref,
    stats_in,
    stats_sum,
    image_buf,
    padded_image,
    padded_grad,
    turned,
    acc,
    sums_out,
    sums_in,
    kept,
    kept_own,
    pixel_out,
    pixel_in,
    line_out,
    line_in,
    owner_out,
    attention_in,
    local_sem,
    image_sem,
    load_sem,
    sums_send,
    sums_recv,
    up_send,
    down_send,
    level_recv,
    pair_send,
    pair_recv,
    pixel_send,
    pixel_recv,
    line_send,
    line_recv,
    owner_send,
    owner_recv,
    attention_send,
    attention_recv,
    weight_send,
    weight_recv,
    stats_send,
    stats_recv,
    far_stats_send,
    far_stats_recv,
    stats_sem,
):
    row, col = lax.axis_index("dp"), lax.axis_index("pix")
    groups = count // 2
    side, level = lax.rem(row, 2), lax.div(row, 2)
    partner = flip(row, 1)
    near, far, cross = peers(col)
    targets = (far, cross, near)
    tokens, channels = grad_ref.shape

    buffers = (attention_all, others_all, words_all)

    def weight_copy(which, hop):
        block = buffers[which].at[far if hop == 2 else col]
        index = 3 * which + hop
        return remote(
            block, block, weight_send.at[index], weight_recv.at[index], (row, far if hop == 0 else near)
        )

    def weight_arrives(which, hop):
        block = buffers[which].at[(far, near, cross)[hop]]
        index = 3 * which + hop
        remote(block, block, weight_send.at[index], weight_recv.at[index], (row, near)).wait_recv()

    def weight_start(which):
        weight_copy(which, 0).start()
        weight_copy(which, 1).start()

    def weight_pass(which):
        weight_arrives(which, 0)
        weight_copy(which, 2).start()

    def weight_end(which):
        weight_arrives(which, 1)
        weight_arrives(which, 2)
        for hop in range(3):
            weight_copy(which, hop).wait_send()

    stats_group = (stats_ref, stats_in, stats_send, stats_recv)
    stats_far = (stats_sum, stats_all_ref, far_stats_send, far_stats_recv, stats_sem)

    def attention_copy(k):
        group = lax.rem(level + k, groups)
        return remote(
            attention_ref.at[group],
            attention_in.at[k],
            attention_send.at[k],
            attention_recv.at[k],
            (2 * group + side, col),
        )

    depth = image_buf.shape[2]
    rows = tokens // PIX
    halo = width
    greet(count, [(row, near), (row, far), (row, cross)])

    def sample_of(step):
        paired, k = turn_of(step)
        return 2 * level_at(level, groups, k) + jnp.where(paired, 1 - side, side)

    def turn_of(step):
        final = step == count - 1
        even = lax.rem(step, 2) == 0
        paired = final | (even & (step > 0))
        k = jnp.where(even, jnp.maximum(lax.div(step, 2) - 1, 0), lax.div(step + 1, 2))
        return paired, jnp.where(final, groups - 1, k)

    has_below, has_above = level > 0, level < groups - 1
    reach = jnp.minimum(level, groups - 1 - level)

    def line_block(origin, upward, source=None):
        block = grads_ref.at[2 * origin + side]
        sem = (up_send if upward else down_send).at[origin]
        target = jnp.minimum(row + 2, count - 1) if upward else jnp.maximum(row - 2, 0)
        source = block if source is None else source
        return remote(source, block, sem, level_recv.at[origin], (target, col))

    def relay(k):
        origin = level_at(level, groups, k)
        block = grads_ref.at[2 * origin + side]
        remote(
            block, block, up_send.at[origin], level_recv.at[origin], (partner, col)
        ).wait_recv()

        @pl.when((origin < level) & has_above)
        def _():
            line_block(origin, True).start()

        @pl.when((origin > level) & has_below)
        def _():
            line_block(origin, False).start()

        pair_copy(k).start()

    def pair_copy(k, source=None):
        block = grads_ref.at[2 * level_at(level, groups, k) + side]
        source = block if source is None else source
        return remote(source, block, pair_send.at[k], pair_recv.at[k], (partner, col))

    def sums_copy(k):
        return remote(
            sums_out,
            sums_in.at[row],
            sums_send.at[k],
            sums_recv.at[k],
            (lax.rem(row + k, count), col),
        )

    loads = [
        pltpu.make_async_copy(kernel_from, kernel_ref, table_sem.at[0]),
        pltpu.make_async_copy(bank_from, bank_ref, table_sem.at[1]),
    ]
    own = pltpu.make_async_copy(grad_ref, grads_ref.at[row], local_sem)
    own.start()
    for load in loads:
        load.start()

    @pl.when(has_above)
    def _():
        line_block(level, True, grad_ref).start()

    @pl.when(has_below)
    def _():
        line_block(level, False, grad_ref).start()

    pair_copy(0, grad_ref).start()

    def fetch(step):
        slot = lax.rem(step, 2)
        return pltpu.make_async_copy(
            images_ref.at[sample_of(step)], image_buf.at[slot], image_sem.at[slot]
        )

    fetch(0).start()
    others_all[col] = others_ref[...]
    words_all[col] = words_ref[...]
    for which in (1, 2):
        weight_start(which)
    products = jnp.zeros((8, channels), floats)

    def add_product(i, total):
        here = pl.ds(pl.multiple_of(i * 64, 64), 64)
        product = grad_ref[here, :].astype(floats) * conv_ref[here, :].astype(floats)
        return total + jnp.sum(product.reshape(8, 8, channels), axis=0)

    products = lax.fori_loop(0, tokens // 64, add_product, products)
    sums_out[...] = jnp.broadcast_to(jnp.sum(products, 0, keepdims=True), (8, channels))
    lax.fori_loop(1, count, lambda k, c: (sums_copy(k).start(), c)[1], 0)
    sums_in[row] = sums_out[...]
    acc[...] = jnp.zeros_like(acc)
    stats_ref[...] = jnp.zeros_like(stats_ref)
    stats_ref[3 * count :, :] = last_ref[...]
    for buffer in (padded_image, padded_grad):
        zeros = jnp.zeros((halo, buffer.shape[1]), halves)
        buffer[0:halo, :] = zeros
        buffer[halo + tokens : halo + tokens + halo, :] = zeros

    def sums_arrive(k, carry):
        origin = lax.rem(row - k + count, count)
        remote(
            sums_out, sums_in.at[origin], sums_send.at[k], sums_recv.at[k], (partner, col)
        ).wait_recv()
        return carry

    def fill(source):
        wide = source.astype(floats)
        place = lax.rem(lax.broadcasted_iota(jnp.int32, wide.shape, 0), width)
        here = slice(halo, halo + tokens)
        padded_image[here, 0:depth] = jnp.where(
            place == 0, 0.0, pltpu.roll(wide, 1, 0)
        ).astype(halves)
        padded_image[here, depth : 2 * depth] = source
        padded_image[here, 2 * depth : 3 * depth] = jnp.where(
            place == width - 1, 0.0, pltpu.roll(wide, tokens - 1, 0)
        ).astype(halves)

    centre = pl.ds(halo, tokens)

    def pixel_copy(step):
        return remote(
            pixel_out.at[lax.rem(step, 2)],
            pixel_in.at[step],
            pixel_send.at[step],
            pixel_recv.at[step],
            (row, near),
        )

    def line_copy(step):
        return remote(
            line_out.at[lax.rem(step, 2)],
            line_in.at[step],
            line_send.at[step],
            line_recv.at[step],
            (row, far),
        )

    def owner_copy(step):
        return remote(
            owner_out.at[lax.rem(step, 2)],
            image_grad_ref.at[row],
            owner_send.at[step],
            owner_recv.at[row],
            (sample_of(step), col),
        )

    def work(step):
        paired, k = turn_of(step)
        sample = sample_of(step)

        @pl.when(paired)
        def _():
            block = grads_ref.at[sample]
            remote(block, block, pair_send.at[k], pair_recv.at[k], (partner, col)).wait_recv()

        distance = lax.div(step + 1, 2)
        odd = lax.rem(step, 2) == 1

        @pl.when(odd & (distance <= reach))
        def _():
            relay(2 * distance - 1)
            relay(2 * distance)

        @pl.when(odd & (distance > reach) & (distance <= groups - 1 - reach))
        def _():
            relay(distance + reach)

        load = pltpu.make_async_copy(
            grads_ref.at[sample], padded_grad.at[centre, :], load_sem
        )
        load.start()
        fetch(step).wait()

        @pl.when(step + 1 < count)
        def _():
            fetch(step + 1).start()

        fill(image_buf[lax.rem(step, 2)])
        load.wait()
        turned[...] = jnp.transpose(padded_grad[centre, :])
        slot = lax.rem(step, 2)

        @pl.when(step >= 2)
        def _():
            pixel_copy(step - 2).wait_send()

        def through(target):
            start = pl.multiple_of(target * rows, rows)
            total = jnp.zeros((rows, 3 * depth), floats)
            for a in range(3):
                window = padded_grad[pl.ds(pl.multiple_of(start + (2 - a) * width, 16), rows), :]
                taps = kernel_ref[sample, 3 * a : 3 * a + 3].reshape(3 * depth, channels)
                total = total + mul_nt(window, taps)
            place = lax.rem(lax.broadcasted_iota(jnp.int32, (rows, depth), 0), width)
            after = pltpu.roll(total[:, 0:depth], rows - 1, 0)
            before = pltpu.roll(total[:, 2 * depth : 3 * depth], 1, 0)
            return (
                total[:, depth : 2 * depth]
                + jnp.where(place == width - 1, 0.0, after)
                + jnp.where(place == 0, 0.0, before)
            )

        def give(i):
            pixel_out[slot, i] = through(jnp.where(i == 0, near, cross)).astype(halves)

        def keep(i):
            kept[slot, i] = through(jnp.where(i == 0, col, far))

        loop(2, give)
        pixel_copy(step).start()
        loop(2, keep)
        style = styles_ref[sample]
        scale = style[0:1, :depth]
        first, second = style[1:2, 0:1], style[2:3, 0:1]
        both = jnp.concatenate(
            [
                jnp.broadcast_to(inverse_ref[pl.ds(sample, 1), :], (8, channels)),
                sums_in[sample],
            ],
            axis=0,
        )
        columns = jnp.transpose(both)
        inverse, total = columns[:, 0:1], columns[:, 8:9]
        factor = inverse * inverse * total
        by_scale = jnp.zeros((1, depth), floats)
        by_first = jnp.zeros((1, depth), floats)
        by_second = jnp.zeros((1, depth), floats)
        for a in range(3):
            three = mul(turned[...], padded_image[pl.ds(a * width, tokens), :])
            for b in range(3):
                tap = 3 * a + b
                found = three[:, b * depth : (b + 1) * depth]
                one, two = bank_ref[0, tap].astype(floats), bank_ref[1, tap].astype(floats)
                selected = first * one + second * two
                modded = inverse * found - factor * (selected * scale)
                by_scale = by_scale + jnp.sum(modded * selected, 0, keepdims=True)
                grad_selected = modded * scale
                acc[0, tap] += first * grad_selected
                acc[1, tap] += second * grad_selected
                by_first = by_first + jnp.sum(grad_selected * one, 0, keepdims=True)
                by_second = by_second + jnp.sum(grad_selected * two, 0, keepdims=True)
        for k, line in enumerate((by_scale, by_first, by_second)):
            stats_ref[pl.ds(k * count + sample, 1), :depth] = line

    def across(step):
        slot = lax.rem(step, 2)
        pixel_copy(step).wait_recv()

        @pl.when(step >= 2)
        def _():
            line_copy(step - 2).wait_send()

        line_out[slot] = (kept[slot, 1] + pixel_in[step, 1].astype(floats)).astype(halves)
        line_copy(step).start()
        kept_own[slot] = kept[slot, 0] + pixel_in[step, 0].astype(floats)

    def home(step):
        slot = lax.rem(step, 2)
        line_copy(step).wait_recv()

        @pl.when(step >= 3)
        def _():
            owner_copy(step - 2).wait_send()

        owner_out[slot] = (kept_own[slot] + line_in[step].astype(floats)).astype(halves)

        @pl.when(step > 0)
        def _():
            owner_copy(step).start()

        @pl.when(step == 0)
        def _():
            mine = pltpu.make_async_copy(owner_out.at[slot], image_grad_ref.at[row], local_sem)
            mine.start()
            mine.wait()

    lax.fori_loop(1, count, sums_arrive, 0)

    own.wait()
    for load in loads:
        load.wait()

    def step_body(step):
        @pl.when(step == 2)
        def _():
            for which in (1, 2):
                weight_pass(which)

        @pl.when(step == count - 2)
        def _():
            lax.fori_loop(1, groups, lambda k, c: (attention_copy(k).start(), c)[1], 0)

        @pl.when(step < count)
        def _():
            work(step)

        @pl.when(step == count)
        def _():
            for turn in range(3):
                group_copy(turn, *stats_group).start()

        @pl.when((step >= 1) & (step <= count))
        def _():
            across(step - 1)

        @pl.when(step >= 2)
        def _():
            home(step - 2)

    loop(count + 2, step_body)
    lax.fori_loop(1, groups, lambda k, c: (attention_copy(k).wait(), c)[1], 0)
    attention_total = attention_ref[level].astype(floats)
    for k in range(1, groups):
        attention_total = attention_total + attention_in[k].astype(floats)
    attention_all[col] = attention_total.astype(halves)
    weight_start(0)
    stats_sum[...] = group_sum(*stats_group)
    far_start(*stats_far)

    def write(index):
        bank_grad_ref[lax.div(index, 9), lax.rem(index, 9)] = jnp.transpose(
            acc[lax.div(index, 9), lax.rem(index, 9)]
        )

    loop(18, write)

    def owner_arrives(k, carry):
        origin = lax.rem(row - k + count, count)
        remote(
            owner_out.at[0],
            image_grad_ref.at[origin],
            owner_send.at[k],
            owner_recv.at[origin],
            (partner, col),
        ).wait_recv()
        return carry

    lax.fori_loop(1, count, owner_arrives, 0)
    weight_pass(0)
    far_end(*stats_far)
    for which in (1, 2, 0):
        weight_end(which)
    for step in (count - 2, count - 1):
        pixel_copy(step).wait_send()
        line_copy(step).wait_send()
        owner_copy(step).wait_send()

    def sent(origin):
        @pl.when((origin <= level) & has_above)
        def _():
            line_block(origin, True).wait_send()

        @pl.when((origin >= level) & has_below)
        def _():
            line_block(origin, False).wait_send()

    loop(groups, sent)
    loop(groups, lambda k: pair_copy(k).wait_send())
    lax.fori_loop(1, count, lambda k, c: (sums_copy(k).wait_send(), c)[1], 0)


def conv_backward(images_all, kernels, bank, styles, inverse, grad, conv, owned, last, width):
    attention, others, words = owned
    count, tokens, depth = images_all.shape
    channels = grad.shape[1]
    rows = tokens // PIX
    groups = count // 2
    piece = (rows, depth)
    return pl.pallas_call(
        partial(conv_back_kernel, count, width),
        out_shape=(
            jax.ShapeDtypeStruct((2, 9, depth, channels), floats),
            jax.ShapeDtypeStruct((PIX,) + attention.shape[1:], halves),
            jax.ShapeDtypeStruct((PIX,) + others.shape, halves),
            jax.ShapeDtypeStruct((PIX,) + words.shape, halves),
            jax.ShapeDtypeStruct((count, 3 * count + 8, 128), floats),
            jax.ShapeDtypeStruct((count,) + piece, halves),
            jax.ShapeDtypeStruct((count, tokens, channels), halves),
        ),
        in_specs=[ANY] * 3 + [VMEM] * 8,
        out_specs=(VMEM,) * 4 + (ANY,) * 3,
        scratch_shapes=[
            pltpu.VMEM(kernels.shape, halves),
            pltpu.VMEM(bank.shape, halves),
            DMA((2,)),
            pltpu.VMEM((3 * count + 8, 128), floats),
            pltpu.VMEM((4, 3 * count + 8, 128), floats),
            pltpu.VMEM((3 * count + 8, 128), floats),
            pltpu.VMEM((2, tokens, depth), halves),
            pltpu.VMEM((tokens + 2 * width, 3 * depth), halves),
            pltpu.VMEM((tokens + 2 * width, channels), halves),
            pltpu.VMEM((channels, tokens), halves),
            pltpu.VMEM((2, 9, channels, depth), floats),
            pltpu.VMEM((8, channels), floats),
            pltpu.VMEM((count, 8, channels), floats),
            pltpu.VMEM((2, 2) + piece, floats),
            pltpu.VMEM((2,) + piece, floats),
            pltpu.VMEM((2, 2) + piece, halves),
            pltpu.VMEM((count, 2) + piece, halves),
            pltpu.VMEM((2,) + piece, halves),
            pltpu.VMEM((count,) + piece, halves),
            pltpu.VMEM((2,) + piece, halves),
            pltpu.VMEM(attention.shape, halves),
            DMA,
            DMA((2,)),
            DMA,
            DMA((count,)),
            DMA((count,)),
            DMA((groups,)),
            DMA((groups,)),
            DMA((groups,)),
            DMA((groups,)),
            DMA((groups,)),
            DMA((count,)),
            DMA((count,)),
            DMA((count,)),
            DMA((count,)),
            DMA((count,)),
            DMA((count,)),
            DMA((groups,)),
            DMA((groups,)),
            DMA((9,)),
            DMA((9,)),
            DMA((3,)),
            DMA((3,)),
            DMA((count,)),
            DMA((count,)),
            DMA,
        ],
        compiler_params=params(4),
        name="conv_backward",
    )(
        images_all,
        kernels,
        bank,
        styles,
        inverse,
        grad,
        conv,
        attention,
        others,
        words,
        last,
    )


def prepare_kernel(
    styled_ref,
    label_ref,
    select_ref,
    modulation_ref,
    rgb_modulation_ref,
    images_ref,
    query_ref,
    key_ref,
    value_ref,
    out_ref,
    cross_query_ref,
    cross_out_ref,
    text_key_ref,
    text_value_ref,
    attention_ref,
    others_ref,
    style_ref,
    rgb_scale_ref,
    parts_ref,
):
    col = lax.axis_index("pix")
    count, rows, depth = parts_ref.shape
    width = attention_ref.shape[1] // 5
    short = text_key_ref.shape[0]
    mine = pl.ds(pl.multiple_of(col * width, width), width)
    for k, source in enumerate((query_ref, key_ref, value_ref)):
        attention_ref[:, k * width : (k + 1) * width] = source[:, mine]
    attention_ref[:, 3 * width :] = jnp.zeros((attention_ref.shape[0], 2 * width), halves)
    for k, source in enumerate((text_key_ref, text_value_ref)):
        attention_ref[0:short, (3 + k) * width : (4 + k) * width] = source[:, mine]
    for k, source in enumerate((out_ref, cross_query_ref, cross_out_ref)):
        others_ref[:, k * width : (k + 1) * width] = source[:, mine]
    styled = styled_ref[...]
    logits = jnp.sum(styled * select_ref[...], -1, keepdims=True)
    first, second = logits[0:1], logits[1:2]
    largest = jnp.maximum(first, second)
    first, second = jnp.exp(first - largest), jnp.exp(second - largest)
    total = first + second
    eight = jnp.broadcast_to(styled, (8, styled.shape[1]))

    def through(matrix):
        return exact(mul, eight, matrix[...]) + 1.0

    scaling = through(modulation_ref)
    rgb_scale_ref[...] = through(rgb_modulation_ref)[0:1]
    same = jnp.concatenate(
        [jnp.broadcast_to(first / total, (1, 128)), jnp.broadcast_to(second / total, (1, 128))]
        + [styled[:, k * 128 : (k + 1) * 128] for k in range(4)]
        + [label_ref[...]],
        axis=0,
    )
    for d in range(count):
        lanes = slice(d * depth, (d + 1) * depth)
        style_ref[d, 0:1, :] = jnp.zeros((1, 128), floats)
        style_ref[d, 0:1, 0:depth] = scaling[0:1, lanes]
        style_ref[d, 1:8, :] = same
        parts_ref[d] = images_ref[:, lanes]


def prepare(styled, label, select_rows, modulation, rgb_modulation, images, weights, count):
    rows, channels = images.shape
    owned, quarter = weights[0].shape[0], channels // PIX
    return pl.pallas_call(
        prepare_kernel,
        out_shape=(
            jax.ShapeDtypeStruct((owned, 5 * quarter), halves),
            jax.ShapeDtypeStruct((owned, 3 * quarter), halves),
            jax.ShapeDtypeStruct((count, 8, 128), floats),
            jax.ShapeDtypeStruct((1, channels), floats),
            jax.ShapeDtypeStruct((count, rows, channels // count), halves),
        ),
        in_specs=[VMEM] * 14,
        out_specs=(VMEM,) * 5,
        compiler_params=pltpu.CompilerParams(vmem_limit_bytes=VMEM_LIMIT),
        name="prepare",
    )(styled, label, select_rows, modulation, rgb_modulation, images, *weights)


def finish_kernel(
    rows_ref,
    stats_ref,
    styles_ref,
    select_ref,
    modulation_ref,
    rgb_modulation_ref,
    attention_ref,
    others_ref,
    words_ref,
    grad_one_ref,
    image_parts_ref,
    grad_query_ref,
    grad_key_ref,
    grad_value_ref,
    grad_out_ref,
    grad_cross_query_ref,
    grad_cross_out_ref,
    grad_text_key_ref,
    grad_text_value_ref,
    grad_image_ref,
    grad_style_ref,
    grad_table_ref,
    grad_select_ref,
    grad_modulation_ref,
    grad_rgb_ref,
    gain_self_ref,
    gain_cross_ref,
    rgb_weight_ref,
    scaling,
    styles_grad,
):
    row = lax.axis_index("dp")
    count, rows, depth = image_parts_ref.shape
    width = words_ref.shape[2] // 2
    for d in range(count):
        lanes = slice(d * depth, (d + 1) * depth)
        grad_image_ref[:, lanes] = grad_one_ref[:, lanes] + image_parts_ref[d].astype(floats)
        scaling[:, lanes] = stats_ref[d, 0:count, 0:depth]
    for k, out in enumerate((grad_query_ref, grad_key_ref, grad_value_ref)):
        for p in range(2 * PIX):
            first = 3 * width + k * 128 if p % 2 == 0 else k * 128
            source = others_ref if p % 2 == 0 else attention_ref
            out[:, p * 128 : (p + 1) * 128] = source[p // 2, :, first : first + 128].astype(floats)
    for buffer, outs in (
        (others_ref, (grad_out_ref, grad_cross_query_ref, grad_cross_out_ref)),
        (words_ref, (grad_text_key_ref, grad_text_value_ref)),
    ):
        for k, out in enumerate(outs):
            for p in range(PIX):
                block = buffer[p, :, k * width : (k + 1) * width].astype(floats)
                out[:, p * width : (p + 1) * width] = block[: out.shape[0]]
    sums = rows_ref[0]
    for d in range(1, count):
        sums = sums + rows_ref[d]
    total = stats_ref[0, 3 * count :, :]
    for d in range(1, count):
        total = total + stats_ref[d, 3 * count :, :]
    gain_self_ref[...] = total
    gain_cross_ref[...] = sums[0:1]
    rgb_weight_ref[...] = sums[2:5]
    mixing, grads = [], []
    for k in (1, 2):
        total = stats_ref[0, k * count : (k + 1) * count, :]
        for d in range(1, count):
            total = total + stats_ref[d, k * count : (k + 1) * count, :]
        grads.append(jnp.sum(total, -1, keepdims=True))
        mixing.append(styles_ref[:, k, :][:, 0:1])
    inner = grads[0] * mixing[0] + grads[1] * mixing[1]
    logits = [m * (g - inner) for m, g in zip(mixing, grads)]
    styled = jnp.concatenate([styles_ref[:, 3 + k, :] for k in range(4)], axis=1)
    rgb = rows_ref[:, 1, :]
    grad_modulation_ref[...] = outer_sum(styled, scaling[...])
    grad_rgb_ref[...] = outer_sum(styled, rgb)
    place = lax.broadcasted_iota(jnp.int32, (count, 128), 1)
    both = jnp.where(place == 0, logits[0], jnp.where(place == 1, logits[1], 0.0))
    grad_select_ref[...] = outer_sum(both, styled)[0:2]
    grad_styles = (
        exact(mul_nt, scaling[...], modulation_ref[...])
        + exact(mul_nt, rgb, rgb_modulation_ref[...])
        + logits[0] * select_ref[0:1, :]
        + logits[1] * select_ref[1:2, :]
    )
    styles_grad[...] = grad_styles
    grad_style_ref[...] = styles_grad[pl.ds(row, 1), :]
    label = styles_ref[:, 7, :][:, 0:1].astype(jnp.int32)
    classes = grad_table_ref.shape[0]
    chosen = lax.broadcasted_iota(jnp.int32, (count, classes), 1) == label
    chosen = chosen.astype(floats).astype(halves)
    grad_table_ref[...] = mul_tn(
        jnp.concatenate([chosen] * 3, axis=0),
        jnp.concatenate(split(grad_styles)[::-1], axis=0),
    )


def finish(
    all_rows,
    all_stats,
    styles,
    select_rows,
    modulation,
    rgb_modulation,
    gathered,
    grad_one,
    image_parts,
    classes,
    text_rows,
):
    count = styles.shape[0]
    rows, channels = grad_one.shape
    owned = gathered[0].shape[1]
    wide = modulation.shape[0]

    def out(*shape):
        return jax.ShapeDtypeStruct(shape, floats)

    return pl.pallas_call(
        finish_kernel,
        out_shape=(out(owned, channels),) * 6
        + (out(text_rows, channels),) * 2
        + (
            out(rows, channels),
            out(1, wide),
            out(classes, wide),
            out(2, wide),
            out(wide, channels),
            out(wide, channels),
            out(8, channels // 8),
            out(1, channels),
            out(3, channels),
        ),
        in_specs=[VMEM] * 11,
        out_specs=(VMEM,) * 17,
        scratch_shapes=[pltpu.VMEM((count, channels), floats), pltpu.VMEM((count, wide), floats)],
        compiler_params=pltpu.CompilerParams(vmem_limit_bytes=VMEM_LIMIT),
        name="finish",
    )(
        all_rows,
        all_stats,
        styles,
        select_rows,
        modulation,
        rgb_modulation,
        *gathered,
        grad_one,
        image_parts,
    )


def on_device(
    images,
    style_codes,
    labels,
    token_ids,
    penalty_mask,
    class_table,
    text_table,
    conv_bank,
    select_weight,
    modulation,
    rgb_modulation,
    w_query,
    w_key,
    w_value,
    w_out,
    c_query,
    c_key,
    c_value,
    c_out,
    gain_self,
    gain_cross,
    rgb_weight,
    out_cotangent,
    rgb_cotangent,
):
    count = lax.axis_size("dp")
    _, height, width, channels = images.shape
    rows = height * width
    quarter = channels // PIX
    depth = channels // count

    owned, text_owned = w_query.shape[0], c_key.shape[0]
    class_row = jnp.take(class_table, labels, axis=0).astype(floats)
    styled = style_codes.astype(floats) + class_row
    label = jnp.broadcast_to(labels.astype(floats).reshape(1, 1), (1, 128))
    select_rows = jnp.pad(select_weight.T, ((0, 6), (0, 0))).astype(floats)
    own = images.reshape(rows, channels)
    attention, others, style, rgb_scale, parts = prepare(
        styled,
        label,
        select_rows,
        modulation,
        rgb_modulation,
        own,
        (w_query, w_key, w_value, w_out, c_query, c_out, c_key, c_value),
        count,
    )
    attention = lax.all_gather(attention, "dp", axis=0, tiled=True)
    others = lax.all_gather(others, ("pix", "dp"), axis=0, tiled=True)
    others = others.reshape(PIX, channels, 3 * quarter)
    bank = conv_bank.reshape(2, 9, depth, quarter)
    bank_turned = bank.transpose(0, 1, 3, 2)
    words = token_ids.shape[1]
    text = jnp.take(text_table, token_ids[0], axis=0)
    text = text.reshape(words, count, text_owned)
    text = jnp.pad(text, ((0, 128 - words), (0, 0), (0, owned - text_owned)))
    text = text.reshape(128, channels)

    images_all, kernels, styles, inverse = gather_inputs(style, bank, parts)
    images_all = images_all.reshape(count, PIX * rows, depth)
    conv, conv_own, hidden_one, normed_one = conv_forward(images_all, kernels, own, gain_self, width)
    query, key, value, totals, attended, text_all = attend_forward(
        normed_one, attention, text
    )
    rgb_rows = jnp.pad(rgb_cotangent.reshape(3, rows).T, ((0, 0), (0, 125)))
    penalty = jnp.broadcast_to(penalty_mask.astype(floats).reshape(1, 1), (1, 128))
    (
        output,
        rgb,
        reduced,
        text_grads,
        grad_two,
        grad_attended,
        small,
        *factors,
    ) = cross_part(
        words,
        attended,
        hidden_one,
        others,
        text_all,
        gain_cross,
        rgb_scale,
        jnp.pad(rgb_weight, ((0, 0), (0, 125))),
        out_cotangent.reshape(rows, channels),
        rgb_rows,
        penalty,
    )
    (
        attention_grads,
        others_owned,
        words_owned,
        grad_one,
        grad_conv,
        last,
        all_rows,
    ) = attend_backward(
        words,
        small,
        grad_attended,
        query,
        key,
        value,
        totals,
        normed_one,
        attention,
        hidden_one,
        conv,
        grad_two,
        gain_self,
        text,
        text_grads,
        reduced.reshape(count // 2, 2, owned, quarter),
        *factors,
    )

    bank_grad, *gathered, all_stats, image_parts, _ = conv_backward(
        images_all,
        kernels,
        bank_turned,
        styles,
        inverse,
        grad_conv.reshape(PIX * rows, quarter),
        conv_own,
        (attention_grads, others_owned, words_owned),
        last,
        width,
    )
    (
        grad_w_query,
        grad_w_key,
        grad_w_value,
        grad_w_out,
        grad_c_query,
        grad_c_out,
        grad_c_key,
        grad_c_value,
        grad_image,
        grad_style,
        grad_table,
        grad_select,
        grad_modulation,
        grad_rgb_modulation,
        grad_gain_self,
        grad_gain_cross,
        grad_rgb_weight,
    ) = finish(
        all_rows,
        all_stats,
        styles,
        select_rows,
        modulation,
        rgb_modulation,
        gathered,
        grad_one,
        image_parts,
        class_table.shape[0],
        text_owned,
    )
    shape = images.shape
    return (
        output.reshape(shape),
        rgb[:, :3].T.reshape(1, 3, height, width),
        grad_image.reshape(shape),
        grad_style,
        grad_table,
        bank_grad.reshape(conv_bank.shape),
        grad_select.T,
        grad_modulation,
        grad_rgb_modulation,
        grad_w_query,
        grad_w_key,
        grad_w_value,
        grad_w_out,
        grad_c_query,
        grad_c_key,
        grad_c_value,
        grad_c_out,
        grad_gain_self.reshape(-1),
        grad_gain_cross.reshape(-1),
        grad_rgb_weight.T,
    )


def solution(mesh):
    return jax.shard_map(
        on_device,
        mesh=mesh,
        in_specs=(
            P("dp", "pix", None, None),
            P("dp", None),
            P("dp"),
            P("dp", None),
            P("dp"),
            P(),
            P(),
            P(None, None, None, "dp", "pix"),
            P(),
            P(),
            P(),
            P("dp", None),
            P("dp", None),
            P("dp", None),
            P("dp", None),
            P("dp", None),
            P("dp", None),
            P("dp", None),
            P("dp", None),
            P(),
            P(),
            P(),
            P("dp", "pix", None, None),
            P("dp", None, "pix", None),
        ),
        out_specs=(
            P("dp", "pix", None, None),
            P("dp", None, "pix", None),
            P("dp", "pix", None, None),
            P("dp", None),
            P(),
            P(None, None, None, "dp", "pix"),
            P(),
            P(),
            P(),
            P("dp", None),
            P("dp", None),
            P("dp", None),
            P("dp", None),
            P("dp", None),
            P("dp", None),
            P("dp", None),
            P("dp", None),
            P(),
            P(),
            P(),
        ),
        check_vma=False,
    )
```

```python
from functools import partial

import jax
import jax.numpy as jnp
from jax import lax
from jax.experimental import pallas as pl
from jax.experimental.pallas import tpu as pltpu
from jax.sharding import PartitionSpec as P

HEAD_DIM = 64
PIX = 4
MESH = pl.DeviceIdType.MESH
VMEM_LIMIT = 60 * 1024 * 1024

penalty_weight = 1.0
highest = lax.Precision.HIGHEST
floats = jnp.float32
halves = jnp.bfloat16

ANY = pl.BlockSpec(memory_space=pl.ANY)
VMEM = pl.BlockSpec(memory_space=pltpu.VMEM)
DMA = pltpu.SemaphoreType.DMA


def params(collective_id):
    return pltpu.CompilerParams(
        collective_id=collective_id, has_side_effects=True, vmem_limit_bytes=VMEM_LIMIT
    )


def remote(src, dst, send_sem, recv_sem, where):
    return pltpu.make_async_remote_copy(
        src_ref=src,
        dst_ref=dst,
        send_sem=send_sem,
        recv_sem=recv_sem,
        device_id=where,
        device_id_type=MESH,
    )


def greet(count, others):
    row, col = lax.axis_index("dp"), lax.axis_index("pix")
    barrier = pltpu.get_barrier_semaphore()

    def one(step, carry):
        pl.semaphore_signal(
            barrier, inc=1, device_id=(lax.rem(row + step, count), col), device_id_type=MESH
        )
        return carry

    if count > 1:
        lax.fori_loop(1, count, one, 0)
    for other in others:
        pl.semaphore_signal(barrier, inc=1, device_id=other, device_id_type=MESH)
    pl.semaphore_wait(barrier, count - 1 + len(others))


def loop(count, body):
    def step(i, carry):
        body(i)
        return carry

    lax.fori_loop(0, count, step, 0)


def flip(index, bit):
    part = lax.rem(lax.div(index, bit), 2)
    return index + bit - 2 * bit * part


def level_at(level, groups, index):
    both = jnp.minimum(level, groups - 1 - level)
    step = lax.div(index + 1, 2)
    near = jnp.where(lax.rem(index, 2) == 1, level - step, level + step)
    rest = index - both
    far = jnp.where(level > groups - 1 - level, level - rest, level + rest)
    return jnp.where(index == 0, level, jnp.where(index <= 2 * both, near, far))


def gather_kernel(
    count,
    style_ref,
    bank_ref,
    parts_ref,
    images_ref,
    kernel_ref,
    styles_ref,
    inverse_ref,
    squares,
    squares_in,
    local_sem,
    style_send,
    style_recv,
    square_send,
    square_recv,
    part_send,
    part_recv,
    core_send,
    core_recv,
    line_send,
    line_recv,
    pass_send,
    pass_recv,
):
    row, col = lax.axis_index("dp"), lax.axis_index("pix")
    near, far = flip(col, 1), flip(col, 2)
    depth = bank_ref.shape[2]
    greet(count, [(row, near), (row, far)])

    def style_copy(step):
        other = lax.rem(row + step, count)
        return remote(
            style_ref.at[other], styles_ref.at[row], style_send.at[step], style_recv.at[step], (other, col)
        )

    def square_copy(step):
        other = lax.rem(row + step, count)
        return remote(
            squares, squares_in.at[row], square_send.at[step], square_recv.at[step], (other, col)
        )

    def part_copy(step):
        other = lax.rem(row + step, count)
        return remote(
            parts_ref.at[other], images_ref.at[row, col], part_send.at[step], part_recv.at[step], (other, col)
        )

    def part_arrives(step):
        origin = lax.rem(row - step + count, count)
        remote(
            parts_ref.at[0], images_ref.at[origin, col], part_send.at[step], part_recv.at[step], (row, near)
        ).wait_recv()

    def core_copy(step):
        origin = lax.rem(row - step + count, count)
        block = images_ref.at[origin, col]
        return remote(block, block, core_send.at[step], core_recv.at[step], (row, near))

    def line_copy(step):
        origin = lax.rem(row - step + count, count)
        block = images_ref.at[origin, col]
        return remote(block, block, line_send.at[step], line_recv.at[step], (row, far))

    def pass_copy(step):
        origin = lax.rem(row - step + count, count)
        block = images_ref.at[origin, far]
        return remote(block, block, pass_send.at[step], pass_recv.at[step], (row, near))

    def core_arrives(step):
        origin = lax.rem(row - step + count, count)
        block = images_ref.at[origin, near]
        remote(block, block, core_send.at[step], core_recv.at[step], (row, near)).wait_recv()

    def line_arrives(step):
        origin = lax.rem(row - step + count, count)
        block = images_ref.at[origin, far]
        remote(block, block, line_send.at[step], line_recv.at[step], (row, far)).wait_recv()

    def pass_arrives(step):
        origin = lax.rem(row - step + count, count)
        block = images_ref.at[origin, flip(near, 2)]
        remote(block, block, pass_send.at[step], pass_recv.at[step], (row, near)).wait_recv()

    own = pltpu.make_async_copy(parts_ref.at[row], images_ref.at[row, col], local_sem)
    own.start()

    def send_all(step):
        style_copy(step).start()

    lax.fori_loop(1, count, lambda i, c: (send_all(i), c)[1], 0)
    lax.fori_loop(1, count, lambda i, c: (part_copy(i).start(), c)[1], 0)
    styles_ref[row] = style_ref[row]
    own.wait()
    line_copy(0).start()
    core_copy(0).start()

    def style_wait(step):
        origin = lax.rem(row - step + count, count)
        remote(
            style_ref.at[0], styles_ref.at[origin], style_send.at[step], style_recv.at[step], (row, near)
        ).wait_recv()

    lax.fori_loop(1, count, lambda i, c: (style_wait(i), c)[1], 0)

    def mixed_tap(sample, tap, column, first, second):
        total = first * bank_ref[0, tap].astype(floats) + second * bank_ref[1, tap].astype(floats)
        return total * column

    def factors(sample):
        block = styles_ref[sample]
        column = jnp.transpose(block)[:depth, 0:1]
        return column, block[1:2, 0:1], block[2:3, 0:1]

    def square_sum(sample):
        column, first, second = factors(sample)
        total = jnp.zeros((depth, bank_ref.shape[3]), floats)
        for tap in range(9):
            modded = mixed_tap(sample, tap, column, first, second)
            total = total + modded * modded
        squares[pl.ds(sample, 1), :] = jnp.sum(total, axis=0, keepdims=True)

    loop(count, square_sum)
    lax.fori_loop(1, count, lambda i, c: (square_copy(i).start(), c)[1], 0)
    squares_in[row] = squares[...]

    def relay(step):
        part_arrives(step)
        line_copy(step).start()
        core_copy(step).start()

    lax.fori_loop(1, count, lambda i, c: (relay(i), c)[1], 0)

    def square_wait(step):
        origin = lax.rem(row - step + count, count)
        remote(
            squares, squares_in.at[origin], square_send.at[step], square_recv.at[step], (row, near)
        ).wait_recv()

    lax.fori_loop(1, count, lambda i, c: (square_wait(i), c)[1], 0)
    inverse_ref[...] = lax.rsqrt(jnp.sum(squares_in[...], axis=0) + 1e-08)

    def forward(step):
        line_arrives(step)
        pass_copy(step).start()

    def make_kernel(sample):
        column, first, second = factors(sample)
        scale = inverse_ref[pl.ds(sample, 1), :]
        for tap in range(9):
            modded = mixed_tap(sample, tap, column, first, second)
            kernel_ref[sample, tap] = (modded * scale).astype(halves)
        forward(sample)

    loop(count, make_kernel)
    loop(count, core_arrives)
    loop(count, pass_arrives)
    lax.fori_loop(
        1,
        count,
        lambda i, c: (
            style_copy(i).wait_send(),
            square_copy(i).wait_send(),
            part_copy(i).wait_send(),
            c,
        )[3],
        0,
    )
    loop(count, lambda i: core_copy(i).wait_send())
    loop(count, lambda i: line_copy(i).wait_send())
    loop(count, lambda i: pass_copy(i).wait_send())


def gather_inputs(style_rows, bank, parts):
    count, rows, depth = parts.shape
    width = bank.shape[-1]
    sems = [DMA((count,)) for _ in range(12)]
    return pl.pallas_call(
        partial(gather_kernel, count),
        out_shape=(
            jax.ShapeDtypeStruct((count, PIX, rows, depth), halves),
            jax.ShapeDtypeStruct((count, 9, depth, width), halves),
            jax.ShapeDtypeStruct((count, 8, 128), floats),
            jax.ShapeDtypeStruct((count, width), floats),
        ),
        in_specs=[VMEM, VMEM, ANY],
        out_specs=(ANY, VMEM, VMEM, VMEM),
        scratch_shapes=[
            pltpu.VMEM((count, width), floats),
            pltpu.VMEM((count, count, width), floats),
            DMA,
        ]
        + sems,
        compiler_params=params(0),
        name="gather_inputs",
    )(style_rows, bank, parts)


def conv_kernel(
    count,
    width,
    images_ref,
    kernel_from,
    own_ref,
    gain_ref,
    conv_ref,
    conv_own_ref,
    hidden_ref,
    normed_ref,
    kernel_ref,
    kernel_sem,
    image_buf,
    padded,
    total,
    pair_out,
    pair_in,
    line_out,
    line_in,
    block_out,
    block_in,
    image_sem,
    pair_send,
    pair_recv,
    line_send,
    line_recv,
    block_send,
    block_recv,
    norm_send,
    norm_recv,
):
    row, col = lax.axis_index("dp"), lax.axis_index("pix")
    groups = count // 2
    slots = pair_out.shape[0]
    side = lax.rem(row, 2)
    level = lax.div(row, 2)
    partner = flip(row, 1)
    near, far = flip(col, 1), flip(col, 2)
    cross = flip(near, 2)
    tokens, depth = image_buf.shape[1], image_buf.shape[2]
    channels = total.shape[1]
    rows = tokens // PIX
    halo = width

    load = pltpu.make_async_copy(kernel_from, kernel_ref, kernel_sem)
    load.start()
    has_below, has_above = level > 0, level < groups - 1
    below, above = jnp.maximum(row - 2, 0), jnp.minimum(row + 2, count - 1)

    barrier = pltpu.get_barrier_semaphore()
    for known, other in ((has_below, below), (has_above, above)):

        @pl.when(known)
        def _(other=other):
            pl.semaphore_signal(barrier, inc=1, device_id=(other, col), device_id_type=MESH)

    for other in ((partner, col), (row, near), (row, far), (row, cross)):
        pl.semaphore_signal(barrier, inc=1, device_id=other, device_id_type=MESH)
    pl.semaphore_wait(barrier, 4 + has_below.astype(jnp.int32) + has_above.astype(jnp.int32))

    def group_of(step):
        return level_at(level, groups, groups - 1 - step)

    def sample_of(index):
        mine = lax.div(index, groups)
        group = group_of(lax.rem(index, groups))
        return 2 * group + jnp.where(mine == 1, side, 1 - side)

    def fetch(index):
        slot = lax.rem(index, 2)
        return pltpu.make_async_copy(
            images_ref.at[sample_of(index)], image_buf.at[slot], image_sem.at[slot]
        )

    load.wait()
    zeros = jnp.zeros((3, halo, depth), halves)
    padded[:, 0:halo, :] = zeros
    padded[:, halo + tokens : halo + tokens + halo, :] = zeros
    fetch(0).start()
    place = lax.rem(lax.broadcasted_iota(jnp.int32, (tokens, depth), 0), width)

    def stage(index):
        fetch(index).wait()

        @pl.when(index + 1 < count)
        def _():
            fetch(index + 1).start()

        source = image_buf[lax.rem(index, 2)]
        wide = source.astype(floats)
        padded[1, halo : halo + tokens, :] = source
        before = jnp.where(place == 0, 0.0, pltpu.roll(wide, 1, 0))
        padded[0, halo : halo + tokens, :] = before.astype(halves)
        after = jnp.where(place == width - 1, 0.0, pltpu.roll(wide, tokens - 1, 0))
        padded[2, halo : halo + tokens, :] = after.astype(halves)

    def rows_of(sample, start):
        acc = jnp.zeros((rows, channels), floats)
        for a in range(3):
            for b in range(3):
                window = padded[b, pl.ds(pl.multiple_of(start + a * width, 16), rows), :]
                acc = acc + jnp.dot(
                    window, kernel_ref[sample, 3 * a + b], preferred_element_type=floats
                )
        return acc

    half = tokens // 2
    per_half = PIX // 2

    def half_of(h):
        return pl.ds(h * half, half)

    def pair_copy(step, h):
        return remote(
            pair_out.at[lax.rem(step, slots), half_of(h)],
            pair_in.at[step, half_of(h)],
            pair_send.at[step, h],
            pair_recv.at[step, h],
            (partner, col),
        )

    def line_copy(step, upward, h):
        group = group_of(step)
        if upward:
            slot, target = group, above
        else:
            slot, target = jnp.where(group == level - 1, groups, group), below
        return remote(
            line_out.at[lax.rem(step, slots), half_of(h)],
            line_in.at[slot, half_of(h)],
            line_send.at[step, h],
            line_recv.at[slot, h],
            (target, col),
        )

    def line_arrives(slot, h):
        remote(
            line_out.at[0, half_of(h)],
            line_in.at[slot, half_of(h)],
            line_send.at[0, h],
            line_recv.at[slot, h],
            (partner, col),
        ).wait_recv()

    def give(step):
        @pl.when(step >= slots)
        def _():
            for h in range(2):
                pair_copy(step - slots, h).wait_send()

        stage(step)
        sample = sample_of(step)
        for h in range(2):

            def chunk(i, h=h):
                start = pl.multiple_of(h * half + i * rows, rows)
                pair_out[lax.rem(step, slots), pl.ds(start, rows), :] = rows_of(
                    sample, start
                ).astype(halves)

            loop(per_half, chunk)
            pair_copy(step, h).start()

    loop(groups, give)

    def keep(step):
        @pl.when(step >= slots)
        def _():
            for h in range(2):
                line_copy(step - slots, True, h).wait_send()

        stage(groups + step)
        group = group_of(step)
        sample = 2 * group + side
        out = lax.rem(step, slots)

        def chunk(i):
            start = pl.multiple_of(i * rows, rows)
            total[pl.ds(start, rows), :] = rows_of(sample, start)

        loop(PIX, chunk)
        passing = jnp.where(group > level, has_below, has_above)
        for h in range(2):
            pair_copy(step, h).wait_recv()

            @pl.when(passing)
            def _(h=h):
                line_arrives(group, h)

                def add(i):
                    here = pl.ds(pl.multiple_of(h * half + i * rows, rows), rows)
                    line_out[out, here, :] = (
                        total[here, :]
                        + pair_in[step, here, :].astype(floats)
                        + line_in[group, here, :].astype(floats)
                    ).astype(halves)

                loop(per_half, add)

            @pl.when(jnp.logical_not(passing))
            def _(h=h):
                def add(i):
                    here = pl.ds(pl.multiple_of(h * half + i * rows, rows), rows)
                    line_out[out, here, :] = (
                        total[here, :] + pair_in[step, here, :].astype(floats)
                    ).astype(halves)

                loop(per_half, add)

            @pl.when(group > level)
            def _(h=h):
                line_copy(step, True, h).start()

            @pl.when(group < level)
            def _(h=h):
                line_copy(step, False, h).start()

    loop(groups - 1, keep)
    last = groups - 1
    stage(count - 1)

    def own_chunk(i):
        start = pl.multiple_of(i * rows, rows)
        total[pl.ds(start, rows), :] = rows_of(row, start)

    loop(PIX, own_chunk)
    for h in range(2):
        for known, slot in ((has_below, level), (has_above, groups)):

            @pl.when(known)
            def _(slot=slot, h=h):
                line_arrives(slot, h)

                def add(i):
                    here = pl.ds(pl.multiple_of(h * half + i * rows, rows), rows)
                    total[here, :] += line_in[slot, here, :].astype(floats)

                loop(per_half, add)

        pair_copy(last, h).wait_recv()

    short = rows // 2
    part = rows // 4

    def block_copy(turn, i, origin=None):
        here = pl.ds(i * short, short)
        return remote(
            block_out.at[turn, here],
            block_in.at[col if origin is None else origin, here],
            block_send.at[2 * turn + i],
            block_recv.at[2 * turn + i],
            (row, (far, cross, near)[turn]),
        )

    for i in range(2):
        for turn, target in enumerate((far, cross, near, col)):
            here = pl.ds(pl.multiple_of(target * rows + i * short, short), short)
            rounded = (total[here, :] + pair_in[last, here, :].astype(floats)).astype(halves)
            conv_own_ref[here, :] = rounded
            if turn < 3:
                block_out[turn, i * short : (i + 1) * short, :] = rounded
                block_copy(turn, i).start()
            else:
                block_in[col, i * short : (i + 1) * short, :] = rounded

    def norm_rows(i):
        here = pl.ds(pl.multiple_of(i * part, part), part)
        for j in range(PIX):
            conv_ref[here, j * channels : (j + 1) * channels] = block_in[j, here, :]
        conv = conv_ref[here, :].astype(floats)
        hidden = own_ref[here, :].astype(floats) + conv * jax.nn.sigmoid(conv)
        hidden_ref[here, :] = hidden
        mean = jnp.mean(hidden * hidden, -1, keepdims=True)
        normed_ref[col, here, :] = (hidden * lax.rsqrt(mean + 1e-06) * gain_ref[...]).astype(halves)

    def norm_copy(hop, i, block):
        source = normed_ref.at[block, pl.ds(i * short, short)]
        index = 2 * hop + i
        return remote(
            source, source, norm_send.at[index], norm_recv.at[index], (row, far if hop == 0 else near)
        )

    for i in range(2):
        for turn, origin in enumerate((far, cross, near)):
            block_copy(turn, i, origin).wait_recv()
        norm_rows(2 * i)
        norm_rows(2 * i + 1)
        norm_copy(0, i, col).start()
        norm_copy(1, i, col).start()
    for i in range(2):
        norm_copy(0, i, far).wait_recv()
        norm_copy(2, i, far).start()
    for i in range(2):
        norm_copy(1, i, near).wait_recv()
        norm_copy(2, i, cross).wait_recv()
        for hop, block in enumerate((col, col, far)):
            norm_copy(hop, i, block).wait_send()
        for turn in range(3):
            block_copy(turn, i).wait_send()
        for step in range(max(0, groups - slots), groups):
            pair_copy(step, i).wait_send()
        for step in range(max(0, groups - 1 - slots), groups - 1):
            line_copy(step, True, i).wait_send()


def conv_forward(images_all, kernels, own, gain, width):
    count, tokens, depth = images_all.shape
    channels = kernels.shape[-1]
    rows, full = own.shape
    groups = count // 2
    slots = min(groups, 4)
    block = (tokens, channels)
    return pl.pallas_call(
        partial(conv_kernel, count, width),
        out_shape=(
            jax.ShapeDtypeStruct((rows, full), halves),
            jax.ShapeDtypeStruct((tokens, channels), halves),
            jax.ShapeDtypeStruct((rows, full), floats),
            jax.ShapeDtypeStruct((PIX, rows, full), halves),
        ),
        in_specs=[ANY, ANY, VMEM, VMEM],
        out_specs=(VMEM, VMEM, VMEM, VMEM),
        scratch_shapes=[
            pltpu.VMEM(kernels.shape, halves),
            DMA,
            pltpu.VMEM((2, tokens, depth), halves),
            pltpu.VMEM((3, tokens + 2 * width, depth), halves),
            pltpu.VMEM(block, floats),
            pltpu.VMEM((slots,) + block, halves),
            pltpu.VMEM((groups,) + block, halves),
            pltpu.VMEM((slots,) + block, halves),
            pltpu.VMEM((groups + 1,) + block, halves),
            pltpu.VMEM((3, rows, channels), halves),
            pltpu.VMEM((PIX, rows, channels), halves),
            DMA((2,)),
            DMA((groups, 2)),
            DMA((groups, 2)),
            DMA((groups, 2)),
            DMA((groups + 1, 2)),
            DMA((6,)),
            DMA((6,)),
            DMA((6,)),
            DMA((6,)),
        ],
        compiler_params=params(1),
        name="conv_forward",
    )(images_all, kernels, own, gain.reshape(1, -1))


def peers(col):
    near, far = flip(col, 1), flip(col, 2)
    return near, far, flip(near, 2)


def greet_pixels(row, others):
    barrier = pltpu.get_barrier_semaphore()
    for other in others:
        pl.semaphore_signal(barrier, inc=1, device_id=(row, other), device_id_type=MESH)
    pl.semaphore_wait(barrier, len(others))


NT = (((1,), (1,)), ((), ()))
TN = (((0,), (0,)), ((), ()))


def mul_nt(a, b, precision=None):
    return lax.dot_general(a, b, NT, preferred_element_type=floats, precision=precision)


def mul_tn(a, b, precision=None):
    return lax.dot_general(a, b, TN, preferred_element_type=floats, precision=precision)


def mul(a, b):
    return jnp.dot(a, b, preferred_element_type=floats)


def split(value):
    high = value.astype(halves)
    rest = value - high.astype(floats)
    middle = rest.astype(halves)
    return high, middle, (rest - middle.astype(floats)).astype(halves)


def exact(product, left, right):
    count = left.shape[0]
    found = product(jnp.concatenate(split(left), axis=0), right)
    return found[2 * count :] + found[count : 2 * count] + found[:count]


def outer_sum(left, right):
    lefts, rights = split(left), split(right)
    pairs = ((0, 2), (2, 0), (1, 1), (0, 1), (1, 0), (0, 0))
    return mul_tn(
        jnp.concatenate([lefts[i] for i, _ in pairs], axis=0),
        jnp.concatenate([rights[j] for _, j in pairs], axis=0),
    )


def attend_kernel(
    normed_from,
    weight_from,
    text_ref,
    query_ref,
    key_ref,
    value_ref,
    total_ref,
    attended_ref,
    text_out_ref,
    normed_ref,
    weight_ref,
    load_sem,
    block_out,
    key_norm,
    block_send,
    block_recv,
    text_send,
    text_recv,
):
    row, col = lax.axis_index("dp"), lax.axis_index("pix")
    near, far, cross = peers(col)
    targets = (far, cross, near)
    loads = [
        pltpu.make_async_copy(weight_from, weight_ref, load_sem.at[0]),
        pltpu.make_async_copy(normed_from, normed_ref, load_sem.at[1]),
    ]
    for load in loads:
        load.start()
    greet_pixels(row, targets)
    for load in loads:
        load.wait()
    rows = normed_ref.shape[1]
    width = query_ref.shape[1]
    heads = width // HEAD_DIM
    score_scale = HEAD_DIM ** (-0.5)

    for j in range(2):
        here = slice(j * width, (j + 1) * width)
        weight = weight_ref[:, (3 + j) * width : (4 + j) * width]
        text_out_ref[col, :, here] = mul(text_ref[...], weight).astype(halves)

    def text_copy(turn):
        block = text_out_ref.at[col]
        return remote(block, block, text_send.at[turn], text_recv.at[turn], (row, targets[turn]))

    for turn in range(3):
        text_copy(turn).start()

    def project(i):
        source = normed_ref[i]
        here = pl.ds(pl.multiple_of(i * rows, rows), rows)
        for j, out in enumerate((query_ref, key_ref, value_ref)):
            out[here, :] = mul(source, weight_ref[:, j * width : (j + 1) * width]).astype(halves)

    loop(PIX, project)
    ones = jnp.ones((8, HEAD_DIM), floats)
    for h in range(heads):
        key = key_ref[:, h * HEAD_DIM : (h + 1) * HEAD_DIM].astype(floats)
        key_norm[h] = score_scale * mul_nt(ones, key * key, highest)

    def attend(target, store):
        here = pl.ds(pl.multiple_of(target * rows, rows), rows)
        for h in range(heads):
            lanes = slice(h * HEAD_DIM, (h + 1) * HEAD_DIM)
            inner = mul_nt(query_ref[here, lanes], key_ref[:, lanes])
            scores = (2.0 * score_scale) * inner - key_norm[h, 0:1, :]
            largest = jnp.max(scores, -1, keepdims=True)
            expanded = jnp.exp(scores - largest)
            summed = jnp.sum(expanded, -1, keepdims=True)
            weights = (expanded * (1.0 / summed)).astype(halves)
            store(lanes, mul(weights, value_ref[:, lanes]).astype(halves))
            total_ref[here, h : h + 1] = largest + jnp.log(summed)

    def block_copy(turn):
        return remote(
            block_out.at[turn],
            attended_ref.at[col],
            block_send.at[turn],
            block_recv.at[turn],
            (row, targets[turn]),
        )

    def turn_body(turn):
        target = jnp.where(turn == 0, far, jnp.where(turn == 1, cross, jnp.where(turn == 2, near, col)))

        def store(lanes, result):
            block_out[turn, :, lanes] = result

        attend(target, store)
        for k in range(3):

            @pl.when(turn == k)
            def _(k=k):
                block_copy(k).start()

    loop(4, turn_body)
    attended_ref[col] = block_out[3]
    for turn in range(3):
        remote(
            block_out.at[turn],
            attended_ref.at[targets[turn]],
            block_send.at[turn],
            block_recv.at[turn],
            (row, near),
        ).wait_recv()
        block = text_out_ref.at[targets[turn]]
        remote(block, block, text_send.at[turn], text_recv.at[turn], (row, near)).wait_recv()
    for turn in range(3):
        block_copy(turn).wait_send()
        text_copy(turn).wait_send()


def attend_forward(normed, weights, text):
    count, rows, full = normed.shape
    tokens, width = count * rows, weights.shape[1] // 5
    heads = width // HEAD_DIM
    flat = jax.ShapeDtypeStruct((tokens, width), halves)
    return pl.pallas_call(
        attend_kernel,
        out_shape=(
            flat,
            flat,
            flat,
            jax.ShapeDtypeStruct((tokens, 128), floats),
            jax.ShapeDtypeStruct((PIX, rows, width), halves),
            jax.ShapeDtypeStruct((PIX, text.shape[0], 2 * width), halves),
        ),
        in_specs=[ANY, ANY, VMEM],
        out_specs=(VMEM,) * 6,
        scratch_shapes=[
            pltpu.VMEM(normed.shape, halves),
            pltpu.VMEM(weights.shape, halves),
            DMA((2,)),
            pltpu.VMEM((4, rows, width), halves),
            pltpu.VMEM((heads, 8, tokens), floats),
            DMA((3,)),
            DMA((3,)),
            DMA((3,)),
            DMA((3,)),
        ],
        compiler_params=params(2),
        name="attend_forward",
    )(normed, weights, text)


def cross_kernel(
    words,
    attended_ref,
    hidden_ref,
    weight_from,
    text_ref,
    gain_ref,
    rgb_scale_ref,
    rgb_weight_ref,
    cotangent_ref,
    rgb_cotangent_ref,
    penalty_ref,
    output_ref,
    rgb_ref,
    reduced_ref,
    text_grad_ref,
    grad_two_ref,
    grad_attended_ref,
    small_ref,
    attended,
    grad_attn,
    normed,
    grad_query,
    two,
    query,
    probs,
    crossed,
    mixed,
    grad_three,
    grad_proj,
    grad_crossed,
    grad_norm,
    weight_ref,
    weight_sem,
    near_out,
    near_in,
    kept,
    line_out,
    line_in,
    near_send,
    near_recv,
    line_send,
    line_recv,
):
    row, col = lax.axis_index("dp"), lax.axis_index("pix")
    near, far, cross = peers(col)
    rows, full = hidden_ref.shape
    tile = full // PIX
    loads = []
    for i in range(3):
        lanes = pl.ds(i * tile, tile)
        loads.append(
            pltpu.make_async_copy(
                weight_from.at[:, :, lanes], weight_ref.at[:, :, lanes], weight_sem.at[i]
            )
        )
        loads[i].start()
    greet_pixels(row, (near, far))
    score_scale = HEAD_DIM ** (-0.5)
    W_OUT, C_QUERY, C_OUT = (slice(i * tile, (i + 1) * tile) for i in range(3))
    part = 64

    def cols(j):
        return pl.ds(pl.multiple_of(j * tile, tile), tile)

    def near_copy(which):
        return remote(
            near_out.at[which], near_in.at[which], near_send.at[which], near_recv.at[which], (row, near)
        )

    def line_copy(which):
        return remote(
            line_out.at[which], line_in.at[which], line_send.at[which], line_recv.at[which], (row, far)
        )

    def start_grad(which, left, right):
        def tile_of(index, targets):
            i, b = lax.div(index, 2), lax.rem(index, 2)
            return i, b, mul_tn(left[:, cols(i)], right[:, cols(jnp.where(b == 0, *targets))])

        def give(index):
            i, b, value = tile_of(index, (near, cross))
            near_out[which, b, cols(i), :] = value.astype(halves)

        def keep(index):
            i, b, value = tile_of(index, (col, far))
            kept[which, b, cols(i), :] = value

        loop(2 * PIX, give)
        near_copy(which).start()
        loop(2 * PIX, keep)

    def pass_grad(which):
        near_copy(which).wait_recv()

        def add(i):
            here = cols(i)
            line_out[which, here, :] = (
                kept[which, 1, here, :] + near_in[which, 1, here, :].astype(floats)
            ).astype(halves)

        loop(PIX, add)
        line_copy(which).start()

    def end_grad(which):
        line_copy(which).wait_recv()

        def add(i):
            here = cols(i)
            reduced_ref[here, which * tile : (which + 1) * tile] = (
                kept[which, 0, here, :]
                + near_in[which, 0, here, :].astype(floats)
                + line_in[which, here, :].astype(floats)
            ).astype(halves)

        loop(PIX, add)
        near_copy(which).wait_send()
        line_copy(which).wait_send()

    for j in range(PIX):
        attended[:, j * tile : (j + 1) * tile] = attended_ref[j]

    def out_two(j):
        two[:, cols(j)] = hidden_ref[:, cols(j)] + mul(attended[...], weight_ref[j, :, W_OUT])

    loads[0].wait()
    loop(PIX, out_two)

    def norm_two(i):
        here = pl.ds(pl.multiple_of(i * part, part), part)
        hidden = two[here, :]
        mean = jnp.mean(hidden * hidden, -1, keepdims=True)
        normed[here, :] = (hidden * lax.rsqrt(mean + 1e-06) * gain_ref[...]).astype(halves)

    loop(rows // part, norm_two)

    def out_query(j):
        query[:, cols(j)] = mul(normed[...], weight_ref[j, :, C_QUERY]).astype(halves)

    loads[1].wait()
    loop(PIX, out_query)
    slots = text_ref.shape[1]
    known = lax.broadcasted_iota(jnp.int32, (rows, slots), 1) < words
    pairs = tile // 128

    def text_lanes(pair, side):
        return pl.ds(pl.multiple_of(side * tile + lax.rem(pair, pairs) * 128, 128), 128)

    def cross_pair(pair):
        here = pl.ds(pl.multiple_of(pair * 128, 128), 128)
        group = lax.div(pair, pairs)
        queries = query[:, here]
        keys = text_ref[group, :, text_lanes(pair, 0)]
        values = text_ref[group, :, text_lanes(pair, 1)]
        outs = []
        for h in range(2):
            lanes = slice(h * HEAD_DIM, (h + 1) * HEAD_DIM)
            scores = score_scale * mul_nt(queries[:, lanes], keys[:, lanes])
            scores = jnp.where(known, scores, -1e30)
            expanded = jnp.exp(scores - jnp.max(scores, -1, keepdims=True))
            prob = expanded / jnp.sum(expanded, -1, keepdims=True)
            probs[2 * pair + h] = prob
            outs.append(mul(prob.astype(halves), values[:, lanes]))
        crossed[:, here] = jnp.concatenate(outs, axis=1).astype(halves)

    def cross_four(i):
        cross_pair(2 * i)
        cross_pair(2 * i + 1)

    loop(full // 256, cross_four)
    rgb_ref[...] = jnp.zeros_like(rgb_ref)

    def out_three(j):
        three = two[:, cols(j)] + mul(crossed[...], weight_ref[j, :, C_OUT])
        output_ref[:, cols(j)] = three
        blend = (three * rgb_scale_ref[:, cols(j)]).astype(halves)
        mixed[:, cols(j)] = blend
        rgb_ref[...] += mul(blend, rgb_weight_ref[cols(j), :])

    loads[2].wait()
    loop(PIX, out_three)
    rgb_grad = rgb_cotangent_ref[...] + penalty_weight * penalty_ref[...] * rgb_ref[...]

    def back_three(j):
        color = mul_tn(rgb_grad, mixed[:, cols(j)].astype(floats), highest)
        small_ref[2:5, cols(j)] = color[0:3]
        grad_mixed = mul_nt(rgb_grad, rgb_weight_ref[cols(j), :].astype(floats), highest)
        small_ref[1:2, cols(j)] = jnp.sum(grad_mixed * output_ref[:, cols(j)], 0, keepdims=True)
        grad = cotangent_ref[:, cols(j)].astype(floats) + grad_mixed * rgb_scale_ref[:, cols(j)]
        grad_three[:, cols(j)] = grad
        grad_proj[:, cols(j)] = grad.astype(halves)

    loop(PIX, back_three)
    start_grad(0, crossed, grad_proj)

    def times_transposed(source, j, which):
        acc = jnp.zeros((rows, tile), floats)
        for i in range(PIX):
            acc = acc + mul_nt(source[:, i * tile : (i + 1) * tile], weight_ref[i, cols(j), which])
        return acc

    def back_crossed(j):
        grad_crossed[:, cols(j)] = times_transposed(grad_proj, j, C_OUT).astype(halves)

    loop(PIX, back_crossed)
    pass_grad(0)

    def back_pair(pair):
        here = pl.ds(pl.multiple_of(pair * 128, 128), 128)
        group = lax.div(pair, pairs)
        queries, grads = query[:, here], grad_crossed[:, here]
        keys = text_ref[group, :, text_lanes(pair, 0)]
        values = text_ref[group, :, text_lanes(pair, 1)]
        grad_q, grad_k, grad_v = [], [], []
        for h in range(2):
            lanes = slice(h * HEAD_DIM, (h + 1) * HEAD_DIM)
            prob = probs[2 * pair + h]
            grad = grads[:, lanes]
            grad_prob = mul_nt(grad, values[:, lanes])
            grad_v.append(mul_tn(prob.astype(halves), grad))
            inner = jnp.sum(grad_prob * prob, -1, keepdims=True)
            score = (prob * (grad_prob - inner)).astype(halves)
            grad_q.append(score_scale * mul(score, keys[:, lanes]))
            grad_k.append(score_scale * mul_tn(score, queries[:, lanes]))
        grad_query[:, here] = jnp.concatenate(grad_q, axis=1).astype(halves)
        text_grad_ref[group, :, text_lanes(pair, 0)] = jnp.concatenate(grad_k, axis=1).astype(halves)
        text_grad_ref[group, :, text_lanes(pair, 1)] = jnp.concatenate(grad_v, axis=1).astype(halves)

    def back_four(i):
        back_pair(2 * i)
        back_pair(2 * i + 1)

    loop(full // 256, back_four)

    def back_query(j):
        grad_norm[:, cols(j)] = times_transposed(grad_query, j, C_QUERY)

    loop(PIX, back_query)
    small_ref[0:1, :] = jnp.zeros((1, full), floats)

    def back_norm(i):
        here = pl.ds(pl.multiple_of(i * part, part), part)
        hidden, grad = two[here, :], grad_norm[here, :]
        inverse = lax.rsqrt(jnp.mean(hidden * hidden, -1, keepdims=True) + 1e-06)
        small_ref[0:1, :] += jnp.sum(grad * hidden * inverse, 0, keepdims=True)
        scaled = grad * gain_ref[...]
        mean = jnp.mean(scaled * hidden, -1, keepdims=True)
        total = grad_three[here, :] + inverse * scaled - hidden * (inverse * inverse * inverse * mean)
        grad_two_ref[here, :] = total
        grad_attn[here, :] = total.astype(halves)

    loop(rows // part, back_norm)

    def back_attended(j):
        grad_attended_ref[j] = times_transposed(grad_attn, j, W_OUT).astype(halves)

    loop(PIX, back_attended)

    small_ref[5:8, :] = jnp.zeros((3, full), floats)
    end_grad(0)


def cross_part(
    words, attended, hidden, weights, text, gain, rgb_scale, rgb_weight, cotangent, rgb_cotangent, penalty
):
    rows, full = hidden.shape
    tile = full // PIX
    heads = full // HEAD_DIM
    wide = pltpu.VMEM((rows, full), floats)
    slim = pltpu.VMEM((rows, full), halves)
    return pl.pallas_call(
        partial(cross_kernel, words),
        out_shape=(
            jax.ShapeDtypeStruct((rows, full), floats),
            jax.ShapeDtypeStruct((rows, 128), floats),
            jax.ShapeDtypeStruct((full, tile), halves),
            jax.ShapeDtypeStruct(text.shape, halves),
            jax.ShapeDtypeStruct((rows, full), floats),
            jax.ShapeDtypeStruct((PIX, rows, tile), halves),
            jax.ShapeDtypeStruct((8, full), floats),
        )
        + (jax.ShapeDtypeStruct((rows, full), halves),) * 4,
        in_specs=[VMEM, VMEM, ANY] + [VMEM] * 7,
        out_specs=(VMEM,) * 11,
        scratch_shapes=[
            wide,
            slim,
            pltpu.VMEM((heads, rows, text.shape[1]), floats),
            slim,
            slim,
            wide,
            slim,
            slim,
            wide,
            pltpu.VMEM(weights.shape, halves),
            DMA((3,)),
            pltpu.VMEM((1, 2, full, tile), halves),
            pltpu.VMEM((1, 2, full, tile), halves),
            pltpu.VMEM((1, 2, full, tile), floats),
            pltpu.VMEM((1, full, tile), halves),
            pltpu.VMEM((1, full, tile), halves),
            DMA((1,)),
            DMA((1,)),
            DMA((1,)),
            DMA((1,)),
        ],
        compiler_params=params(6),
        name="cross_part",
    )(
        attended,
        hidden,
        weights,
        text,
        gain.reshape(1, -1),
        rgb_scale,
        rgb_weight,
        cotangent,
        rgb_cotangent,
        penalty,
    )


def group_copy(turn, source, landed, send, recv):
    row, col = lax.axis_index("dp"), lax.axis_index("pix")
    near, far, cross = peers(col)
    target = (far, cross, near)[turn]
    return remote(source, landed.at[turn], send.at[turn], recv.at[turn], (row, target))


def group_sum(source, landed, send, recv):
    col = lax.axis_index("pix")
    _, far, cross = peers(col)
    for turn in range(3):
        group_copy(turn, source, landed, send, recv).wait()
    landed[3] = source[...]
    total = None
    for which in range(PIX):
        turn = jnp.where(
            which == col, 3, jnp.where(which == far, 0, jnp.where(which == cross, 1, 2))
        )
        total = landed[turn] if total is None else total + landed[turn]
    return total


def far_copy_of(k, total, everyone, send, recv):
    row, col = lax.axis_index("dp"), lax.axis_index("pix")
    other = lax.rem(row + k, everyone.shape[0])
    return remote(total, everyone.at[row], send.at[k], recv.at[k], (other, col))


def far_start(total, everyone, send, recv, sem):
    row, count = lax.axis_index("dp"), everyone.shape[0]
    pltpu.make_async_copy(total, everyone.at[row], sem).start()
    lax.fori_loop(
        1, count, lambda k, c: (far_copy_of(k, total, everyone, send, recv).start(), c)[1], 0
    )


def far_end(total, everyone, send, recv, sem):
    row, col = lax.axis_index("dp"), lax.axis_index("pix")
    count = everyone.shape[0]
    pltpu.make_async_copy(total, everyone.at[row], sem).wait()

    def arrive(k, carry):
        origin = lax.rem(row - k + count, count)
        remote(
            total, everyone.at[origin], send.at[k], recv.at[k], (row, flip(col, 1))
        ).wait_recv()
        return carry

    lax.fori_loop(1, count, arrive, 0)
    lax.fori_loop(
        1, count, lambda k, c: (far_copy_of(k, total, everyone, send, recv).wait_send(), c)[1], 0
    )


def attend_back_kernel(
    grad_ref,
    query_ref,
    key_ref,
    value_ref,
    total_ref,
    normed_from,
    weight_from,
    hidden_from,
    conv_from,
    grad_two_from,
    gain_ref,
    text_ref,
    text_grad_ref,
    reduced_ref,
    attended_ref,
    grad_attn_ref,
    normed_two_ref,
    grad_cross_ref,
    rows_ref,
    attention_ref,
    others_ref,
    text_owned_ref,
    grad_one_ref,
    grad_conv_ref,
    last_ref,
    rows_all_ref,
    small_ref,
    rows_in,
    rows_sum,
    normed_ref,
    weight_ref,
    hidden_ref,
    conv_ref,
    grad_two_ref,
    load_sem,
    grads,
    grad_query,
    grad_key,
    grad_value,
    key_acc,
    value_acc,
    totals,
    pair_out,
    pair_in,
    line_out,
    line_in,
    own,
    conv_out,
    text_in,
    near_out,
    near_in,
    near_kept,
    far_out,
    far_in,
    side_in,
    level_out,
    level_in,
    out_grad,
    out_side_in,
    out_level_out,
    out_level_in,
    words_grad,
    words_side_in,
    words_level_out,
    words_level_in,
    attention_grad,
    attention_in,
    attention_out,
    attention_landed,
    grad_send,
    grad_recv,
    text_send,
    text_recv,
    pair_send,
    pair_recv,
    line_send,
    line_recv,
    conv_send,
    conv_recv,
    near_send,
    near_recv,
    far_send,
    far_recv,
    attention_send,
    attention_recv,
    landed_send,
    landed_recv,
    rows_send,
    rows_recv,
    far_rows_send,
    far_rows_recv,
    rows_sem,
    *reduce_sems,
):
    row, col = lax.axis_index("dp"), lax.axis_index("pix")
    near, far, cross = peers(col)
    targets = (far, cross, near)
    _, groups, _, owned, _ = attention_grad.shape
    side, level = lax.rem(row, 2), lax.div(row, 2)
    partner = flip(row, 1)
    loads = [
        pltpu.make_async_copy(source, buffer, load_sem.at[i])
        for i, (source, buffer) in enumerate(
            (
                (normed_from, normed_ref),
                (weight_from.at[:, pl.ds(0, weight_ref.shape[1])], weight_ref),
                (hidden_from, hidden_ref),
                (conv_from, conv_ref),
                (grad_two_from, grad_two_ref),
            )
        )
    ]
    for load in loads:
        load.start()
    greet(2 * groups, [(row, near), (row, far), (row, cross)])
    rows_group = (rows_ref, rows_in, rows_send, rows_recv)
    rows_far = (rows_sum, rows_all_ref, far_rows_send, far_rows_recv, rows_sem)
    rows, full = hidden_ref.shape
    tokens, width = query_ref.shape
    heads = width // HEAD_DIM
    score_scale = HEAD_DIM ** (-0.5)

    def grad_copy(turn):
        return remote(
            grad_ref.at[targets[turn]],
            grads.at[col],
            grad_send.at[turn],
            grad_recv.at[turn],
            (row, targets[turn]),
        )

    used = text_in.shape[1]

    def text_copy(turn):
        return remote(
            text_grad_ref.at[targets[turn], pl.ds(0, used), :],
            text_in.at[turn],
            text_send.at[turn],
            text_recv.at[turn],
            (row, targets[turn]),
        )

    for turn in range(3):
        grad_copy(turn).start()
    for turn in range(3):
        text_copy(turn).start()

    def reduction(which, source, arrived, out, landed):
        side_send, side_recv, level_send, level_recv = reduce_sems[4 * which : 4 * which + 4]

        def to_side():
            return remote(source.at[:, 1 - side], arrived, side_send, side_recv, (partner, col))

        def to_level(k):
            group = lax.rem(level + k, groups)
            return remote(
                out.at[group], landed.at[k], level_send.at[k], level_recv.at[k], (2 * group + side, col)
            )

        def middle():
            to_side().wait_recv()

            def add(group):
                out[group] = (
                    source[group, side].astype(floats) + arrived[group].astype(floats)
                ).astype(halves)

            loop(groups, add)
            lax.fori_loop(1, groups, lambda k, c: (to_level(k).start(), c)[1], 0)

        def finish():
            total = out[level].astype(floats)
            for k in range(1, groups):
                to_level(k).wait()
                total = total + landed[k].astype(floats)
            to_side().wait_send()
            return total.astype(halves)

        return to_side, middle, finish

    sides = reduction(0, reduced_ref, side_in, level_out, level_in)
    word = reduction(1, words_grad, words_side_in, words_level_out, words_level_in)
    outs = [
        reduction(
            2 + w, out_grad.at[w], out_side_in.at[w], out_level_out.at[w], out_level_in.at[w]
        )
        for w in range(2)
    ]
    sides[0]().start()
    for turn in range(3):
        group_copy(turn, *rows_group).start()

    def near_copy(which):
        return remote(
            near_out.at[which], near_in.at[which], near_send.at[which], near_recv.at[which], (row, near)
        )

    def far_copy(which):
        return remote(
            far_out.at[which], far_in.at[which], far_send.at[which], far_recv.at[which], (row, far)
        )

    def row_tile(i):
        return pl.ds(pl.multiple_of(i * width, width), width)

    lefts, rights = (attended_ref, normed_two_ref), (grad_attn_ref, grad_cross_ref)
    per_tile = width // (2 * owned)
    for which in range(2):

        def out_tile(index, first, second, which=which):
            i, b = lax.div(index, 2), lax.rem(index, 2)
            right = rights[which][:, row_tile(jnp.where(b == 0, first, second))]
            return i, b, mul_tn(lefts[which][:, row_tile(i)], right)

        def out_give(index, which=which, out_tile=out_tile):
            i, b, value = out_tile(index, near, cross)
            near_out[which, b, row_tile(i), :] = value.astype(halves)

        def out_keep(index, which=which, out_tile=out_tile):
            i, b, value = out_tile(index, col, far)
            near_kept[which, b, row_tile(i), :] = value

        loop(2 * PIX, out_give)
        near_copy(which).start()
        loop(2 * PIX, out_keep)

    def out_pass():
        for which in range(2):
            near_copy(which).wait_recv()

            def add(i, which=which):
                here = row_tile(i)
                far_out[which, here, :] = (
                    near_kept[which, 1, here, :] + near_in[which, 1, here, :].astype(floats)
                ).astype(halves)

            loop(PIX, add)
            far_copy(which).start()

    def out_end(which):
        far_copy(which).wait_recv()

        def add(i):
            here = row_tile(i)
            value = (
                near_kept[which, 0, here, :]
                + near_in[which, 0, here, :].astype(floats)
                + far_in[which, here, :].astype(floats)
            ).astype(halves)
            out_grad[which, pl.ds(i * per_tile, per_tile)] = value.reshape(
                per_tile, 2, owned, width
            )

        loop(PIX, add)
        outs[which][0]().start()

    def words_grads():
        text_total = text_grad_ref[col, 0:used, :].astype(floats)
        for turn in range(3):
            text_copy(turn).wait_recv()
            text_total = text_total + text_in[turn].astype(floats)
        text_total = jnp.concatenate(
            [text_total, jnp.zeros((text_ref.shape[0] - used, 2 * width), floats)], axis=0
        )

        def put(j):
            for k in range(2):
                right = text_total[:, k * width : (k + 1) * width]
                value = mul_tn(text_ref[:, row_tile(j)].astype(floats), right, highest)
                words_grad[pl.ds(j * per_tile, per_tile), :, :, k * width : (k + 1) * width] = (
                    value.astype(halves).reshape(per_tile, 2, owned, width)
                )

        loop(full // width, put)
        word[0]().start()

    def attention_copy(part, j):
        here = pl.ds(j * per_tile, per_tile)
        return remote(
            attention_grad.at[part, here, 1 - side],
            attention_in.at[part, here],
            attention_send.at[part, j],
            attention_recv.at[part, j],
            (partner, col),
        )

    def weight_grads(part):
        lanes = slice(part * 128, (part + 1) * 128)

        def tile(j):
            here = pl.ds(j * per_tile, per_tile)
            for k, right in enumerate((grad_query, grad_key, grad_value)):
                acc = jnp.zeros((width, 128), floats)
                for i in range(PIX):
                    acc = acc + mul_tn(
                        normed_ref[i, :, row_tile(j)], right[i * rows : (i + 1) * rows, lanes]
                    )
                attention_grad[part, here, :, :, k * 128 : (k + 1) * 128] = acc.astype(
                    halves
                ).reshape(per_tile, 2, owned, 128)
            attention_copy(part, j).start()

        loop(full // width, tile)

    def landed_copy(k):
        group = lax.rem(level + k, groups)
        return remote(
            attention_out.at[group],
            attention_landed.at[k],
            landed_send.at[k],
            landed_recv.at[k],
            (2 * group + side, col),
        )

    def attention_sum(part, out):
        def add(j):
            attention_copy(part, j).wait_recv()
            here = pl.ds(j * per_tile, per_tile)
            out[here] = (
                attention_grad[part, here, side].astype(floats)
                + attention_in[part, here].astype(floats)
            ).astype(halves)

        loop(full // width, add)

    def attention_level():
        attention_sum(0, attention_out)
        lax.fori_loop(1, groups, lambda k, c: (landed_copy(k).start(), c)[1], 0)

    def between(h):
        if h == 0:
            words_grads()
            sides[1]()
        if h == 1:
            for load in loads:
                load.wait()
            weight_grads(0)
            rows_sum[...] = group_sum(*rows_group)
            far_start(*rows_far)
        if h == 2:
            word[1]()
            out_end(0)
        if h == 3:
            out_end(1)
            attention_level()

    grads[col] = grad_ref[col]
    totals[...] = jnp.transpose(total_ref[...])
    for turn in range(3):
        remote(
            grad_ref.at[0],
            grads.at[targets[turn]],
            grad_send.at[turn],
            grad_recv.at[turn],
            (row, near),
        ).wait_recv()
    out_pass()
    ones = jnp.ones((rows, HEAD_DIM), halves)
    for h in range(heads):
        lanes = slice(h * HEAD_DIM, (h + 1) * HEAD_DIM)
        keys, values = key_ref[:, lanes], value_ref[:, lanes]
        wide = keys.astype(floats)
        norm = score_scale * jnp.sum(wide * wide, -1, keepdims=True)
        key_acc[...] = jnp.zeros_like(key_acc)
        value_acc[...] = jnp.zeros_like(value_acc)

        def block(i, lanes=lanes, keys=keys, values=values, norm=norm, h=h):
            here = pl.ds(pl.multiple_of(i * rows, rows), rows)
            queries, grad = query_ref[here, lanes], grads[i, :, lanes]
            inner = mul_nt(keys, queries)
            prob = jnp.exp((2.0 * score_scale) * inner - norm - totals[h : h + 1, here])
            grad_prob = mul_nt(values, grad)
            value_acc[...] += mul(prob.astype(halves), grad)
            mean = jnp.sum(grad_prob * prob, 0, keepdims=True)
            score = (prob * (grad_prob - mean)).astype(halves)
            key_acc[...] += mul(score, jnp.concatenate([queries, ones], axis=1))
            grad_query[here, lanes] = (2.0 * score_scale * mul_tn(score, keys)).astype(halves)

        loop(PIX, block)
        acc = key_acc[...]
        grad_key[:, lanes] = (
            2.0 * score_scale * (acc[:, :HEAD_DIM] - wide * acc[:, HEAD_DIM : HEAD_DIM + 1])
        ).astype(halves)
        grad_value[:, lanes] = value_acc[...].astype(halves)
        between(h)

    def norm_grad(block, store):
        here = pl.ds(pl.multiple_of(block * rows, rows), rows)

        def tile(j):
            cols = pl.ds(pl.multiple_of(j * width, width), width)
            acc = jnp.zeros((rows, width), floats)
            for k, source in enumerate((grad_query, grad_key, grad_value)):
                acc = acc + mul_nt(source[here, :], weight_ref[cols, k * width : (k + 1) * width])
            store(cols, acc)

        loop(full // width, tile)

    def pair_copy(turn):
        return remote(
            pair_out.at[turn], pair_in.at[turn], pair_send.at[turn], pair_recv.at[turn], (row, near)
        )

    for turn, target in enumerate((cross, near)):

        def store(cols, value, turn=turn):
            pair_out[turn, :, cols] = value.astype(halves)

        norm_grad(target, store)
        pair_copy(turn).start()
    half = rows // 2

    def line_copy(i):
        here = pl.ds(i * half, half)
        return remote(
            line_out.at[here], line_in.at[here], line_send.at[i], line_recv.at[i], (row, far)
        )

    def store_far(cols, value):
        line_out[:, cols] = (value + pair_in[0, :, cols].astype(floats)).astype(halves)

    pair_copy(0).wait_recv()
    norm_grad(far, store_far)
    line_copy(0).start()
    line_copy(1).start()

    def store_own(cols, value):
        own[:, cols] = value + pair_in[1, :, cols].astype(floats)

    pair_copy(1).wait_recv()
    norm_grad(col, store_own)

    weight_grads(1)
    outs[0][1]()
    outs[1][1]()
    small_ref[...] = jnp.zeros_like(small_ref)
    part = 64

    def back_norm(i):
        here = pl.ds(pl.multiple_of(i * part, part), part)
        hidden = hidden_ref[here, :]
        grad = own[here, :] + line_in[here, :].astype(floats)
        inverse = lax.rsqrt(jnp.mean(hidden * hidden, -1, keepdims=True) + 1e-06)
        small_ref[0:1, :] += jnp.sum(grad * hidden * inverse, 0, keepdims=True)
        scaled = grad * gain_ref[...]
        mean = jnp.mean(scaled * hidden, -1, keepdims=True)
        total = (
            grad_two_ref[here, :] + inverse * scaled - hidden * (inverse * inverse * inverse * mean)
        )
        grad_one_ref[here, :] = total
        conv = conv_ref[here, :].astype(floats)
        gate = jax.nn.sigmoid(conv)
        result = (total * gate * (1.0 + conv * (1.0 - gate))).astype(halves)
        for j in range(PIX):
            conv_out[j, here, :] = result[:, j * width : (j + 1) * width]

    def conv_copy(turn, i, block=None):
        here = pl.ds(i * half, half)
        return remote(
            conv_out.at[targets[turn], here],
            grad_conv_ref.at[col if block is None else block, here],
            conv_send.at[2 * turn + i],
            conv_recv.at[2 * turn + i],
            (row, targets[turn]),
        )

    per_half = half // part
    for i in range(2):
        line_copy(i).wait_recv()
        lax.fori_loop(i * per_half, (i + 1) * per_half, lambda j, c: (back_norm(j), c)[1], 0)
        for turn in range(3):
            conv_copy(turn, i).start()
    grad_conv_ref[col] = conv_out[col]
    for i in range(2):
        for turn in range(3):
            conv_copy(turn, i, targets[turn]).wait_recv()
    for turn in range(3):
        conv_copy(turn, 0).wait_send()
        conv_copy(turn, 1).wait_send()
        grad_copy(turn).wait_send()
        text_copy(turn).wait_send()
    for j in range(8):
        last_ref[j : j + 1, :] = small_ref[0:1, j * 128 : (j + 1) * 128]
    far_end(*rows_far)
    for w in range(2):
        others_ref[:, w * width : (w + 1) * width] = outs[w][2]()
    others_ref[:, 2 * width : 3 * width] = sides[2]()
    total = attention_out[level].astype(floats)
    for k in range(1, groups):
        landed_copy(k).wait()
        total = total + attention_landed[k].astype(floats)
    others_ref[:, 3 * width :] = total.astype(halves)
    text_owned_ref[...] = word[2]()

    attention_sum(1, attention_ref)
    for p in range(2):
        loop(full // width, lambda j, p=p: attention_copy(p, j).wait_send())
    for which in range(2):
        near_copy(which).wait_send()
        far_copy(which).wait_send()
    pair_copy(0).wait_send()
    pair_copy(1).wait_send()
    line_copy(0).wait_send()
    line_copy(1).wait_send()


def attend_backward(
    words,
    small,
    grad,
    query,
    key,
    value,
    totals,
    normed,
    weights,
    hidden,
    conv,
    grad_two,
    gain,
    text,
    text_grads,
    reduced,
    *factors,
):
    rows, full = hidden.shape
    groups, _, owned, _ = reduced.shape
    used = -(-words // 16) * 16
    tokens, width = query.shape
    flat = pltpu.VMEM((tokens, width), halves)
    return pl.pallas_call(
        attend_back_kernel,
        out_shape=(
            jax.ShapeDtypeStruct((groups, owned, 384), halves),
            jax.ShapeDtypeStruct((owned, 3 * width + 384), halves),
            jax.ShapeDtypeStruct((owned, 2 * width), halves),
            jax.ShapeDtypeStruct((rows, full), floats),
            jax.ShapeDtypeStruct((PIX, rows, width), halves),
            jax.ShapeDtypeStruct((8, 128), floats),
            jax.ShapeDtypeStruct((2 * groups,) + small.shape, floats),
        ),
        in_specs=[VMEM] * 5 + [ANY] * 5 + [VMEM] * 9,
        out_specs=(VMEM,) * 6 + (ANY,),
        scratch_shapes=[
            pltpu.VMEM((8, full), floats),
            pltpu.VMEM((4,) + small.shape, floats),
            pltpu.VMEM(small.shape, floats),
            pltpu.VMEM(normed.shape, halves),
            pltpu.VMEM((full, 3 * width), halves),
            pltpu.VMEM((rows, full), floats),
            pltpu.VMEM((rows, full), halves),
            pltpu.VMEM((rows, full), floats),
            DMA((5,)),
            pltpu.VMEM((PIX, rows, width), halves),
            flat,
            flat,
            flat,
            pltpu.VMEM((tokens, 2 * HEAD_DIM), floats),
            pltpu.VMEM((tokens, HEAD_DIM), floats),
            pltpu.VMEM((128, tokens), floats),
            pltpu.VMEM((2, rows, full), halves),
            pltpu.VMEM((2, rows, full), halves),
            pltpu.VMEM((rows, full), halves),
            pltpu.VMEM((rows, full), halves),
            pltpu.VMEM((rows, full), floats),
            pltpu.VMEM((PIX, rows, width), halves),
            pltpu.VMEM((3, used, 2 * width), halves),
            pltpu.VMEM((2, 2, full, width), halves),
            pltpu.VMEM((2, 2, full, width), halves),
            pltpu.VMEM((2, 2, full, width), floats),
            pltpu.VMEM((2, full, width), halves),
            pltpu.VMEM((2, full, width), halves),
            pltpu.VMEM((groups, owned, width), halves),
            pltpu.VMEM((groups, owned, width), halves),
            pltpu.VMEM((groups, owned, width), halves),
            pltpu.VMEM((2, groups, 2, owned, width), halves),
            pltpu.VMEM((2, groups, owned, width), halves),
            pltpu.VMEM((2, groups, owned, width), halves),
            pltpu.VMEM((2, groups, owned, width), halves),
            pltpu.VMEM((groups, 2, owned, 2 * width), halves),
            pltpu.VMEM((groups, owned, 2 * width), halves),
            pltpu.VMEM((groups, owned, 2 * width), halves),
            pltpu.VMEM((groups, owned, 2 * width), halves),
            pltpu.VMEM((2, groups, 2, owned, 384), halves),
            pltpu.VMEM((2, groups, owned, 384), halves),
            pltpu.VMEM((groups, owned, 384), halves),
            pltpu.VMEM((groups, owned, 384), halves),
            DMA((3,)),
            DMA((3,)),
            DMA((3,)),
            DMA((3,)),
            DMA((2,)),
            DMA((2,)),
            DMA((2,)),
            DMA((2,)),
            DMA((6,)),
            DMA((6,)),
            DMA((2,)),
            DMA((2,)),
            DMA((2,)),
            DMA((2,)),
            DMA((2, PIX)),
            DMA((2, PIX)),
            DMA((groups,)),
            DMA((groups,)),
            DMA((3,)),
            DMA((3,)),
            DMA((2 * groups,)),
            DMA((2 * groups,)),
            DMA,
        ]
        + [DMA, DMA, DMA((groups,)), DMA((groups,))] * 4,
        compiler_params=params(3),
        name="attend_backward",
    )(
        grad,
        query,
        key,
        value,
        totals,
        normed,
        weights,
        hidden,
        conv,
        grad_two,
        gain.reshape(1, -1),
        text,
        text_grads,
        reduced,
        *factors,
        small,
    )


def conv_back_kernel(
    count,
    width,
    images_ref,
    kernel_from,
    bank_from,
    styles_ref,
    inverse_ref,
    grad_ref,
    conv_ref,
    attention_ref,
    others_ref,
    words_ref,
    last_ref,
    bank_grad_ref,
    attention_all,
    others_all,
    words_all,
    stats_all_ref,
    image_grad_ref,
    grads_ref,
    kernel_ref,
    bank_ref,
    bank_raw,
    table_sem,
    stats_ref,
    stats_in,
    stats_sum,
    image_buf,
    padded_image,
    padded_grad,
    turned,
    acc,
    sums_out,
    sums_in,
    kept,
    kept_own,
    pixel_out,
    pixel_in,
    line_out,
    line_in,
    owner_out,
    attention_in,
    local_sem,
    image_sem,
    load_sem,
    sums_send,
    sums_recv,
    up_send,
    down_send,
    level_recv,
    pair_send,
    pair_recv,
    pixel_send,
    pixel_recv,
    line_send,
    line_recv,
    owner_send,
    owner_recv,
    attention_send,
    attention_recv,
    weight_send,
    weight_recv,
    stats_send,
    stats_recv,
    far_stats_send,
    far_stats_recv,
    stats_sem,
):
    row, col = lax.axis_index("dp"), lax.axis_index("pix")
    groups = count // 2
    side, level = lax.rem(row, 2), lax.div(row, 2)
    partner = flip(row, 1)
    near, far, cross = peers(col)
    targets = (far, cross, near)
    tokens, channels = grad_ref.shape

    buffers = (attention_all, others_all, words_all)

    def weight_copy(which, hop):
        block = buffers[which].at[far if hop == 2 else col]
        index = 3 * which + hop
        return remote(
            block, block, weight_send.at[index], weight_recv.at[index], (row, far if hop == 0 else near)
        )

    def weight_arrives(which, hop):
        block = buffers[which].at[(far, near, cross)[hop]]
        index = 3 * which + hop
        remote(block, block, weight_send.at[index], weight_recv.at[index], (row, near)).wait_recv()

    def weight_start(which):
        weight_copy(which, 0).start()
        weight_copy(which, 1).start()

    def weight_pass(which):
        weight_arrives(which, 0)
        weight_copy(which, 2).start()

    def weight_end(which):
        weight_arrives(which, 1)
        weight_arrives(which, 2)
        for hop in range(3):
            weight_copy(which, hop).wait_send()

    stats_group = (stats_ref, stats_in, stats_send, stats_recv)
    stats_far = (stats_sum, stats_all_ref, far_stats_send, far_stats_recv, stats_sem)

    def attention_copy(k):
        group = lax.rem(level + k, groups)
        return remote(
            attention_ref.at[group],
            attention_in.at[k],
            attention_send.at[k],
            attention_recv.at[k],
            (2 * group + side, col),
        )

    depth = image_buf.shape[2]
    rows = tokens // PIX
    halo = width
    greet(count, [(row, near), (row, far), (row, cross)])

    def sample_of(step):
        paired, k = turn_of(step)
        return 2 * level_at(level, groups, k) + jnp.where(paired, 1 - side, side)

    def turn_of(step):
        final = step == count - 1
        even = lax.rem(step, 2) == 0
        paired = final | (even & (step > 0))
        k = jnp.where(even, jnp.maximum(lax.div(step, 2) - 1, 0), lax.div(step + 1, 2))
        return paired, jnp.where(final, groups - 1, k)

    has_below, has_above = level > 0, level < groups - 1
    reach = jnp.minimum(level, groups - 1 - level)

    def line_block(origin, upward, source=None):
        block = grads_ref.at[2 * origin + side]
        sem = (up_send if upward else down_send).at[origin]
        target = jnp.minimum(row + 2, count - 1) if upward else jnp.maximum(row - 2, 0)
        source = block if source is None else source
        return remote(source, block, sem, level_recv.at[origin], (target, col))

    def relay(k):
        origin = level_at(level, groups, k)
        block = grads_ref.at[2 * origin + side]
        remote(
            block, block, up_send.at[origin], level_recv.at[origin], (partner, col)
        ).wait_recv()

        @pl.when((origin < level) & has_above)
        def _():
            line_block(origin, True).start()

        @pl.when((origin > level) & has_below)
        def _():
            line_block(origin, False).start()

        pair_copy(k).start()

    def pair_copy(k, source=None):
        block = grads_ref.at[2 * level_at(level, groups, k) + side]
        source = block if source is None else source
        return remote(source, block, pair_send.at[k], pair_recv.at[k], (partner, col))

    def sums_copy(k):
        return remote(
            sums_out,
            sums_in.at[row],
            sums_send.at[k],
            sums_recv.at[k],
            (lax.rem(row + k, count), col),
        )

    loads = [
        pltpu.make_async_copy(kernel_from, kernel_ref, table_sem.at[0]),
        pltpu.make_async_copy(bank_from, bank_raw, table_sem.at[1]),
    ]
    own = pltpu.make_async_copy(grad_ref, grads_ref.at[row], local_sem)
    own.start()
    for load in loads:
        load.start()

    @pl.when(has_above)
    def _():
        line_block(level, True, grad_ref).start()

    @pl.when(has_below)
    def _():
        line_block(level, False, grad_ref).start()

    pair_copy(0, grad_ref).start()

    def fetch(step):
        slot = lax.rem(step, 2)
        return pltpu.make_async_copy(
            images_ref.at[sample_of(step)], image_buf.at[slot], image_sem.at[slot]
        )

    fetch(0).start()
    others_all[col] = others_ref[...]
    words_all[col] = words_ref[...]
    for which in (1, 2):
        weight_start(which)
    products = jnp.zeros((8, channels), floats)

    def add_product(i, total):
        here = pl.ds(pl.multiple_of(i * 64, 64), 64)
        product = grad_ref[here, :].astype(floats) * conv_ref[here, :].astype(floats)
        return total + jnp.sum(product.reshape(8, 8, channels), axis=0)

    products = lax.fori_loop(0, tokens // 64, add_product, products)
    sums_out[...] = jnp.broadcast_to(jnp.sum(products, 0, keepdims=True), (8, channels))
    lax.fori_loop(1, count, lambda k, c: (sums_copy(k).start(), c)[1], 0)
    sums_in[row] = sums_out[...]
    acc[...] = jnp.zeros_like(acc)
    stats_ref[...] = jnp.zeros_like(stats_ref)
    stats_ref[3 * count :, :] = last_ref[...]
    for buffer in (padded_image, padded_grad):
        zeros = jnp.zeros((halo, buffer.shape[1]), halves)
        buffer[0:halo, :] = zeros
        buffer[halo + tokens : halo + tokens + halo, :] = zeros

    def sums_arrive(k, carry):
        origin = lax.rem(row - k + count, count)
        remote(
            sums_out, sums_in.at[origin], sums_send.at[k], sums_recv.at[k], (partner, col)
        ).wait_recv()
        return carry

    def fill(source):
        wide = source.astype(floats)
        place = lax.rem(lax.broadcasted_iota(jnp.int32, wide.shape, 0), width)
        here = slice(halo, halo + tokens)
        padded_image[here, 0:depth] = jnp.where(
            place == 0, 0.0, pltpu.roll(wide, 1, 0)
        ).astype(halves)
        padded_image[here, depth : 2 * depth] = source
        padded_image[here, 2 * depth : 3 * depth] = jnp.where(
            place == width - 1, 0.0, pltpu.roll(wide, tokens - 1, 0)
        ).astype(halves)

    centre = pl.ds(halo, tokens)

    def pixel_copy(step):
        return remote(
            pixel_out.at[lax.rem(step, 2)],
            pixel_in.at[step],
            pixel_send.at[step],
            pixel_recv.at[step],
            (row, near),
        )

    def line_copy(step):
        return remote(
            line_out.at[lax.rem(step, 2)],
            line_in.at[step],
            line_send.at[step],
            line_recv.at[step],
            (row, far),
        )

    def owner_copy(step):
        return remote(
            owner_out.at[lax.rem(step, 2)],
            image_grad_ref.at[row],
            owner_send.at[step],
            owner_recv.at[row],
            (sample_of(step), col),
        )

    def work(step):
        paired, k = turn_of(step)
        sample = sample_of(step)

        @pl.when(paired)
        def _():
            block = grads_ref.at[sample]
            remote(block, block, pair_send.at[k], pair_recv.at[k], (partner, col)).wait_recv()

        distance = lax.div(step + 1, 2)
        odd = lax.rem(step, 2) == 1

        @pl.when(odd & (distance <= reach))
        def _():
            relay(2 * distance - 1)
            relay(2 * distance)

        @pl.when(odd & (distance > reach) & (distance <= groups - 1 - reach))
        def _():
            relay(distance + reach)

        load = pltpu.make_async_copy(
            grads_ref.at[sample], padded_grad.at[centre, :], load_sem
        )
        load.start()
        fetch(step).wait()

        @pl.when(step + 1 < count)
        def _():
            fetch(step + 1).start()

        fill(image_buf[lax.rem(step, 2)])
        load.wait()
        turned[...] = jnp.transpose(padded_grad[centre, :])
        slot = lax.rem(step, 2)

        @pl.when(step >= 2)
        def _():
            pixel_copy(step - 2).wait_send()

        def through(target):
            start = pl.multiple_of(target * rows, rows)
            total = jnp.zeros((rows, 3 * depth), floats)
            for a in range(3):
                window = padded_grad[pl.ds(pl.multiple_of(start + (2 - a) * width, 16), rows), :]
                taps = kernel_ref[sample, 3 * a : 3 * a + 3].reshape(3 * depth, channels)
                total = total + mul_nt(window, taps)
            place = lax.rem(lax.broadcasted_iota(jnp.int32, (rows, depth), 0), width)
            after = pltpu.roll(total[:, 0:depth], rows - 1, 0)
            before = pltpu.roll(total[:, 2 * depth : 3 * depth], 1, 0)
            return (
                total[:, depth : 2 * depth]
                + jnp.where(place == width - 1, 0.0, after)
                + jnp.where(place == 0, 0.0, before)
            )

        def give(i):
            pixel_out[slot, i] = through(jnp.where(i == 0, near, cross)).astype(halves)

        def keep(i):
            kept[slot, i] = through(jnp.where(i == 0, col, far))

        loop(2, give)
        pixel_copy(step).start()
        loop(2, keep)
        style = styles_ref[sample]
        scale = style[0:1, :depth]
        first, second = style[1:2, 0:1], style[2:3, 0:1]
        both = jnp.concatenate(
            [
                jnp.broadcast_to(inverse_ref[pl.ds(sample, 1), :], (8, channels)),
                sums_in[sample],
            ],
            axis=0,
        )
        columns = jnp.transpose(both)
        inverse, total = columns[:, 0:1], columns[:, 8:9]
        factor = inverse * inverse * total
        by_scale = jnp.zeros((1, depth), floats)
        by_first = jnp.zeros((1, depth), floats)
        by_second = jnp.zeros((1, depth), floats)
        for a in range(3):
            three = mul(turned[...], padded_image[pl.ds(a * width, tokens), :])
            for b in range(3):
                tap = 3 * a + b
                found = three[:, b * depth : (b + 1) * depth]
                one, two = bank_ref[0, tap].astype(floats), bank_ref[1, tap].astype(floats)
                selected = first * one + second * two
                modded = inverse * found - factor * (selected * scale)
                by_scale = by_scale + jnp.sum(modded * selected, 0, keepdims=True)
                grad_selected = modded * scale
                acc[0, tap] += first * grad_selected
                acc[1, tap] += second * grad_selected
                by_first = by_first + jnp.sum(grad_selected * one, 0, keepdims=True)
                by_second = by_second + jnp.sum(grad_selected * two, 0, keepdims=True)
        for k, line in enumerate((by_scale, by_first, by_second)):
            stats_ref[pl.ds(k * count + sample, 1), :depth] = line

    def across(step):
        slot = lax.rem(step, 2)
        pixel_copy(step).wait_recv()

        @pl.when(step >= 2)
        def _():
            line_copy(step - 2).wait_send()

        line_out[slot] = (kept[slot, 1] + pixel_in[step, 1].astype(floats)).astype(halves)
        line_copy(step).start()
        kept_own[slot] = kept[slot, 0] + pixel_in[step, 0].astype(floats)

    def home(step):
        slot = lax.rem(step, 2)
        line_copy(step).wait_recv()

        @pl.when(step >= 3)
        def _():
            owner_copy(step - 2).wait_send()

        owner_out[slot] = (kept_own[slot] + line_in[step].astype(floats)).astype(halves)

        @pl.when(step > 0)
        def _():
            owner_copy(step).start()

        @pl.when(step == 0)
        def _():
            mine = pltpu.make_async_copy(owner_out.at[slot], image_grad_ref.at[row], local_sem)
            mine.start()
            mine.wait()

    lax.fori_loop(1, count, sums_arrive, 0)

    own.wait()
    for load in loads:
        load.wait()

    def turn_bank(index):
        i, j = lax.div(index, 9), lax.rem(index, 9)
        bank_ref[i, j] = jnp.transpose(bank_raw[i, j].astype(floats)).astype(halves)

    loop(18, turn_bank)

    def step_body(step):
        @pl.when(step == 2)
        def _():
            for which in (1, 2):
                weight_pass(which)

        @pl.when(step == count - 2)
        def _():
            lax.fori_loop(1, groups, lambda k, c: (attention_copy(k).start(), c)[1], 0)

        @pl.when(step < count)
        def _():
            work(step)

        @pl.when(step == count)
        def _():
            for turn in range(3):
                group_copy(turn, *stats_group).start()

        @pl.when((step >= 1) & (step <= count))
        def _():
            across(step - 1)

        @pl.when(step >= 2)
        def _():
            home(step - 2)

    loop(count + 2, step_body)
    lax.fori_loop(1, groups, lambda k, c: (attention_copy(k).wait(), c)[1], 0)
    attention_total = attention_ref[level].astype(floats)
    for k in range(1, groups):
        attention_total = attention_total + attention_in[k].astype(floats)
    attention_all[col] = attention_total.astype(halves)
    weight_start(0)
    stats_sum[...] = group_sum(*stats_group)
    far_start(*stats_far)

    def write(index):
        bank_grad_ref[lax.div(index, 9), lax.rem(index, 9)] = jnp.transpose(
            acc[lax.div(index, 9), lax.rem(index, 9)]
        )

    loop(18, write)

    def owner_arrives(k, carry):
        origin = lax.rem(row - k + count, count)
        remote(
            owner_out.at[0],
            image_grad_ref.at[origin],
            owner_send.at[k],
            owner_recv.at[origin],
            (partner, col),
        ).wait_recv()
        return carry

    lax.fori_loop(1, count, owner_arrives, 0)
    weight_pass(0)
    far_end(*stats_far)
    for which in (1, 2, 0):
        weight_end(which)
    for step in (count - 2, count - 1):
        pixel_copy(step).wait_send()
        line_copy(step).wait_send()
        owner_copy(step).wait_send()

    def sent(origin):
        @pl.when((origin <= level) & has_above)
        def _():
            line_block(origin, True).wait_send()

        @pl.when((origin >= level) & has_below)
        def _():
            line_block(origin, False).wait_send()

    loop(groups, sent)
    loop(groups, lambda k: pair_copy(k).wait_send())
    lax.fori_loop(1, count, lambda k, c: (sums_copy(k).wait_send(), c)[1], 0)


def conv_backward(images_all, kernels, bank, styles, inverse, grad, conv, owned, last, width):
    attention, others, words = owned
    count, tokens, depth = images_all.shape
    channels = grad.shape[1]
    rows = tokens // PIX
    groups = count // 2
    piece = (rows, depth)
    return pl.pallas_call(
        partial(conv_back_kernel, count, width),
        out_shape=(
            jax.ShapeDtypeStruct((2, 9, depth, channels), floats),
            jax.ShapeDtypeStruct((PIX,) + attention.shape[1:], halves),
            jax.ShapeDtypeStruct((PIX,) + others.shape, halves),
            jax.ShapeDtypeStruct((PIX,) + words.shape, halves),
            jax.ShapeDtypeStruct((count, 3 * count + 8, 128), floats),
            jax.ShapeDtypeStruct((count,) + piece, halves),
            jax.ShapeDtypeStruct((count, tokens, channels), halves),
        ),
        in_specs=[ANY] * 3 + [VMEM] * 8,
        out_specs=(VMEM,) * 4 + (ANY,) * 3,
        scratch_shapes=[
            pltpu.VMEM(kernels.shape, halves),
            pltpu.VMEM((2, 9, channels, depth), halves),
            pltpu.VMEM(bank.shape, halves),
            DMA((2,)),
            pltpu.VMEM((3 * count + 8, 128), floats),
            pltpu.VMEM((4, 3 * count + 8, 128), floats),
            pltpu.VMEM((3 * count + 8, 128), floats),
            pltpu.VMEM((2, tokens, depth), halves),
            pltpu.VMEM((tokens + 2 * width, 3 * depth), halves),
            pltpu.VMEM((tokens + 2 * width, channels), halves),
            pltpu.VMEM((channels, tokens), halves),
            pltpu.VMEM((2, 9, channels, depth), floats),
            pltpu.VMEM((8, channels), floats),
            pltpu.VMEM((count, 8, channels), floats),
            pltpu.VMEM((2, 2) + piece, floats),
            pltpu.VMEM((2,) + piece, floats),
            pltpu.VMEM((2, 2) + piece, halves),
            pltpu.VMEM((count, 2) + piece, halves),
            pltpu.VMEM((2,) + piece, halves),
            pltpu.VMEM((count,) + piece, halves),
            pltpu.VMEM((2,) + piece, halves),
            pltpu.VMEM(attention.shape, halves),
            DMA,
            DMA((2,)),
            DMA,
            DMA((count,)),
            DMA((count,)),
            DMA((groups,)),
            DMA((groups,)),
            DMA((groups,)),
            DMA((groups,)),
            DMA((groups,)),
            DMA((count,)),
            DMA((count,)),
            DMA((count,)),
            DMA((count,)),
            DMA((count,)),
            DMA((count,)),
            DMA((groups,)),
            DMA((groups,)),
            DMA((9,)),
            DMA((9,)),
            DMA((3,)),
            DMA((3,)),
            DMA((count,)),
            DMA((count,)),
            DMA,
        ],
        compiler_params=params(4),
        name="conv_backward",
    )(
        images_all,
        kernels,
        bank,
        styles,
        inverse,
        grad,
        conv,
        attention,
        others,
        words,
        last,
    )


def prepare_kernel(
    styled_ref,
    label_ref,
    select_ref,
    modulation_ref,
    rgb_modulation_ref,
    images_ref,
    query_ref,
    key_ref,
    value_ref,
    out_ref,
    cross_query_ref,
    cross_out_ref,
    text_key_ref,
    text_value_ref,
    attention_ref,
    others_ref,
    style_ref,
    rgb_scale_ref,
    parts_ref,
):
    col = lax.axis_index("pix")
    count, rows, depth = parts_ref.shape
    width = attention_ref.shape[1] // 5
    short = text_key_ref.shape[0]
    mine = pl.ds(pl.multiple_of(col * width, width), width)
    for k, source in enumerate((query_ref, key_ref, value_ref)):
        attention_ref[:, k * width : (k + 1) * width] = source[:, mine]
    attention_ref[:, 3 * width :] = jnp.zeros((attention_ref.shape[0], 2 * width), halves)
    for k, source in enumerate((text_key_ref, text_value_ref)):
        attention_ref[0:short, (3 + k) * width : (4 + k) * width] = source[:, mine]
    for k, source in enumerate((out_ref, cross_query_ref, cross_out_ref)):
        others_ref[:, k * width : (k + 1) * width] = source[:, mine]
    styled = styled_ref[...]
    logits = jnp.sum(styled * select_ref[...].astype(floats), -1, keepdims=True)
    first, second = logits[0:1], logits[1:2]
    largest = jnp.maximum(first, second)
    first, second = jnp.exp(first - largest), jnp.exp(second - largest)
    total = first + second
    eight = jnp.broadcast_to(styled, (8, styled.shape[1]))

    def through(matrix):
        return exact(mul, eight, matrix[...]) + 1.0

    scaling = through(modulation_ref)
    rgb_scale_ref[...] = through(rgb_modulation_ref)[0:1]
    same = jnp.concatenate(
        [jnp.broadcast_to(first / total, (1, 128)), jnp.broadcast_to(second / total, (1, 128))]
        + [styled[:, k * 128 : (k + 1) * 128] for k in range(4)]
        + [jnp.full((1, 128), label_ref[0, 0].astype(floats))],
        axis=0,
    )
    for d in range(count):
        lanes = slice(d * depth, (d + 1) * depth)
        style_ref[d, 0:1, :] = jnp.zeros((1, 128), floats)
        style_ref[d, 0:1, 0:depth] = scaling[0:1, lanes]
        style_ref[d, 1:8, :] = same
        parts_ref[d] = images_ref[:, lanes]


def prepare(styled, label, select_rows, modulation, rgb_modulation, images, weights, count):
    rows, channels = images.shape
    owned, quarter = weights[0].shape[0], channels // PIX
    return pl.pallas_call(
        prepare_kernel,
        out_shape=(
            jax.ShapeDtypeStruct((owned, 5 * quarter), halves),
            jax.ShapeDtypeStruct((owned, 3 * quarter), halves),
            jax.ShapeDtypeStruct((count, 8, 128), floats),
            jax.ShapeDtypeStruct((1, channels), floats),
            jax.ShapeDtypeStruct((count, rows, channels // count), halves),
        ),
        in_specs=[VMEM, pl.BlockSpec(memory_space=pltpu.SMEM)] + [VMEM] * 12,
        out_specs=(VMEM,) * 5,
        compiler_params=pltpu.CompilerParams(vmem_limit_bytes=VMEM_LIMIT),
        name="prepare",
    )(styled, label, select_rows, modulation, rgb_modulation, images, *weights)


def finish_kernel(
    rows_ref,
    stats_ref,
    styles_ref,
    select_ref,
    modulation_ref,
    rgb_modulation_ref,
    attention_ref,
    others_ref,
    words_ref,
    grad_one_ref,
    image_parts_ref,
    grad_query_ref,
    grad_key_ref,
    grad_value_ref,
    grad_out_ref,
    grad_cross_query_ref,
    grad_cross_out_ref,
    grad_text_key_ref,
    grad_text_value_ref,
    grad_image_ref,
    grad_style_ref,
    grad_table_ref,
    grad_select_ref,
    grad_modulation_ref,
    grad_rgb_ref,
    gain_self_ref,
    gain_cross_ref,
    rgb_weight_ref,
    scaling,
    styles_grad,
):
    row = lax.axis_index("dp")
    count, rows, depth = image_parts_ref.shape
    width = words_ref.shape[2] // 2
    for d in range(count):
        lanes = slice(d * depth, (d + 1) * depth)
        grad_image_ref[:, lanes] = grad_one_ref[:, lanes] + image_parts_ref[d].astype(floats)
        scaling[:, lanes] = stats_ref[d, 0:count, 0:depth]
    for k, out in enumerate((grad_query_ref, grad_key_ref, grad_value_ref)):
        for p in range(2 * PIX):
            first = 3 * width + k * 128 if p % 2 == 0 else k * 128
            source = others_ref if p % 2 == 0 else attention_ref
            out[:, p * 128 : (p + 1) * 128] = source[p // 2, :, first : first + 128].astype(floats)
    for buffer, outs in (
        (others_ref, (grad_out_ref, grad_cross_query_ref, grad_cross_out_ref)),
        (words_ref, (grad_text_key_ref, grad_text_value_ref)),
    ):
        for k, out in enumerate(outs):
            for p in range(PIX):
                block = buffer[p, :, k * width : (k + 1) * width].astype(floats)
                out[:, p * width : (p + 1) * width] = block[: out.shape[0]]
    sums = rows_ref[0]
    for d in range(1, count):
        sums = sums + rows_ref[d]
    total = stats_ref[0, 3 * count :, :]
    for d in range(1, count):
        total = total + stats_ref[d, 3 * count :, :]
    gain_self_ref[...] = total
    gain_cross_ref[...] = sums[0:1]
    rgb_weight_ref[...] = sums[2:5]
    mixing, grads = [], []
    for k in (1, 2):
        total = stats_ref[0, k * count : (k + 1) * count, :]
        for d in range(1, count):
            total = total + stats_ref[d, k * count : (k + 1) * count, :]
        grads.append(jnp.sum(total, -1, keepdims=True))
        mixing.append(styles_ref[:, k, :][:, 0:1])
    inner = grads[0] * mixing[0] + grads[1] * mixing[1]
    logits = [m * (g - inner) for m, g in zip(mixing, grads)]
    styled = jnp.concatenate([styles_ref[:, 3 + k, :] for k in range(4)], axis=1)
    rgb = rows_ref[:, 1, :]
    grad_modulation_ref[...] = outer_sum(styled, scaling[...])
    grad_rgb_ref[...] = outer_sum(styled, rgb)
    place = lax.broadcasted_iota(jnp.int32, (count, 128), 1)
    both = jnp.where(place == 0, logits[0], jnp.where(place == 1, logits[1], 0.0))
    grad_select_ref[...] = outer_sum(both, styled)[0:2]
    select = select_ref[...].astype(floats)
    grad_styles = (
        exact(mul_nt, scaling[...], modulation_ref[...])
        + exact(mul_nt, rgb, rgb_modulation_ref[...])
        + logits[0] * select[0:1]
        + logits[1] * select[1:2]
    )
    styles_grad[...] = grad_styles
    grad_style_ref[...] = styles_grad[pl.ds(row, 1), :]
    label = styles_ref[:, 7, :][:, 0:1].astype(jnp.int32)
    classes = grad_table_ref.shape[0]
    chosen = lax.broadcasted_iota(jnp.int32, (count, classes), 1) == label
    chosen = chosen.astype(floats).astype(halves)
    grad_table_ref[...] = mul_tn(
        jnp.concatenate([chosen] * 3, axis=0),
        jnp.concatenate(split(grad_styles)[::-1], axis=0),
    )


def finish(
    all_rows,
    all_stats,
    styles,
    select_rows,
    modulation,
    rgb_modulation,
    gathered,
    grad_one,
    image_parts,
    classes,
    text_rows,
):
    count = styles.shape[0]
    rows, channels = grad_one.shape
    owned = gathered[0].shape[1]
    wide = modulation.shape[0]

    def out(*shape):
        return jax.ShapeDtypeStruct(shape, floats)

    return pl.pallas_call(
        finish_kernel,
        out_shape=(out(owned, channels),) * 6
        + (out(text_rows, channels),) * 2
        + (
            out(rows, channels),
            out(1, wide),
            out(classes, wide),
            out(2, wide),
            out(wide, channels),
            out(wide, channels),
            out(8, channels // 8),
            out(1, channels),
            out(3, channels),
        ),
        in_specs=[VMEM] * 11,
        out_specs=(VMEM,) * 17,
        scratch_shapes=[pltpu.VMEM((count, channels), floats), pltpu.VMEM((count, wide), floats)],
        compiler_params=pltpu.CompilerParams(vmem_limit_bytes=VMEM_LIMIT),
        name="finish",
    )(
        all_rows,
        all_stats,
        styles,
        select_rows,
        modulation,
        rgb_modulation,
        *gathered,
        grad_one,
        image_parts,
    )


def on_device(
    images,
    style_codes,
    labels,
    token_ids,
    penalty_mask,
    class_table,
    text_table,
    conv_bank,
    select_weight,
    modulation,
    rgb_modulation,
    w_query,
    w_key,
    w_value,
    w_out,
    c_query,
    c_key,
    c_value,
    c_out,
    gain_self,
    gain_cross,
    rgb_weight,
    out_cotangent,
    rgb_cotangent,
):
    count = lax.axis_size("dp")
    _, height, width, channels = images.shape
    rows = height * width
    quarter = channels // PIX
    depth = channels // count

    owned, text_owned = w_query.shape[0], c_key.shape[0]
    class_row = jnp.take(class_table, labels, axis=0).astype(floats)
    styled = style_codes.astype(floats) + class_row
    label = labels.reshape(1, 1)
    select_rows = select_weight.T
    own = images.reshape(rows, channels)
    attention, others, style, rgb_scale, parts = prepare(
        styled,
        label,
        select_rows,
        modulation,
        rgb_modulation,
        own,
        (w_query, w_key, w_value, w_out, c_query, c_out, c_key, c_value),
        count,
    )
    attention = lax.all_gather(attention, "dp", axis=0, tiled=True)
    others = lax.all_gather(others, ("pix", "dp"), axis=0, tiled=True)
    others = others.reshape(PIX, channels, 3 * quarter)
    bank = conv_bank.reshape(2, 9, depth, quarter)
    words = token_ids.shape[1]
    text = jnp.take(text_table, token_ids[0], axis=0)
    text = text.reshape(words, count, text_owned)
    text = jnp.pad(text, ((0, 128 - words), (0, 0), (0, owned - text_owned)))
    text = text.reshape(128, channels)

    images_all, kernels, styles, inverse = gather_inputs(style, bank, parts)
    images_all = images_all.reshape(count, PIX * rows, depth)
    conv, conv_own, hidden_one, normed_one = conv_forward(images_all, kernels, own, gain_self, width)
    query, key, value, totals, attended, text_all = attend_forward(
        normed_one, attention, text
    )
    rgb_rows = jnp.pad(rgb_cotangent.reshape(3, rows).T, ((0, 0), (0, 125)))
    penalty = jnp.broadcast_to(penalty_mask.astype(floats).reshape(1, 1), (1, 128))
    (
        output,
        rgb,
        reduced,
        text_grads,
        grad_two,
        grad_attended,
        small,
        *factors,
    ) = cross_part(
        words,
        attended,
        hidden_one,
        others,
        text_all,
        gain_cross,
        rgb_scale,
        jnp.pad(rgb_weight, ((0, 0), (0, 125))),
        out_cotangent.reshape(rows, channels),
        rgb_rows,
        penalty,
    )
    (
        attention_grads,
        others_owned,
        words_owned,
        grad_one,
        grad_conv,
        last,
        all_rows,
    ) = attend_backward(
        words,
        small,
        grad_attended,
        query,
        key,
        value,
        totals,
        normed_one,
        attention,
        hidden_one,
        conv,
        grad_two,
        gain_self,
        text,
        text_grads,
        reduced.reshape(count // 2, 2, owned, quarter),
        *factors,
    )

    bank_grad, *gathered, all_stats, image_parts, _ = conv_backward(
        images_all,
        kernels,
        bank,
        styles,
        inverse,
        grad_conv.reshape(PIX * rows, quarter),
        conv_own,
        (attention_grads, others_owned, words_owned),
        last,
        width,
    )
    (
        grad_w_query,
        grad_w_key,
        grad_w_value,
        grad_w_out,
        grad_c_query,
        grad_c_out,
        grad_c_key,
        grad_c_value,
        grad_image,
        grad_style,
        grad_table,
        grad_select,
        grad_modulation,
        grad_rgb_modulation,
        grad_gain_self,
        grad_gain_cross,
        grad_rgb_weight,
    ) = finish(
        all_rows,
        all_stats,
        styles,
        select_rows,
        modulation,
        rgb_modulation,
        gathered,
        grad_one,
        image_parts,
        class_table.shape[0],
        text_owned,
    )
    shape = images.shape
    return (
        output.reshape(shape),
        rgb[:, :3].T.reshape(1, 3, height, width),
        grad_image.reshape(shape),
        grad_style,
        grad_table,
        bank_grad.reshape(conv_bank.shape),
        grad_select.T,
        grad_modulation,
        grad_rgb_modulation,
        grad_w_query,
        grad_w_key,
        grad_w_value,
        grad_w_out,
        grad_c_query,
        grad_c_key,
        grad_c_value,
        grad_c_out,
        grad_gain_self.reshape(-1),
        grad_gain_cross.reshape(-1),
        grad_rgb_weight.T,
    )


def solution(mesh):
    return jax.shard_map(
        on_device,
        mesh=mesh,
        in_specs=(
            P("dp", "pix", None, None),
            P("dp", None),
            P("dp"),
            P("dp", None),
            P("dp"),
            P(),
            P(),
            P(None, None, None, "dp", "pix"),
            P(),
            P(),
            P(),
            P("dp", None),
            P("dp", None),
            P("dp", None),
            P("dp", None),
            P("dp", None),
            P("dp", None),
            P("dp", None),
            P("dp", None),
            P(),
            P(),
            P(),
            P("dp", "pix", None, None),
            P("dp", None, "pix", None),
        ),
        out_specs=(
            P("dp", "pix", None, None),
            P("dp", None, "pix", None),
            P("dp", "pix", None, None),
            P("dp", None),
            P(),
            P(None, None, None, "dp", "pix"),
            P(),
            P(),
            P(),
            P("dp", None),
            P("dp", None),
            P("dp", None),
            P("dp", None),
            P("dp", None),
            P("dp", None),
            P("dp", None),
            P("dp", None),
            P(),
            P(),
            P(),
        ),
        check_vma=False,
    )
```
